32 devices in a mesh: dp: 2 (over y), context: 4 (over z), tensor: 4 (over x, core).
Axes of the slice: x: 2, y: 2, z: 4, core: 2. Of those that a mesh axis runs over, the one named last changes fastest.
Arguments:
- hidden_in: bfloat16 [2, 4, 1024, 768], P(None, 'dp', 'context'), may hold values from -6 to 6
- segment_ids: int32 [2, 4, 1024], P(None, 'dp'), may hold values from 0 to 17, as said below
- norm_gain: float32 [768], replicated, may hold values from 0.5 to 1.5
- head_projection: bfloat16 [768, 2, 1536], P(('dp', 'context'), None, 'tensor'), may hold values from -0.21875 to 0.21875
- shared_projection: bfloat16 [768, 256], P(('dp', 'context')), may hold values from -0.21875 to 0.21875
- step_projection: bfloat16 [768, 24], P(('dp', 'context'), 'tensor'), may hold values from -0.21875 to 0.21875
- conv_heads: float32 [4, 1536], P(None, 'tensor'), may hold values from -3 to 3
- bias_heads: float32 [1536], P('tensor'), may hold values from -0.5 to 0.5
- conv_shared: float32 [4, 256], replicated, may hold values from -3 to 3
- bias_shared: float32 [256], replicated, may hold values from -0.5 to 0.5
- step_bias: float32 [24], P('tensor'), may hold values from -7 to -4
- log_decay: float32 [24], P('tensor'), may hold values from 0 to 1.5
- skip_gain: float32 [24], P('tensor'), may hold values from 0.5 to 1.5
- gate_gain: float32 [1536], P('tensor'), may hold values from 0.5 to 1.5
- output_weight: bfloat16 [1536, 768], P('tensor', ('dp', 'context')), may hold values from -0.15625 to 0.15625
- out_cotangent: bfloat16 [2, 4, 1024, 768], P(None, 'dp', 'context'), may hold values from -6 to 6
Outputs:
- block_out: bfloat16 [2, 4, 1024, 768], P(None, 'dp', 'context')
- input_grad: bfloat16 [2, 4, 1024, 768], P(None, 'dp', 'context')
- grad_norm_gain: float32 [768], replicated
- grad_proj_heads: float32 [768, 2, 1536], P(('dp', 'context'), None, 'tensor')
- grad_proj_shared: float32 [768, 256], P(('dp', 'context'), 'tensor')
- grad_proj_step: float32 [768, 24], P(('dp', 'context'), 'tensor')
- grad_conv_heads: float32 [4, 1536], P(None, 'tensor')
- grad_bias_heads: float32 [1536], P('tensor')
- grad_conv_shared: float32 [4, 256], replicated
- grad_bias_shared: float32 [256], replicated
- grad_step_bias: float32 [24], P('tensor')
- grad_log_decay: float32 [24], P('tensor')
- grad_skip_gain: float32 [24], P('tensor')
- grad_gate_gain: float32 [1536], P('tensor')
- grad_out_weight: float32 [1536, 768], P('tensor', ('dp', 'context'))
The draws below stay inside these ranges and needn't reach their ends.
Inputs may be any that keep to these rules, and one draw needn't show every extreme that they name: `segment_ids`: in each row segment numbers start at 0, never fall and rise by one at each document boundary.
All inputs are finite; a program needn't handle non-finite values.
Results may differ from the reference program's by a relative error of at most 0.014.
Values may be sent and summed in bfloat16 or wider, within the bound.
A program may use at most 128 MiB of HBM per device.

```python
import math
import jax
import jax.numpy as jnp
from jax import lax

D = 768
HEADS = 24
HEAD_DIM = 64
STATE = 128
KERNEL = 4
INNER = 1536
SEQ_MIN = 1024
MICRO = 2
SEQ_DEV = 2
BATCH = 4
TOK_CTX = 256


def draw_segment_ids(key, part):
    key = jax.random.fold_in(key, 11)
    length = SEQ_MIN
    shortest = max(KERNEL, 60 * length // 1024)
    longest = max(shortest + 1, 800 * length // 1024)
    number = length // shortest + 1
    rowcount = MICRO * BATCH
    keys = jax.random.split(key, 5)
    lengths = jax.random.randint(keys[0], (rowcount, number), shortest, longest + 1)
    endings = jnp.cumsum(lengths, axis=1)
    places = jnp.arange(length, dtype=jnp.int32)
    regular = jnp.sum((endings[:, None, :] <= places[None, :, None]).astype(jnp.int32), axis=2)
    opening = jax.random.randint(keys[1], (rowcount, 1), 1, TOK_CTX)
    closing = jax.random.randint(keys[2], (rowcount, 1), length - TOK_CTX + 1, length)
    choose = jax.random.randint(keys[3], (rowcount, 2), 0, 2)
    choose = choose.at[0].set(1)
    spanning = (places[None, :] >= opening).astype(jnp.int32) * choose[:, :1] + (places[None, :] >= closing).astype(jnp.int32) * choose[:, 1:]
    blocks = rowcount // SEQ_DEV
    chosen = jax.random.randint(keys[4], (blocks, 1), 0, SEQ_DEV)
    picked = (jnp.arange(SEQ_DEV)[None, :] == chosen).reshape(rowcount)
    result = jnp.where(picked[:, None], spanning, regular)
    dense_row = (chosen[0, 0] + 1) % SEQ_DEV
    is_dense = (jnp.arange(rowcount) == dense_row) & (SEQ_DEV > 1)
    packed = (places // shortest).astype(jnp.int32)
    result = jnp.where(is_dense[:, None], packed[None, :], result)
    return result.reshape(MICRO, BATCH, length).astype(jnp.int32)


def levels(stream_key, dims, pieces, smallest, high):
    def one(dim, shards_of):
        steps = jax.random.uniform(jax.random.fold_in(jax.random.fold_in(stream_key, 6), dim), (shards_of,), jnp.float32, smallest / len(pieces), high / len(pieces))
        return jnp.repeat(jnp.exp(steps), dims[dim] // shards_of).reshape((-1,) + (1,) * (len(dims) - dim - 1))

    gain = one(*pieces[0])
    for cut in pieces[1:]:
        gain = gain * one(*cut)
    return gain


def scatter_about(stream_key, dims, scale, reach, cuts=(), kind=jnp.bfloat16):
    gain = levels(stream_key, dims, cuts, -0.22, 0.18) if cuts else 1.0
    values = jax.random.normal(stream_key, dims, jnp.float32) * scale * gain
    return jnp.minimum(jnp.maximum(values, -reach), reach).astype(kind)


def setup_inputs(seed: int = 0) -> dict:
    key_list = jax.random.split(jax.random.key(seed), 17)
    hidden_in = scatter_about(key_list[0], (MICRO, BATCH, SEQ_MIN, D), 1.0, 6.0, ((1, 2), (2, 4)))
    segment_ids = draw_segment_ids(jax.random.fold_in(key_list[16], 71), 0)
    norm_gain = jnp.clip(1.0 + 0.1 * jax.random.normal(key_list[2], (D,), jnp.float32), 0.5, 1.5)
    head_projection = scatter_about(key_list[3], (D, 2, INNER), D ** -0.5, 0.21875, ((0, 8), (2, 4)))
    shared_projection = scatter_about(key_list[4], (D, 2 * STATE), D ** -0.5, 0.21875, ((0, 8),))
    step_projection = scatter_about(key_list[5], (D, HEADS), D ** -0.5, 0.21875, ((0, 8), (1, 4)))
    conv_heads = scatter_about(key_list[6], (KERNEL, INNER), KERNEL ** -0.5, 3.0, ((1, 4),), jnp.float32)
    bias_heads = jnp.clip(jax.random.uniform(key_list[7], (INNER,), jnp.float32, -0.5, 0.5) * levels(key_list[7], (INNER,), ((0, 4),), -0.4, 0.0), -0.5, 0.5)
    conv_shared = scatter_about(key_list[8], (KERNEL, 2 * STATE), KERNEL ** -0.5, 3.0, (), jnp.float32)
    bias_shared = jnp.clip(jax.random.uniform(key_list[9], (2 * STATE,), jnp.float32, -0.5, 0.5), -0.5, 0.5)
    step_bias = jnp.clip(-7.0 + 3.0 * jax.random.uniform(key_list[10], (HEADS,), jnp.float32) ** levels(key_list[10], (HEADS,), ((0, 4),), -0.2, 0.2), -7.0, -4.0)
    log_decay = jnp.clip(1.5 * jax.random.uniform(key_list[11], (HEADS,), jnp.float32) ** levels(key_list[11], (HEADS,), ((0, 4),), -0.2, 0.2), 0.0, 1.5)
    skip_gain = jnp.clip(0.5 + 1.0 * jax.random.uniform(key_list[12], (HEADS,), jnp.float32) ** levels(key_list[12], (HEADS,), ((0, 4),), -0.2, 0.2), 0.5, 1.5)
    gate_gain = jnp.clip(1.0 + 0.1 * jax.random.normal(key_list[13], (INNER,), jnp.float32), 0.5, 1.5)
    output_weight = scatter_about(key_list[14], (INNER, D), INNER ** -0.5, 0.15625, ((0, 4), (1, 8)))
    out_cotangent = scatter_about(key_list[15], (MICRO, BATCH, SEQ_MIN, D), 1.0, 6.0, ((1, 2), (2, 4)))
    return dict(hidden_in=hidden_in, segment_ids=segment_ids, norm_gain=norm_gain, head_projection=head_projection, shared_projection=shared_projection, step_projection=step_projection, conv_heads=conv_heads, bias_heads=bias_heads, conv_shared=conv_shared, bias_shared=bias_shared, step_bias=step_bias, log_decay=log_decay, skip_gain=skip_gain, gate_gain=gate_gain, output_weight=output_weight, out_cotangent=out_cotangent)


EPS = 1e-05
HIGH_ACCURACY = lax.Precision.HIGHEST

@jax.custom_vjp
def reduced_precision(v):
    return lax.optimization_barrier(v.astype(jnp.bfloat16)).astype(jnp.float32)

@jax.custom_vjp
def reduced_backward(v):
    return v

def low_keep(v):
    return (reduced_precision(v), None)

def low_pass(kept, grad):
    return (grad,)

def back_keep(v):
    return (v, None)

def back_low(kept, grad):
    return (reduced_precision(grad),)
reduced_precision.defvjp(low_keep, low_pass)
reduced_backward.defvjp(back_keep, back_low)

def conv_ext(extended, kernel, offsets, seg_ext):
    margin = kernel.shape[0] - 1
    length = extended.shape[1] - margin
    current = seg_ext[:, margin:]
    summed = extended[:, margin:] * kernel[0] + offsets
    for lagging in range(1, margin + 1):
        anchor = margin - lagging
        linked = (seg_ext[:, anchor:anchor + length] == current).astype(jnp.float32)
        summed = summed + extended[:, anchor:anchor + length] * kernel[lagging] * linked[:, :, None]
    return summed

def ssd_local(heads_x, steps, decay_rate, b_matrix, c_matrix, segments, previous):
    length = segments.shape[1]
    growth = steps * decay_rate
    running = jnp.cumsum(growth, axis=1)
    places = jnp.arange(length)
    causal = places[:, None] >= places[None, :]
    linked = (segments[:, :, None] == segments[:, None, :]) & causal[None]
    by_head = jnp.swapaxes(running, 1, 2)
    spread = by_head[:, :, :, None] - by_head[:, :, None, :]
    masked = jnp.broadcast_to(linked[:, None], spread.shape)
    decays = jnp.where(masked, jnp.exp(jnp.where(masked, spread, 0.0)), 0.0)
    scores = jnp.einsum('stn,sun->stu', c_matrix, b_matrix, precision=HIGH_ACCURACY)
    weights = decays * scores[:, None] * jnp.swapaxes(steps, 1, 2)[:, :, None, :]
    inside = jnp.einsum('shtu,suhp->sthp', weights, heads_x, precision=HIGH_ACCURACY)
    carried = (segments == previous[:, None]).astype(jnp.float32)
    leading = jnp.exp(running) * carried[:, :, None]
    closing = (segments == segments[:, -1:]).astype(jnp.float32)
    trailing = jnp.exp(running[:, -1:, :] - running) * closing[:, :, None] * steps
    scaled_x = heads_x * trailing[..., None]
    fresh = jnp.einsum('suhp,sun->shpn', scaled_x, b_matrix, precision=HIGH_ACCURACY)
    return (inside, fresh, leading)

def apply_state(c_matrix, leading, state_in):
    readout = jnp.einsum('stn,shpn->sthp', c_matrix, state_in, precision=HIGH_ACCURACY)
    return readout * leading[..., None]

def ssd_sequence(heads_x, steps, decay_rate, b_matrix, c_matrix, segments):
    number, length = segments.shape
    blocks = length // TOK_CTX

    def split(values):
        return jnp.swapaxes(values.reshape((number, blocks, TOK_CTX) + values.shape[2:]), 0, 1)
    previous_all = jnp.pad(segments, ((0, 0), (1, 0)), constant_values=-1)[:, :length]
    previous_blocks = split(previous_all)[:, :, 0]

    def one_block(state, inputs):
        part_x, part_step, part_b, part_c, part_seg, part_prev = inputs
        inside, fresh, leading = ssd_local(part_x, part_step, decay_rate, part_b, part_c, part_seg, part_prev)
        output = inside + apply_state(part_c, leading, state)
        state = leading[:, -1, :, None, None] * state + fresh
        return (state, output)
    start_state = jnp.zeros((number, HEADS, HEAD_DIM, STATE), jnp.float32)
    _, outputs = lax.scan(jax.checkpoint(one_block), start_state, (split(heads_x), split(steps), split(b_matrix), split(c_matrix), split(segments), previous_blocks))
    return jnp.swapaxes(outputs, 0, 1).reshape(number, length, HEADS, HEAD_DIM)

def block_forward(params, hidden, segments):
    norm_gain, head_projection, shared_projection, step_projection, conv_heads, bias_heads, conv_shared, bias_shared, step_bias, log_decay, skip_gain, gate_gain, output_weight = params
    number, length, _ = hidden.shape
    rms_in = lax.rsqrt(lax.optimization_barrier(jnp.mean(hidden * hidden, axis=-1, keepdims=True)) + EPS)
    normalized_input = reduced_precision(hidden * rms_in * norm_gain)
    head_projection_out = reduced_backward(reduced_precision(jnp.einsum('yfz,zuo->yfuo', normalized_input, head_projection, precision=HIGH_ACCURACY)))
    shared_projection_out = reduced_backward(reduced_precision(jnp.einsum('tfn,no->tfo', normalized_input, shared_projection, precision=HIGH_ACCURACY)))
    unshaped_step = reduced_backward(reduced_precision(jnp.einsum('anp,py->any', normalized_input, step_projection, precision=HIGH_ACCURACY)))
    gate_in = head_projection_out[:, :, 0]
    channels = jnp.concatenate([head_projection_out[:, :, 1], shared_projection_out], axis=-1)
    margin = KERNEL - 1
    extended = jnp.pad(channels, ((0, 0), (margin, 0), (0, 0)))
    seg_ext = jnp.pad(segments, ((0, 0), (margin, 0)), constant_values=-1)
    kernel = jnp.concatenate([conv_heads, conv_shared], axis=1)
    offsets = jnp.concatenate([bias_heads, bias_shared])
    mixed = reduced_precision(jax.nn.silu(conv_ext(extended, kernel, offsets, seg_ext)))
    heads_x = mixed[..., :INNER].reshape(number, length, HEADS, HEAD_DIM)
    b_matrix = mixed[..., INNER:INNER + STATE]
    c_matrix = mixed[..., INNER + STATE:]
    steps = jax.nn.softplus(unshaped_step + step_bias)
    decay_rate = -jnp.exp(log_decay)
    ssd = ssd_sequence(heads_x, steps, decay_rate, b_matrix, c_matrix, segments) + skip_gain[:, None] * heads_x
    gated = ssd.reshape(number, length, INNER) * jax.nn.silu(gate_in)
    rms_gate = lax.rsqrt(lax.optimization_barrier(jnp.mean(gated * gated, axis=-1, keepdims=True)) + EPS)
    normalized_output = reduced_precision(gated * rms_gate * gate_gain)
    branch_result = jnp.einsum('xrm,mz->xrz', normalized_output, output_weight, precision=HIGH_ACCURACY)
    return hidden + branch_result

def reference(hidden_in, segment_ids, norm_gain, head_projection, shared_projection, step_projection, conv_heads, bias_heads, conv_shared, bias_shared, step_bias, log_decay, skip_gain, gate_gain, output_weight, out_cotangent):
    params = tuple((weight.astype(jnp.float32) for weight in (norm_gain, head_projection, shared_projection, step_projection, conv_heads, bias_heads, conv_shared, bias_shared, step_bias, log_decay, skip_gain, gate_gain, output_weight)))
    all_rows = MICRO * BATCH
    group = math.gcd(all_rows, max(1, 4096 // SEQ_MIN))
    hidden = hidden_in.astype(jnp.float32).reshape(all_rows // group, group, SEQ_MIN, D)
    output_adjoint = out_cotangent.astype(jnp.float32).reshape(all_rows // group, group, SEQ_MIN, D)
    segments = segment_ids.reshape(all_rows // group, group, SEQ_MIN)

    def one_group(carry, inputs):
        group_hidden, group_seg, group_cot = inputs
        result, pullback = jax.vjp(lambda weights, values: block_forward(weights, values, group_seg), params, group_hidden)
        grad_params, grad_hidden = pullback(group_cot)
        carry = jax.tree.map(jnp.add, carry, grad_params)
        return (carry, (result.astype(jnp.bfloat16), grad_hidden.astype(jnp.bfloat16)))
    zeros = jax.tree.map(jnp.zeros_like, params)
    sums, (results, grads) = lax.scan(one_group, zeros, (hidden, segments, output_adjoint))
    block_out = results.reshape(MICRO, BATCH, SEQ_MIN, D)
    input_grad = grads.reshape(MICRO, BATCH, SEQ_MIN, D)
    return (block_out, input_grad, sums[0], sums[1], sums[2], sums[3], sums[4], sums[5], sums[6], sums[7], sums[8], sums[9], sums[10], sums[11], sums[12])
```

```python
import functools
import types

import jax
import jax.numpy as jnp
from jax import lax
from jax.experimental import pallas as pl
from jax.experimental.pallas import tpu as pltpu
from jax.sharding import PartitionSpec as P

EPS = 1e-05
F32 = jnp.float32
BF16 = jnp.bfloat16
MESH = pl.DeviceIdType.MESH
LANES = 128
HALO = 16
EDGE = 8


def nn(a, b):
    return lax.dot_general(a, b, (((1,), (0,)), ((), ())), preferred_element_type=F32)


def nt(a, b):
    return lax.dot_general(a, b, (((1,), (1,)), ((), ())), preferred_element_type=F32)


def tn(a, b):
    return lax.dot_general(a, b, (((0,), (0,)), ((), ())), preferred_element_type=F32)


def pieces_of(value, count):
    pieces = []
    for _ in range(count):
        piece = value.astype(BF16)
        pieces.append(piece)
        value = value - piece.astype(F32)
    return pieces


def exact_left(ones, value):
    return sum(nn(ones, piece) for piece in pieces_of(value, 3))


def exact_right(value, ones):
    return sum(nn(piece, ones) for piece in pieces_of(value, 2))


def sigmoid(value):
    return 1.0 / (1.0 + jnp.exp(-value))


def iota(shape, dim):
    return lax.broadcasted_iota(jnp.int32, shape, dim)


def kernel(z, names, *refs):
    m = types.SimpleNamespace(**dict(zip(names, refs)))
    R, T, D, C, H, S = z.R, z.T, z.D, z.C, z.H, z.S
    rp, nd, nc, ntn = z.rp, z.nd, z.nc, z.ntn
    pairs = H // 2
    head = C // H
    V = C + S
    half = T // 2
    d, c, t = lax.axis_index("dp"), lax.axis_index("context"), lax.axis_index("tensor")
    odd = lax.rem(t, 2)
    across = t + 1 - 2 * odd
    far = lax.rem(t + 2, 4) if ntn == 4 else t

    def at_ctx(k):
        return lax.rem(c + k, nc)

    def at_dp(k):
        return lax.rem(d + k, nd)

    def at_ten(k):
        return lax.rem(t + k, ntn)

    def block(dd, cc):
        return pl.ds(pl.multiple_of((dd * nc + cc) * rp, 16), rp)

    def row(r):
        return pl.ds(pl.multiple_of(r * T, 16), T)

    def copy(src, dst, send, recv, dev):
        return pltpu.make_async_remote_copy(
            src_ref=src, dst_ref=dst, send_sem=send, recv_sem=recv, device_id=dev, device_id_type=MESH
        )

    barrier = pltpu.get_barrier_semaphore()
    peers = [(d, at_ctx(k), t) for k in range(1, nc)]
    peers += [(at_dp(k), c, t) for k in range(1, nd)]
    peers += [(d, c, at_ten(k)) for k in range(1, ntn)]
    for peer in peers:
        pl.semaphore_signal(barrier, inc=1, device_id=peer, device_id_type=MESH)
    pl.semaphore_wait(barrier, len(peers))

    wsrc, wall = (m.w0, m.w1), (m.wg0, m.wg1)

    def w_own(part):
        whole = wall[part].at[block(d, c)]
        out = []
        for k in range(1, nc):
            out.append(
                copy(wsrc[part], whole, m.w_send.at[part, k, 0], m.w_recv.at[part, d, c], (d, at_ctx(k), t))
            )
        for k in range(1, nd):
            out.append(
                copy(wsrc[part], whole, m.w_send.at[part, 0, k], m.w_recv.at[part, d, c], (at_dp(k), c, t))
            )
        return out

    def w_pass(part, j):
        cc = at_ctx(nc - j)
        whole = wall[part].at[block(d, cc)]
        return [
            copy(whole, whole, m.w_send.at[part, j, k], m.w_recv.at[part, d, cc], (at_dp(k), c, t))
            for k in range(1, nd)
        ]

    def w_arrived(part, dd, cc):
        whole = wall[part].at[block(dd, cc)]
        copy(wsrc[part], whole, m.w_send.at[part, 0, 0], m.w_recv.at[part, dd, cc], (d, c, t)).wait_recv()

    def w_relay(part):
        for j in range(1, nc):
            w_arrived(part, d, at_ctx(nc - j))
            for one in w_pass(part, j):
                one.start()

    def w_rest(part):
        for k in range(1, nd):
            for j in range(nc):
                w_arrived(part, at_dp(nd - k), at_ctx(nc - j))
        wall[part][block(d, c), :] = wsrc[part][...]

    def w_sent(part):
        for one in w_own(part):
            one.wait_send()
        for j in range(1, nc):
            for one in w_pass(part, j):
                one.wait_send()

    def halo_copy(r):
        return copy(
            m.hid.at[pl.ds(pl.multiple_of(r * T + T - HALO, 16), HALO)],
            m.hh.at[pl.ds(pl.multiple_of(r * HALO, 16), HALO)],
            m.h_send.at[r],
            m.h_recv.at[r],
            (d, c + 1, t),
        )

    for one in w_own(0):
        one.start()

    @pl.when(c < nc - 1)
    def _():
        for r in range(R):
            halo_copy(r).start()

    gain_in = m.ng[0:1, :]

    def normalize(u):
        u = u.astype(F32)
        mean = jnp.sum(u * u, axis=-1, keepdims=True) * (1.0 / z.d_true)
        return (u * lax.rsqrt(mean + EPS)) * gain_in

    @pl.loop(0, R)
    def _(r):
        value = normalize(m.hid[row(r), :]).astype(BF16)
        m.nrm[row(r), :] = value
        m.nrmt[:, row(r)] = jnp.transpose(value)
        m.cott[:, row(r)] = jnp.transpose(m.cot[row(r), :])

    w_relay(0)
    for one in w_own(1):
        one.start()

    @pl.when(c == 0)
    def _():
        m.hh[...] = jnp.zeros_like(m.hh)
        m.sin[...] = jnp.zeros_like(m.sin)

    @pl.when(c == nc - 1)
    def _():
        m.gin[...] = jnp.zeros_like(m.gin)
        m.dce[...] = jnp.zeros_like(m.dce)

    m.sm[t] = jnp.zeros((8, z.WL), F32)
    m.drow[...] = jnp.zeros_like(m.drow)
    m.tot[...] = jnp.zeros_like(m.tot)

    @pl.when(c > 0)
    def _():
        for r in range(R):
            halo_copy(r).wait_recv()

    m.nrmh[...] = normalize(m.hh[...]).astype(BF16)
    w_rest(0)

    def rounded(value):
        return value.astype(BF16).astype(F32)

    halo_v = rounded(nn(m.nrmh[...], m.wg0[:, :V]))
    for r in range(R):
        m.vext[r, 0:EDGE, :] = halo_v[r * HALO + HALO - EDGE : (r + 1) * HALO]

    low_lanes = iota((T, LANES), 1) < head
    lane = iota((T, LANES), 1)
    lower = (iota((T, T), 0) >= iota((T, T), 1)).astype(BF16)
    upper = (iota((T, T), 0) <= iota((T, T), 1)).astype(BF16)
    fold = (iota((C, LANES), 0) // head == iota((C, LANES), 1)).astype(BF16)

    def spread(values):
        return jnp.concatenate(
            [
                jnp.where(low_lanes, values[:, 2 * p : 2 * p + 1], values[:, 2 * p + 1 : 2 * p + 2])
                for p in range(pairs)
            ],
            axis=1,
        )

    def state_copy(r):
        return copy(m.ssend.at[r], m.sin.at[r], m.s_send.at[r], m.s_recv.at[r], (d, c + 1, t))

    def grad_copy(r):
        return copy(m.gsend.at[r], m.gin.at[r], m.g_send.at[r], m.g_recv.at[r], (d, c - 1, t))

    def edge_copy(r):
        return copy(m.dconv.at[r, pl.ds(0, EDGE)], m.dce.at[r], m.e_send.at[r], m.e_recv.at[r], (d, c - 1, t))

    def leads(r):
        run = m.run[row(r), :]
        seg = m.segc[row(r), :]
        last = run[T - 1 : T, :]
        lead = jnp.exp(run) * seg[:, 6:7]
        trail = jnp.exp(last - run) * seg[:, 7:8]
        return lead, trail

    @pl.loop(0, R)
    def _(r):
        acc = nn(m.nrm[row(r), :], m.wg0[...])
        m.vext[r, pl.ds(EDGE, T), :] = rounded(acc[:, :V])
        raw = rounded(acc[:, V : V + LANES])
        seg = m.segc[row(r), :]
        for a in range(0, V, LANES):
            part = slice(a, a + LANES)
            conv = m.vext[r, pl.ds(EDGE, T), part] * m.par[0:1, part] + m.par[4:5, part]
            for j in range(1, z.K):
                conv = conv + m.vext[r, pl.ds(EDGE - j, T), part] * m.par[j : j + 1, part] * seg[:, j - 1 : j]
            logistic = sigmoid(conv)
            m.mix[row(r), part] = (conv * logistic).astype(BF16)
            m.slope[row(r), part] = logistic * (1.0 + conv * (1.0 - logistic))
        pre = raw + m.par[7:8, :LANES]
        step = jnp.maximum(pre, 0.0) + jnp.log1p(jnp.exp(-jnp.abs(pre)))
        m.pre[row(r), :] = pre
        m.step[row(r), :] = step
        run = exact_left(lower, step * m.par[8:9, :LANES])
        m.run[row(r), :] = run
        m.runr[r] = jnp.transpose(run)[0:8, :]
        lead, trail = leads(r)
        scaled = m.mix[row(r), :C].astype(F32) * spread(step)
        m.xs[row(r), :] = scaled.astype(BF16)
        ending = (scaled * spread(trail)).astype(BF16)
        m.fresh[r] = tn(ending, m.mix[row(r), C : C + LANES])

        @pl.when(c == 0)
        def _():
            m.ssend[r] = m.fresh[r].astype(BF16)
            state_copy(r).start()

    w_relay(1)

    @pl.loop(0, R)
    def _(r):
        b, cm = m.mix[row(r), C : C + LANES], m.mix[row(r), C + LANES : V]
        same = (m.segc[row(r), 8:9] == m.segr[pl.ds(r, 1), :]) & (iota((T, T), 0) >= iota((T, T), 1))
        m.scores[...] = jnp.where(same, nt(cm, b), 0.0)
        run = m.run[row(r), :]
        for p in range(pairs):
            part = slice(p * LANES, (p + 1) * LANES)
            both = []
            for h in (2 * p, 2 * p + 1):
                decay = jnp.exp(jnp.minimum(run[:, h : h + 1] - m.runr[r, h : h + 1, :], 0.0))
                both.append(nn((decay * m.scores[...]).astype(BF16), m.xs[row(r), part]))
            m.ins[row(r), part] = jnp.where(low_lanes, both[0], both[1])

        @pl.when(c > 0)
        def _():
            state_copy(r).wait_recv()

            @pl.when(c < nc - 1)
            def _():
                lead, _ = leads(r)
                for h in range(H):
                    here = slice(h * head, (h + 1) * head)
                    keep = lead[T - 1 : T, h : h + 1]
                    m.ssend[r, here, :] = (
                        m.fresh[r, here, :] + keep * m.sin[r, here, :].astype(F32)
                    ).astype(BF16)
                state_copy(r).start()

    w_rest(1)

    def sums_copy(r, k):
        return copy(
            m.sums.at[t, r], m.sums.at[t, r], m.x_send.at[r, k], m.x_recv.at[r, t], (d, c, at_ten(k))
        )

    def sums_arrived(r, who):
        copy(
            m.sums.at[who, r], m.sums.at[who, r], m.x_send.at[r, 0], m.x_recv.at[r, who], (d, c, t)
        ).wait_recv()

    def mine(r):
        return pl.ds(pl.multiple_of(r * T + odd * half, 16), half)

    def theirs(r):
        return pl.ds(pl.multiple_of(r * T + (1 - odd) * half, 16), half)

    def near_copy(a, r):
        return copy(m.as_.at[a, r], m.ar_.at[a, r], m.a_send.at[a, r], m.a_recv.at[a, r], (d, c, across))

    def far_copy(a, r):
        return copy(m.bs_.at[a, r], m.br_.at[a, r], m.b_send.at[a, r], m.b_recv.at[a, r], (d, c, far))

    def back_copy(a, r):
        out = (m.out, m.ing)[a].at[mine(r)]
        return copy(out, out, m.c_send.at[a, r], m.c_recv.at[a, r], (d, c, across))

    def back_arrived(a, r):
        out = (m.out, m.ing)[a].at[theirs(r)]
        copy(out, out, m.c_send.at[a, r], m.c_recv.at[a, r], (d, c, across)).wait_recv()

    def chip_sum(a, r):
        near_copy(a, r).wait_recv()
        m.bs_[a, r] = (m.keep[a, r].astype(F32) + m.ar_[a, r].astype(F32)).astype(BF16)
        if ntn == 4:
            far_copy(a, r).start()

    def full_sum(a, r):
        total = m.bs_[a, r].astype(F32)
        if ntn == 4:
            far_copy(a, r).wait_recv()
            total = total + m.br_[a, r].astype(F32)
        return total

    @pl.loop(0, R)
    def _(r):
        b, cm = m.mix[row(r), C : C + LANES], m.mix[row(r), C + LANES : V]
        lead, _ = leads(r)
        carried = nt(cm, m.sin[r]) * spread(lead)
        m.ys[row(r), :] = carried
        ssd = m.ins[row(r), :] + carried + m.par[6:7, :C] * m.mix[row(r), :C].astype(F32)
        m.ssd[row(r), :] = ssd
        gate = rounded(nn(m.nrm[row(r), :], m.wg1[:, :C]))
        m.zv[row(r), :] = gate.astype(BF16)
        gated = ssd * (gate * sigmoid(gate))
        m.gated[row(r), :C] = gated
        dy = nn(m.cot[row(r), :], m.wg1[:, C:])
        m.dy[row(r), :] = dy
        gain = m.par[5:6, :C]
        squares = jnp.sum(gated * gated, axis=-1, keepdims=True)
        inner = jnp.sum(dy * gain * gated, axis=-1, keepdims=True)
        both = jnp.where(lane == 0, squares, jnp.where(lane == 1, inner, 0.0))
        m.sums[t, r] = jnp.transpose(both)[0:8, :]
        for k in range(1, ntn):
            sums_copy(r, k).start()
        m.yg[row(r), :] = (gated * gain).astype(BF16)
        m.as_[0, r] = nt(m.yg[theirs(r), :], m.wg1[:, C:]).astype(BF16)
        near_copy(0, r).start()
        m.keep[0, r] = nt(m.yg[mine(r), :], m.wg1[:, C:])

    @pl.loop(0, R)
    def _(r):
        chip_sum(0, r)
        for k in range(1, ntn):
            sums_arrived(r, at_ten(k))
        total = m.sums[0, r]
        for who in range(1, ntn):
            total = total + m.sums[who, r]
        m.tot[0:8, :] = total
        columns = jnp.transpose(m.tot[...])
        scale = lax.rsqrt(columns[:, 0:1] * (1.0 / (C * ntn)) + EPS)
        m.rms[row(r), :] = jnp.broadcast_to(scale, (T, LANES))
        inner = columns[:, 1:2] * (1.0 / (C * ntn)) * scale * scale * scale
        gated, dy, gate, ssd = m.gated[row(r), :C], m.dy[row(r), :], m.zv[row(r), :].astype(F32), m.ssd[row(r), :]
        gain = m.par[5:6, :C]
        normal = gated * scale
        m.sm[t, 5:6, :C] += jnp.sum(dy * normal, axis=0, keepdims=True)
        m.yg[row(r), :] = (normal * gain).astype(BF16)
        d_gated = scale * dy * gain - gated * inner
        logistic = sigmoid(gate)
        m.dz[row(r), :] = (d_gated * ssd * (logistic * (1.0 + gate * (1.0 - logistic)))).astype(BF16)
        d_ssd = d_gated * (gate * logistic)
        m.ssd[row(r), :] = d_ssd
        lead, _ = leads(r)
        weighted = (d_ssd * spread(lead)).astype(BF16)
        m.wds[row(r), :] = weighted
        m.local[r] = tn(weighted, m.mix[row(r), C + LANES : V])

        @pl.when(c == nc - 1)
        def _():
            m.gsend[r] = m.local[r].astype(BF16)
            if nc > 1:
                grad_copy(r).start()

    gall, gyr, gzs, gzr = (m.ga0, m.ga1), (m.gy0, m.gy1), (m.gz0, m.gz1), (m.gr0, m.gr1)
    gwide = (z.G0, 2 * C)

    def rs_dp(part, j, k):
        cc = at_ctx(j)
        return copy(
            gall[part].at[block(at_dp(k), cc)],
            gyr[part].at[k - 1, pl.ds(pl.multiple_of(cc * rp, 16), rp)],
            m.ry_send.at[part, j, k - 1],
            m.ry_recv.at[part, j, k - 1],
            (at_dp(k), c, t),
        )

    def rs_ctx(part, j):
        cc = at_ctx(j)
        return copy(
            gzs[part].at[pl.ds(pl.multiple_of(cc * rp, 16), rp)],
            gzr[part].at[c],
            m.rz_send.at[part, j],
            m.rz_recv.at[part, c],
            (d, cc, t),
        )

    def rs_arrived(part, cc):
        copy(gzr[part].at[cc], gzr[part].at[cc], m.rz_send.at[part, 0], m.rz_recv.at[part, cc], (d, c, t)).wait_recv()

    order = [j for j in range(1, nc)] + [0]

    def rs_start(part):
        for j in order:
            for k in range(1, nd):
                rs_dp(part, j, k).start()

    def rs_middle(part):
        for j in order:
            cc = at_ctx(j)
            total = gall[part][block(d, cc), :].astype(F32)
            for k in range(1, nd):
                rs_dp(part, j, k).wait_recv()
                total = total + gyr[part][k - 1, pl.ds(pl.multiple_of(cc * rp, 16), rp), :].astype(F32)
            if j == 0:
                gzr[part][c] = total.astype(BF16)
            else:
                gzs[part][pl.ds(pl.multiple_of(cc * rp, 16), rp), :] = total.astype(BF16)
                rs_ctx(part, j).start()

    def rs_end(part):
        for k in range(1, nc):
            rs_arrived(part, at_ctx(k))
        total = gzr[part][0].astype(F32)
        for cc in range(1, nc):
            total = total + gzr[part][cc].astype(F32)
        return total

    def rs_sent(part):
        for j in range(nc):
            for k in range(1, nd):
                rs_dp(part, j, k).wait_send()
            if j:
                rs_ctx(part, j).wait_send()

    m.ga1[:, C:] = nn(m.cott[...], m.yg[...]).astype(BF16)
    m.ga1[:, :C] = nn(m.nrmt[...], m.dz[...]).astype(BF16)
    rs_start(1)

    @pl.loop(0, R)
    def _(r):
        b, cm = m.mix[row(r), C : C + LANES], m.mix[row(r), C + LANES : V]
        same = (m.segc[row(r), 8:9] == m.segr[pl.ds(r, 1), :]) & (iota((T, T), 0) <= iota((T, T), 1))
        m.scores[...] = jnp.where(same, nt(b, cm), 0.0)
        run = m.run[row(r), :]
        losses = jnp.zeros((T, LANES), F32)
        for p in range(pairs):
            part = slice(p * LANES, (p + 1) * LANES)
            ds_pair = m.ssd[row(r), part].astype(BF16)
            xs_pair = m.xs[row(r), part]
            both = []
            for h in (2 * p, 2 * p + 1):
                pick = low_lanes if h % 2 == 0 else ~low_lanes
                decay = jnp.exp(jnp.minimum(m.runr[r, h : h + 1, :] - run[:, h : h + 1], 0.0))
                weight = decay * m.scores[...]
                both.append(nn(weight.astype(BF16), ds_pair))
                d_weight = nt(jnp.where(pick, xs_pair, jnp.zeros_like(xs_pair)), ds_pair)
                flow = d_weight * weight
                if h == 0:
                    m.dsc[...] = d_weight * decay
                else:
                    m.dsc[...] += d_weight * decay
                losses = jnp.where(lane == h, jnp.sum(flow, axis=1, keepdims=True), losses)
                m.drow[h : h + 1, :] = jnp.sum(flow, axis=0, keepdims=True)
            m.ins[row(r), part] = jnp.where(low_lanes, both[0], both[1])
        d_scores = jnp.where(same, m.dsc[...], 0.0).astype(BF16)
        m.gated[row(r), :LANES] = nn(d_scores, cm)
        m.gated[row(r), LANES:S] = tn(d_scores, b)
        m.drun[row(r), :] = (
            jnp.transpose(m.drow[...])
            - losses
            + exact_right(m.ssd[row(r), :] * m.ys[row(r), :], fold)
        )

        @pl.when(c < nc - 1)
        def _():
            grad_copy(r).wait_recv()

            @pl.when(c > 0)
            def _():
                lead, _ = leads(r)
                for h in range(H):
                    here = slice(h * head, (h + 1) * head)
                    keep = lead[T - 1 : T, h : h + 1]
                    m.gsend[r, here, :] = (
                        m.local[r, here, :] + keep * m.gin[r, here, :].astype(F32)
                    ).astype(BF16)
                grad_copy(r).start()

    rs_middle(1)

    @pl.loop(0, R)
    def _(r):
        value = m.hid[mine(r), :].astype(F32) + m.rms[mine(r), 0:1] * full_sum(0, r)
        m.out[mine(r), :] = value.astype(BF16)
        back_copy(0, r).start()

    @pl.loop(0, R)
    def _(r):
        b, cm = m.mix[row(r), C : C + LANES], m.mix[row(r), C + LANES : V]
        lead, trail = leads(r)
        grad = m.gin[r]
        trailing = spread(trail)
        reach = nt(b, grad)
        scaled = m.xs[row(r), :].astype(F32) * trailing
        through = exact_right(scaled * reach, fold)
        d_run = m.drun[row(r), :] - through
        ends = jnp.sum(through, axis=0, keepdims=True)
        for h in range(H):
            here = slice(h * head, (h + 1) * head)
            joint = m.gin[r, here, :].astype(F32) * m.sin[r, here, :].astype(F32)
            joint = jnp.sum(jnp.sum(joint, axis=0, keepdims=True), axis=1, keepdims=True)
            ends = ends + jnp.where(lane[0:1] == h, joint * lead[T - 1 : T, :], 0.0)
        d_run = d_run + jnp.where(iota((T, LANES), 0) == T - 1, ends, 0.0)
        d_growth = exact_left(upper, d_run)
        step = m.step[row(r), :]
        d_xs = m.ins[row(r), :] + trailing * reach
        x = m.mix[row(r), :C].astype(F32)
        d_ssd = m.ssd[row(r), :]
        rate = m.par[8:9, :LANES]
        d_step = exact_right(d_xs * x, fold) + rate * d_growth
        m.sm[t, 7:8, LANES : 2 * LANES] += jnp.sum(step * d_growth, axis=0, keepdims=True) * rate
        m.sm[t, 7:8, 3 * LANES : 3 * LANES + C] += jnp.sum(d_ssd * x, axis=0, keepdims=True)
        d_pre = d_step * sigmoid(m.pre[row(r), :])
        m.sm[t, 7:8, :LANES] += jnp.sum(d_pre, axis=0, keepdims=True)
        m.dv[row(r), V:] = jnp.where(lane < H, d_pre, 0.0).astype(BF16)
        m.dconv[r, pl.ds(0, T), :C] = (d_xs * spread(step) + m.par[6:7, :C] * d_ssd) * m.slope[row(r), :C]
        m.dconv[r, pl.ds(0, T), C : C + LANES] = (
            m.gated[row(r), :LANES] + nn(scaled.astype(BF16), grad)
        ) * m.slope[row(r), C : C + LANES]
        m.dconv[r, pl.ds(0, T), C + LANES :] = (
            m.gated[row(r), LANES:S] + nn(m.wds[row(r), :], m.sin[r])
        ) * m.slope[row(r), C + LANES :]

        @pl.when(c > 0)
        def _():
            edge_copy(r).start()

        seg = m.segc[row(r), :]
        for a in range(0, V, LANES):
            part = slice(a, a + LANES)
            d_conv = m.dconv[r, pl.ds(0, T), part]
            m.sm[t, 4:5, part] += jnp.sum(d_conv, axis=0, keepdims=True)
            m.sm[t, 0:1, part] += jnp.sum(d_conv * m.vext[r, pl.ds(EDGE, T), part], axis=0, keepdims=True)
            for j in range(1, z.K):
                m.sm[t, j : j + 1, part] += jnp.sum(
                    d_conv * m.vext[r, pl.ds(EDGE - j, T), part] * seg[:, j - 1 : j], axis=0, keepdims=True
                )

    @pl.loop(0, R)
    def _(r):
        @pl.when(c < nc - 1)
        def _():
            edge_copy(r).wait_recv()

        m.dconv[r, pl.ds(T, EDGE), :] = m.dce[r]
        seg = m.segc[row(r), :]
        for a in range(0, V, LANES):
            part = slice(a, a + LANES)
            d_v = m.dconv[r, pl.ds(0, T), part] * m.par[0:1, part]
            for j in range(1, z.K):
                d_v = d_v + m.dconv[r, pl.ds(j, T), part] * m.par[j : j + 1, part] * seg[:, j + 2 : j + 3]
            m.dv[row(r), part] = d_v.astype(BF16)

        def d_normed(rows):
            return nt(m.dv[rows, :], m.wg0[...]) + nt(m.dz[rows, :], m.wg1[:, :C])

        def unit_of(rows):
            u = m.hid[rows, :].astype(F32)
            mean = jnp.sum(u * u, axis=-1, keepdims=True) * (1.0 / z.d_true)
            return u * lax.rsqrt(mean + EPS)

        value = d_normed(theirs(r))
        m.as_[1, r] = value.astype(BF16)
        near_copy(1, r).start()
        m.sm[t, 6:7, :D] += jnp.sum(value * unit_of(theirs(r)), axis=0, keepdims=True)
        value = d_normed(mine(r))
        m.keep[1, r] = value
        m.sm[t, 6:7, :D] += jnp.sum(value * unit_of(mine(r)), axis=0, keepdims=True)

    width = S // ntn
    m.ga0[:, :C] = nn(m.nrmt[...], m.dv[:, :C]).astype(BF16)
    m.ga0[:, C : C + LANES] = nn(m.nrmt[...], m.dv[:, V:]).astype(BF16)

    def share_copy():
        return copy(m.shs, m.shr, m.sh_send.at[0], m.sh_recv.at[0], (d, c, across))

    quarters = [m.dv[:, C + k * width : C + (k + 1) * width] for k in range(ntn)]
    for parity in range(2):
        chosen = jnp.concatenate(quarters[parity::2], axis=1)
        value = nn(m.nrmt[...], chosen)

        @pl.when(odd == parity)
        def _():
            m.shk[...] = value

        @pl.when(odd != parity)
        def _():
            m.shs[...] = value.astype(BF16)

    share_copy().start()

    @pl.loop(0, R)
    def _(r):
        chip_sum(1, r)

    share_copy().wait_recv()
    m.ga0[:, C + LANES : C + LANES + z.Q] = (m.shk[...] + m.shr[...].astype(F32)).astype(BF16)
    rs_start(0)

    def small_ten(k):
        return copy(m.sm.at[t], m.sm.at[t], m.st_send.at[k], m.st_recv.at[t], (d, c, at_ten(k)))

    def small_dp(k):
        return copy(m.sd.at[d], m.sd.at[d], m.sd_send.at[k], m.sd_recv.at[d], (at_dp(k), c, t))

    def small_ctx(k):
        return copy(m.sc.at[c], m.sc.at[c], m.sc_send.at[k], m.sc_recv.at[c], (d, at_ctx(k), t))

    def arrived(buf, sems, who):
        copy(buf.at[who], buf.at[who], sems.at[who], sems.at[who], (d, c, t)).wait_recv()

    for k in range(1, ntn):
        small_ten(k).start()
    for k in range(1, ntn):
        arrived(m.sm, m.st_recv, at_ten(k))
    common = m.sm[0]
    for who in range(1, ntn):
        common = common + m.sm[who]
    rows8, lanes8 = iota((8, z.WL), 0), iota((8, z.WL), 1)
    shared_here = (rows8 == 6) | ((rows8 < 5) & (lanes8 >= C))
    m.sd[d] = jnp.where(shared_here, common, m.sm[t])
    for k in range(1, nd):
        small_dp(k).start()

    @pl.loop(0, R)
    def _(r):
        u = m.hid[mine(r), :].astype(F32)
        mean = jnp.sum(u * u, axis=-1, keepdims=True) * (1.0 / z.d_true)
        scale = lax.rsqrt(mean + EPS)
        unit = u * scale
        d_unit = full_sum(1, r) * gain_in
        inner = jnp.sum(d_unit * unit, axis=-1, keepdims=True) * (1.0 / z.d_true)
        value = m.cot[mine(r), :].astype(F32) + scale * (d_unit - unit * inner)
        m.ing[mine(r), :] = value.astype(BF16)
        back_copy(1, r).start()

    rs_middle(0)

    for k in range(1, nd):
        arrived(m.sd, m.sd_recv, at_dp(k))
    total = m.sd[0]
    for who in range(1, nd):
        total = total + m.sd[who]
    m.sc[c] = total
    for k in range(1, nc):
        small_ctx(k).start()

    m.gw1[...] = rs_end(1)
    m.gw0[...] = rs_end(0)

    if ntn == 4:
        def last_copy():
            return copy(m.ls, m.lr, m.sh_send.at[1], m.sh_recv.at[1], (d, c, far))

        m.ls[...] = m.gw0[:, C + LANES : C + LANES + z.Q]
        last_copy().start()

    for k in range(1, nc):
        arrived(m.sc, m.sc_recv, at_ctx(k))
    total = m.sc[0]
    for who in range(1, nc):
        total = total + m.sc[who]
    m.small[...] = total

    if ntn == 4:
        last_copy().wait_recv()
        m.gw0[:, C + LANES : C + LANES + z.Q] = m.ls[...] + m.lr[...]
        last_copy().wait_send()

    for a in range(2):
        for r in range(R):
            back_arrived(a, r)
            back_copy(a, r).wait_send()
            near_copy(a, r).wait_send()
            if ntn == 4:
                far_copy(a, r).wait_send()
    for part in range(2):
        w_sent(part)
        rs_sent(part)
    for r in range(R):
        for k in range(1, ntn):
            sums_copy(r, k).wait_send()

        @pl.when(c < nc - 1)
        def _():
            halo_copy(r).wait_send()
            state_copy(r).wait_send()

        @pl.when(c > 0)
        def _():
            grad_copy(r).wait_send()
            edge_copy(r).wait_send()

    share_copy().wait_send()
    for k in range(1, ntn):
        small_ten(k).wait_send()
    for k in range(1, nd):
        small_dp(k).wait_send()
    for k in range(1, nc):
        small_ctx(k).wait_send()


def on_device(z, hidden_in, segment_ids, norm_gain, head_projection, shared_projection, step_projection,
              conv_heads, bias_heads, conv_shared, bias_shared, step_bias, log_decay, skip_gain, gate_gain,
              output_weight, out_cotangent):
    R, T, D, C, H, S = z.R, z.T, z.D, z.C, z.H, z.S
    rp, nd, nc, ntn = z.rp, z.nd, z.nc, z.ntn
    V = C + S
    blocks = nd * nc

    def widen(value):
        if rp == z.rows:
            return value
        value = value.reshape(value.shape[:-1] + (blocks, z.rows))
        value = jnp.pad(value, [(0, 0)] * (value.ndim - 1) + [(0, rp - z.rows)])
        return value.reshape(value.shape[:-2] + (D,))

    def narrow(value):
        if rp == z.rows:
            return value
        return value.reshape(value.shape[:-1] + (blocks, rp))[..., : z.rows].reshape(value.shape[:-1] + (z.d_true,))

    hid = widen(hidden_in.reshape(R * T, z.d_true))
    cot = widen(out_cotangent.reshape(R * T, z.d_true))
    w0 = jnp.concatenate(
        [head_projection[:, 1], shared_projection, jnp.pad(step_projection, ((0, 0), (0, LANES - H)))], axis=1
    )
    w1 = jnp.concatenate([head_projection[:, 0], output_weight.T], axis=1)
    if rp != z.rows:
        w0 = jnp.pad(w0, ((0, rp - z.rows), (0, 0)))
        w1 = jnp.pad(w1, ((0, rp - z.rows), (0, 0)))
    begin = lax.axis_index("context") * T
    margin = z.K - 1
    ids = segment_ids.reshape(R, segment_ids.shape[-1])
    ids = jnp.pad(ids, ((0, 0), (margin, 0)), constant_values=-1)
    ids = jnp.pad(ids, ((0, 0), (0, margin)), constant_values=-2)
    ids = lax.dynamic_slice_in_dim(ids, begin, T + 2 * margin, 1)
    now = ids[:, margin : margin + T]
    columns = [now == ids[:, margin - j : margin - j + T] for j in range(1, z.K)]
    columns += [now == ids[:, margin + j : margin + j + T] for j in range(1, z.K)]
    columns += [now == ids[:, margin - 1 : margin], now == now[:, T - 1 : T]]
    columns = [value.astype(F32) for value in columns] + [now.astype(F32)]
    columns += [jnp.zeros((R, T), F32)] * (16 - len(columns))
    segc = jnp.stack(columns, axis=-1).reshape(R * T, 16)
    segr = jnp.pad(now.astype(F32), ((0, -R % 8), (0, 0)))

    def line(value):
        value = value.reshape(-1, value.shape[-1])
        return jnp.pad(value, ((0, 0), (0, V - value.shape[-1])))

    par = jnp.concatenate(
        [
            jnp.concatenate([conv_heads, conv_shared], axis=1),
            jnp.concatenate([bias_heads, bias_shared])[None],
            line(gate_gain),
            line(jnp.repeat(skip_gain, C // H)),
            line(step_bias),
            line(-jnp.exp(log_decay)),
        ],
        axis=0,
    )
    par = jnp.pad(par, ((0, 16 - par.shape[0]), (0, 0)))
    ng = jnp.broadcast_to(widen(norm_gain[None]), (8, D))

    dma, vmem = pltpu.SemaphoreType.DMA, pltpu.VMEM
    N = R * T
    half = T // 2
    k0 = max(nd - 1, 1)
    ins = dict(hid=hid, cot=cot, w0=w0, w1=w1, segc=segc, segr=segr, par=par, ng=ng)
    outs = dict(
        out=jax.ShapeDtypeStruct((N, D), BF16),
        ing=jax.ShapeDtypeStruct((N, D), BF16),
        gw0=jax.ShapeDtypeStruct((rp, z.G0), F32),
        gw1=jax.ShapeDtypeStruct((rp, 2 * C), F32),
        small=jax.ShapeDtypeStruct((8, z.WL), F32),
    )
    scratch = dict(
        wg0=vmem((D, V + LANES), BF16), wg1=vmem((D, 2 * C), BF16),
        hh=vmem((R * HALO, D), BF16), nrmh=vmem((R * HALO, D), BF16),
        nrm=vmem((N, D), BF16), nrmt=vmem((D, N), BF16), cott=vmem((D, N), BF16),
        vext=vmem((R, EDGE + T, V), F32), mix=vmem((N, V), BF16), slope=vmem((N, V), F32),
        pre=vmem((N, LANES), F32), step=vmem((N, LANES), F32), run=vmem((N, LANES), F32),
        runr=vmem((R, 8, T), F32), xs=vmem((N, C), BF16),
        fresh=vmem((R, C, LANES), F32), local=vmem((R, C, LANES), F32),
        ssend=vmem((R, C, LANES), BF16), sin=vmem((R, C, LANES), BF16),
        gsend=vmem((R, C, LANES), BF16), gin=vmem((R, C, LANES), BF16),
        scores=vmem((T, T), F32), dsc=vmem((T, T), F32), drow=vmem((LANES, T), F32), tot=vmem((LANES, T), F32),
        ins=vmem((N, C), F32), ys=vmem((N, C), F32), ssd=vmem((N, C), F32), zv=vmem((N, C), BF16),
        gated=vmem((N, max(C, S)), F32), dy=vmem((N, C), F32),
        yg=vmem((N, C), BF16), dz=vmem((N, C), BF16), wds=vmem((N, C), BF16),
        rms=vmem((N, LANES), F32), sums=vmem((ntn, R, 8, T), F32),
        as_=vmem((2, R, half, D), BF16), ar_=vmem((2, R, half, D), BF16),
        bs_=vmem((2, R, half, D), BF16), br_=vmem((2, R, half, D), BF16), keep=vmem((2, R, half, D), F32),
        ga0=vmem((D, z.G0), BF16), ga1=vmem((D, 2 * C), BF16),
        gy0=vmem((k0, nc * rp, z.G0), BF16), gy1=vmem((k0, nc * rp, 2 * C), BF16),
        gz0=vmem((nc * rp, z.G0), BF16), gz1=vmem((nc * rp, 2 * C), BF16),
        gr0=vmem((nc, rp, z.G0), BF16), gr1=vmem((nc, rp, 2 * C), BF16),
        drun=vmem((N, LANES), F32),
        dconv=vmem((R, T + EDGE, V), F32), dce=vmem((R, EDGE, V), F32), dv=vmem((N, V + LANES), BF16),
        shs=vmem((D, z.Q), BF16), shr=vmem((D, z.Q), BF16), shk=vmem((D, z.Q), F32),
        ls=vmem((rp, z.Q), F32), lr=vmem((rp, z.Q), F32),
        sm=vmem((ntn, 8, z.WL), F32), sd=vmem((nd, 8, z.WL), F32), sc=vmem((nc, 8, z.WL), F32),
        w_send=dma((2, nc, nd)), w_recv=dma((2, nd, nc)), h_send=dma((R,)), h_recv=dma((R,)),
        s_send=dma((R,)), s_recv=dma((R,)), g_send=dma((R,)), g_recv=dma((R,)), e_send=dma((R,)), e_recv=dma((R,)),
        x_send=dma((R, ntn)), x_recv=dma((R, ntn)),
        a_send=dma((2, R)), a_recv=dma((2, R)), b_send=dma((2, R)), b_recv=dma((2, R)),
        c_send=dma((2, R)), c_recv=dma((2, R)),
        ry_send=dma((2, nc, k0)), ry_recv=dma((2, nc, k0)), rz_send=dma((2, nc)), rz_recv=dma((2, nc)),
        sh_send=dma((2,)), sh_recv=dma((2,)),
        st_send=dma((ntn,)), st_recv=dma((ntn,)), sd_send=dma((nd,)), sd_recv=dma((nd,)),
        sc_send=dma((nc,)), sc_recv=dma((nc,)),
    )
    names = list(ins) + list(outs) + list(scratch)
    whole = pl.BlockSpec(memory_space=pltpu.VMEM)
    out, ing, gw0, gw1, small = pl.pallas_call(
        functools.partial(kernel, z, names),
        out_shape=list(outs.values()),
        in_specs=[whole] * len(ins),
        out_specs=[whole] * len(outs),
        scratch_shapes=list(scratch.values()),
        compiler_params=pltpu.CompilerParams(
            collective_id=0, has_side_effects=True, vmem_limit_bytes=z.limit
        ),
    )(*ins.values())

    block_out = narrow(out).reshape(hidden_in.shape)
    input_grad = narrow(ing).reshape(hidden_in.shape)
    gw0, gw1 = gw0[: z.rows], gw1[: z.rows]
    grad_heads = jnp.stack([gw1[:, :C], gw0[:, :C]], axis=1)
    rank = lax.axis_index("tensor")
    width = S // ntn
    grad_shared = lax.dynamic_slice_in_dim(gw0, C + LANES + (rank // 2) * width, width, 1)
    grad_step = gw0[:, C : C + H]
    skip = small[7, 3 * LANES : 3 * LANES + C].reshape(H, C // H).sum(axis=1)
    return (
        block_out,
        input_grad,
        narrow(small[6, :D]),
        grad_heads,
        grad_shared,
        grad_step,
        small[0 : z.K, :C],
        small[4, :C],
        small[0 : z.K, C:V],
        small[4, C:V],
        small[7, :H],
        small[7, LANES : LANES + H],
        skip,
        small[5, :C],
        gw1[:, C:].T,
    )


def solution(mesh):
    nd, nc, ntn = (mesh.shape[name] for name in ("dp", "context", "tensor"))

    def body(*args):
        hidden, heads, shared = args[0], args[3], args[4]
        micro, seqs, tokens, width = hidden.shape
        rows = heads.shape[0]
        rp = -(-rows // 16) * 16
        inner = heads.shape[2]
        z = types.SimpleNamespace(
            R=micro * seqs, T=tokens, d_true=width, D=rp * nd * nc, rows=rows, rp=rp, nd=nd, nc=nc, ntn=ntn,
            C=inner, H=args[10].shape[0], S=shared.shape[1], K=args[6].shape[0],
            Q=shared.shape[1] // 2, G0=inner + LANES + shared.shape[1] // 2, limit=62 << 20,
        )
        z.WL = max(inner + z.S, z.D, 3 * LANES + inner)
        return on_device(z, *args)

    return jax.shard_map(
        body,
        mesh=mesh,
        in_specs=(
            P(None, "dp", "context", None),
            P(None, "dp", None),
            P(),
            P(("dp", "context"), None, "tensor"),
            P(("dp", "context"), None),
            P(("dp", "context"), "tensor"),
            P(None, "tensor"),
            P("tensor"),
            P(),
            P(),
            P("tensor"),
            P("tensor"),
            P("tensor"),
            P("tensor"),
            P("tensor", ("dp", "context")),
            P(None, "dp", "context", None),
        ),
        out_specs=(
            P(None, "dp", "context", None),
            P(None, "dp", "context", None),
            P(),
            P(("dp", "context"), None, "tensor"),
            P(("dp", "context"), "tensor"),
            P(("dp", "context"), "tensor"),
            P(None, "tensor"),
            P("tensor"),
            P(),
            P(),
            P("tensor"),
            P("tensor"),
            P("tensor"),
            P("tensor"),
            P("tensor", ("dp", "context")),
        ),
        check_vma=False,
    )
```

```python
import functools
import types

import jax
import jax.numpy as jnp
from jax import lax
from jax.experimental import pallas as pl
from jax.experimental.pallas import tpu as pltpu
from jax.sharding import PartitionSpec as P

EPS = 1e-05
F32 = jnp.float32
BF16 = jnp.bfloat16
MESH = pl.DeviceIdType.MESH
LANES = 128
HALO = 16
EDGE = 8
PIECES = 5


def nn(a, b):
    return lax.dot_general(a, b, (((1,), (0,)), ((), ())), preferred_element_type=F32)


def nt(a, b):
    return lax.dot_general(a, b, (((1,), (1,)), ((), ())), preferred_element_type=F32)


def tn(a, b):
    return lax.dot_general(a, b, (((0,), (0,)), ((), ())), preferred_element_type=F32)


def pieces_of(value, count):
    pieces = []
    for _ in range(count):
        piece = value.astype(BF16)
        pieces.append(piece)
        value = value - piece.astype(F32)
    return pieces


def exact_left(ones, value):
    return sum(nn(ones, piece) for piece in pieces_of(value, 3))


def exact_right(value, ones):
    return sum(nn(piece, ones) for piece in pieces_of(value, 2))


def sigmoid(value):
    return 0.5 * jnp.tanh(0.5 * value) + 0.5


def iota(shape, dim):
    return lax.broadcasted_iota(jnp.int32, shape, dim)


def kernel(z, names, *refs):
    m = types.SimpleNamespace(**dict(zip(names, refs)))
    R, T, D, C, H, S = z.R, z.T, z.D, z.C, z.H, z.S
    rp, nd, nc, ntn = z.rp, z.nd, z.nc, z.ntn
    pairs = H // 2
    head = C // H
    V = C + S
    half = T // 2
    d, c, t = lax.axis_index("dp"), lax.axis_index("context"), lax.axis_index("tensor")
    odd = lax.rem(t, 2)
    across = t + 1 - 2 * odd
    far = lax.rem(t + 2, 4) if ntn == 4 else t

    def at_ctx(k):
        return lax.rem(c + k, nc)

    def at_dp(k):
        return lax.rem(d + k, nd)

    def at_ten(k):
        return lax.rem(t + k, ntn)

    def rows_at(place, size):
        return pl.ds(pl.multiple_of(place * size, 16), size)

    def block(dd, cc):
        return rows_at(dd * nc + cc, rp)

    def row(r):
        return rows_at(r, T)

    def copy(src, dst, send, recv, dev):
        return pltpu.make_async_remote_copy(
            src_ref=src, dst_ref=dst, send_sem=send, recv_sem=recv, device_id=dev, device_id_type=MESH
        )

    def load(which):
        return pltpu.make_async_copy((m.hid, m.cot)[which], (m.hv, m.cv)[which], m.l_in.at[which])

    load(0).start()
    load(1).start()
    barrier = pltpu.get_barrier_semaphore()
    peers = [(d, at_ctx(k), t) for k in range(1, nc)]
    peers += [(at_dp(k), c, t) for k in range(1, nd)]
    peers += [(d, c, at_ten(k)) for k in range(1, ntn)]
    for peer in peers:
        pl.semaphore_signal(barrier, inc=1, device_id=peer, device_id_type=MESH)

    m.wx[block(d, c), :] = m.hp[1]
    m.ws[block(d, c), pl.ds(pl.multiple_of(odd * z.Q, LANES), z.Q)] = jnp.where(
        odd == 0, m.shp[:, : z.Q], m.shp[:, z.Q :]
    )
    m.tile[...] = jnp.zeros_like(m.tile)
    m.tile[0:rp, 0:H] = m.stp[...].astype(F32)
    m.wt[d * nc + c] = jnp.transpose(m.tile[...])[0:HALO, :].astype(BF16)
    pl.semaphore_wait(barrier, len(peers))

    def slot(p, dd, cc):
        if p == 2:
            return m.wt.at[dd * nc + cc]
        if p == 1:
            return m.ws.at[block(dd, cc), pl.ds(pl.multiple_of(odd * z.Q, LANES), z.Q)]
        return (m.wx, m.ws, m.wt, m.wz, m.wo)[p].at[block(dd, cc)]

    def w_ctx(p, s, right):
        to = c + s if right else c - s
        here = slot(p, d, c)
        return copy(here, here, m.wz_send.at[p, int(right), s], m.w_recv.at[p, d, c], (d, to, t))

    def w_dp(p, cc, k):
        here = slot(p, d, cc)
        return copy(here, here, m.wd_send.at[p, cc, k], m.w_recv.at[p, d, cc], (at_dp(k), c, t))

    def w_arrived(p, dd, cc):
        there = slot(p, dd, cc)
        copy(there, there, m.wd_send.at[p, cc, 0], m.w_recv.at[p, dd, cc], (d, c, t)).wait_recv()

    def w_start(p):
        for k in range(1, nd):
            w_dp(p, c, k).start()
        for s in range(1, nc):
            pl.when(c + s < nc)(lambda: w_ctx(p, s, True).start())
            pl.when(c - s >= 0)(lambda: w_ctx(p, s, False).start())

    def w_relay(p):
        def one(cc):
            w_arrived(p, d, cc)
            for k in range(1, nd):
                w_dp(p, cc, k).start()

        for s in range(1, nc):
            pl.when(c - s >= 0)(lambda: one(c - s))
            pl.when(c + s < nc)(lambda: one(c + s))

    def w_rest(p):
        for k in range(1, nd):
            for cc in range(nc):
                w_arrived(p, at_dp(k), cc)

    def w_sent(p):
        for cc in range(nc):
            for k in range(1, nd):
                w_dp(p, cc, k).wait_send()
        for s in range(1, nc):
            pl.when(c + s < nc)(lambda: w_ctx(p, s, True).wait_send())
            pl.when(c - s >= 0)(lambda: w_ctx(p, s, False).wait_send())

    def half_copy():
        here = m.ws.at[:, pl.ds(pl.multiple_of(odd * z.Q, LANES), z.Q)]
        return copy(here, here, m.sh_send.at[2], m.sh_recv.at[2], (d, c, across))

    def half_arrived():
        there = m.ws.at[:, pl.ds(pl.multiple_of((1 - odd) * z.Q, LANES), z.Q)]
        copy(there, there, m.sh_send.at[2], m.sh_recv.at[2], (d, c, across)).wait_recv()

    def halo_copy(r):
        return copy(
            m.hv.at[pl.ds(pl.multiple_of(r * T + T - HALO, 16), HALO)],
            m.hh.at[rows_at(r, HALO)],
            m.h_send.at[r],
            m.h_recv.at[r],
            (d, c + 1, t),
        )

    for p in range(3):
        w_start(p)
    load(0).wait()

    @pl.when(c < nc - 1)
    def _():
        for r in range(R):
            halo_copy(r).start()

    m.par[...] = jnp.zeros_like(m.par)
    m.par[0 : z.K, :C] = m.ch[...]
    m.par[0 : z.K, C:] = m.cs[...]
    m.par[4:5, :C] = m.bh[...]
    m.par[4:5, C:] = m.bs[...]
    m.par[5:6, :C] = m.gg[...]
    for h in range(H):
        m.par[6:7, h * head : (h + 1) * head] = jnp.broadcast_to(m.sk[0:1, h : h + 1], (1, head))
    m.par[7:8, 0:H] = m.sb[...]
    m.par[8:9, 0:H] = -jnp.exp(m.ld[...])
    m.wz[block(d, c), :] = m.hp[0]
    eye = (iota((rp, rp), 0) == iota((rp, rp), 1)).astype(BF16)
    m.wo[block(d, c), :] = nt(eye, m.ow[...]).astype(BF16)

    gain_in = m.ng[...]

    def normalize(u):
        u = u.astype(F32)
        mean = jnp.sum(u * u, axis=-1, keepdims=True) * (1.0 / z.d_true)
        return (u * lax.rsqrt(mean + EPS)) * gain_in

    @pl.loop(0, R)
    def _(r):
        m.nrm[row(r), :] = normalize(m.hv[row(r), :]).astype(BF16)

    length = m.seg.shape[-1]
    begin = c * T
    seqs = m.seg.shape[1]

    def ids_at(place, size):
        place = pl.multiple_of(place, LANES)
        lines = [m.seg[r // seqs, r % seqs : r % seqs + 1, pl.ds(place, size)] for r in range(R)]
        return jnp.concatenate(lines + [jnp.zeros_like(lines[0])] * (-R % 8), axis=0).astype(F32)

    now = ids_at(begin, T)
    before = jnp.where(c == 0, -1.0, ids_at(jnp.maximum(begin - LANES, 0), LANES))
    behind = jnp.where(c == nc - 1, -2.0, ids_at(jnp.minimum(begin + T, length - LANES), LANES))
    m.segr[...] = now
    m.segb[...] = before
    m.sega[...] = behind
    carried = (now == before[:, LANES - 1 : LANES]).astype(F32)
    closing = (now == now[:, T - 1 : T]).astype(F32)
    m.tot[...] = jnp.zeros_like(m.tot)
    for r in range(R):
        m.tot[0:1, :] = now[r : r + 1]
        m.tot[1:2, :] = carried[r : r + 1]
        m.tot[2:3, :] = closing[r : r + 1]
        m.segc[r * T : (r + 1) * T, :] = jnp.transpose(m.tot[...])
    away = iota((T, T), 0) - iota((T, T), 1)
    for j in range(1, z.K):
        m.diag[j - 1] = (away == j).astype(BF16)
        m.diag[z.K + j - 2] = (away == -j).astype(BF16)
    m.lower[...] = (away >= 0).astype(BF16)
    m.upper[...] = (away <= 0).astype(BF16)

    @pl.loop(0, R)
    def _(r):
        m.same[r] = (m.segc[row(r), 0:1] == m.segr[pl.ds(r, 1), :]).astype(BF16)

    @pl.when(c == 0)
    def _():
        m.hh[...] = jnp.zeros_like(m.hh)
        m.sin[...] = jnp.zeros_like(m.sin)

    @pl.when(c == nc - 1)
    def _():
        m.gin[...] = jnp.zeros_like(m.gin)
        m.dce[...] = jnp.zeros_like(m.dce)

    m.sm[t] = jnp.zeros((8, z.WL), F32)
    m.drow[...] = jnp.zeros_like(m.drow)

    w_relay(0)
    w_start(3)

    @pl.when(c > 0)
    def _():
        for r in range(R):
            halo_copy(r).wait_recv()

    m.nrmh[...] = normalize(m.hh[...]).astype(BF16)
    w_relay(1)
    w_relay(2)
    w_start(4)
    w_rest(0)

    low_lanes = iota((T, LANES), 1) < head
    lane = iota((T, LANES), 1)
    fold = (iota((C, LANES), 0) // head == iota((C, LANES), 1)).astype(BF16)

    def spread(values):
        return jnp.concatenate(
            [
                jnp.where(low_lanes, values[:, 2 * p : 2 * p + 1], values[:, 2 * p + 1 : 2 * p + 2])
                for p in range(pairs)
            ],
            axis=1,
        )

    def state_copy(r):
        return copy(m.ssend.at[r], m.sin.at[r], m.s_send.at[r], m.s_recv.at[r], (d, c + 1, t))

    def grad_copy(r):
        return copy(m.gsend.at[r], m.gin.at[r], m.g_send.at[r], m.g_recv.at[r], (d, c - 1, t))

    def edge_copy(r):
        return copy(m.edge.at[r], m.dce.at[r], m.e_send.at[r], m.e_recv.at[r], (d, c - 1, t))

    def leads(r):
        run = m.run[row(r), :]
        seg = m.segc[row(r), :]
        last = run[T - 1 : T, :]
        lead = jnp.exp(run) * seg[:, 1:2]
        trail = jnp.exp(last - run) * seg[:, 2:3]
        return lead, trail

    def convolve(r, lanes):
        seg = m.segc[row(r), :]
        reach = iota((EDGE, HALO), 1) - HALO - iota((EDGE, HALO), 0)
        near = seg[0:EDGE, 0:1] == m.segb[pl.ds(r, 1), LANES - HALO : LANES]
        for a in range(lanes[0], lanes[1], LANES):
            part = slice(a, a + LANES)
            value = m.v[row(r), part]
            before = m.vh[rows_at(r, HALO), part]
            conv = value.astype(F32) * m.par[0:1, part] + m.par[4:5, part]
            first = jnp.zeros((EDGE, LANES), F32)
            for j in range(1, z.K):
                tap = m.par[j : j + 1, part]
                conv = conv + nn(m.diag[j - 1] * m.same[r], value) * tap
                first = first + nn((near & (reach == -j)).astype(BF16), before) * tap
            conv = jnp.concatenate([conv[0:EDGE] + first, conv[EDGE:]], axis=0)
            logistic = sigmoid(conv)
            m.mix[row(r), part] = (conv * logistic).astype(BF16)
            m.slope[row(r), part] = logistic * (1.0 + conv * (1.0 - logistic))

    m.vh[:, :C] = nn(m.nrmh[...], m.wx[...]).astype(BF16)

    @pl.loop(0, R)
    def _(r):
        m.v[row(r), :C] = nn(m.nrm[row(r), :], m.wx[...]).astype(BF16)
        convolve(r, (0, C))

    w_rest(1)
    half_copy().start()
    w_rest(2)
    m.tile[...] = jnp.zeros_like(m.tile)

    @pl.loop(0, nd * nc)
    def _(b):
        m.tile[0:HALO, :] = m.wt[b].astype(F32)
        m.wst[rows_at(b, rp), :] = jnp.transpose(m.tile[...])[0:rp, :].astype(BF16)

    half_arrived()
    w_relay(3)
    m.vh[:, C:] = nn(m.nrmh[...], m.ws[...]).astype(BF16)

    @pl.loop(0, R)
    def _(r):
        m.v[row(r), C:] = nn(m.nrm[row(r), :], m.ws[...]).astype(BF16)
        raw = nn(m.nrm[row(r), :], m.wst[...]).astype(BF16).astype(F32)
        convolve(r, (C, V))
        pre = raw + m.par[7:8, :LANES]
        step = jnp.maximum(pre, 0.0) + jnp.log1p(jnp.exp(-jnp.abs(pre)))
        m.pre[row(r), :] = pre
        m.step[row(r), :] = step
        run = exact_left(m.lower[...], step * m.par[8:9, :LANES])
        m.run[row(r), :] = run
        m.runr[r] = jnp.transpose(run)[0:8, :]
        lead, trail = leads(r)
        scaled = m.mix[row(r), :C].astype(F32) * spread(step)
        m.xs[row(r), :] = scaled.astype(BF16)
        ending = (scaled * spread(trail)).astype(BF16)
        m.fresh[r] = tn(ending, m.mix[row(r), C : C + LANES])

        @pl.when(c == 0)
        def _():
            m.ssend[r] = m.fresh[r].astype(BF16)
            state_copy(r).start()

    load(1).wait()

    @pl.loop(0, R)
    def _(r):
        b, cm = m.mix[row(r), C : C + LANES], m.mix[row(r), C + LANES : V]
        m.scores[...] = nt(cm, b) * (m.same[r] * m.lower[...]).astype(F32)
        run = m.run[row(r), :]
        for p in range(pairs):
            part = slice(p * LANES, (p + 1) * LANES)
            both = []
            for h in (2 * p, 2 * p + 1):
                decay = jnp.exp(jnp.minimum(run[:, h : h + 1] - m.runr[r, h : h + 1, :], 0.0))
                both.append(nn((decay * m.scores[...]).astype(BF16), m.xs[row(r), part]))
            m.ins[row(r), part] = jnp.where(low_lanes, both[0], both[1])
        m.nrmt[:, row(r)] = jnp.transpose(m.nrm[row(r), :])
        m.cott[:, row(r)] = jnp.transpose(m.cv[row(r), :])

        @pl.when(c > 0)
        def _():
            state_copy(r).wait_recv()

            @pl.when(c < nc - 1)
            def _():
                lead, _ = leads(r)
                for h in range(H):
                    here = slice(h * head, (h + 1) * head)
                    keep = lead[T - 1 : T, h : h + 1]
                    m.ssend[r, here, :] = (
                        m.fresh[r, here, :] + keep * m.sin[r, here, :].astype(F32)
                    ).astype(BF16)
                state_copy(r).start()

    w_relay(4)
    w_rest(3)
    w_rest(4)

    def sums_copy(r, k):
        return copy(
            m.sums.at[t, r], m.sums.at[t, r], m.x_send.at[r, k], m.x_recv.at[r, t], (d, c, at_ten(k))
        )

    def sums_arrived(r, who):
        copy(
            m.sums.at[who, r], m.sums.at[who, r], m.x_send.at[r, 0], m.x_recv.at[r, who], (d, c, t)
        ).wait_recv()

    def mine(r):
        return pl.ds(pl.multiple_of(r * T + odd * half, 16), half)

    def theirs(r):
        return pl.ds(pl.multiple_of(r * T + (1 - odd) * half, 16), half)

    def near_copy(a, r):
        return copy(m.as_.at[a, r], m.ar_.at[a, r], m.a_send.at[a, r], m.a_recv.at[a, r], (d, c, across))

    def far_copy(a, r):
        return copy(m.bs_.at[a, r], m.br_.at[a, r], m.b_send.at[a, r], m.b_recv.at[a, r], (d, c, far))

    def back_copy(a, r):
        out = (m.ov, m.iv)[a].at[mine(r)]
        return copy(out, out, m.c_send.at[a, r], m.c_recv.at[a, r], (d, c, across))

    def back_arrived(a, r):
        out = (m.ov, m.iv)[a].at[theirs(r)]
        copy(out, out, m.c_send.at[a, r], m.c_recv.at[a, r], (d, c, across)).wait_recv()

    def chip_sum(a, r):
        near_copy(a, r).wait_recv()
        m.bs_[a, r] = (m.keep[a, r].astype(F32) + m.ar_[a, r].astype(F32)).astype(BF16)
        if ntn == 4:
            far_copy(a, r).start()

    def full_sum(a, r):
        total = m.bs_[a, r].astype(F32)
        if ntn == 4:
            far_copy(a, r).wait_recv()
            total = total + m.br_[a, r].astype(F32)
        return total

    @pl.loop(0, R)
    def _(r):
        b, cm = m.mix[row(r), C : C + LANES], m.mix[row(r), C + LANES : V]
        lead, _ = leads(r)
        carried = nt(cm, m.sin[r]) * spread(lead)
        m.ys[row(r), :] = carried
        ssd = m.ins[row(r), :] + carried + m.par[6:7, :C] * m.mix[row(r), :C].astype(F32)
        m.ssd[row(r), :] = ssd
        gate = nn(m.nrm[row(r), :], m.wz[...]).astype(BF16).astype(F32)
        m.zv[row(r), :] = gate.astype(BF16)
        gated = ssd * (gate * sigmoid(gate))
        m.gated[row(r), :C] = gated
        dy = nn(m.cv[row(r), :], m.wo[...])
        m.dy[row(r), :] = dy
        gain = m.par[5:6, :C]
        squares = jnp.sum(gated * gated, axis=-1, keepdims=True)
        inner = jnp.sum(dy * gain * gated, axis=-1, keepdims=True)
        both = jnp.where(lane == 0, squares, jnp.where(lane == 1, inner, 0.0))
        m.sums[t, r] = jnp.transpose(both)[0:8, :]
        for k in range(1, ntn):
            sums_copy(r, k).start()
        m.yg[row(r), :] = (gated * gain).astype(BF16)
        m.as_[0, r] = nt(m.yg[theirs(r), :], m.wo[...]).astype(BF16)
        near_copy(0, r).start()
        m.keep[0, r] = nt(m.yg[mine(r), :], m.wo[...])

    @pl.loop(0, R)
    def _(r):
        chip_sum(0, r)
        for k in range(1, ntn):
            sums_arrived(r, at_ten(k))
        total = m.sums[0, r]
        for who in range(1, ntn):
            total = total + m.sums[who, r]
        m.tot[0:8, :] = total
        columns = jnp.transpose(m.tot[...])
        scale = lax.rsqrt(columns[:, 0:1] * (1.0 / (C * ntn)) + EPS)
        m.rms[row(r), :] = jnp.broadcast_to(scale, (T, LANES))
        inner = columns[:, 1:2] * (1.0 / (C * ntn)) * scale * scale * scale
        gated, dy, gate, ssd = m.gated[row(r), :C], m.dy[row(r), :], m.zv[row(r), :].astype(F32), m.ssd[row(r), :]
        gain = m.par[5:6, :C]
        normal = gated * scale
        m.sm[t, 5:6, :C] += jnp.sum(dy * normal, axis=0, keepdims=True)
        m.yg[row(r), :] = (normal * gain).astype(BF16)
        d_gated = scale * dy * gain - gated * inner
        logistic = sigmoid(gate)
        m.dz[row(r), :] = (d_gated * ssd * (logistic * (1.0 + gate * (1.0 - logistic)))).astype(BF16)
        d_ssd = d_gated * (gate * logistic)
        m.ssd[row(r), :] = d_ssd
        lead, _ = leads(r)
        weighted = (d_ssd * spread(lead)).astype(BF16)
        m.wds[row(r), :] = weighted
        m.local[r] = tn(weighted, m.mix[row(r), C + LANES : V])

        @pl.when(c == nc - 1)
        def _():
            m.gsend[r] = m.local[r].astype(BF16)
            if nc > 1:
                grad_copy(r).start()

    gall, gyr, gzs, gzr = (m.ga0, m.ga1, m.ga2), (m.gy0, m.gy1, m.gy2), (m.gz0, m.gz1, m.gz2), (m.gr0, m.gr1, m.gr2)
    tall = (rp, rp, rp + HALO)

    def rs_dp(part, j, k):
        cc = at_ctx(j)
        return copy(
            gall[part].at[rows_at(at_dp(k) * nc + cc, tall[part])],
            gyr[part].at[k - 1, rows_at(cc, tall[part])],
            m.ry_send.at[part, j, k - 1],
            m.ry_recv.at[part, j, k - 1],
            (at_dp(k), c, t),
        )

    def rs_ctx(part, j):
        cc = at_ctx(j)
        return copy(
            gzs[part].at[rows_at(cc, tall[part])],
            gzr[part].at[c],
            m.rz_send.at[part, j],
            m.rz_recv.at[part, c],
            (d, cc, t),
        )

    def rs_arrived(part, cc):
        copy(gzr[part].at[cc], gzr[part].at[cc], m.rz_send.at[part, 0], m.rz_recv.at[part, cc], (d, c, t)).wait_recv()

    def rs_start(part):
        for j in list(range(1, nc)) + [0]:
            for k in range(1, nd):
                rs_dp(part, j, k).start()

    def rs_middle(part, j):
        cc = at_ctx(j)
        total = gall[part][rows_at(d * nc + cc, tall[part]), :].astype(F32)
        for k in range(1, nd):
            rs_dp(part, j, k).wait_recv()
            total = total + gyr[part][k - 1, rows_at(cc, tall[part]), :].astype(F32)
        own = j == 0

        def keep():
            gzr[part][c] = total.astype(BF16)

        def send():
            gzs[part][rows_at(cc, tall[part]), :] = total.astype(BF16)
            rs_ctx(part, j).start()

        if isinstance(j, int):
            keep() if own else send()
        else:
            pl.when(own)(keep)
            pl.when(jnp.logical_not(own))(send)

    def rs_end(part):
        for k in range(1, nc):
            rs_arrived(part, at_ctx(k))
        total = gzr[part][0].astype(F32)
        for cc in range(1, nc):
            total = total + gzr[part][cc].astype(F32)
        return total

    def rs_sent(part):
        for j in range(nc):
            for k in range(1, nd):
                rs_dp(part, j, k).wait_send()
            if j:
                rs_ctx(part, j).wait_send()

    m.ga1[:, C:] = nn(m.cott[...], m.yg[...]).astype(BF16)
    m.ga1[:, :C] = nn(m.nrmt[...], m.dz[...]).astype(BF16)
    rs_start(1)

    @pl.loop(0, R)
    def _(r):
        b, cm = m.mix[row(r), C : C + LANES], m.mix[row(r), C + LANES : V]
        m.mask[...] = (m.same[r] * m.upper[...]).astype(F32)
        m.scores[...] = nt(b, cm) * m.mask[...]
        run = m.run[row(r), :]
        losses = jnp.zeros((T, LANES), F32)
        for p in range(pairs):
            part = slice(p * LANES, (p + 1) * LANES)
            ds_pair = m.ssd[row(r), part].astype(BF16)
            xs_pair = m.xs[row(r), part]
            both = []
            for h in (2 * p, 2 * p + 1):
                pick = low_lanes if h % 2 == 0 else ~low_lanes
                decay = jnp.exp(jnp.minimum(m.runr[r, h : h + 1, :] - run[:, h : h + 1], 0.0))
                weight = decay * m.scores[...]
                both.append(nn(weight.astype(BF16), ds_pair))
                d_weight = nt(jnp.where(pick, xs_pair, jnp.zeros_like(xs_pair)), ds_pair)
                flow = d_weight * weight
                if h == 0:
                    m.dsc[...] = d_weight * decay
                else:
                    m.dsc[...] += d_weight * decay
                losses = jnp.where(lane == h, jnp.sum(flow, axis=1, keepdims=True), losses)
                m.drow[h : h + 1, :] = jnp.sum(flow, axis=0, keepdims=True)
            m.ins[row(r), part] = jnp.where(low_lanes, both[0], both[1])
        d_scores = (m.dsc[...] * m.mask[...]).astype(BF16)
        m.gated[row(r), :LANES] = nn(d_scores, cm)
        m.gated[row(r), LANES:S] = tn(d_scores, b)
        m.drun[row(r), :] = (
            jnp.transpose(m.drow[...])
            - losses
            + exact_right(m.ssd[row(r), :] * m.ys[row(r), :], fold)
        )

        @pl.when(c < nc - 1)
        def _():
            grad_copy(r).wait_recv()

            @pl.when(c > 0)
            def _():
                lead, _ = leads(r)
                for h in range(H):
                    here = slice(h * head, (h + 1) * head)
                    keep = lead[T - 1 : T, h : h + 1]
                    m.gsend[r, here, :] = (
                        m.local[r, here, :] + keep * m.gin[r, here, :].astype(F32)
                    ).astype(BF16)
                grad_copy(r).start()

    def final_out(r):
        value = m.hv[mine(r), :].astype(F32) + m.rms[mine(r), 0:1] * full_sum(0, r)
        m.ov[mine(r), :] = value.astype(BF16)
        back_copy(0, r).start()

    def adjoint(r):
        b, cm = m.mix[row(r), C : C + LANES], m.mix[row(r), C + LANES : V]
        lead, trail = leads(r)
        grad = m.gin[r]
        trailing = spread(trail)
        reach = nt(b, grad)
        scaled = m.xs[row(r), :].astype(F32) * trailing
        through = exact_right(scaled * reach, fold)
        d_run = m.drun[row(r), :] - through
        ends = jnp.sum(through, axis=0, keepdims=True)
        for h in range(H):
            here = slice(h * head, (h + 1) * head)
            joint = m.gin[r, here, :].astype(F32) * m.sin[r, here, :].astype(F32)
            joint = jnp.sum(jnp.sum(joint, axis=0, keepdims=True), axis=1, keepdims=True)
            ends = ends + jnp.where(lane[0:1] == h, joint * lead[T - 1 : T, :], 0.0)
        d_run = d_run + jnp.where(iota((T, LANES), 0) == T - 1, ends, 0.0)
        d_growth = exact_left(m.upper[...], d_run)
        step = m.step[row(r), :]
        d_xs = m.ins[row(r), :] + trailing * reach
        x = m.mix[row(r), :C].astype(F32)
        d_ssd = m.ssd[row(r), :]
        rate = m.par[8:9, :LANES]
        d_step = exact_right(d_xs * x, fold) + rate * d_growth
        m.sm[t, 7:8, LANES : 2 * LANES] += jnp.sum(step * d_growth, axis=0, keepdims=True) * rate
        m.sm[t, 7:8, 3 * LANES : 3 * LANES + C] += jnp.sum(d_ssd * x, axis=0, keepdims=True)
        d_pre = d_step * sigmoid(m.pre[row(r), :])
        m.sm[t, 7:8, :LANES] += jnp.sum(d_pre, axis=0, keepdims=True)
        m.dv[row(r), V:] = jnp.where(lane < H, d_pre, 0.0).astype(BF16)
        ring = lax.rem(r, 2)
        m.dcf[ring, :, :C] = (d_xs * spread(step) + m.par[6:7, :C] * d_ssd) * m.slope[row(r), :C]
        m.dcf[ring, :, C : C + LANES] = (
            m.gated[row(r), :LANES] + nn(scaled.astype(BF16), grad)
        ) * m.slope[row(r), C : C + LANES]
        m.dcf[ring, :, C + LANES :] = (
            m.gated[row(r), LANES:S] + nn(m.wds[row(r), :], m.sin[r])
        ) * m.slope[row(r), C + LANES :]

        @pl.when(c > 0)
        def _():
            m.edge[r] = m.dcf[ring, 0:EDGE, :]
            edge_copy(r).start()

    def finish(r):
        @pl.when(c < nc - 1)
        def _():
            edge_copy(r).wait_recv()

        ring = lax.rem(r, 2)
        seg = m.segc[row(r), :]
        reach = iota((EDGE, HALO), 1) + EDGE - iota((EDGE, HALO), 0)
        near = seg[T - EDGE : T, 0:1] == m.sega[pl.ds(r, 1), 0:HALO]
        for a in range(0, V, LANES):
            part = slice(a, a + LANES)
            d_conv = m.dcf[ring, :, part]
            low = d_conv.astype(BF16)
            after = m.dce[r, :, part]
            after = jnp.concatenate([after, jnp.zeros_like(after)], axis=0).astype(BF16)
            value = m.v[row(r), part].astype(F32)
            m.sm[t, 4:5, part] += jnp.sum(d_conv, axis=0, keepdims=True)
            m.sm[t, 0:1, part] += jnp.sum(d_conv * value, axis=0, keepdims=True)
            d_v = d_conv * m.par[0:1, part]
            for j in range(1, z.K):
                moved = nn(m.diag[z.K + j - 2] * m.same[r], low)
                last = nn((near & (reach == j)).astype(BF16), after)
                moved = jnp.concatenate([moved[: T - EDGE], moved[T - EDGE :] + last], axis=0)
                d_v = d_v + moved * m.par[j : j + 1, part]
                m.sm[t, j : j + 1, part] += jnp.sum(moved * value, axis=0, keepdims=True)
            m.dv[row(r), part] = d_v.astype(BF16)

        def d_normed(rows):
            return (
                nt(m.dv[rows, :C], m.wx[...])
                + nt(m.dv[rows, C:V], m.ws[...])
                + nt(m.dv[rows, V:], m.wst[...])
                + nt(m.dz[rows, :], m.wz[...])
            )

        def unit_of(rows):
            u = m.hv[rows, :].astype(F32)
            mean = jnp.sum(u * u, axis=-1, keepdims=True) * (1.0 / z.d_true)
            return u * lax.rsqrt(mean + EPS)

        value = d_normed(theirs(r))
        m.as_[1, r] = value.astype(BF16)
        near_copy(1, r).start()
        m.sm[t, 6:7, :D] += jnp.sum(value * unit_of(theirs(r)), axis=0, keepdims=True)
        value = d_normed(mine(r))
        m.keep[1, r] = value
        m.sm[t, 6:7, :D] += jnp.sum(value * unit_of(mine(r)), axis=0, keepdims=True)

    @pl.loop(0, max(R + 2, nc))
    def _(i):
        @pl.when(i < R)
        def _():
            final_out(i)
            adjoint(i)

        @pl.when(i < nc)
        def _():
            rs_middle(1, lax.rem(i + 1, nc))

        @pl.when((i >= 1) & (i < R + 1))
        def _():
            finish(i - 1)

        @pl.when((i >= 2) & (i < R + 2))
        def _():
            chip_sum(1, i - 2)

    width = S // ntn
    quarters = [m.dv[:, C + k * width : C + (k + 1) * width] for k in range(ntn)]
    value = nn(m.nrmt[...], jnp.concatenate(quarters[0::2] + quarters[1::2], axis=1))

    def share_copy():
        return copy(m.shs, m.shr, m.sh_send.at[0], m.sh_recv.at[0], (d, c, across))

    m.shk[...] = jnp.where(odd == 0, value[:, : z.Q], value[:, z.Q :])
    m.shs[...] = jnp.where(odd == 0, value[:, z.Q :], value[:, : z.Q]).astype(BF16)
    share_copy().start()
    steps = tn(m.dv[:, V:], m.nrm[...])[0:HALO, :]

    def small_ten(k):
        return copy(m.sm.at[t], m.sm.at[t], m.st_send.at[k], m.st_recv.at[t], (d, c, at_ten(k)))

    def small_dp(k):
        return copy(m.sd.at[d], m.sd.at[d], m.sd_send.at[k], m.sd_recv.at[d], (at_dp(k), c, t))

    def small_ctx(k):
        return copy(m.sc.at[c], m.sc.at[c], m.sc_send.at[k], m.sc_recv.at[c], (d, at_ctx(k), t))

    def arrived(buf, sems, who):
        copy(buf.at[who], buf.at[who], sems.at[who], sems.at[who], (d, c, t)).wait_recv()

    for k in range(1, ntn):
        small_ten(k).start()

    m.ga0[...] = nn(m.nrmt[...], m.dv[:, :C]).astype(BF16)
    share_copy().wait_recv()
    for b in range(nd * nc):
        here = slice(b * rp, (b + 1) * rp)
        there = b * (rp + HALO)
        m.ga2[there : there + rp, :] = (m.shk[here, :] + m.shr[here, :].astype(F32)).astype(BF16)
        m.ga2[there + rp : there + rp + HALO, :] = jnp.concatenate(
            [steps[:, here], jnp.zeros((HALO, LANES - rp), F32)], axis=1
        ).astype(BF16)
    rs_start(2)
    rs_start(0)

    for k in range(1, ntn):
        arrived(m.sm, m.st_recv, at_ten(k))
    common = m.sm[0]
    for who in range(1, ntn):
        common = common + m.sm[who]
    rows8, lanes8 = iota((8, z.WL), 0), iota((8, z.WL), 1)
    shared_here = (rows8 == 6) | ((rows8 < 5) & (lanes8 >= C))
    m.sd[d] = jnp.where(shared_here, common, m.sm[t])
    for k in range(1, nd):
        small_dp(k).start()

    def store(a, r):
        return pltpu.make_async_copy((m.ov, m.iv)[a].at[row(r)], (m.out, m.ing)[a].at[row(r)], m.l_out.at[a, r])

    for r in range(R):
        back_arrived(0, r)
        store(0, r).start()
    for j in list(range(1, nc)) + [0]:
        rs_middle(2, j)

    @pl.loop(0, R)
    def _(r):
        u = m.hv[mine(r), :].astype(F32)
        mean = jnp.sum(u * u, axis=-1, keepdims=True) * (1.0 / z.d_true)
        scale = lax.rsqrt(mean + EPS)
        unit = u * scale
        d_unit = full_sum(1, r) * gain_in
        inner = jnp.sum(d_unit * unit, axis=-1, keepdims=True) * (1.0 / z.d_true)
        value = m.cv[mine(r), :].astype(F32) + scale * (d_unit - unit * inner)
        m.iv[mine(r), :] = value.astype(BF16)
        back_copy(1, r).start()

        @pl.when(r < nc)
        def _():
            rs_middle(0, lax.rem(r + 1, nc))

    for j in range(R + 1, nc + 1):
        rs_middle(0, j % nc)

    for k in range(1, nd):
        arrived(m.sd, m.sd_recv, at_dp(k))
    total = m.sd[0]
    for who in range(1, nd):
        total = total + m.sd[who]
    m.sc[c] = total
    for k in range(1, nc):
        small_ctx(k).start()

    def last_copy():
        return copy(m.ls, m.lr, m.sh_send.at[1], m.sh_recv.at[1], (d, c, far))

    value = rs_end(2)
    if ntn == 4:
        m.ls[...] = value
        last_copy().start()
    else:
        m.gw2[...] = value
    m.gw1[...] = rs_end(1)

    for r in range(R):
        back_arrived(1, r)
        store(1, r).start()

    for k in range(1, nc):
        arrived(m.sc, m.sc_recv, at_ctx(k))
    total = m.sc[0]
    for who in range(1, nc):
        total = total + m.sc[who]
    m.small[...] = total

    if ntn == 4:
        last_copy().wait_recv()
        m.gw2[0:rp, :] = m.ls[0:rp, :] + m.lr[0:rp, :]
        m.gw2[rp:, :] = m.ls[rp:, :]
        last_copy().wait_send()

    m.gw0[...] = rs_end(0)

    for a in range(2):
        for r in range(R):
            store(a, r).wait()
            back_copy(a, r).wait_send()
            near_copy(a, r).wait_send()
            if ntn == 4:
                far_copy(a, r).wait_send()
    for p in range(PIECES):
        w_sent(p)
    half_copy().wait_send()
    for part in range(3):
        rs_sent(part)
    for r in range(R):
        for k in range(1, ntn):
            sums_copy(r, k).wait_send()

        @pl.when(c < nc - 1)
        def _():
            halo_copy(r).wait_send()
            state_copy(r).wait_send()

        @pl.when(c > 0)
        def _():
            grad_copy(r).wait_send()
            edge_copy(r).wait_send()

    share_copy().wait_send()
    for k in range(1, ntn):
        small_ten(k).wait_send()
    for k in range(1, nd):
        small_dp(k).wait_send()
    for k in range(1, nc):
        small_ctx(k).wait_send()


def finishing(z, out, ing, gw0, gw1, gw2, small, *outs):
    (o_out, o_ing, norm, heads, shared, step, taps, bias, staps, sbias, dsb, drate, dskip, gain, outw, tile, wide, sems) = outs
    C, S, D, H, rp, rows = z.C, z.S, z.D, z.H, z.rp, z.rows
    V = C + S
    head = C // H
    moves = [pltpu.make_async_copy(out, o_out, sems.at[0]), pltpu.make_async_copy(ing, o_ing, sems.at[1])]
    for move in moves:
        move.start()
    norm[...] = small[6:7, :D]
    heads[:, 0, :] = gw1[0:rows, :C]
    heads[:, 1, :] = gw0[0:rows, :]
    width = S // z.ntn
    pair = gw2[0:rows, :]
    if z.ntn == 4:
        upper = lax.axis_index("tensor") >= 2
        shared[...] = jnp.where(upper, pair[:, width:], pair[:, :width])
    else:
        shared[...] = pair
    tile[...] = jnp.zeros_like(tile)
    tile[0:HALO, :] = gw2[rp : rp + HALO, :]
    step[...] = jnp.transpose(tile[...])[0:rows, 0:H]
    taps[...] = small[0 : z.K, :C]
    bias[...] = small[4:5, :C]
    staps[...] = small[0 : z.K, C:V]
    sbias[...] = small[4:5, C:V]
    dsb[...] = small[7:8, :H]
    drate[...] = small[7:8, LANES : LANES + H]
    lanes = iota((1, H), 1)
    skip = jnp.zeros((1, H), F32)
    for h in range(H):
        begin = 3 * LANES + h * head
        skip = jnp.where(lanes == h, jnp.sum(small[7:8, begin : begin + head], axis=1, keepdims=True), skip)
    dskip[...] = skip
    gain[...] = small[5:6, :C]
    wide[...] = jnp.zeros_like(wide)
    wide[0:rp, :] = gw1[:, C:]
    outw[...] = jnp.transpose(wide[...])[:, 0:rows]
    for move in moves:
        move.wait()


def on_device(z, hidden_in, segment_ids, norm_gain, head_projection, shared_projection, step_projection,
              conv_heads, bias_heads, conv_shared, bias_shared, step_bias, log_decay, skip_gain, gate_gain,
              output_weight, out_cotangent):
    R, T, D, C, H, S = z.R, z.T, z.D, z.C, z.H, z.S
    rp, nd, nc, ntn, rows = z.rp, z.nd, z.nc, z.ntn, z.rows
    V = C + S
    blocks = nd * nc

    def widen(value):
        if rp == rows:
            return value
        value = value.reshape(value.shape[:-1] + (blocks, rows))
        value = jnp.pad(value, [(0, 0)] * (value.ndim - 1) + [(0, rp - rows)])
        return value.reshape(value.shape[:-2] + (D,))

    def narrow(value):
        if rp == rows:
            return value
        return value.reshape(value.shape[:-1] + (blocks, rp))[..., :rows].reshape(value.shape[:-1] + (z.d_true,))

    def taller(value, dim):
        if rp == rows:
            return value
        return jnp.pad(value, [(0, rp - rows if k == dim else 0) for k in range(value.ndim)])

    dma, vmem = pltpu.SemaphoreType.DMA, pltpu.VMEM
    N = R * T
    half = T // 2
    k0 = max(nd - 1, 1)
    ins = dict(
        hid=widen(hidden_in.reshape(N, z.d_true)), cot=widen(out_cotangent.reshape(N, z.d_true)),
        seg=segment_ids, ng=widen(norm_gain[None]), hp=taller(jnp.moveaxis(head_projection, 1, 0), 1),
        shp=taller(shared_projection, 0), stp=taller(step_projection, 0), ow=taller(output_weight, 1),
        ch=conv_heads, bh=bias_heads[None], cs=conv_shared, bs=bias_shared[None], sb=step_bias[None],
        ld=log_decay[None], sk=skip_gain[None], gg=gate_gain[None],
    )
    outs = dict(
        out=jax.ShapeDtypeStruct((N, D), BF16),
        ing=jax.ShapeDtypeStruct((N, D), BF16),
        gw0=jax.ShapeDtypeStruct((rp, C), F32),
        gw1=jax.ShapeDtypeStruct((rp, 2 * C), F32),
        gw2=jax.ShapeDtypeStruct((rp + HALO, z.Q), F32),
        small=jax.ShapeDtypeStruct((8, z.WL), F32),
    )
    scratch = dict(
        hv=vmem((N, D), BF16), cv=vmem((N, D), BF16), ov=vmem((N, D), BF16), iv=vmem((N, D), BF16),
        wx=vmem((D, C), BF16), ws=vmem((D, S), BF16), wt=vmem((blocks, HALO, LANES), BF16), wst=vmem((D, LANES), BF16),
        wz=vmem((D, C), BF16), wo=vmem((D, C), BF16), tile=vmem((LANES, LANES), F32), par=vmem((16, V), F32),
        segc=vmem((N, LANES), F32), segr=vmem((8 * -(-R // 8), T), F32),
        segb=vmem((8 * -(-R // 8), LANES), F32), sega=vmem((8 * -(-R // 8), LANES), F32),
        diag=vmem((2 * z.K - 2, T, T), BF16), lower=vmem((T, T), BF16), upper=vmem((T, T), BF16),
        same=vmem((R, T, T), BF16), mask=vmem((T, T), F32),
        hh=vmem((R * HALO, D), BF16), nrmh=vmem((R * HALO, D), BF16), vh=vmem((R * HALO, V), BF16),
        nrm=vmem((N, D), BF16), nrmt=vmem((D, N), BF16), cott=vmem((D, N), BF16),
        v=vmem((N, V), BF16), mix=vmem((N, V), BF16), slope=vmem((N, V), F32),
        pre=vmem((N, LANES), F32), step=vmem((N, LANES), F32), run=vmem((N, LANES), F32),
        runr=vmem((R, 8, T), F32), xs=vmem((N, C), BF16),
        fresh=vmem((R, C, LANES), F32), local=vmem((R, C, LANES), F32),
        ssend=vmem((R, C, LANES), BF16), sin=vmem((R, C, LANES), BF16),
        gsend=vmem((R, C, LANES), BF16), gin=vmem((R, C, LANES), BF16),
        scores=vmem((T, T), F32), dsc=vmem((T, T), F32), drow=vmem((LANES, T), F32), tot=vmem((LANES, T), F32),
        ins=vmem((N, C), F32), ys=vmem((N, C), F32), ssd=vmem((N, C), F32), zv=vmem((N, C), BF16),
        gated=vmem((N, max(C, S)), F32), dy=vmem((N, C), F32),
        yg=vmem((N, C), BF16), dz=vmem((N, C), BF16), wds=vmem((N, C), BF16),
        rms=vmem((N, LANES), F32), sums=vmem((ntn, R, 8, T), F32),
        as_=vmem((2, R, half, D), BF16), ar_=vmem((2, R, half, D), BF16),
        bs_=vmem((2, R, half, D), BF16), br_=vmem((2, R, half, D), BF16), keep=vmem((2, R, half, D), F32),
        ga0=vmem((D, C), BF16), ga1=vmem((D, 2 * C), BF16), ga2=vmem((blocks * (rp + HALO), z.Q), BF16),
        gy0=vmem((k0, nc * rp, C), BF16), gy1=vmem((k0, nc * rp, 2 * C), BF16), gy2=vmem((k0, nc * (rp + HALO), z.Q), BF16),
        gz0=vmem((nc * rp, C), BF16), gz1=vmem((nc * rp, 2 * C), BF16), gz2=vmem((nc * (rp + HALO), z.Q), BF16),
        gr0=vmem((nc, rp, C), BF16), gr1=vmem((nc, rp, 2 * C), BF16), gr2=vmem((nc, rp + HALO, z.Q), BF16),
        drun=vmem((N, LANES), F32), dcf=vmem((2, T, V), F32), edge=vmem((R, EDGE, V), F32),
        dce=vmem((R, EDGE, V), F32), dv=vmem((N, V + LANES), BF16),
        shs=vmem((D, z.Q), BF16), shr=vmem((D, z.Q), BF16), shk=vmem((D, z.Q), F32),
        ls=vmem((rp + HALO, z.Q), F32), lr=vmem((rp + HALO, z.Q), F32),
        sm=vmem((ntn, 8, z.WL), F32), sd=vmem((nd, 8, z.WL), F32), sc=vmem((nc, 8, z.WL), F32),
        l_in=dma((2,)), l_out=dma((2, R)),
        wz_send=dma((PIECES, 2, nc)), wd_send=dma((PIECES, nc, nd)), w_recv=dma((PIECES, nd, nc)),
        h_send=dma((R,)), h_recv=dma((R,)),
        s_send=dma((R,)), s_recv=dma((R,)), g_send=dma((R,)), g_recv=dma((R,)), e_send=dma((R,)), e_recv=dma((R,)),
        x_send=dma((R, ntn)), x_recv=dma((R, ntn)),
        a_send=dma((2, R)), a_recv=dma((2, R)), b_send=dma((2, R)), b_recv=dma((2, R)),
        c_send=dma((2, R)), c_recv=dma((2, R)),
        ry_send=dma((3, nc, k0)), ry_recv=dma((3, nc, k0)), rz_send=dma((3, nc)), rz_recv=dma((3, nc)),
        sh_send=dma((3,)), sh_recv=dma((3,)),
        st_send=dma((ntn,)), st_recv=dma((ntn,)), sd_send=dma((nd,)), sd_recv=dma((nd,)),
        sc_send=dma((nc,)), sc_recv=dma((nc,)),
    )
    names = list(ins) + list(outs) + list(scratch)
    whole = pl.BlockSpec(memory_space=pltpu.VMEM)
    large = pl.BlockSpec(memory_space=pl.ANY)
    raw = pl.pallas_call(
        functools.partial(kernel, z, names),
        out_shape=list(outs.values()),
        in_specs=[large] * 2 + [whole] * (len(ins) - 2),
        out_specs=[large] * 2 + [whole] * (len(outs) - 2),
        scratch_shapes=list(scratch.values()),
        compiler_params=pltpu.CompilerParams(
            collective_id=0, has_side_effects=True, vmem_limit_bytes=z.limit
        ),
    )(*ins.values())

    shapes = [
        ((N, D), BF16), ((N, D), BF16), ((1, D), F32), ((rows, 2, C), F32), ((rows, S // ntn), F32), ((rows, H), F32),
        ((z.K, C), F32), ((1, C), F32), ((z.K, S), F32), ((1, S), F32), ((1, H), F32), ((1, H), F32), ((1, H), F32),
        ((1, C), F32), ((C, rows), F32),
    ]
    outs = pl.pallas_call(
        functools.partial(finishing, z),
        out_shape=[jax.ShapeDtypeStruct(*shape) for shape in shapes],
        in_specs=[large] * 2 + [whole] * 4,
        out_specs=[large] * 2 + [whole] * (len(shapes) - 2),
        scratch_shapes=[vmem((LANES, LANES), F32), vmem((LANES, C), F32), dma((2,))],
    )(*raw)
    (block_out, input_grad, norm, heads, shared, step, taps, bias, staps, sbias, dsb, drate, dskip, gain, outw) = outs
    return (
        narrow(block_out).reshape(hidden_in.shape),
        narrow(input_grad).reshape(hidden_in.shape),
        narrow(norm)[0],
        heads, shared, step, taps, bias[0], staps, sbias[0], dsb[0], drate[0], dskip[0], gain[0], outw,
    )


def solution(mesh):
    nd, nc, ntn = (mesh.shape[name] for name in ("dp", "context", "tensor"))

    def body(*args):
        hidden, heads, shared = args[0], args[3], args[4]
        micro, seqs, tokens, width = hidden.shape
        rows = heads.shape[0]
        rp = -(-rows // 16) * 16
        inner = heads.shape[2]
        z = types.SimpleNamespace(
            R=micro * seqs, T=tokens, d_true=width, D=rp * nd * nc, rows=rows, rp=rp, nd=nd, nc=nc, ntn=ntn,
            C=inner, H=args[10].shape[0], S=shared.shape[1], K=args[6].shape[0],
            Q=shared.shape[1] // 2, limit=62 << 20,
        )
        z.WL = max(inner + z.S, z.D, 3 * LANES + inner)
        return on_device(z, *args)

    return jax.shard_map(
        body,
        mesh=mesh,
        in_specs=(
            P(None, "dp", "context", None),
            P(None, "dp", None),
            P(),
            P(("dp", "context"), None, "tensor"),
            P(("dp", "context"), None),
            P(("dp", "context"), "tensor"),
            P(None, "tensor"),
            P("tensor"),
            P(),
            P(),
            P("tensor"),
            P("tensor"),
            P("tensor"),
            P("tensor"),
            P("tensor", ("dp", "context")),
            P(None, "dp", "context", None),
        ),
        out_specs=(
            P(None, "dp", "context", None),
            P(None, "dp", "context", None),
            P(),
            P(("dp", "context"), None, "tensor"),
            P(("dp", "context"), "tensor"),
            P(("dp", "context"), "tensor"),
            P(None, "tensor"),
            P("tensor"),
            P(),
            P(),
            P("tensor"),
            P("tensor"),
            P("tensor"),
            P("tensor"),
            P("tensor", ("dp", "context")),
        ),
        check_vma=False,
    )
```

```python
import functools
import types

import jax
import jax.numpy as jnp
from jax import lax
from jax.experimental import pallas as pl
from jax.experimental.pallas import tpu as pltpu
from jax.sharding import PartitionSpec as P

EPS = 1e-05
F32 = jnp.float32
BF16 = jnp.bfloat16
MESH = pl.DeviceIdType.MESH
LANES = 128
HALO = 16
EDGE = 8
PIECES = 5
WIDE = 256
GROUP = 8


def nn(a, b):
    return lax.dot_general(a, b, (((1,), (0,)), ((), ())), preferred_element_type=F32)


def nt(a, b):
    return lax.dot_general(a, b, (((1,), (1,)), ((), ())), preferred_element_type=F32)


def tn(a, b):
    return lax.dot_general(a, b, (((0,), (0,)), ((), ())), preferred_element_type=F32)


def pieces_of(value, count):
    pieces = []
    for _ in range(count):
        piece = value.astype(BF16)
        pieces.append(piece)
        value = value - piece.astype(F32)
    return pieces


def exact_rows(value, ones):
    pieces = [piece.astype(F32) for piece in pieces_of(value, 3)]
    stacked = jnp.concatenate(pieces + [jnp.zeros_like(value)], axis=0).astype(BF16)
    out = nn(stacked, ones)
    return out[0:8] + out[8:16] + out[16:24]


def exact_right(value, ones):
    return sum(nn(piece, ones) for piece in pieces_of(value, 2))


def sigmoid(value):
    return 0.5 * jnp.tanh(0.5 * value) + 0.5


def iota(shape, dim):
    return lax.broadcasted_iota(jnp.int32, shape, dim)


def kernel(z, names, *refs):
    m = types.SimpleNamespace(**dict(zip(names, refs)))
    R, T, D, C, H, S = z.R, z.T, z.D, z.C, z.H, z.S
    rp, nd, nc, ntn = z.rp, z.nd, z.nc, z.ntn
    pairs = H // 2
    head = C // H
    V = C + S
    Z = V + LANES
    half = T // 2
    d, c, t = lax.axis_index("dp"), lax.axis_index("context"), lax.axis_index("tensor")
    odd = lax.rem(t, 2)
    across = t + 1 - 2 * odd
    far = lax.rem(t + 2, 4) if ntn == 4 else t

    def at_ctx(k):
        return lax.rem(c + k, nc)

    def at_dp(k):
        return lax.rem(d + k, nd)

    def at_ten(k):
        return lax.rem(t + k, ntn)

    def rows_at(place, size):
        return pl.ds(pl.multiple_of(place * size, 16), size)

    def block(dd, cc):
        return rows_at(dd * nc + cc, rp)

    def row(r):
        return rows_at(r, T)

    def lanes_at(place, size):
        return pl.ds(pl.multiple_of(place, LANES), size)

    def copy(src, dst, send, recv, dev):
        return pltpu.make_async_remote_copy(
            src_ref=src, dst_ref=dst, send_sem=send, recv_sem=recv, device_id=dev, device_id_type=MESH
        )

    def load(which):
        return pltpu.make_async_copy((m.hid, m.cot)[which], (m.hv, m.cv)[which], m.l_in.at[which])

    load(0).start()
    load(1).start()
    barrier = pltpu.get_barrier_semaphore()
    peers = [(d, at_ctx(k), t) for k in range(1, nc)]
    peers += [(at_dp(k), c, t) for k in range(1, nd)]
    peers += [(d, c, at_ten(k)) for k in range(1, ntn)]
    for peer in peers:
        pl.semaphore_signal(barrier, inc=1, device_id=peer, device_id_type=MESH)

    m.wall[block(d, c), 0:C] = m.hp[:, 1, :]
    m.wall[block(d, c), lanes_at(C + odd * z.Q, z.Q)] = jnp.where(odd == 0, m.shp[:, : z.Q], m.shp[:, z.Q :])
    m.wt[d * nc + c] = jnp.zeros((GROUP, LANES), F32)
    m.wt[d * nc + c, 0:H, 0:rp] = m.stp[...].astype(F32)
    pl.semaphore_wait(barrier, len(peers))

    def slot(p, dd, cc):
        if p == 2:
            return m.wt.at[dd * nc + cc]
        if p == 4:
            return m.wo.at[block(dd, cc)]
        place, size = ((0, C), (C + odd * z.Q, z.Q), None, (Z, C))[p]
        return m.wall.at[block(dd, cc), lanes_at(place, size)]

    def w_ctx(p, s, right):
        to = c + s if right else c - s
        here = slot(p, d, c)
        return copy(here, here, m.wz_send.at[p, int(right), s], m.w_recv.at[p, d, c], (d, to, t))

    def w_dp(p, cc, k):
        here = slot(p, d, cc)
        return copy(here, here, m.wd_send.at[p, cc, k], m.w_recv.at[p, d, cc], (at_dp(k), c, t))

    def w_arrived(p, dd, cc):
        there = slot(p, dd, cc)
        copy(there, there, m.wd_send.at[p, cc, 0], m.w_recv.at[p, dd, cc], (d, c, t)).wait_recv()

    def w_start(p):
        for k in range(1, nd):
            w_dp(p, c, k).start()
        for s in range(1, nc):
            pl.when(c + s < nc)(lambda: w_ctx(p, s, True).start())
            pl.when(c - s >= 0)(lambda: w_ctx(p, s, False).start())

    def w_relay(p):
        def one(cc):
            w_arrived(p, d, cc)
            for k in range(1, nd):
                w_dp(p, cc, k).start()

        for s in range(1, nc):
            pl.when(c - s >= 0)(lambda: one(c - s))
            pl.when(c + s < nc)(lambda: one(c + s))

    def w_rest(p):
        for k in range(1, nd):
            for cc in range(nc):
                w_arrived(p, at_dp(k), cc)

    def w_sent(p):
        for cc in range(nc):
            for k in range(1, nd):
                w_dp(p, cc, k).wait_send()
        for s in range(1, nc):
            pl.when(c + s < nc)(lambda: w_ctx(p, s, True).wait_send())
            pl.when(c - s >= 0)(lambda: w_ctx(p, s, False).wait_send())

    def half_copy():
        here = m.wall.at[:, lanes_at(C + odd * z.Q, z.Q)]
        return copy(here, here, m.sh_send.at[2], m.sh_recv.at[2], (d, c, across))

    def half_arrived():
        there = m.wall.at[:, lanes_at(C + (1 - odd) * z.Q, z.Q)]
        copy(there, there, m.sh_send.at[2], m.sh_recv.at[2], (d, c, across)).wait_recv()

    def halo_copy(r):
        return copy(
            m.hv.at[pl.ds(pl.multiple_of(r * T + T - HALO, 16), HALO)],
            m.hh.at[rows_at(r, HALO)],
            m.h_send.at[r],
            m.h_recv.at[r],
            (d, c + 1, t),
        )

    for p in range(3):
        w_start(p)
    load(0).wait()

    @pl.when(c < nc - 1)
    def _():
        for r in range(R):
            halo_copy(r).start()

    m.wall[block(d, c), Z:] = m.hp[:, 0, :]
    m.wo[block(d, c), :] = m.ow[...]

    m.par[0 : z.K, :C] = m.ch[...]
    m.par[0 : z.K, C:] = m.cs[...]
    m.par[4:5, :C] = m.bh[...][None]
    m.par[4:5, C:] = m.bs[...][None]
    m.par[5:6, :C] = m.gg[...][None]
    for h in range(H):
        m.par[6:7, h * head : (h + 1) * head] = jnp.broadcast_to(m.sk[0:1, h : h + 1], (1, head))
    m.gain[0:1, :] = m.ng[...][None]
    m.tile[...] = jnp.zeros_like(m.tile)
    m.tile[0:1, 0:H] = m.sb[...]
    m.tile[1:2, 0:H] = -jnp.exp(m.ld[...])
    turned = jnp.transpose(m.tile[...])
    m.hcol[...] = turned[0:GROUP, :]
    bias_col, rate_col = m.hcol[:, 0:1], m.hcol[:, 1:2]
    gain_in = m.gain[0:1, :]

    def normalize(u):
        u = u.astype(F32)
        mean = jnp.sum(u * u, axis=-1, keepdims=True) * (1.0 / z.d_true)
        return (u * lax.rsqrt(mean + EPS)) * gain_in

    length = m.seg.shape[-1]
    begin = c * T
    seqs = m.seg.shape[1]

    def ids_at(place, size):
        place = pl.multiple_of(place, LANES)
        lines = [m.seg[r // seqs, r % seqs : r % seqs + 1, pl.ds(place, size)] for r in range(R)]
        return jnp.concatenate(lines + [jnp.zeros_like(lines[0])] * (-R % 8), axis=0).astype(F32)

    now = ids_at(begin, T)
    before = jnp.where(c == 0, -1.0, ids_at(jnp.maximum(begin - LANES, 0), LANES))
    behind = jnp.where(c == nc - 1, -2.0, ids_at(jnp.minimum(begin + T, length - LANES), LANES))
    m.segr[...] = now
    m.segb[...] = before
    m.sega[...] = behind
    m.carried[...] = (now == before[:, LANES - 1 : LANES]).astype(F32)
    m.closing[...] = (now == now[:, T - 1 : T]).astype(F32)
    m.tot[...] = jnp.zeros_like(m.tot)
    m.tot[0 : now.shape[0], :] = now
    m.segc[...] = jnp.transpose(m.tot[...])
    away = iota((T, T), 0) - iota((T, T), 1)
    m.lower[...] = (away >= 0).astype(BF16)
    m.upper[...] = (away <= 0).astype(BF16)
    for r in range(R):
        same = m.segc[:, r : r + 1] == m.segr[r : r + 1, :]
        m.past[r] = (same & (away >= 0)).astype(BF16)
        m.next[r] = (same & (away <= 0)).astype(BF16)
        for j in range(1, z.K):
            m.down[r, j - 1] = (same & (away == j)).astype(BF16)
            m.up[r, j - 1] = (same & (away == -j)).astype(BF16)

    @pl.when(c == 0)
    def _():
        m.hh[...] = jnp.zeros_like(m.hh)
        m.sin[...] = jnp.zeros_like(m.sin)

    @pl.when(c == nc - 1)
    def _():
        m.gin[...] = jnp.zeros_like(m.gin)
        m.dce[...] = jnp.zeros_like(m.dce)

    m.sm[t] = jnp.zeros((8, z.WL), F32)
    m.hacc[...] = jnp.zeros_like(m.hacc)
    m.drow[...] = jnp.zeros_like(m.drow)
    m.gstep[...] = jnp.zeros_like(m.gstep)

    @pl.loop(0, R)
    def _(r):
        value = normalize(m.hv[row(r), :]).astype(BF16)
        m.nrm[row(r), :] = value
        m.nrmt[:, row(r)] = jnp.transpose(value)

    w_relay(0)
    w_start(3)
    load(1).wait()

    @pl.loop(0, R)
    def _(r):
        m.cott[:, row(r)] = jnp.transpose(m.cv[row(r), :])

    @pl.when(c > 0)
    def _():
        for r in range(R):
            halo_copy(r).wait_recv()

    m.nrmh[...] = normalize(m.hh[...]).astype(BF16)
    w_relay(1)
    w_relay(2)
    w_start(4)
    w_rest(0)

    low_lanes = iota((T, LANES), 1) < head
    lane = iota((T, LANES), 1)
    fold = (iota((C, LANES), 0) // head == iota((C, LANES), 1)).astype(F32)
    fold_run = fold.astype(BF16)
    fold_through = (
        (iota((C, LANES), 0) // head == iota((C, LANES), 1) - GROUP).astype(F32) - fold
    ).astype(BF16)
    fold_step = (iota((C, LANES), 0) // head == iota((C, LANES), 1) - 2 * GROUP).astype(BF16)
    RUN, STEP, LEAD, TRAIL = 0, GROUP, 2 * GROUP, 3 * GROUP

    def widened(values, base, p):
        a = base + 2 * p
        return jnp.where(low_lanes[: values.shape[0]], values[:, a : a + 1], values[:, a + 1 : a + 2])

    def spread(values, base):
        return jnp.concatenate([widened(values, base, p) for p in range(pairs)], axis=1)

    def state_copy(r):
        return copy(m.ssend.at[r], m.sin.at[r], m.s_send.at[r], m.s_recv.at[r], (d, c + 1, t))

    def grad_copy(r):
        return copy(m.gsend.at[r], m.gin.at[r], m.g_send.at[r], m.g_recv.at[r], (d, c - 1, t))

    def edge_copy(r):
        return copy(m.edge.at[r], m.dce.at[r], m.e_send.at[r], m.e_recv.at[r], (d, c - 1, t))

    def kept(r):
        return spread(m.cols[pl.ds(r * T + T - 1, 1), :], LEAD)

    def pair(p):
        return slice(p * LANES, (p + 1) * LANES)

    def convolve(r, lanes):
        reach = iota((EDGE, HALO), 1) - HALO - iota((EDGE, HALO), 0)
        seg = m.past[r]
        for a in range(lanes[0], lanes[1], WIDE):
            part = slice(a, min(a + WIDE, lanes[1]))
            value = m.v[row(r), part]
            before = m.vh[rows_at(r, HALO), part]
            conv = value.astype(F32) * m.par[0:1, part] + m.par[4:5, part]
            first = jnp.zeros((EDGE, conv.shape[1]), F32)
            for j in range(1, z.K):
                tap = m.par[j : j + 1, part]
                conv = conv + nn(m.down[r, j - 1], value) * tap
                first = first + nn(m.early[r, j - 1], before) * tap
            conv = jnp.concatenate([conv[0:EDGE] + first, conv[EDGE:]], axis=0)
            logistic = sigmoid(conv)
            m.mix[row(r), part] = (conv * logistic).astype(BF16)
            m.slope[row(r), part] = logistic * (1.0 + conv * (1.0 - logistic))

    reach = iota((HALO, HALO), 1) - HALO - iota((HALO, HALO), 0)
    ahead = iota((HALO, HALO), 1) + HALO - iota((HALO, HALO), 0)
    for r in range(R):
        near = m.segc[0:HALO, r : r + 1] == m.segb[r : r + 1, LANES - HALO : LANES]
        late = m.segc[T - HALO : T, r : r + 1] == m.sega[r : r + 1, 0:HALO]
        for j in range(1, z.K):
            m.early[r, j - 1] = (near & (reach == -j)).astype(BF16)[0:EDGE]
            m.late[r, j - 1] = (late & (ahead == j)).astype(BF16)

    m.vh[:, :C] = nn(m.nrmh[...], m.wall[:, :C]).astype(BF16)

    @pl.loop(0, R)
    def _(r):
        m.v[row(r), :C] = nn(m.nrm[row(r), :], m.wall[:, :C]).astype(BF16)
        convolve(r, (0, C))

    w_rest(1)
    half_copy().start()
    w_rest(2)
    m.wst[...] = jnp.concatenate([m.wt[b, :, 0:rp] for b in range(nd * nc)], axis=1)
    raw = nn(
        jnp.concatenate([m.wst[...], jnp.zeros((GROUP, D), F32)], axis=0).astype(BF16), m.nrmt[...]
    )[0:GROUP]
    pre = raw.astype(BF16).astype(F32) + bias_col
    m.pre[...] = pre
    m.step[...] = jnp.maximum(pre, 0.0) + jnp.log1p(jnp.exp(-jnp.abs(pre)))

    m.tile[...] = jnp.zeros_like(m.tile)
    for b in range(nd * nc):
        m.tile[0:GROUP, :] = m.wt[b]
        m.wall[b * rp : (b + 1) * rp, V:Z] = jnp.transpose(m.tile[...])[0:rp, :].astype(BF16)

    @pl.loop(0, R)
    def _(r):
        step = m.step[:, row(r)]
        run = exact_rows(step * rate_col, m.upper[...])
        m.runr[r] = run
        m.tot[0:GROUP, :] = run
        m.tot[GROUP : 2 * GROUP, :] = step
        m.tot[2 * GROUP : 3 * GROUP, :] = jnp.exp(run) * m.carried[pl.ds(r, 1), :]
        m.tot[3 * GROUP : 4 * GROUP, :] = jnp.exp(run[:, T - 1 : T] - run) * m.closing[pl.ds(r, 1), :]
        m.cols[row(r), :] = jnp.transpose(m.tot[...])
        for p in range(pairs):
            scaled = m.mix[row(r), pair(p)].astype(F32) * widened(m.cols[row(r), :], STEP, p)
            m.xs[row(r), pair(p)] = scaled.astype(BF16)
            m.xt[row(r), pair(p)] = (scaled * widened(m.cols[row(r), :], TRAIL, p)).astype(BF16)

    half_arrived()
    w_relay(3)
    m.vh[:, C:] = nn(m.nrmh[...], m.wall[:, C:V]).astype(BF16)

    @pl.loop(0, R)
    def _(r):
        m.v[row(r), C:] = nn(m.nrm[row(r), :], m.wall[:, C:V]).astype(BF16)
        convolve(r, (C, V))
        m.fresh[r] = tn(m.mix[row(r), C : C + LANES], m.xt[row(r), :])

        @pl.when(c == 0)
        def _():
            m.ssend[r] = m.fresh[r].astype(BF16)
            state_copy(r).start()

    @pl.loop(0, R)
    def _(r):
        b, cm = m.mix[row(r), C : C + LANES], m.mix[row(r), C + LANES : V]
        m.scores[...] = nt(cm, b) * m.past[r].astype(F32)
        for p in range(pairs):
            for a in range(0, T, LANES):
                rows, seen = slice(a, a + LANES), a + LANES
                here = pl.ds(pl.multiple_of(r * T, 16) + a, LANES)
                both = []
                for h in (2 * p, 2 * p + 1):
                    decay = jnp.exp(jnp.minimum(m.cols[here, h : h + 1] - m.runr[r, h : h + 1, :seen], 0.0))
                    weight = (decay * m.scores[rows, :seen]).astype(BF16)
                    both.append(nn(weight, m.xs[pl.ds(pl.multiple_of(r * T, 16), seen), pair(p)]))
                m.ins[here, pair(p)] = jnp.where(low_lanes[:LANES], both[0], both[1])

        @pl.when(c > 0)
        def _():
            state_copy(r).wait_recv()

            @pl.when(c < nc - 1)
            def _():
                m.ssend[r] = (m.fresh[r] + kept(r) * m.sin[r].astype(F32)).astype(BF16)
                state_copy(r).start()

    w_relay(4)
    w_rest(3)
    w_rest(4)

    def sums_copy(r, k):
        return copy(
            m.sums.at[t, r], m.sums.at[t, r], m.x_send.at[r, k], m.x_recv.at[r, t], (d, c, at_ten(k))
        )

    def sums_arrived(r, who):
        copy(
            m.sums.at[who, r], m.sums.at[who, r], m.x_send.at[r, 0], m.x_recv.at[r, who], (d, c, t)
        ).wait_recv()

    def mine(r):
        return pl.ds(pl.multiple_of(r * T + odd * half, 16), half)

    def theirs(r):
        return pl.ds(pl.multiple_of(r * T + (1 - odd) * half, 16), half)

    def near_copy(a, r):
        return copy(m.as_.at[a, r], m.ar_.at[a, r], m.a_send.at[a, r], m.a_recv.at[a, r], (d, c, across))

    def far_copy(a, r):
        return copy(m.bs_.at[a, r], m.br_.at[a, r], m.b_send.at[a, r], m.b_recv.at[a, r], (d, c, far))

    def back_copy(a, r):
        out = (m.ov, m.iv)[a].at[mine(r)]
        return copy(out, out, m.c_send.at[a, r], m.c_recv.at[a, r], (d, c, across))

    def back_arrived(a, r):
        out = (m.ov, m.iv)[a].at[theirs(r)]
        copy(out, out, m.c_send.at[a, r], m.c_recv.at[a, r], (d, c, across)).wait_recv()

    def give(a, r, value):
        first, second = value[:half], value[half:]
        m.as_[a, r] = jnp.where(odd == 0, second, first).astype(BF16)
        near_copy(a, r).start()
        m.keep[r] = jnp.where(odd == 0, first, second)

    def chip_sum(a, r):
        near_copy(a, r).wait_recv()
        m.bs_[a, r] = (m.keep[r] + m.ar_[a, r].astype(F32)).astype(BF16)
        if ntn == 4:
            far_copy(a, r).start()

    def full_sum(a, r):
        total = m.bs_[a, r].astype(F32)
        if ntn == 4:
            far_copy(a, r).wait_recv()
            total = total + m.br_[a, r].astype(F32)
        return total

    @pl.loop(0, R)
    def _(r):
        cm = m.mix[row(r), C + LANES : V]
        gate = nn(m.nrm[row(r), :], m.wall[:, Z:])
        m.zv[row(r), :] = gate.astype(BF16)
        m.dy[row(r), :] = nn(m.cv[row(r), :], m.wo[...])
        m.ys[row(r), :] = nn(cm, m.sin[r])
        squares = jnp.zeros((T, LANES), F32)
        inner = jnp.zeros((T, LANES), F32)
        for p in range(pairs):
            carried = m.ys[row(r), pair(p)] * widened(m.cols[row(r), :], LEAD, p)
            m.ys[row(r), pair(p)] = carried
            ssd = m.ins[row(r), pair(p)] + carried + m.par[6:7, pair(p)] * m.mix[row(r), pair(p)].astype(F32)
            m.ssd[row(r), pair(p)] = ssd
            gate = m.zv[row(r), pair(p)].astype(F32)
            gated = ssd * (gate * sigmoid(gate))
            m.gated[row(r), pair(p)] = gated
            scaled = gated * m.par[5:6, pair(p)]
            m.yg[row(r), pair(p)] = scaled.astype(BF16)
            squares = squares + gated * gated
            inner = inner + scaled * m.dy[row(r), pair(p)]
        squares = jnp.sum(squares, axis=-1, keepdims=True)
        inner = jnp.sum(inner, axis=-1, keepdims=True)
        both = jnp.where(lane == 0, squares, jnp.where(lane == 1, inner, 0.0))
        m.sums[t, r] = jnp.transpose(both)[0:8, :]
        for k in range(1, ntn):
            sums_copy(r, k).start()
        give(0, r, nt(m.yg[row(r), :], m.wo[...]))

    @pl.loop(0, R)
    def _(r):
        chip_sum(0, r)
        for k in range(1, ntn):
            sums_arrived(r, at_ten(k))
        total = m.sums[0, r]
        for who in range(1, ntn):
            total = total + m.sums[who, r]
        scale = lax.rsqrt(total[0:1] * (1.0 / (C * ntn)) + EPS)
        inner = total[1:2] * (1.0 / (C * ntn)) * scale * scale * scale
        m.tot[0:1, :] = scale
        m.tot[1:2, :] = inner
        columns = jnp.transpose(m.tot[...])
        m.rms[row(r), :] = columns
        scale = jnp.broadcast_to(columns[:, 0:1], (T, LANES))
        inner = jnp.broadcast_to(columns[:, 1:2], (T, LANES))
        for p in range(pairs):
            gated, dy, ssd = m.gated[row(r), pair(p)], m.dy[row(r), pair(p)], m.ssd[row(r), pair(p)]
            gate = m.zv[row(r), pair(p)].astype(F32)
            gain = m.par[5:6, pair(p)]
            normal = gated * scale
            m.sm[t, 5:6, pair(p)] += jnp.sum(dy * normal, axis=0, keepdims=True)
            m.yg[row(r), pair(p)] = (normal * gain).astype(BF16)
            d_gated = scale * dy * gain - gated * inner
            logistic = sigmoid(gate)
            m.dcat[row(r), Z + p * LANES : Z + (p + 1) * LANES] = (
                d_gated * ssd * (logistic * (1.0 + gate * (1.0 - logistic)))
            ).astype(BF16)
            d_ssd = d_gated * (gate * logistic)
            m.ssd[row(r), pair(p)] = d_ssd
            m.wds[row(r), pair(p)] = (d_ssd * widened(m.cols[row(r), :], LEAD, p)).astype(BF16)
        m.local[r] = tn(m.mix[row(r), C + LANES : V], m.wds[row(r), :])

        @pl.when(c == nc - 1)
        def _():
            m.gsend[r] = m.local[r].astype(BF16)
            if nc > 1:
                grad_copy(r).start()

    gall, gyr, gzs, gzr = (m.ga0, m.ga1, m.ga2), (m.gy0, m.gy1, m.gy2), (m.gz0, m.gz1, m.gz2), (m.gr0, m.gr1, m.gr2)
    tall = (rp, rp, rp + HALO)

    def rs_dp(part, j, k):
        cc = at_ctx(j)
        return copy(
            gall[part].at[rows_at(at_dp(k) * nc + cc, tall[part])],
            gyr[part].at[k - 1, rows_at(cc, tall[part])],
            m.ry_send.at[part, j, k - 1],
            m.ry_recv.at[part, j, k - 1],
            (at_dp(k), c, t),
        )

    def rs_ctx(part, j):
        cc = at_ctx(j)
        return copy(
            gzs[part].at[rows_at(cc, tall[part])],
            gzr[part].at[c],
            m.rz_send.at[part, j],
            m.rz_recv.at[part, c],
            (d, cc, t),
        )

    def rs_arrived(part, cc):
        copy(gzr[part].at[cc], gzr[part].at[cc], m.rz_send.at[part, 0], m.rz_recv.at[part, cc], (d, c, t)).wait_recv()

    def rs_start(part):
        for j in list(range(1, nc)) + [0]:
            for k in range(1, nd):
                rs_dp(part, j, k).start()

    def rs_middle(part, j):
        cc = at_ctx(j)
        total = gall[part][rows_at(d * nc + cc, tall[part]), :].astype(F32)
        for k in range(1, nd):
            rs_dp(part, j, k).wait_recv()
            total = total + gyr[part][k - 1, rows_at(cc, tall[part]), :].astype(F32)
        own = j == 0

        def keep():
            gzr[part][c] = total.astype(BF16)

        def send():
            gzs[part][rows_at(cc, tall[part]), :] = total.astype(BF16)
            rs_ctx(part, j).start()

        if isinstance(j, int):
            keep() if own else send()
        else:
            pl.when(own)(keep)
            pl.when(jnp.logical_not(own))(send)

    def rs_end(part):
        for k in range(1, nc):
            rs_arrived(part, at_ctx(k))
        total = gzr[part][0].astype(F32)
        for cc in range(1, nc):
            total = total + gzr[part][cc].astype(F32)
        return total

    def rs_sent(part):
        for j in range(nc):
            for k in range(1, nd):
                rs_dp(part, j, k).wait_send()
            if j:
                rs_ctx(part, j).wait_send()

    m.ga1[:, C:] = nn(m.cott[...], m.yg[...]).astype(BF16)
    m.ga1[:, :C] = nn(m.nrmt[...], m.dcat[:, Z:]).astype(BF16)
    rs_start(1)

    @pl.loop(0, R)
    def _(r):
        b, cm = m.mix[row(r), C : C + LANES], m.mix[row(r), C + LANES : V]
        m.scores[...] = nt(b, cm) * m.next[r].astype(F32)
        start = pl.multiple_of(r * T, 16)
        for a in range(0, T, LANES):
            rows, here, after = slice(a, a + LANES), pl.ds(start + a, LANES), pl.ds(start + a, T - a)
            losses = jnp.zeros((LANES, LANES), F32)
            for p in range(pairs):
                ds_pair = m.ssd[after, pair(p)].astype(BF16)
                xs_pair = m.xs[here, pair(p)]
                both = []
                for h in (2 * p, 2 * p + 1):
                    pick = low_lanes[:LANES] if h % 2 == 0 else ~low_lanes[:LANES]
                    decay = jnp.exp(jnp.minimum(m.runr[r, h : h + 1, a:] - m.cols[here, h : h + 1], 0.0))
                    weight = decay * m.scores[rows, a:]
                    both.append(nn(weight.astype(BF16), ds_pair))
                    d_weight = nt(jnp.where(pick, xs_pair, jnp.zeros_like(xs_pair)), ds_pair)
                    flow = d_weight * weight
                    if h == 0:
                        m.dsc[rows, a:] = d_weight * decay
                    else:
                        m.dsc[rows, a:] += d_weight * decay
                    losses = jnp.where(lane[:LANES] == h, jnp.sum(flow, axis=1, keepdims=True), losses)
                    down = jnp.sum(flow, axis=0, keepdims=True)
                    if a == 0:
                        m.drow[r, h : h + 1, :] = down
                    else:
                        m.drow[r, h : h + 1, a:] += down
                m.ins[here, pair(p)] = jnp.where(low_lanes[:LANES], both[0], both[1])
            m.drun[here, :] = exact_right(m.ssd[here, :] * m.ys[here, :], fold_run) - losses
            d_scores = (m.dsc[rows, a:] * m.next[r, rows, a:].astype(F32)).astype(BF16)
            m.gated[here, :LANES] = nn(d_scores, m.mix[after, C + LANES : V])
            d_after = tn(d_scores, m.mix[here, C : C + LANES])
            if a == 0:
                m.gated[after, LANES:S] = d_after
            else:
                m.gated[after, LANES:S] += d_after

        @pl.when(c < nc - 1)
        def _():
            grad_copy(r).wait_recv()

            @pl.when(c > 0)
            def _():
                m.gsend[r] = (m.local[r] + kept(r) * m.gin[r].astype(F32)).astype(BF16)
                grad_copy(r).start()

    def final_out(r):
        value = m.hv[mine(r), :].astype(F32) + m.rms[mine(r), 0:1] * full_sum(0, r)
        m.ov[mine(r), :] = value.astype(BF16)
        back_copy(0, r).start()

    def adjoint(r):
        b = m.mix[row(r), C : C + LANES]
        grad = m.gin[r]
        ring = lax.rem(r, 2)
        for p in range(pairs):
            trailing = widened(m.cols[row(r), :], TRAIL, p)
            reach = nn(b, m.gin[r, :, pair(p)]) * trailing
            x = m.mix[row(r), pair(p)].astype(F32)
            d_xs = m.ins[row(r), pair(p)] + reach
            d_ssd = m.ssd[row(r), pair(p)]
            m.prod[:, pair(p)] = m.xs[row(r), pair(p)].astype(F32) * reach
            m.prod[:, C + p * LANES : C + (p + 1) * LANES] = d_xs * x
            m.sm[t, 7:8, LANES + p * LANES : 2 * LANES + p * LANES] += jnp.sum(d_ssd * x, axis=0, keepdims=True)
            m.dcf[ring, :, pair(p)] = (
                d_xs * widened(m.cols[row(r), :], STEP, p) + m.par[6:7, pair(p)] * d_ssd
            ) * m.slope[row(r), pair(p)]
        m.dcf[ring, :, C : C + LANES] = (
            m.gated[row(r), :LANES] + nt(m.xt[row(r), :], grad)
        ) * m.slope[row(r), C : C + LANES]
        m.dcf[ring, :, C + LANES :] = (
            m.gated[row(r), LANES:S] + nt(m.wds[row(r), :], m.sin[r])
        ) * m.slope[row(r), C + LANES :]

        @pl.when(c > 0)
        def _():
            m.edge[r] = m.dcf[ring, 0:EDGE, :]
            edge_copy(r).start()

        m.drun[row(r), :] += exact_right(m.prod[:, :C], fold_through) + exact_right(m.prod[:, C:], fold_step)
        joint = jnp.sum(grad.astype(F32) * m.sin[r].astype(F32), axis=0, keepdims=True)
        joint = exact_right(jnp.broadcast_to(joint, (8, C)), fold_run)[0:1]
        last = m.cols[pl.ds(r * T + T - 1, 1), :]
        kept_lanes = jnp.concatenate([last[:, LEAD : LEAD + H], jnp.zeros((1, LANES - H), F32)], axis=1)
        m.drun[pl.ds(r * T + T - 1, 1), :] += joint * kept_lanes
        turned = jnp.transpose(m.drun[row(r), :])
        through = jnp.sum(turned[GROUP : 2 * GROUP], axis=1, keepdims=True)
        d_run = turned[0:GROUP] + m.drow[r]
        d_run = d_run + jnp.where(iota((GROUP, T), 1) == T - 1, through, 0.0)
        d_growth = exact_rows(d_run, m.lower[...])
        d_step = turned[2 * GROUP : 3 * GROUP] + rate_col * d_growth
        d_pre = d_step * sigmoid(m.pre[:, row(r)])
        m.hacc[0:GROUP, :] += d_pre
        m.hacc[GROUP : 2 * GROUP, :] += m.step[:, row(r)] * d_growth * rate_col
        d_pre = jnp.where(iota((GROUP, T), 0) < H, d_pre, 0.0)
        m.gstep[...] += nn(jnp.concatenate([d_pre, jnp.zeros_like(d_pre)], axis=0).astype(BF16), m.nrm[row(r), :])
        m.tot[0:GROUP, :] = d_pre
        m.dcat[row(r), V:Z] = jnp.transpose(m.tot[...]).astype(BF16)

    def finish(r):
        @pl.when(c < nc - 1)
        def _():
            edge_copy(r).wait_recv()

        ring = lax.rem(r, 2)
        for a in range(0, V, WIDE):
            part = slice(a, min(a + WIDE, V))
            d_conv = m.dcf[ring, :, part]
            low = d_conv.astype(BF16)
            after = m.dce[r, :, part]
            after = jnp.concatenate([after, jnp.zeros_like(after)], axis=0).astype(BF16)
            value = m.v[row(r), part].astype(F32)
            m.sm[t, 4:5, part] += jnp.sum(d_conv, axis=0, keepdims=True)
            m.sm[t, 0:1, part] += jnp.sum(d_conv * value, axis=0, keepdims=True)
            d_v = d_conv * m.par[0:1, part]
            for j in range(1, z.K):
                moved = nn(m.up[r, j - 1], low)
                last = nn(m.late[r, j - 1], after)
                moved = jnp.concatenate([moved[: T - HALO], moved[T - HALO :] + last], axis=0)
                d_v = d_v + moved * m.par[j : j + 1, part]
                m.sm[t, j : j + 1, part] += jnp.sum(moved * value, axis=0, keepdims=True)
            m.dcat[row(r), part] = d_v.astype(BF16)

        value = nt(m.dcat[row(r), :], m.wall[...])
        give(1, r, value)
        u = m.hv[row(r), :].astype(F32)
        mean = jnp.sum(u * u, axis=-1, keepdims=True) * (1.0 / z.d_true)
        m.sm[t, 6:7, :D] += jnp.sum(value * (u * lax.rsqrt(mean + EPS)), axis=0, keepdims=True)

    m.tot[...] = jnp.zeros_like(m.tot)

    @pl.loop(0, max(R + 2, nc))
    def _(i):
        @pl.when(i < R)
        def _():
            final_out(i)
            adjoint(i)

        @pl.when(i < nc)
        def _():
            rs_middle(1, lax.rem(i + 1, nc))

        @pl.when((i >= 1) & (i < R + 1))
        def _():
            finish(i - 1)

        @pl.when((i >= 2) & (i < R + 2))
        def _():
            chip_sum(1, i - 2)

    width = S // ntn
    quarters = [m.dcat[:, C + k * width : C + (k + 1) * width] for k in range(ntn)]
    value = nn(m.nrmt[...], jnp.concatenate(quarters[0::2] + quarters[1::2], axis=1))

    def share_copy():
        return copy(m.shs, m.shr, m.sh_send.at[0], m.sh_recv.at[0], (d, c, across))

    m.shk[...] = jnp.where(odd == 0, value[:, : z.Q], value[:, z.Q :])
    m.shs[...] = jnp.where(odd == 0, value[:, z.Q :], value[:, : z.Q]).astype(BF16)
    share_copy().start()

    def small_ten(k):
        return copy(m.sm.at[t], m.sm.at[t], m.st_send.at[k], m.st_recv.at[t], (d, c, at_ten(k)))

    def small_dp(k):
        return copy(m.sd.at[d], m.sd.at[d], m.sd_send.at[k], m.sd_recv.at[d], (at_dp(k), c, t))

    def small_ctx(k):
        return copy(m.sc.at[c], m.sc.at[c], m.sc_send.at[k], m.sc_recv.at[c], (d, at_ctx(k), t))

    def arrived(buf, sems, who):
        copy(buf.at[who], buf.at[who], sems.at[who], sems.at[who], (d, c, t)).wait_recv()

    m.tile[...] = jnp.zeros_like(m.tile)
    m.tile[0 : 2 * GROUP, :] = jnp.broadcast_to(
        jnp.sum(m.hacc[...], axis=1, keepdims=True), (2 * GROUP, LANES)
    )
    m.sm[t, 7:8, 0:LANES] = jnp.transpose(m.tile[...])[0:1, :]
    for k in range(1, ntn):
        small_ten(k).start()

    m.ga0[...] = nn(m.nrmt[...], m.dcat[:, :C]).astype(BF16)
    share_copy().wait_recv()
    for b in range(nd * nc):
        here = slice(b * rp, (b + 1) * rp)
        there = b * (rp + HALO)
        m.ga2[there : there + rp, :] = (m.shk[here, :] + m.shr[here, :].astype(F32)).astype(BF16)
        steps = m.gstep[:, here]
        m.ga2[there + rp : there + rp + HALO, :] = jnp.concatenate(
            [steps, jnp.zeros((HALO, LANES - rp), F32)], axis=1
        ).astype(BF16)
    rs_start(2)
    rs_start(0)

    for k in range(1, ntn):
        arrived(m.sm, m.st_recv, at_ten(k))
    common = m.sm[0]
    for who in range(1, ntn):
        common = common + m.sm[who]
    rows8, lanes8 = iota((8, z.WL), 0), iota((8, z.WL), 1)
    shared_here = (rows8 == 6) | ((rows8 < 5) & (lanes8 >= C))
    m.sd[d] = jnp.where(shared_here, common, m.sm[t])
    for k in range(1, nd):
        small_dp(k).start()

    def store(a, r):
        return pltpu.make_async_copy((m.ov, m.iv)[a].at[row(r)], (m.out, m.ing)[a].at[row(r)], m.l_out.at[a, r])

    for r in range(R):
        back_arrived(0, r)
        store(0, r).start()
    for j in list(range(1, nc)) + [0]:
        rs_middle(2, j)

    @pl.loop(0, R)
    def _(r):
        u = m.hv[mine(r), :].astype(F32)
        mean = jnp.sum(u * u, axis=-1, keepdims=True) * (1.0 / z.d_true)
        scale = lax.rsqrt(mean + EPS)
        unit = u * scale
        d_unit = full_sum(1, r) * gain_in
        inner = jnp.sum(d_unit * unit, axis=-1, keepdims=True) * (1.0 / z.d_true)
        value = m.cv[mine(r), :].astype(F32) + scale * (d_unit - unit * inner)
        m.iv[mine(r), :] = value.astype(BF16)
        back_copy(1, r).start()

        @pl.when(r < nc)
        def _():
            rs_middle(0, lax.rem(r + 1, nc))

    for j in range(R + 1, nc + 1):
        rs_middle(0, j % nc)

    for k in range(1, nd):
        arrived(m.sd, m.sd_recv, at_dp(k))
    total = m.sd[0]
    for who in range(1, nd):
        total = total + m.sd[who]
    m.sc[c] = total
    for k in range(1, nc):
        small_ctx(k).start()

    def last_copy():
        return copy(m.ls, m.lr, m.sh_send.at[1], m.sh_recv.at[1], (d, c, far))

    value = rs_end(2)
    if ntn == 4:
        m.ls[...] = value
        last_copy().start()
    else:
        m.gw2[...] = value
    m.gw1[...] = rs_end(1)

    for r in range(R):
        back_arrived(1, r)
        store(1, r).start()

    for k in range(1, nc):
        arrived(m.sc, m.sc_recv, at_ctx(k))
    total = m.sc[0]
    for who in range(1, nc):
        total = total + m.sc[who]
    m.small[...] = total

    if ntn == 4:
        last_copy().wait_recv()
        m.gw2[0:rp, :] = m.ls[0:rp, :] + m.lr[0:rp, :]
        m.gw2[rp:, :] = m.ls[rp:, :]
        last_copy().wait_send()

    m.gw0[...] = rs_end(0)

    for a in range(2):
        for r in range(R):
            store(a, r).wait()
            back_copy(a, r).wait_send()
            near_copy(a, r).wait_send()
            if ntn == 4:
                far_copy(a, r).wait_send()
    for p in range(PIECES):
        w_sent(p)
    half_copy().wait_send()
    for part in range(3):
        rs_sent(part)
    for r in range(R):
        for k in range(1, ntn):
            sums_copy(r, k).wait_send()

        @pl.when(c < nc - 1)
        def _():
            halo_copy(r).wait_send()
            state_copy(r).wait_send()

        @pl.when(c > 0)
        def _():
            grad_copy(r).wait_send()
            edge_copy(r).wait_send()

    share_copy().wait_send()
    for k in range(1, ntn):
        small_ten(k).wait_send()
    for k in range(1, nd):
        small_dp(k).wait_send()
    for k in range(1, nc):
        small_ctx(k).wait_send()


def finishing(z, out, ing, gw0, gw1, gw2, small, *outs):
    (o_out, o_ing, norm, heads, shared, step, taps, bias, staps, sbias, dsb, drate, dskip, gain, outw, tile, sems) = outs
    C, S, D, H, rp, rows = z.C, z.S, z.D, z.H, z.rp, z.rows
    V = C + S
    head = C // H
    moves = [pltpu.make_async_copy(out, o_out, sems.at[0]), pltpu.make_async_copy(ing, o_ing, sems.at[1])]
    for move in moves:
        move.start()
    norm[...] = small[6, :D]
    heads[:, 0, :] = gw1[0:rows, :C]
    heads[:, 1, :] = gw0[0:rows, :]
    width = S // z.ntn
    tile[...] = jnp.zeros_like(tile)
    tile[0:rp, :] = gw2[0:rp, :]
    pair = jnp.transpose(tile[...])
    if z.ntn == 4:
        upper = lax.axis_index("tensor") >= 2
        pair = jnp.where(upper, pair[width:], pair[:width])
    shared[...] = pair[:, 0:rows]
    step[...] = gw2[rp : rp + H, 0:rows]
    taps[...] = small[0 : z.K, :C]
    bias[...] = small[4, :C]
    staps[...] = small[0 : z.K, C:V]
    sbias[...] = small[4, C:V]
    dsb[...] = small[7, :H]
    drate[...] = small[7, GROUP : GROUP + H]
    lanes = iota((1, H), 1)
    skip = jnp.zeros((1, H), F32)
    for h in range(H):
        begin = LANES + h * head
        skip = jnp.where(lanes == h, jnp.sum(small[7:8, begin : begin + head], axis=1, keepdims=True), skip)
    tile[0:1, 0:H] = skip
    dskip[...] = tile[0, 0:H]
    gain[...] = small[5, :C]
    outw[...] = gw1[0:rows, C:]
    for move in moves:
        move.wait()


def on_device(z, hidden_in, segment_ids, norm_gain, head_projection, shared_projection, step_projection,
              conv_heads, bias_heads, conv_shared, bias_shared, step_bias, log_decay, skip_gain, gate_gain,
              output_weight, out_cotangent):
    R, T, D, C, H, S = z.R, z.T, z.D, z.C, z.H, z.S
    rp, nd, nc, ntn, rows = z.rp, z.nd, z.nc, z.ntn, z.rows
    V = C + S
    blocks = nd * nc
    R8 = 8 * -(-R // 8)

    def widen(value):
        if rp == rows:
            return value
        value = value.reshape(value.shape[:-1] + (blocks, rows))
        value = jnp.pad(value, [(0, 0)] * (value.ndim - 1) + [(0, rp - rows)])
        return value.reshape(value.shape[:-2] + (D,))

    def narrow(value):
        if rp == rows:
            return value
        return value.reshape(value.shape[:-1] + (blocks, rp))[..., :rows].reshape(value.shape[:-1] + (z.d_true,))

    def taller(value, dim):
        if rp == rows:
            return value
        return jnp.pad(value, [(0, rp - rows if k == dim else 0) for k in range(value.ndim)])

    dma, vmem = pltpu.SemaphoreType.DMA, pltpu.VMEM
    N = R * T
    half = T // 2
    k0 = max(nd - 1, 1)
    ins = dict(
        hid=widen(hidden_in.reshape(N, z.d_true)), cot=widen(out_cotangent.reshape(N, z.d_true)),
        seg=segment_ids, ng=widen(norm_gain), hp=taller(head_projection, 0),
        shp=taller(shared_projection, 0), stp=taller(step_projection.T, 1), ow=taller(output_weight.T, 0),
        ch=conv_heads, bh=bias_heads, cs=conv_shared, bs=bias_shared, sb=step_bias[None],
        ld=log_decay[None], sk=skip_gain[None], gg=gate_gain,
    )
    outs = dict(
        out=jax.ShapeDtypeStruct((N, D), BF16),
        ing=jax.ShapeDtypeStruct((N, D), BF16),
        gw0=jax.ShapeDtypeStruct((rp, C), F32),
        gw1=jax.ShapeDtypeStruct((rp, 2 * C), F32),
        gw2=jax.ShapeDtypeStruct((rp + HALO, z.Q), F32),
        small=jax.ShapeDtypeStruct((8, z.WL), F32),
    )
    scratch = dict(
        hv=vmem((N, D), BF16), cv=vmem((N, D), BF16), ov=vmem((N, D), BF16), iv=vmem((N, D), BF16),
        wall=vmem((D, V + LANES + C), BF16), wo=vmem((D, C), BF16), wt=vmem((blocks, GROUP, LANES), F32),
        wst=vmem((GROUP, D), F32), hcol=vmem((GROUP, LANES), F32), tile=vmem((LANES, LANES), F32), gain=vmem((8, D), F32), par=vmem((16, V), F32),
        segc=vmem((T, LANES), F32), segr=vmem((R8, T), F32), carried=vmem((R8, T), F32), closing=vmem((R8, T), F32),
        segb=vmem((R8, LANES), F32), sega=vmem((R8, LANES), F32),
        early=vmem((R, z.K - 1, EDGE, HALO), BF16), late=vmem((R, z.K - 1, HALO, HALO), BF16),
        down=vmem((R, z.K - 1, T, T), BF16), up=vmem((R, z.K - 1, T, T), BF16), lower=vmem((T, T), BF16), upper=vmem((T, T), BF16),
        past=vmem((R, T, T), BF16), next=vmem((R, T, T), BF16),
        hh=vmem((R * HALO, D), BF16), nrmh=vmem((R * HALO, D), BF16), vh=vmem((R * HALO, V), BF16),
        nrm=vmem((N, D), BF16), nrmt=vmem((D, N), BF16), cott=vmem((D, N), BF16),
        v=vmem((N, V), BF16), mix=vmem((N, V), BF16), slope=vmem((N, V), F32),
        pre=vmem((GROUP, N), F32), step=vmem((GROUP, N), F32), cols=vmem((N, LANES), F32), xt=vmem((N, C), BF16),
        runr=vmem((R, 8, T), F32), xs=vmem((N, C), BF16),
        fresh=vmem((R, LANES, C), F32), local=vmem((R, LANES, C), F32),
        ssend=vmem((R, LANES, C), BF16), sin=vmem((R, LANES, C), BF16),
        gsend=vmem((R, LANES, C), BF16), gin=vmem((R, LANES, C), BF16),
        scores=vmem((T, T), F32), dsc=vmem((T, T), F32), drow=vmem((R, GROUP, T), F32), tot=vmem((LANES, T), F32),
        ins=vmem((N, C), F32), ys=vmem((N, C), F32), ssd=vmem((N, C), F32), zv=vmem((N, C), BF16),
        gated=vmem((N, max(C, S)), F32), dy=vmem((N, C), F32),
        yg=vmem((N, C), BF16), wds=vmem((N, C), BF16),
        rms=vmem((N, LANES), F32), sums=vmem((ntn, R, 8, T), F32),
        as_=vmem((2, R, half, D), BF16), ar_=vmem((2, R, half, D), BF16),
        bs_=vmem((2, R, half, D), BF16), br_=vmem((2, R, half, D), BF16), keep=vmem((R, half, D), F32),
        ga0=vmem((D, C), BF16), ga1=vmem((D, 2 * C), BF16), ga2=vmem((blocks * (rp + HALO), z.Q), BF16),
        gy0=vmem((k0, nc * rp, C), BF16), gy1=vmem((k0, nc * rp, 2 * C), BF16), gy2=vmem((k0, nc * (rp + HALO), z.Q), BF16),
        gz0=vmem((nc * rp, C), BF16), gz1=vmem((nc * rp, 2 * C), BF16), gz2=vmem((nc * (rp + HALO), z.Q), BF16),
        gr0=vmem((nc, rp, C), BF16), gr1=vmem((nc, rp, 2 * C), BF16), gr2=vmem((nc, rp + HALO, z.Q), BF16),
        drun=vmem((N, LANES), F32), dcf=vmem((2, T, V), F32), edge=vmem((R, EDGE, V), F32),
        dce=vmem((R, EDGE, V), F32), dcat=vmem((N, V + LANES + C), BF16),
        prod=vmem((T, 2 * C), F32), hacc=vmem((2 * GROUP, T), F32), gstep=vmem((HALO, D), F32),
        shs=vmem((D, z.Q), BF16), shr=vmem((D, z.Q), BF16), shk=vmem((D, z.Q), F32),
        ls=vmem((rp + HALO, z.Q), F32), lr=vmem((rp + HALO, z.Q), F32),
        sm=vmem((ntn, 8, z.WL), F32), sd=vmem((nd, 8, z.WL), F32), sc=vmem((nc, 8, z.WL), F32),
        l_in=dma((2,)), l_out=dma((2, R)),
        wz_send=dma((PIECES, 2, nc)), wd_send=dma((PIECES, nc, nd)), w_recv=dma((PIECES, nd, nc)),
        h_send=dma((R,)), h_recv=dma((R,)),
        s_send=dma((R,)), s_recv=dma((R,)), g_send=dma((R,)), g_recv=dma((R,)), e_send=dma((R,)), e_recv=dma((R,)),
        x_send=dma((R, ntn)), x_recv=dma((R, ntn)),
        a_send=dma((2, R)), a_recv=dma((2, R)), b_send=dma((2, R)), b_recv=dma((2, R)),
        c_send=dma((2, R)), c_recv=dma((2, R)),
        ry_send=dma((3, nc, k0)), ry_recv=dma((3, nc, k0)), rz_send=dma((3, nc)), rz_recv=dma((3, nc)),
        sh_send=dma((3,)), sh_recv=dma((3,)),
        st_send=dma((ntn,)), st_recv=dma((ntn,)), sd_send=dma((nd,)), sd_recv=dma((nd,)),
        sc_send=dma((nc,)), sc_recv=dma((nc,)),
    )
    names = list(ins) + list(outs) + list(scratch)
    whole = pl.BlockSpec(memory_space=pltpu.VMEM)
    large = pl.BlockSpec(memory_space=pl.ANY)
    raw = pl.pallas_call(
        functools.partial(kernel, z, names),
        out_shape=list(outs.values()),
        in_specs=[large] * 2 + [whole] * (len(ins) - 2),
        out_specs=[large] * 2 + [whole] * (len(outs) - 2),
        scratch_shapes=list(scratch.values()),
        compiler_params=pltpu.CompilerParams(
            collective_id=0, has_side_effects=True, vmem_limit_bytes=z.limit
        ),
    )(*ins.values())

    shapes = [
        ((N, D), BF16), ((N, D), BF16), ((D,), F32), ((rows, 2, C), F32), ((S // ntn, rows), F32), ((H, rows), F32),
        ((z.K, C), F32), ((C,), F32), ((z.K, S), F32), ((S,), F32), ((H,), F32), ((H,), F32), ((H,), F32),
        ((C,), F32), ((rows, C), F32),
    ]
    outs = pl.pallas_call(
        functools.partial(finishing, z),
        out_shape=[jax.ShapeDtypeStruct(*shape) for shape in shapes],
        in_specs=[whole] * 6,
        out_specs=[large] * 2 + [whole] * (len(shapes) - 2),
        scratch_shapes=[vmem((LANES, LANES), F32), dma((2,))],
        compiler_params=pltpu.CompilerParams(vmem_limit_bytes=16 << 20),
    )(*raw)
    (block_out, input_grad, norm, heads, shared, step, taps, bias, staps, sbias, dsb, drate, dskip, gain, outw) = outs
    return (
        narrow(block_out).reshape(hidden_in.shape),
        narrow(input_grad).reshape(hidden_in.shape),
        narrow(norm),
        heads, shared.T, step.T, taps, bias, staps, sbias, dsb, drate, dskip, gain, outw.T,
    )


def solution(mesh):
    nd, nc, ntn = (mesh.shape[name] for name in ("dp", "context", "tensor"))

    def body(*args):
        hidden, heads, shared = args[0], args[3], args[4]
        micro, seqs, tokens, width = hidden.shape
        rows = heads.shape[0]
        rp = -(-rows // 16) * 16
        inner = heads.shape[2]
        z = types.SimpleNamespace(
            R=micro * seqs, T=tokens, d_true=width, D=rp * nd * nc, rows=rows, rp=rp, nd=nd, nc=nc, ntn=ntn,
            C=inner, H=args[10].shape[0], S=shared.shape[1], K=args[6].shape[0],
            Q=shared.shape[1] // 2, limit=62 << 20,
        )
        z.WL = max(inner + z.S, z.D, LANES + inner)
        return on_device(z, *args)

    return jax.shard_map(
        body,
        mesh=mesh,
        in_specs=(
            P(None, "dp", "context", None),
            P(None, "dp", None),
            P(),
            P(("dp", "context"), None, "tensor"),
            P(("dp", "context"), None),
            P(("dp", "context"), "tensor"),
            P(None, "tensor"),
            P("tensor"),
            P(),
            P(),
            P("tensor"),
            P("tensor"),
            P("tensor"),
            P("tensor"),
            P("tensor", ("dp", "context")),
            P(None, "dp", "context", None),
        ),
        out_specs=(
            P(None, "dp", "context", None),
            P(None, "dp", "context", None),
            P(),
            P(("dp", "context"), None, "tensor"),
            P(("dp", "context"), "tensor"),
            P(("dp", "context"), "tensor"),
            P(None, "tensor"),
            P("tensor"),
            P(),
            P(),
            P("tensor"),
            P("tensor"),
            P("tensor"),
            P("tensor"),
            P("tensor", ("dp", "context")),
        ),
        check_vma=False,
    )
```

```python
import functools
import types

import jax
import jax.numpy as jnp
from jax import lax
from jax.experimental import pallas as pl
from jax.experimental.pallas import tpu as pltpu
from jax.sharding import PartitionSpec as P

EPS = 1e-05
F32 = jnp.float32
BF16 = jnp.bfloat16
MESH = pl.DeviceIdType.MESH
LANES = 128
HALO = 16
EDGE = 8
PIECES = 4
WIDE = 256
GROUP = 8


def nn(a, b):
    return lax.dot_general(a, b, (((1,), (0,)), ((), ())), preferred_element_type=F32)


def nt(a, b):
    return lax.dot_general(a, b, (((1,), (1,)), ((), ())), preferred_element_type=F32)


def tn(a, b):
    return lax.dot_general(a, b, (((0,), (0,)), ((), ())), preferred_element_type=F32)


def pieces_of(value, count):
    pieces = []
    for _ in range(count):
        piece = value.astype(BF16)
        pieces.append(piece)
        value = value - piece.astype(F32)
    return pieces


def exact_rows(value, ones):
    pieces = [piece.astype(F32) for piece in pieces_of(value, 3)]
    stacked = jnp.concatenate(pieces + [jnp.zeros_like(value)], axis=0).astype(BF16)
    out = nn(stacked, ones)
    return out[0:8] + out[8:16] + out[16:24]


def exact_right(value, ones):
    return sum(nn(piece, ones) for piece in pieces_of(value, 2))


def sigmoid(value):
    return 0.5 * jnp.tanh(0.5 * value) + 0.5


def iota(shape, dim):
    return lax.broadcasted_iota(jnp.int32, shape, dim)


def kernel(z, names, *refs):
    m = types.SimpleNamespace(**dict(zip(names, refs)))
    R, T, D, C, H, S = z.R, z.T, z.D, z.C, z.H, z.S
    rp, nd, nc, ntn = z.rp, z.nd, z.nc, z.ntn
    pairs = H // 2
    head = C // H
    V = C + S
    Z = V + LANES
    Q = z.Q
    BX, CX = slice(0, Q), slice(Q + C, V)
    half = T // 2
    d, c, t = lax.axis_index("dp"), lax.axis_index("context"), lax.axis_index("tensor")
    odd = lax.rem(t, 2)
    across = t + 1 - 2 * odd
    far = lax.rem(t + 2, 4) if ntn == 4 else t

    def at_ctx(k):
        return lax.rem(c + k, nc)

    def at_dp(k):
        return lax.rem(d + k, nd)

    def at_ten(k):
        return lax.rem(t + k, ntn)

    def rows_at(place, size):
        return pl.ds(pl.multiple_of(place * size, 16), size)

    def block(dd, cc):
        return rows_at(dd * nc + cc, rp)

    def row(r):
        return rows_at(r, T)

    def lanes_at(place, size):
        return pl.ds(pl.multiple_of(place, LANES), size)

    def copy(src, dst, send, recv, dev):
        return pltpu.make_async_remote_copy(
            src_ref=src, dst_ref=dst, send_sem=send, recv_sem=recv, device_id=dev, device_id_type=MESH
        )

    def load(which):
        return pltpu.make_async_copy((m.hid, m.cot)[which], (m.hv, m.cv)[which], m.l_in.at[which])

    load(0).start()
    load(1).start()
    barrier = pltpu.get_barrier_semaphore()
    peers = [(d, at_ctx(k), t) for k in range(1, nc)]
    peers += [(at_dp(k), c, t) for k in range(1, nd)]
    peers += [(d, c, at_ten(k)) for k in range(1, ntn)]
    for peer in peers:
        pl.semaphore_signal(barrier, inc=1, device_id=peer, device_id_type=MESH)

    m.wall[block(d, c), Q : Q + C] = m.hp[:, 1, :]
    m.wall[block(d, c), lanes_at(odd * (Q + C), Q)] = jnp.where(odd == 0, m.shp[:, :Q], m.shp[:, Q:])
    m.wt[d * nc + c] = jnp.zeros((GROUP, LANES), F32)
    m.wt[d * nc + c, 0:H, 0:rp] = m.stp[...].astype(F32)
    pl.semaphore_wait(barrier, len(peers))

    def subs(p):
        return z.SUB if p == 0 else 1

    def slot(p, dd, cc, u):
        if p == 1:
            return m.wt.at[dd * nc + cc]
        if p == 3:
            return m.wo.at[block(dd, cc)]
        place, size = ((odd * Q, Q + C), None, (Z, C))[p]
        rows = rp // subs(p)
        return m.wall.at[rows_at((dd * nc + cc) * subs(p) + u, rows), lanes_at(place, size)]

    def w_ctx(p, u, s, right):
        cc, to = (c - s, c + 1) if right else (c + s, c - 1)
        here = slot(p, d, cc, u)
        return copy(here, here, m.wz_send.at[p, int(right), s, u], m.w_recv.at[p, d, cc, u], (d, to, t))

    def w_dp(p, u, cc, k):
        here = slot(p, d, cc, u)
        return copy(here, here, m.wd_send.at[p, cc, k, u], m.w_recv.at[p, d, cc, u], (at_dp(k), c, t))

    def w_arrived(p, u, dd, cc):
        there = slot(p, dd, cc, u)
        copy(there, there, m.wd_send.at[p, cc, 0, u], m.w_recv.at[p, dd, cc, u], (d, c, t)).wait_recv()

    def w_each(p, s, act):
        for u in range(subs(p)):
            if s < nc - 1:
                pl.when((c - s >= 0) & (c < nc - 1))(lambda: act(w_ctx(p, u, s, True)))
                pl.when((c + s < nc) & (c > 0))(lambda: act(w_ctx(p, u, s, False)))
            for k in range(1, nd):
                if s == 0:
                    act(w_dp(p, u, c, k))
                else:
                    pl.when(c - s >= 0)(lambda: act(w_dp(p, u, c - s, k)))
                    pl.when(c + s < nc)(lambda: act(w_dp(p, u, c + s, k)))

    def w_start(p):
        w_each(p, 0, lambda one: one.start())

    def w_step(p, s):
        for u in range(subs(p)):
            for right in (True, False):
                cc = c - s if right else c + s

                @pl.when((cc >= 0) & (cc < nc))
                def _():
                    w_arrived(p, u, d, cc)
                    if s < nc - 1:
                        pl.when(c < nc - 1 if right else c > 0)(lambda: w_ctx(p, u, s, right).start())
                    for k in range(1, nd):
                        w_dp(p, u, cc, k).start()

    def w_rest(p):
        for k in range(1, nd):
            for cc in range(nc):
                for u in range(subs(p)):
                    w_arrived(p, u, at_dp(k), cc)

    def w_sent(p):
        for s in range(nc):
            w_each(p, s, lambda one: one.wait_send())

    def half_rows(dd):
        return rows_at(dd, nc * rp)

    def half_copy(k):
        here = m.wall.at[half_rows(at_dp(k)), lanes_at(odd * (Q + C), Q)]
        return copy(here, here, m.wh_send.at[k], m.wh_recv.at[k], (d, c, across))

    def half_arrived(k):
        there = m.wall.at[half_rows(at_dp(k)), lanes_at((1 - odd) * (Q + C), Q)]
        copy(there, there, m.wh_send.at[k], m.wh_recv.at[k], (d, c, across)).wait_recv()

    def halo_copy(r):
        return copy(
            m.hv.at[pl.ds(pl.multiple_of(r * T + T - HALO, 16), HALO)],
            m.hh.at[rows_at(r, HALO)],
            m.h_send.at[r],
            m.h_recv.at[r],
            (d, c + 1, t),
        )

    w_start(0)
    w_start(1)
    load(0).wait()

    @pl.when(c < nc - 1)
    def _():
        for r in range(R):
            halo_copy(r).start()

    m.wall[block(d, c), Z:] = m.hp[:, 0, :]
    m.wo[block(d, c), :] = m.ow[...]

    m.par[0 : z.K, BX] = m.cs[:, :Q]
    m.par[0 : z.K, Q : Q + C] = m.ch[...]
    m.par[0 : z.K, CX] = m.cs[:, Q:]
    m.par[5:6, :S] = m.bs[...][None]
    m.par[4:5, BX] = m.par[5:6, :Q]
    m.par[4:5, Q : Q + C] = m.bh[...][None]
    m.par[4:5, CX] = m.par[5:6, Q:S]
    m.par[5:6, :C] = m.gg[...][None]
    for h in range(H):
        m.par[6:7, h * head : (h + 1) * head] = jnp.broadcast_to(m.sk[0:1, h : h + 1], (1, head))
    m.gain[0:1, :] = m.ng[...][None]
    m.tile[...] = jnp.zeros_like(m.tile)
    m.tile[0:1, 0:H] = m.sb[...]
    m.tile[1:2, 0:H] = -jnp.exp(m.ld[...])
    turned = jnp.transpose(m.tile[...])
    m.hcol[...] = turned[0:GROUP, :]
    bias_col, rate_col = m.hcol[:, 0:1], m.hcol[:, 1:2]
    gain_in = m.gain[0:1, :]

    def normalize(u):
        u = u.astype(F32)
        mean = jnp.sum(u * u, axis=-1, keepdims=True) * (1.0 / z.d_true)
        return (u * lax.rsqrt(mean + EPS)) * gain_in

    length = m.seg.shape[-1]
    begin = c * T
    seqs = m.seg.shape[1]

    def ids_at(place, size):
        place = pl.multiple_of(place, LANES)
        lines = [m.seg[r // seqs, r % seqs : r % seqs + 1, pl.ds(place, size)] for r in range(R)]
        return jnp.concatenate(lines + [jnp.zeros_like(lines[0])] * (-R % 8), axis=0).astype(F32)

    now = ids_at(begin, T)
    before = jnp.where(c == 0, -1.0, ids_at(jnp.maximum(begin - LANES, 0), LANES))
    behind = jnp.where(c == nc - 1, -2.0, ids_at(jnp.minimum(begin + T, length - LANES), LANES))
    m.segr[...] = now
    m.segb[...] = before
    m.sega[...] = behind
    m.carried[...] = (now == before[:, LANES - 1 : LANES]).astype(F32)
    m.closing[...] = (now == now[:, T - 1 : T]).astype(F32)
    m.tot[...] = jnp.zeros_like(m.tot)
    m.tot[0 : now.shape[0], :] = now
    m.segc[...] = jnp.transpose(m.tot[...])
    away = iota((T, T), 0) - iota((T, T), 1)
    m.lower[...] = (away >= 0).astype(BF16)
    m.upper[...] = (away <= 0).astype(BF16)
    for r in range(R):
        same = m.segc[:, r : r + 1] == m.segr[r : r + 1, :]
        m.past[r] = (same & (away >= 0)).astype(BF16)
        m.next[r] = (same & (away <= 0)).astype(BF16)
        for j in range(1, z.K):
            m.down[r, j - 1] = (same & (away == j)).astype(BF16)
            m.up[r, j - 1] = (same & (away == -j)).astype(BF16)

    @pl.when(c == 0)
    def _():
        m.hh[...] = jnp.zeros_like(m.hh)
        m.sin[...] = jnp.zeros_like(m.sin)

    @pl.when(c == nc - 1)
    def _():
        m.gin[...] = jnp.zeros_like(m.gin)
        m.dce[...] = jnp.zeros_like(m.dce)

    m.sm[t] = jnp.zeros((8, z.WL), F32)
    m.hacc[...] = jnp.zeros_like(m.hacc)
    m.drow[...] = jnp.zeros_like(m.drow)
    m.gstep[...] = jnp.zeros_like(m.gstep)

    @pl.loop(0, R)
    def _(r):
        value = normalize(m.hv[row(r), :]).astype(BF16)
        m.nrm[row(r), :] = value
        m.nrmt[:, row(r)] = jnp.transpose(value)

    load(1).wait()

    @pl.loop(0, R)
    def _(r):
        m.cott[:, row(r)] = jnp.transpose(m.cv[row(r), :])

    reach = iota((HALO, HALO), 1) - HALO - iota((HALO, HALO), 0)
    ahead = iota((HALO, HALO), 1) + HALO - iota((HALO, HALO), 0)
    m.early[...] = jnp.zeros_like(m.early)
    for r in range(R):
        near = m.segc[0:HALO, r : r + 1] == m.segb[r : r + 1, LANES - HALO : LANES]
        late = m.segc[T - HALO : T, r : r + 1] == m.sega[r : r + 1, 0:HALO]
        for j in range(1, z.K):
            first = ((r * (z.K - 1)) + j - 1) * HALO
            m.early[first : first + HALO, r * HALO : (r + 1) * HALO] = (near & (reach == -j)).astype(BF16)
            m.late[r, (j - 1) * HALO : j * HALO, :] = (late & (ahead == j)).astype(BF16)

    w_step(0, 1)
    w_start(2)
    w_step(1, 1)

    @pl.when(c > 0)
    def _():
        for r in range(R):
            halo_copy(r).wait_recv()

    m.nrmh[...] = normalize(m.hh[...]).astype(BF16)
    for s in range(2, nc):
        w_step(0, s)
        w_step(1, s)
    half_copy(0).start()
    w_start(3)
    w_rest(1)

    m.tile[...] = jnp.zeros_like(m.tile)
    for b in range(nd * nc):
        m.tile[0:GROUP, :] = m.wt[b]
        m.wall[b * rp : (b + 1) * rp, V:Z] = jnp.transpose(m.tile[...])[0:rp, :].astype(BF16)
    w_rest(0)
    for k in range(1, nd):
        half_copy(k).start()

    low_lanes = iota((T, LANES), 1) < head
    lane = iota((T, LANES), 1)
    fold = (iota((C, LANES), 0) // head == iota((C, LANES), 1)).astype(F32)
    fold_run = fold.astype(BF16)
    fold_through = (
        (iota((C, LANES), 0) // head == iota((C, LANES), 1) - GROUP).astype(F32) - fold
    ).astype(BF16)
    fold_step = (iota((C, LANES), 0) // head == iota((C, LANES), 1) - 2 * GROUP).astype(BF16)
    RUN, STEP, LEAD, TRAIL = 0, GROUP, 2 * GROUP, 3 * GROUP

    def widened(values, base, p):
        a = base + 2 * p
        return jnp.where(low_lanes[: values.shape[0]], values[:, a : a + 1], values[:, a + 1 : a + 2])

    def spread(values, base):
        return jnp.concatenate([widened(values, base, p) for p in range(pairs)], axis=1)

    def state_copy(r):
        return copy(m.ssend.at[r], m.sin.at[r], m.s_send.at[r], m.s_recv.at[r], (d, c + 1, t))

    def grad_copy(r):
        return copy(m.gsend.at[r], m.gin.at[r], m.g_send.at[r], m.g_recv.at[r], (d, c - 1, t))

    def edge_copy(r):
        return copy(m.edge.at[r], m.dce.at[r], m.e_send.at[r], m.e_recv.at[r], (d, c - 1, t))

    def kept(r):
        return spread(m.cols[pl.ds(r * T + T - 1, 1), :], LEAD)

    def pair(p):
        return slice(p * LANES, (p + 1) * LANES)

    def lanes_of(p):
        return slice(Q + p * LANES, Q + (p + 1) * LANES)

    def serve_state(r):
        state_copy(r).wait_recv()

        @pl.when(c < nc - 1)
        def _():
            m.ssend[r] = (m.fresh[r] + kept(r) * m.sin[r].astype(F32)).astype(BF16)
            state_copy(r).start()

    def serve_grad(r):
        grad_copy(r).wait_recv()

        @pl.when(c > 0)
        def _():
            m.gsend[r] = (m.local[r] + kept(r) * m.gin[r].astype(F32)).astype(BF16)
            grad_copy(r).start()

    hops = nc - 1 - c
    soon = R == 4 and nc > 2
    if soon:
        state_late = (c > 2) | ((c == 2) & (nc > 3))
        grad_late = hops > 2
    else:
        state_late, grad_late = c > 0, hops > 0

    def state_point(place, r):
        if soon:
            for who, item in place:
                @pl.when((c == who) & r)
                def _():
                    serve_state(item)

    def grad_point(place, r):
        if soon:
            for who, item in place:
                @pl.when((hops == who) & r)
                def _():
                    serve_grad(item)

    for k in range(nd):
        half_arrived(k)
    halo_v = nn(m.nrmh[...], m.wall[:, :V]).astype(BF16)
    m.hfix[...] = nn(m.early[...], halo_v)

    @pl.loop(0, R)
    def _(r):
        acc = nn(m.nrm[row(r), :], m.wall[:, :Z])
        m.v[row(r), :] = acc[:, :V].astype(BF16)
        raw = jnp.transpose(acc[:, V:].astype(BF16).astype(F32))[0:GROUP]
        pre = raw + bias_col
        step = jnp.maximum(pre, 0.0) + jnp.log1p(jnp.exp(-jnp.abs(pre)))
        m.pre[:, row(r)] = pre
        m.step[:, row(r)] = step
        run = exact_rows(step * rate_col, m.upper[...])
        m.runr[r] = run
        m.tot[0:GROUP, :] = run
        m.tot[GROUP : 2 * GROUP, :] = step
        m.tot[2 * GROUP : 3 * GROUP, :] = jnp.exp(run) * m.carried[pl.ds(r, 1), :]
        m.tot[3 * GROUP : 4 * GROUP, :] = jnp.exp(run[:, T - 1 : T] - run) * m.closing[pl.ds(r, 1), :]
        m.cols[row(r), :] = jnp.transpose(m.tot[...])
        for a in range(0, V, WIDE):
            part = slice(a, min(a + WIDE, V))
            value = m.v[row(r), part]
            conv = value.astype(F32) * m.par[0:1, part] + m.par[4:5, part]
            first = jnp.zeros((EDGE, conv.shape[1]), F32)
            for j in range(1, z.K):
                tap = m.par[j : j + 1, part]
                conv = conv + nn(m.down[r, j - 1], value) * tap
                first = first + m.hfix[pl.ds((r * (z.K - 1) + j - 1) * HALO, EDGE), part] * tap
            conv = jnp.concatenate([conv[0:EDGE] + first, conv[EDGE:]], axis=0)
            logistic = sigmoid(conv)
            m.mix[row(r), part] = (conv * logistic).astype(BF16)
            m.slope[row(r), part] = logistic * (1.0 + conv * (1.0 - logistic))
        state_point([(1, 0)], r == 2)
        state_point([(1, 1)], r == 3)
        for p in range(pairs):
            scaled = m.mix[row(r), lanes_of(p)].astype(F32) * widened(m.cols[row(r), :], STEP, p)
            m.xs[row(r), pair(p)] = scaled.astype(BF16)
            m.xt[row(r), pair(p)] = (scaled * widened(m.cols[row(r), :], TRAIL, p)).astype(BF16)
        m.fresh[r] = tn(m.mix[row(r), BX], m.xt[row(r), :])

        @pl.when(c == 0)
        def _():
            m.ssend[r] = m.fresh[r].astype(BF16)
            state_copy(r).start()

        for s in range(1, min(nc, R + 1)):
            pl.when(r == s - 1)(lambda: w_step(2, s))

    for s in range(R + 1, nc):
        w_step(2, s)
    state_point([(2, 0)], True)

    @pl.loop(0, R)
    def _(r):
        b, cm = m.mix[row(r), BX], m.mix[row(r), CX]
        m.scores[...] = nt(cm, b) * m.past[r].astype(F32)
        for p in range(pairs):
            for a in range(0, T, LANES):
                rows, seen = slice(a, a + LANES), a + LANES
                here = pl.ds(pl.multiple_of(r * T, 16) + a, LANES)
                both = []
                for h in (2 * p, 2 * p + 1):
                    decay = jnp.exp(jnp.minimum(m.cols[here, h : h + 1] - m.runr[r, h : h + 1, :seen], 0.0))
                    weight = (decay * m.scores[rows, :seen]).astype(BF16)
                    both.append(nn(weight, m.xs[pl.ds(pl.multiple_of(r * T, 16), seen), pair(p)]))
                m.ins[here, pair(p)] = jnp.where(low_lanes[:LANES], both[0], both[1])
        for s in range(1, min(nc, R + 1)):
            pl.when(r == s - 1)(lambda: w_step(3, s))
        state_point([(1, 2)], r == 0)
        state_point([(2, 1)], r == 2)

    for s in range(R + 1, nc):
        w_step(3, s)
    state_point([(1, 3)], True)
    w_rest(2)
    w_rest(3)

    def sums_copy(r, k):
        return copy(
            m.sums.at[t, r], m.sums.at[t, r], m.x_send.at[r, k], m.x_recv.at[r, t], (d, c, at_ten(k))
        )

    def sums_arrived(r, who):
        copy(
            m.sums.at[who, r], m.sums.at[who, r], m.x_send.at[r, 0], m.x_recv.at[r, who], (d, c, t)
        ).wait_recv()

    def mine(r):
        return pl.ds(pl.multiple_of(r * T + odd * half, 16), half)

    def theirs(r):
        return pl.ds(pl.multiple_of(r * T + (1 - odd) * half, 16), half)

    def near_copy(a, r):
        return copy(m.as_.at[a, r], m.ar_.at[a, r], m.a_send.at[a, r], m.a_recv.at[a, r], (d, c, across))

    def far_copy(a, r):
        return copy(m.bs_.at[a, r], m.br_.at[a, r], m.b_send.at[a, r], m.b_recv.at[a, r], (d, c, far))

    def back_copy(a, r):
        out = (m.ov, m.iv)[a].at[mine(r)]
        return copy(out, out, m.c_send.at[a, r], m.c_recv.at[a, r], (d, c, across))

    def back_arrived(a, r):
        out = (m.ov, m.iv)[a].at[theirs(r)]
        copy(out, out, m.c_send.at[a, r], m.c_recv.at[a, r], (d, c, across)).wait_recv()

    def give(a, r, value):
        first, second = value[:half], value[half:]
        m.as_[a, r] = jnp.where(odd == 0, second, first).astype(BF16)
        near_copy(a, r).start()
        m.keep[r] = jnp.where(odd == 0, first, second)

    def chip_sum(a, r):
        near_copy(a, r).wait_recv()
        m.bs_[a, r] = (m.keep[r] + m.ar_[a, r].astype(F32)).astype(BF16)
        if ntn == 4:
            far_copy(a, r).start()

    def full_sum(a, r):
        total = m.bs_[a, r].astype(F32)
        if ntn == 4:
            far_copy(a, r).wait_recv()
            total = total + m.br_[a, r].astype(F32)
        return total

    def serve_late(r):
        if soon and nc > 3:
            pl.when((c > 2) | (r >= 2))(lambda: serve_state(r))
        else:
            serve_state(r)

    def gating(r):
        pl.when(state_late)(lambda: serve_late(r))
        cm = m.mix[row(r), CX]
        gate = nn(m.nrm[row(r), :], m.wall[:, Z:])
        m.zv[row(r), :] = gate.astype(BF16)
        m.dy[row(r), :] = nn(m.cv[row(r), :], m.wo[...])
        m.ys[row(r), :] = nn(cm, m.sin[r])
        squares = jnp.zeros((T, LANES), F32)
        inner = jnp.zeros((T, LANES), F32)
        for p in range(pairs):
            carried = m.ys[row(r), pair(p)] * widened(m.cols[row(r), :], LEAD, p)
            m.ys[row(r), pair(p)] = carried
            ssd = m.ins[row(r), pair(p)] + carried + m.par[6:7, pair(p)] * m.mix[row(r), lanes_of(p)].astype(F32)
            m.ssd[row(r), pair(p)] = ssd
            gate = m.zv[row(r), pair(p)].astype(F32)
            gated = ssd * (gate * sigmoid(gate))
            m.gated[row(r), pair(p)] = gated
            scaled = gated * m.par[5:6, pair(p)]
            m.yg[row(r), pair(p)] = scaled.astype(BF16)
            squares = squares + gated * gated
            inner = inner + scaled * m.dy[row(r), pair(p)]
        squares = jnp.sum(squares, axis=-1, keepdims=True)
        inner = jnp.sum(inner, axis=-1, keepdims=True)
        both = jnp.where(lane == 0, squares, jnp.where(lane == 1, inner, 0.0))
        m.sums[t, r] = jnp.transpose(both)[0:8, :]
        for k in range(1, ntn):
            sums_copy(r, k).start()
        give(0, r, nt(m.yg[row(r), :], m.wo[...]))

    def ungating(r):
        for k in range(1, ntn):
            sums_arrived(r, at_ten(k))
        total = m.sums[0, r]
        for who in range(1, ntn):
            total = total + m.sums[who, r]
        scale = lax.rsqrt(total[0:1] * (1.0 / (C * ntn)) + EPS)
        inner = total[1:2] * (1.0 / (C * ntn)) * scale * scale * scale
        m.tot[0:1, :] = scale
        m.tot[1:2, :] = inner
        columns = jnp.transpose(m.tot[...])
        m.rms[row(r), :] = columns
        scale = jnp.broadcast_to(columns[:, 0:1], (T, LANES))
        inner = jnp.broadcast_to(columns[:, 1:2], (T, LANES))
        for p in range(pairs):
            gated, dy, ssd = m.gated[row(r), pair(p)], m.dy[row(r), pair(p)], m.ssd[row(r), pair(p)]
            gate = m.zv[row(r), pair(p)].astype(F32)
            gain = m.par[5:6, pair(p)]
            normal = gated * scale
            m.sm[t, 5:6, pair(p)] += jnp.sum(dy * normal, axis=0, keepdims=True)
            m.yg[row(r), pair(p)] = (normal * gain).astype(BF16)
            d_gated = scale * dy * gain - gated * inner
            logistic = sigmoid(gate)
            m.dcat[row(r), Z + p * LANES : Z + (p + 1) * LANES] = (
                d_gated * ssd * (logistic * (1.0 + gate * (1.0 - logistic)))
            ).astype(BF16)
            d_ssd = d_gated * (gate * logistic)
            m.ssd[row(r), pair(p)] = d_ssd
            m.wds[row(r), pair(p)] = (d_ssd * widened(m.cols[row(r), :], LEAD, p)).astype(BF16)
        m.local[r] = tn(m.mix[row(r), CX], m.wds[row(r), :])

        @pl.when(c == nc - 1)
        def _():
            m.gsend[r] = m.local[r].astype(BF16)
            if nc > 1:
                grad_copy(r).start()

    @pl.loop(0, R + 1)
    def _(i):
        pl.when(i < R)(lambda: gating(i))

        @pl.when(i >= 1)
        def _():
            ungating(i - 1)

        grad_point([(1, 0)], i == 3)
        grad_point([(1, 1)], i == 4)
        pl.when(i >= 1)(lambda: chip_sum(0, i - 1))

    gall, gyr, gzs, gzr = (m.ga0, m.ga1, m.ga2), (m.gy0, m.gy1, m.gy2), (m.gz0, m.gz1, m.gz2), (m.gr0, m.gr1, m.gr2)
    tall = (rp, rp, rp + HALO)

    def rs_dp(part, j, k):
        cc = at_ctx(j)
        return copy(
            gall[part].at[rows_at(at_dp(k) * nc + cc, tall[part])],
            gyr[part].at[k - 1, rows_at(cc, tall[part])],
            m.ry_send.at[part, j, k - 1],
            m.ry_recv.at[part, j, k - 1],
            (at_dp(k), c, t),
        )

    def rs_ctx(part, j):
        cc = at_ctx(j)
        return copy(
            gzs[part].at[rows_at(cc, tall[part])],
            gzr[part].at[c],
            m.rz_send.at[part, j],
            m.rz_recv.at[part, c],
            (d, cc, t),
        )

    def rs_arrived(part, cc):
        copy(gzr[part].at[cc], gzr[part].at[cc], m.rz_send.at[part, 0], m.rz_recv.at[part, cc], (d, c, t)).wait_recv()

    def rs_start(part):
        for j in list(range(1, nc)) + [0]:
            for k in range(1, nd):
                rs_dp(part, j, k).start()

    def rs_middle(part, j):
        cc = at_ctx(j)
        total = gall[part][rows_at(d * nc + cc, tall[part]), :].astype(F32)
        for k in range(1, nd):
            rs_dp(part, j, k).wait_recv()
            total = total + gyr[part][k - 1, rows_at(cc, tall[part]), :].astype(F32)
        own = j == 0

        def keep():
            gzr[part][c] = total.astype(BF16)

        def send():
            gzs[part][rows_at(cc, tall[part]), :] = total.astype(BF16)
            rs_ctx(part, j).start()

        if isinstance(j, int):
            keep() if own else send()
        else:
            pl.when(own)(keep)
            pl.when(jnp.logical_not(own))(send)

    def rs_end(part):
        for k in range(1, nc):
            rs_arrived(part, at_ctx(k))
        total = gzr[part][0].astype(F32)
        for cc in range(1, nc):
            total = total + gzr[part][cc].astype(F32)
        return total

    def rs_sent(part):
        for j in range(nc):
            for k in range(1, nd):
                rs_dp(part, j, k).wait_send()
            if j:
                rs_ctx(part, j).wait_send()

    m.ga1[:, C:] = nn(m.cott[...], m.yg[...]).astype(BF16)
    m.ga1[:, :C] = nn(m.nrmt[...], m.dcat[:, Z:]).astype(BF16)
    rs_start(1)
    grad_point([(1, 2), (2, 0)], True)

    @pl.loop(0, R)
    def _(r):
        b, cm = m.mix[row(r), BX], m.mix[row(r), CX]
        m.scores[...] = nt(b, cm) * m.next[r].astype(F32)
        start = pl.multiple_of(r * T, 16)
        for a in range(0, T, LANES):
            rows, here, after = slice(a, a + LANES), pl.ds(start + a, LANES), pl.ds(start + a, T - a)
            losses = jnp.zeros((LANES, LANES), F32)
            for p in range(pairs):
                ds_pair = m.ssd[after, pair(p)].astype(BF16)
                xs_pair = m.xs[here, pair(p)]
                both = []
                for h in (2 * p, 2 * p + 1):
                    pick = low_lanes[:LANES] if h % 2 == 0 else ~low_lanes[:LANES]
                    decay = jnp.exp(jnp.minimum(m.runr[r, h : h + 1, a:] - m.cols[here, h : h + 1], 0.0))
                    weight = decay * m.scores[rows, a:]
                    both.append(nn(weight.astype(BF16), ds_pair))
                    d_weight = nt(jnp.where(pick, xs_pair, jnp.zeros_like(xs_pair)), ds_pair)
                    flow = d_weight * weight
                    if h == 0:
                        m.dsc[rows, a:] = d_weight * decay
                    else:
                        m.dsc[rows, a:] += d_weight * decay
                    losses = jnp.where(lane[:LANES] == h, jnp.sum(flow, axis=1, keepdims=True), losses)
                    down = jnp.sum(flow, axis=0, keepdims=True)
                    if a == 0:
                        m.drow[r, h : h + 1, :] = down
                    else:
                        m.drow[r, h : h + 1, a:] += down
                m.ins[here, pair(p)] = jnp.where(low_lanes[:LANES], both[0], both[1])
            m.drun[here, :] = exact_right(m.ssd[here, :] * m.ys[here, :], fold_run) - losses
            d_scores = (m.dsc[rows, a:] * m.next[r, rows, a:].astype(F32)).astype(BF16)
            m.gated[here, :LANES] = nn(d_scores, m.mix[after, CX])
            d_after = tn(d_scores, m.mix[here, BX])
            if a == 0:
                m.gated[after, LANES:S] = d_after
            else:
                m.gated[after, LANES:S] += d_after

        grad_point([(1, 3), (2, 1)], r == 0)
        grad_point([(2, 2)], r == 1)
        grad_point([(2, 3)], r == 2)

    def final_out(r):
        value = m.hv[mine(r), :].astype(F32) + m.rms[mine(r), 0:1] * full_sum(0, r)
        m.ov[mine(r), :] = value.astype(BF16)
        back_copy(0, r).start()

    def adjoint(r):
        pl.when(grad_late)(lambda: serve_grad(r))
        b = m.mix[row(r), BX]
        grad = m.gin[r]
        ring = lax.rem(r, 2)
        for p in range(pairs):
            trailing = widened(m.cols[row(r), :], TRAIL, p)
            reach = nn(b, m.gin[r, :, pair(p)]) * trailing
            x = m.mix[row(r), lanes_of(p)].astype(F32)
            d_xs = m.ins[row(r), pair(p)] + reach
            d_ssd = m.ssd[row(r), pair(p)]
            m.prod[:, pair(p)] = m.xs[row(r), pair(p)].astype(F32) * reach
            m.prod[:, C + p * LANES : C + (p + 1) * LANES] = d_xs * x
            m.sm[t, 7:8, LANES + p * LANES : 2 * LANES + p * LANES] += jnp.sum(d_ssd * x, axis=0, keepdims=True)
            m.dcf[ring, :, lanes_of(p)] = (
                d_xs * widened(m.cols[row(r), :], STEP, p) + m.par[6:7, pair(p)] * d_ssd
            ) * m.slope[row(r), lanes_of(p)]
        m.dcf[ring, :, BX] = (
            m.gated[row(r), :LANES] + nt(m.xt[row(r), :], grad)
        ) * m.slope[row(r), BX]
        m.dcf[ring, :, CX] = (
            m.gated[row(r), LANES:S] + nt(m.wds[row(r), :], m.sin[r])
        ) * m.slope[row(r), CX]

        @pl.when(c > 0)
        def _():
            m.edge[r] = m.dcf[ring, 0:EDGE, :]
            edge_copy(r).start()

        m.drun[row(r), :] += exact_right(m.prod[:, :C], fold_through) + exact_right(m.prod[:, C:], fold_step)
        joint = jnp.sum(grad.astype(F32) * m.sin[r].astype(F32), axis=0, keepdims=True)
        joint = exact_right(jnp.broadcast_to(joint, (8, C)), fold_run)[0:1]
        last = m.cols[pl.ds(r * T + T - 1, 1), :]
        kept_lanes = jnp.concatenate([last[:, LEAD : LEAD + H], jnp.zeros((1, LANES - H), F32)], axis=1)
        m.drun[pl.ds(r * T + T - 1, 1), :] += joint * kept_lanes
        turned = jnp.transpose(m.drun[row(r), :])
        through = jnp.sum(turned[GROUP : 2 * GROUP], axis=1, keepdims=True)
        d_run = turned[0:GROUP] + m.drow[r]
        d_run = d_run + jnp.where(iota((GROUP, T), 1) == T - 1, through, 0.0)
        d_growth = exact_rows(d_run, m.lower[...])
        d_step = turned[2 * GROUP : 3 * GROUP] + rate_col * d_growth
        d_pre = d_step * sigmoid(m.pre[:, row(r)])
        m.hacc[0:GROUP, :] += d_pre
        m.hacc[GROUP : 2 * GROUP, :] += m.step[:, row(r)] * d_growth * rate_col
        d_pre = jnp.where(iota((GROUP, T), 0) < H, d_pre, 0.0)
        m.gstep[...] += nn(jnp.concatenate([d_pre, jnp.zeros_like(d_pre)], axis=0).astype(BF16), m.nrm[row(r), :])
        m.tot[0:GROUP, :] = d_pre
        m.dcat[row(r), V:Z] = jnp.transpose(m.tot[...]).astype(BF16)

    def finish(r):
        @pl.when(c < nc - 1)
        def _():
            edge_copy(r).wait_recv()

        ring = lax.rem(r, 2)
        edge = m.dce[r]
        edge = jnp.concatenate([edge, jnp.zeros_like(edge)], axis=0).astype(BF16)
        m.lfix[...] = nn(m.late[r], edge)
        for a in range(0, V, WIDE):
            part = slice(a, min(a + WIDE, V))
            d_conv = m.dcf[ring, :, part]
            low = d_conv.astype(BF16)
            value = m.v[row(r), part].astype(F32)
            m.sm[t, 4:5, part] += jnp.sum(d_conv, axis=0, keepdims=True)
            m.sm[t, 0:1, part] += jnp.sum(d_conv * value, axis=0, keepdims=True)
            d_v = d_conv * m.par[0:1, part]
            for j in range(1, z.K):
                moved = nn(m.up[r, j - 1], low)
                moved = jnp.concatenate(
                    [moved[: T - HALO], moved[T - HALO :] + m.lfix[(j - 1) * HALO : j * HALO, part]], axis=0
                )
                d_v = d_v + moved * m.par[j : j + 1, part]
                m.sm[t, j : j + 1, part] += jnp.sum(moved * value, axis=0, keepdims=True)
            m.dcat[row(r), part] = d_v.astype(BF16)

    def finish_norm(r):
        value = nt(m.dcat[row(r), :], m.wall[...])
        give(1, r, value)
        u = m.hv[row(r), :].astype(F32)
        mean = jnp.sum(u * u, axis=-1, keepdims=True) * (1.0 / z.d_true)
        m.sm[t, 6:7, :D] += jnp.sum(value * (u * lax.rsqrt(mean + EPS)), axis=0, keepdims=True)

    m.tot[...] = jnp.zeros_like(m.tot)

    @pl.loop(0, max(R + 1, nc))
    def _(i):
        @pl.when(i < R)
        def _():
            final_out(i)
            adjoint(i)

        @pl.when(i < nc)
        def _():
            rs_middle(1, lax.rem(i + 1, nc))

        @pl.when((i >= 1) & (i < R + 1))
        def _():
            finish(i - 1)

        @pl.when((i >= 1) & (i < R))
        def _():
            finish_norm(i - 1)

        @pl.when((i >= 2) & (i < R + 1))
        def _():
            chip_sum(1, i - 2)

    width = S // ntn
    starts = [k * width + (C if k * width >= Q else 0) for k in range(ntn)]
    quarters = [m.dcat[:, first : first + width] for first in starts]
    value = nn(m.nrmt[...], jnp.concatenate(quarters[0::2] + quarters[1::2], axis=1))

    def share_copy():
        return copy(m.shs, m.shr, m.sh_send.at[0], m.sh_recv.at[0], (d, c, across))

    m.shk[...] = jnp.where(odd == 0, value[:, : z.Q], value[:, z.Q :])
    m.shs[...] = jnp.where(odd == 0, value[:, z.Q :], value[:, : z.Q]).astype(BF16)
    share_copy().start()

    def small_ten(k):
        return copy(m.sm.at[t], m.sm.at[t], m.st_send.at[k], m.st_recv.at[t], (d, c, at_ten(k)))

    def small_dp(k):
        return copy(m.sd.at[d], m.sd.at[d], m.sd_send.at[k], m.sd_recv.at[d], (at_dp(k), c, t))

    def small_ctx(k):
        return copy(m.sc.at[c], m.sc.at[c], m.sc_send.at[k], m.sc_recv.at[c], (d, at_ctx(k), t))

    def arrived(buf, sems, who):
        copy(buf.at[who], buf.at[who], sems.at[who], sems.at[who], (d, c, t)).wait_recv()

    m.ga0[...] = nn(m.nrmt[...], m.dcat[:, Q : Q + C]).astype(BF16)
    share_copy().wait_recv()
    for b in range(nd * nc):
        here = slice(b * rp, (b + 1) * rp)
        there = b * (rp + HALO)
        m.ga2[there : there + rp, :] = (m.shk[here, :] + m.shr[here, :].astype(F32)).astype(BF16)
        steps = m.gstep[:, here]
        m.ga2[there + rp : there + rp + HALO, :] = jnp.concatenate(
            [steps, jnp.zeros((HALO, LANES - rp), F32)], axis=1
        ).astype(BF16)
    rs_start(2)
    rs_start(0)
    finish_norm(R - 1)
    m.tile[...] = jnp.zeros_like(m.tile)
    m.tile[0 : 2 * GROUP, :] = jnp.broadcast_to(
        jnp.sum(m.hacc[...], axis=1, keepdims=True), (2 * GROUP, LANES)
    )
    m.sm[t, 7:8, 0:LANES] = jnp.transpose(m.tile[...])[0:1, :]
    for k in range(1, ntn):
        small_ten(k).start()

    chip_sum(1, R - 1)

    for k in range(1, ntn):
        arrived(m.sm, m.st_recv, at_ten(k))
    common = m.sm[0]
    for who in range(1, ntn):
        common = common + m.sm[who]
    rows8, lanes8 = iota((8, z.WL), 0), iota((8, z.WL), 1)
    shared_here = (rows8 == 6) | ((rows8 < 5) & ((lanes8 < Q) | (lanes8 >= Q + C)))
    m.sd[d] = jnp.where(shared_here, common, m.sm[t])
    for k in range(1, nd):
        small_dp(k).start()

    def store(a, r):
        return pltpu.make_async_copy((m.ov, m.iv)[a].at[row(r)], (m.out, m.ing)[a].at[row(r)], m.l_out.at[a, r])

    for r in range(R):
        back_arrived(0, r)
        store(0, r).start()
    for j in list(range(1, nc)) + [0]:
        rs_middle(2, j)

    @pl.loop(0, R)
    def _(r):
        u = m.hv[mine(r), :].astype(F32)
        mean = jnp.sum(u * u, axis=-1, keepdims=True) * (1.0 / z.d_true)
        scale = lax.rsqrt(mean + EPS)
        unit = u * scale
        d_unit = full_sum(1, r) * gain_in
        inner = jnp.sum(d_unit * unit, axis=-1, keepdims=True) * (1.0 / z.d_true)
        value = m.cv[mine(r), :].astype(F32) + scale * (d_unit - unit * inner)
        m.iv[mine(r), :] = value.astype(BF16)
        back_copy(1, r).start()

        @pl.when(r < nc)
        def _():
            rs_middle(0, lax.rem(r + 1, nc))

    for j in range(R + 1, nc + 1):
        rs_middle(0, j % nc)

    for k in range(1, nd):
        arrived(m.sd, m.sd_recv, at_dp(k))
    total = m.sd[0]
    for who in range(1, nd):
        total = total + m.sd[who]
    m.sc[c] = total
    for k in range(1, nc):
        small_ctx(k).start()

    def last_copy():
        return copy(m.ls, m.lr, m.sh_send.at[1], m.sh_recv.at[1], (d, c, far))

    value = rs_end(2)
    if ntn == 4:
        m.ls[...] = value
        last_copy().start()
    else:
        m.gw2[...] = value
    m.gw1[...] = rs_end(1)

    for r in range(R):
        back_arrived(1, r)
        store(1, r).start()

    for k in range(1, nc):
        arrived(m.sc, m.sc_recv, at_ctx(k))
    total = m.sc[0]
    for who in range(1, nc):
        total = total + m.sc[who]
    m.small[...] = total

    if ntn == 4:
        last_copy().wait_recv()
        m.gw2[0:rp, :] = m.ls[0:rp, :] + m.lr[0:rp, :]
        m.gw2[rp:, :] = m.ls[rp:, :]
        last_copy().wait_send()

    m.gw0[...] = rs_end(0)

    for a in range(2):
        for r in range(R):
            store(a, r).wait()
            back_copy(a, r).wait_send()
            near_copy(a, r).wait_send()
            if ntn == 4:
                far_copy(a, r).wait_send()
    for p in range(PIECES):
        w_sent(p)
    for k in range(nd):
        half_copy(k).wait_send()
    for part in range(3):
        rs_sent(part)
    for r in range(R):
        for k in range(1, ntn):
            sums_copy(r, k).wait_send()

        @pl.when(c < nc - 1)
        def _():
            halo_copy(r).wait_send()
            state_copy(r).wait_send()

        @pl.when(c > 0)
        def _():
            grad_copy(r).wait_send()
            edge_copy(r).wait_send()

    share_copy().wait_send()
    for k in range(1, ntn):
        small_ten(k).wait_send()
    for k in range(1, nd):
        small_dp(k).wait_send()
    for k in range(1, nc):
        small_ctx(k).wait_send()


def finishing(z, out, ing, gw0, gw1, gw2, small, *outs):
    (o_out, o_ing, norm, heads, shared, step, taps, bias, staps, sbias, dsb, drate, dskip, gain, outw, tile, sems) = outs
    C, S, D, H, rp, rows = z.C, z.S, z.D, z.H, z.rp, z.rows
    V = C + S
    head = C // H
    moves = [pltpu.make_async_copy(out, o_out, sems.at[0]), pltpu.make_async_copy(ing, o_ing, sems.at[1])]
    for move in moves:
        move.start()
    norm[...] = small[6, :D]
    heads[:, 0, :] = gw1[0:rows, :C]
    heads[:, 1, :] = gw0[0:rows, :]
    width = S // z.ntn
    tile[...] = jnp.zeros_like(tile)
    tile[0:rp, :] = gw2[0:rp, :]
    pair = jnp.transpose(tile[...])
    if z.ntn == 4:
        upper = lax.axis_index("tensor") >= 2
        pair = jnp.where(upper, pair[width:], pair[:width])
    shared[...] = pair[:, 0:rows]
    step[...] = gw2[rp : rp + H, 0:rows]
    Q = z.Q
    taps[...] = small[0 : z.K, Q : Q + C]
    bias[...] = small[4, Q : Q + C]
    staps[:, :Q] = small[0 : z.K, :Q]
    staps[:, Q:] = small[0 : z.K, Q + C : V]
    sbias[...] = jnp.concatenate([small[4:5, :Q], small[4:5, Q + C : V]], axis=1)[0]
    dsb[...] = small[7, :H]
    drate[...] = small[7, GROUP : GROUP + H]
    lanes = iota((1, H), 1)
    skip = jnp.zeros((1, H), F32)
    for h in range(H):
        begin = LANES + h * head
        skip = jnp.where(lanes == h, jnp.sum(small[7:8, begin : begin + head], axis=1, keepdims=True), skip)
    tile[0:1, 0:H] = skip
    dskip[...] = tile[0, 0:H]
    gain[...] = small[5, :C]
    outw[...] = gw1[0:rows, C:]
    for move in moves:
        move.wait()


def on_device(z, hidden_in, segment_ids, norm_gain, head_projection, shared_projection, step_projection,
              conv_heads, bias_heads, conv_shared, bias_shared, step_bias, log_decay, skip_gain, gate_gain,
              output_weight, out_cotangent):
    R, T, D, C, H, S = z.R, z.T, z.D, z.C, z.H, z.S
    rp, nd, nc, ntn, rows = z.rp, z.nd, z.nc, z.ntn, z.rows
    V = C + S
    blocks = nd * nc
    R8 = 8 * -(-R // 8)

    def widen(value):
        if rp == rows:
            return value
        value = value.reshape(value.shape[:-1] + (blocks, rows))
        value = jnp.pad(value, [(0, 0)] * (value.ndim - 1) + [(0, rp - rows)])
        return value.reshape(value.shape[:-2] + (D,))

    def narrow(value):
        if rp == rows:
            return value
        return value.reshape(value.shape[:-1] + (blocks, rp))[..., :rows].reshape(value.shape[:-1] + (z.d_true,))

    def taller(value, dim):
        if rp == rows:
            return value
        return jnp.pad(value, [(0, rp - rows if k == dim else 0) for k in range(value.ndim)])

    dma, vmem = pltpu.SemaphoreType.DMA, pltpu.VMEM
    N = R * T
    half = T // 2
    k0 = max(nd - 1, 1)
    ins = dict(
        hid=widen(hidden_in.reshape(N, z.d_true)), cot=widen(out_cotangent.reshape(N, z.d_true)),
        seg=segment_ids, ng=widen(norm_gain), hp=taller(head_projection, 0),
        shp=taller(shared_projection, 0), stp=taller(step_projection.T, 1), ow=taller(output_weight.T, 0),
        ch=conv_heads, bh=bias_heads, cs=conv_shared, bs=bias_shared, sb=step_bias[None],
        ld=log_decay[None], sk=skip_gain[None], gg=gate_gain,
    )
    outs = dict(
        out=jax.ShapeDtypeStruct((N, D), BF16),
        ing=jax.ShapeDtypeStruct((N, D), BF16),
        gw0=jax.ShapeDtypeStruct((rp, C), F32),
        gw1=jax.ShapeDtypeStruct((rp, 2 * C), F32),
        gw2=jax.ShapeDtypeStruct((rp + HALO, z.Q), F32),
        small=jax.ShapeDtypeStruct((8, z.WL), F32),
    )
    scratch = dict(
        hv=vmem((N, D), BF16), cv=vmem((N, D), BF16), ov=vmem((N, D), BF16), iv=vmem((N, D), BF16),
        wall=vmem((D, V + LANES + C), BF16), wo=vmem((D, C), BF16), wt=vmem((blocks, GROUP, LANES), F32),
        hcol=vmem((GROUP, LANES), F32), tile=vmem((LANES, LANES), F32), gain=vmem((8, D), F32), par=vmem((16, V), F32),
        segc=vmem((T, LANES), F32), segr=vmem((R8, T), F32), carried=vmem((R8, T), F32), closing=vmem((R8, T), F32),
        segb=vmem((R8, LANES), F32), sega=vmem((R8, LANES), F32),
        early=vmem((R * (z.K - 1) * HALO, R * HALO), BF16), late=vmem((R, (z.K - 1) * HALO, HALO), BF16),
        hfix=vmem((R * (z.K - 1) * HALO, V), F32), lfix=vmem(((z.K - 1) * HALO, V), F32),
        down=vmem((R, z.K - 1, T, T), BF16), up=vmem((R, z.K - 1, T, T), BF16), lower=vmem((T, T), BF16), upper=vmem((T, T), BF16),
        past=vmem((R, T, T), BF16), next=vmem((R, T, T), BF16),
        hh=vmem((R * HALO, D), BF16), nrmh=vmem((R * HALO, D), BF16),
        nrm=vmem((N, D), BF16), nrmt=vmem((D, N), BF16), cott=vmem((D, N), BF16),
        v=vmem((N, V), BF16), mix=vmem((N, V), BF16), slope=vmem((N, V), F32),
        pre=vmem((GROUP, N), F32), step=vmem((GROUP, N), F32), cols=vmem((N, LANES), F32), xt=vmem((N, C), BF16),
        runr=vmem((R, 8, T), F32), xs=vmem((N, C), BF16),
        fresh=vmem((R, LANES, C), F32), local=vmem((R, LANES, C), F32),
        ssend=vmem((R, LANES, C), BF16), sin=vmem((R, LANES, C), BF16),
        gsend=vmem((R, LANES, C), BF16), gin=vmem((R, LANES, C), BF16),
        scores=vmem((T, T), F32), dsc=vmem((T, T), F32), drow=vmem((R, GROUP, T), F32), tot=vmem((LANES, T), F32),
        ins=vmem((N, C), F32), ys=vmem((N, C), F32), ssd=vmem((N, C), F32), zv=vmem((N, C), BF16),
        gated=vmem((N, max(C, S)), F32), dy=vmem((N, C), F32),
        yg=vmem((N, C), BF16), wds=vmem((N, C), BF16),
        rms=vmem((N, LANES), F32), sums=vmem((ntn, R, 8, T), F32),
        as_=vmem((2, R, half, D), BF16), ar_=vmem((2, R, half, D), BF16),
        bs_=vmem((2, R, half, D), BF16), br_=vmem((2, R, half, D), BF16), keep=vmem((R, half, D), F32),
        ga0=vmem((D, C), BF16), ga1=vmem((D, 2 * C), BF16), ga2=vmem((blocks * (rp + HALO), z.Q), BF16),
        gy0=vmem((k0, nc * rp, C), BF16), gy1=vmem((k0, nc * rp, 2 * C), BF16), gy2=vmem((k0, nc * (rp + HALO), z.Q), BF16),
        gz0=vmem((nc * rp, C), BF16), gz1=vmem((nc * rp, 2 * C), BF16), gz2=vmem((nc * (rp + HALO), z.Q), BF16),
        gr0=vmem((nc, rp, C), BF16), gr1=vmem((nc, rp, 2 * C), BF16), gr2=vmem((nc, rp + HALO, z.Q), BF16),
        drun=vmem((N, LANES), F32), dcf=vmem((2, T, V), F32), edge=vmem((R, EDGE, V), F32),
        dce=vmem((R, EDGE, V), F32), dcat=vmem((N, V + LANES + C), BF16),
        prod=vmem((T, 2 * C), F32), hacc=vmem((2 * GROUP, T), F32), gstep=vmem((HALO, D), F32),
        shs=vmem((D, z.Q), BF16), shr=vmem((D, z.Q), BF16), shk=vmem((D, z.Q), F32),
        ls=vmem((rp + HALO, z.Q), F32), lr=vmem((rp + HALO, z.Q), F32),
        sm=vmem((ntn, 8, z.WL), F32), sd=vmem((nd, 8, z.WL), F32), sc=vmem((nc, 8, z.WL), F32),
        l_in=dma((2,)), l_out=dma((2, R)),
        wz_send=dma((PIECES, 2, nc, z.SUB)), wd_send=dma((PIECES, nc, nd, z.SUB)), w_recv=dma((PIECES, nd, nc, z.SUB)),
        wh_send=dma((nd,)), wh_recv=dma((nd,)),
        h_send=dma((R,)), h_recv=dma((R,)),
        s_send=dma((R,)), s_recv=dma((R,)), g_send=dma((R,)), g_recv=dma((R,)), e_send=dma((R,)), e_recv=dma((R,)),
        x_send=dma((R, ntn)), x_recv=dma((R, ntn)),
        a_send=dma((2, R)), a_recv=dma((2, R)), b_send=dma((2, R)), b_recv=dma((2, R)),
        c_send=dma((2, R)), c_recv=dma((2, R)),
        ry_send=dma((3, nc, k0)), ry_recv=dma((3, nc, k0)), rz_send=dma((3, nc)), rz_recv=dma((3, nc)),
        sh_send=dma((2,)), sh_recv=dma((2,)),
        st_send=dma((ntn,)), st_recv=dma((ntn,)), sd_send=dma((nd,)), sd_recv=dma((nd,)),
        sc_send=dma((nc,)), sc_recv=dma((nc,)),
    )
    names = list(ins) + list(outs) + list(scratch)
    whole = pl.BlockSpec(memory_space=pltpu.VMEM)
    large = pl.BlockSpec(memory_space=pl.ANY)
    raw = pl.pallas_call(
        functools.partial(kernel, z, names),
        out_shape=list(outs.values()),
        in_specs=[large] * 2 + [whole] * (len(ins) - 2),
        out_specs=[large] * 2 + [whole] * (len(outs) - 2),
        scratch_shapes=list(scratch.values()),
        compiler_params=pltpu.CompilerParams(
            collective_id=0, has_side_effects=True, vmem_limit_bytes=z.limit
        ),
    )(*ins.values())

    shapes = [
        ((N, D), BF16), ((N, D), BF16), ((D,), F32), ((rows, 2, C), F32), ((S // ntn, rows), F32), ((H, rows), F32),
        ((z.K, C), F32), ((C,), F32), ((z.K, S), F32), ((S,), F32), ((H,), F32), ((H,), F32), ((H,), F32),
        ((C,), F32), ((rows, C), F32),
    ]
    outs = pl.pallas_call(
        functools.partial(finishing, z),
        out_shape=[jax.ShapeDtypeStruct(*shape) for shape in shapes],
        in_specs=[whole] * 6,
        out_specs=[large] * 2 + [whole] * (len(shapes) - 2),
        scratch_shapes=[vmem((LANES, LANES), F32), dma((2,))],
        compiler_params=pltpu.CompilerParams(vmem_limit_bytes=z.limit),
    )(*raw)
    (block_out, input_grad, norm, heads, shared, step, taps, bias, staps, sbias, dsb, drate, dskip, gain, outw) = outs
    return (
        narrow(block_out).reshape(hidden_in.shape),
        narrow(input_grad).reshape(hidden_in.shape),
        narrow(norm),
        heads, shared.T, step.T, taps, bias, staps, sbias, dsb, drate, dskip, gain, outw.T,
    )


def solution(mesh):
    nd, nc, ntn = (mesh.shape[name] for name in ("dp", "context", "tensor"))

    def body(*args):
        hidden, heads, shared = args[0], args[3], args[4]
        micro, seqs, tokens, width = hidden.shape
        rows = heads.shape[0]
        rp = -(-rows // 16) * 16
        inner = heads.shape[2]
        z = types.SimpleNamespace(
            R=micro * seqs, T=tokens, d_true=width, D=rp * nd * nc, rows=rows, rp=rp, nd=nd, nc=nc, ntn=ntn,
            C=inner, H=args[10].shape[0], S=shared.shape[1], K=args[6].shape[0],
            Q=shared.shape[1] // 2, limit=62 << 20,
            SUB=3 if rp % 48 == 0 else 1,
        )
        z.WL = max(inner + z.S, z.D, LANES + inner)
        return on_device(z, *args)

    return jax.shard_map(
        body,
        mesh=mesh,
        in_specs=(
            P(None, "dp", "context", None),
            P(None, "dp", None),
            P(),
            P(("dp", "context"), None, "tensor"),
            P(("dp", "context"), None),
            P(("dp", "context"), "tensor"),
            P(None, "tensor"),
            P("tensor"),
            P(),
            P(),
            P("tensor"),
            P("tensor"),
            P("tensor"),
            P("tensor"),
            P("tensor", ("dp", "context")),
            P(None, "dp", "context", None),
        ),
        out_specs=(
            P(None, "dp", "context", None),
            P(None, "dp", "context", None),
            P(),
            P(("dp", "context"), None, "tensor"),
            P(("dp", "context"), "tensor"),
            P(("dp", "context"), "tensor"),
            P(None, "tensor"),
            P("tensor"),
            P(),
            P(),
            P("tensor"),
            P("tensor"),
            P("tensor"),
            P("tensor"),
            P("tensor", ("dp", "context")),
        ),
        check_vma=False,
    )
```

```python
import functools
import types

import jax
import jax.numpy as jnp
from jax import lax
from jax.experimental import pallas as pl
from jax.experimental.pallas import tpu as pltpu
from jax.sharding import PartitionSpec as P

EPS = 1e-05
F32 = jnp.float32
BF16 = jnp.bfloat16
MESH = pl.DeviceIdType.MESH
LANES = 128
HALO = 16
EDGE = 8
PIECES = 4
WIDE = 256
GROUP = 8


def nn(a, b):
    return lax.dot_general(a, b, (((1,), (0,)), ((), ())), preferred_element_type=F32)


def nt(a, b):
    return lax.dot_general(a, b, (((1,), (1,)), ((), ())), preferred_element_type=F32)


def tn(a, b):
    return lax.dot_general(a, b, (((0,), (0,)), ((), ())), preferred_element_type=F32)


def pieces_of(value, count):
    pieces = []
    for _ in range(count):
        piece = value.astype(BF16)
        pieces.append(piece)
        value = value - piece.astype(F32)
    return pieces


def exact_rows(value, ones):
    pieces = [piece.astype(F32) for piece in pieces_of(value, 3)]
    stacked = jnp.concatenate(pieces + [jnp.zeros_like(value)], axis=0).astype(BF16)
    out = nn(stacked, ones)
    return out[0:8] + out[8:16] + out[16:24]


def exact_right(value, ones):
    return sum(nn(piece, ones) for piece in pieces_of(value, 2))


def sigmoid(value):
    return 0.5 * jnp.tanh(0.5 * value) + 0.5


def iota(shape, dim):
    return lax.broadcasted_iota(jnp.int32, shape, dim)


def kernel(z, names, *refs):
    m = types.SimpleNamespace(**dict(zip(names, refs)))
    R, T, D, C, H, S = z.R, z.T, z.D, z.C, z.H, z.S
    rp, nd, nc, ntn = z.rp, z.nd, z.nc, z.ntn
    pairs = H // 2
    head = C // H
    V = C + S
    Z = V + LANES
    Q = z.Q
    BX, CX = slice(0, Q), slice(Q + C, V)
    half = T // 2
    d, c, t = lax.axis_index("dp"), lax.axis_index("context"), lax.axis_index("tensor")
    odd = lax.rem(t, 2)
    across = t + 1 - 2 * odd
    far = lax.rem(t + 2, 4) if ntn == 4 else t

    def at_ctx(k):
        return lax.rem(c + k, nc)

    def at_dp(k):
        return lax.rem(d + k, nd)

    def at_ten(k):
        return lax.rem(t + k, ntn)

    def rows_at(place, size):
        return pl.ds(pl.multiple_of(place * size, 16), size)

    def block(dd, cc):
        return rows_at(dd * nc + cc, rp)

    def row(r):
        return rows_at(r, T)

    def lanes_at(place, size):
        return pl.ds(pl.multiple_of(place, LANES), size)

    def copy(src, dst, send, recv, dev):
        return pltpu.make_async_remote_copy(
            src_ref=src, dst_ref=dst, send_sem=send, recv_sem=recv, device_id=dev, device_id_type=MESH
        )

    def load(which):
        return pltpu.make_async_copy((m.hid, m.cot)[which], (m.hv, m.cv)[which], m.l_in.at[which])

    load(0).start()
    load(1).start()
    barrier = pltpu.get_barrier_semaphore()
    others = [(at_dp(k), at_ctx(j), t) for k in range(nd) for j in range(nc) if k or j]
    peers = list(others)
    peers += [(d, c, at_ten(k)) for k in range(1, ntn)]
    for peer in peers:
        pl.semaphore_signal(barrier, inc=1, device_id=peer, device_id_type=MESH)

    m.wall[block(d, c), Q : Q + C] = m.hp[:, 1, :]
    m.wall[block(d, c), lanes_at(odd * (Q + C), Q)] = jnp.where(odd == 0, m.shp[:, :Q], m.shp[:, Q:])
    m.wt[d * nc + c] = jnp.zeros((GROUP, LANES), F32)
    m.wt[d * nc + c, 0:H, 0:rp] = m.stp[...].astype(F32)
    pl.semaphore_wait(barrier, len(peers))

    def subs(p):
        return z.SUB if p == 0 else 1

    def slot(p, dd, cc, u):
        if p == 1:
            return m.wt.at[dd * nc + cc]
        if p == 3:
            return m.wo.at[block(dd, cc)]
        place, size = ((odd * Q, Q + C), None, (Z, C))[p]
        rows = rp // subs(p)
        return m.wall.at[rows_at((dd * nc + cc) * subs(p) + u, rows), lanes_at(place, size)]

    def w_ctx(p, u, s, right):
        cc, to = (c - s, c + 1) if right else (c + s, c - 1)
        here = slot(p, d, cc, u)
        return copy(here, here, m.wz_send.at[p, int(right), s, u], m.w_recv.at[p, d, cc, u], (d, to, t))

    def w_dp(p, u, cc, k):
        here = slot(p, d, cc, u)
        return copy(here, here, m.wd_send.at[p, cc, k, u], m.w_recv.at[p, d, cc, u], (at_dp(k), c, t))

    def w_arrived(p, u, dd, cc):
        there = slot(p, dd, cc, u)
        copy(there, there, m.wd_send.at[p, cc, 0, u], m.w_recv.at[p, dd, cc, u], (d, c, t)).wait_recv()

    def w_each(p, s, act):
        for u in range(subs(p)):
            if s < nc - 1:
                pl.when((c - s >= 0) & (c < nc - 1))(lambda: act(w_ctx(p, u, s, True)))
                pl.when((c + s < nc) & (c > 0))(lambda: act(w_ctx(p, u, s, False)))
            for k in range(1, nd):
                if s == 0:
                    act(w_dp(p, u, c, k))
                else:
                    pl.when(c - s >= 0)(lambda: act(w_dp(p, u, c - s, k)))
                    pl.when(c + s < nc)(lambda: act(w_dp(p, u, c + s, k)))

    def w_start(p):
        w_each(p, 0, lambda one: one.start())

    def w_step(p, s):
        for u in range(subs(p)):
            for right in (True, False):
                cc = c - s if right else c + s

                @pl.when((cc >= 0) & (cc < nc))
                def _():
                    w_arrived(p, u, d, cc)
                    if s < nc - 1:
                        pl.when(c < nc - 1 if right else c > 0)(lambda: w_ctx(p, u, s, right).start())
                    for k in range(1, nd):
                        w_dp(p, u, cc, k).start()

    def w_rest(p):
        for k in range(1, nd):
            for cc in range(nc):
                for u in range(subs(p)):
                    w_arrived(p, u, at_dp(k), cc)

    def w_sent(p):
        for s in range(nc):
            w_each(p, s, lambda one: one.wait_send())

    def half_rows(dd):
        return rows_at(dd, nc * rp)

    def half_copy(k):
        here = m.wall.at[half_rows(at_dp(k)), lanes_at(odd * (Q + C), Q)]
        return copy(here, here, m.wh_send.at[k], m.wh_recv.at[k], (d, c, across))

    def half_arrived(k):
        there = m.wall.at[half_rows(at_dp(k)), lanes_at((1 - odd) * (Q + C), Q)]
        copy(there, there, m.wh_send.at[k], m.wh_recv.at[k], (d, c, across)).wait_recv()

    def halo_copy(r):
        return copy(
            m.hv.at[pl.ds(pl.multiple_of(r * T + T - HALO, 16), HALO)],
            m.hh.at[rows_at(r, HALO)],
            m.h_send.at[r],
            m.h_recv.at[r],
            (d, c + 1, t),
        )

    w_start(0)
    w_start(1)
    load(0).wait()

    @pl.when(c < nc - 1)
    def _():
        for r in range(R):
            halo_copy(r).start()

    m.wall[block(d, c), Z:] = m.hp[:, 0, :]
    m.wo[block(d, c), :] = m.ow[...]

    m.par[0 : z.K, BX] = m.cs[:, :Q]
    m.par[0 : z.K, Q : Q + C] = m.ch[...]
    m.par[0 : z.K, CX] = m.cs[:, Q:]
    m.par[5:6, :S] = m.bs[...][None]
    m.par[4:5, BX] = m.par[5:6, :Q]
    m.par[4:5, Q : Q + C] = m.bh[...][None]
    m.par[4:5, CX] = m.par[5:6, Q:S]
    m.par[5:6, :C] = m.gg[...][None]
    for h in range(H):
        m.par[6:7, h * head : (h + 1) * head] = jnp.broadcast_to(m.sk[0:1, h : h + 1], (1, head))
    m.gain[0:1, :] = m.ng[...][None]
    m.tile[...] = jnp.zeros_like(m.tile)
    m.tile[0:1, 0:H] = m.sb[...]
    m.tile[1:2, 0:H] = -jnp.exp(m.ld[...])
    turned = jnp.transpose(m.tile[...])
    m.hcol[...] = turned[0:GROUP, :]
    bias_col, rate_col = m.hcol[:, 0:1], m.hcol[:, 1:2]
    gain_in = m.gain[0:1, :]

    def normalize(u):
        u = u.astype(F32)
        mean = jnp.sum(u * u, axis=-1, keepdims=True) * (1.0 / z.d_true)
        return (u * lax.rsqrt(mean + EPS)) * gain_in

    length = m.seg.shape[-1]
    begin = c * T
    seqs = m.seg.shape[1]

    def ids_at(place, size):
        place = pl.multiple_of(place, LANES)
        lines = [m.seg[r // seqs, r % seqs : r % seqs + 1, pl.ds(place, size)] for r in range(R)]
        return jnp.concatenate(lines + [jnp.zeros_like(lines[0])] * (-R % 8), axis=0).astype(F32)

    now = ids_at(begin, T)
    before = jnp.where(c == 0, -1.0, ids_at(jnp.maximum(begin - LANES, 0), LANES))
    behind = jnp.where(c == nc - 1, -2.0, ids_at(jnp.minimum(begin + T, length - LANES), LANES))
    m.segr[...] = now
    m.segb[...] = before
    m.sega[...] = behind
    m.carried[...] = (now == before[:, LANES - 1 : LANES]).astype(F32)
    m.closing[...] = (now == now[:, T - 1 : T]).astype(F32)
    m.tot[...] = jnp.zeros_like(m.tot)
    m.tot[0 : now.shape[0], :] = now
    m.segc[...] = jnp.transpose(m.tot[...])
    away = iota((T, T), 0) - iota((T, T), 1)
    m.lower[...] = (away >= 0).astype(BF16)
    m.upper[...] = (away <= 0).astype(BF16)
    for r in range(R):
        same = m.segc[:, r : r + 1] == m.segr[r : r + 1, :]
        m.past[r] = (same & (away >= 0)).astype(BF16)
        m.next[r] = (same & (away <= 0)).astype(BF16)
        for j in range(1, z.K):
            m.down[r, j - 1] = (same & (away == j)).astype(BF16)
            m.up[r, j - 1] = (same & (away == -j)).astype(BF16)

    @pl.when(c == 0)
    def _():
        m.hh[...] = jnp.zeros_like(m.hh)
        m.sin[...] = jnp.zeros_like(m.sin)

    @pl.when(c == nc - 1)
    def _():
        m.gin[...] = jnp.zeros_like(m.gin)
        m.dce[...] = jnp.zeros_like(m.dce)

    m.sm[...] = jnp.zeros_like(m.sm)
    m.hacc[...] = jnp.zeros_like(m.hacc)
    m.drow[...] = jnp.zeros_like(m.drow)
    m.gstep[...] = jnp.zeros_like(m.gstep)

    @pl.loop(0, R)
    def _(r):
        value = normalize(m.hv[row(r), :]).astype(BF16)
        m.nrm[row(r), :] = value
        m.nrmt[:, row(r)] = jnp.transpose(value)

    load(1).wait()

    @pl.loop(0, R)
    def _(r):
        m.cott[:, row(r)] = jnp.transpose(m.cv[row(r), :])

    reach = iota((HALO, HALO), 1) - HALO - iota((HALO, HALO), 0)
    ahead = iota((HALO, HALO), 1) + HALO - iota((HALO, HALO), 0)
    m.early[...] = jnp.zeros_like(m.early)
    for r in range(R):
        near = m.segc[0:HALO, r : r + 1] == m.segb[r : r + 1, LANES - HALO : LANES]
        late = m.segc[T - HALO : T, r : r + 1] == m.sega[r : r + 1, 0:HALO]
        for j in range(1, z.K):
            first = ((r * (z.K - 1)) + j - 1) * HALO
            m.early[first : first + HALO, r * HALO : (r + 1) * HALO] = (near & (reach == -j)).astype(BF16)
            m.late[r, (j - 1) * HALO : j * HALO, :] = (late & (ahead == j)).astype(BF16)

    w_step(0, 1)
    w_step(1, 1)
    w_start(2)

    @pl.when(c > 0)
    def _():
        for r in range(R):
            halo_copy(r).wait_recv()

    m.nrmh[...] = normalize(m.hh[...]).astype(BF16)
    for s in range(2, nc):
        w_step(0, s)
        w_step(1, s)
        if s == 2:
            w_start(3)
    half_copy(0).start()
    w_step(2, 1)
    w_rest(1)

    m.tile[...] = jnp.zeros_like(m.tile)
    for b in range(nd * nc):
        m.tile[0:GROUP, :] = m.wt[b]
        m.wall[b * rp : (b + 1) * rp, V:Z] = jnp.transpose(m.tile[...])[0:rp, :].astype(BF16)
    w_rest(0)
    for k in range(1, nd):
        half_copy(k).start()
    w_step(3, 1)
    if nc > 2:
        w_step(2, 2)

    low_lanes = iota((T, LANES), 1) < head
    lane = iota((T, LANES), 1)
    fold = (iota((C, LANES), 0) // head == iota((C, LANES), 1)).astype(F32)
    fold_run = fold.astype(BF16)
    fold_through = (
        (iota((C, LANES), 0) // head == iota((C, LANES), 1) - GROUP).astype(F32) - fold
    ).astype(BF16)
    fold_step = (iota((C, LANES), 0) // head == iota((C, LANES), 1) - 2 * GROUP).astype(BF16)
    RUN, STEP, LEAD, TRAIL = 0, GROUP, 2 * GROUP, 3 * GROUP

    def widened(values, base, p):
        a = base + 2 * p
        return jnp.where(low_lanes[: values.shape[0]], values[:, a : a + 1], values[:, a + 1 : a + 2])

    def spread(values, base):
        return jnp.concatenate([widened(values, base, p) for p in range(pairs)], axis=1)

    def state_copy(r):
        return copy(m.ssend.at[r], m.sin.at[r], m.s_send.at[r], m.s_recv.at[r], (d, c + 1, t))

    def grad_copy(r):
        return copy(m.gsend.at[r], m.gin.at[r], m.g_send.at[r], m.g_recv.at[r], (d, c - 1, t))

    def edge_copy(r):
        return copy(m.edge.at[r], m.dce.at[r], m.e_send.at[r], m.e_recv.at[r], (d, c - 1, t))

    def kept(r):
        return spread(m.cols[pl.ds(r * T + T - 1, 1), :], LEAD)

    def pair(p):
        return slice(p * LANES, (p + 1) * LANES)

    def lanes_of(p):
        return slice(Q + p * LANES, Q + (p + 1) * LANES)

    def serve_state(r):
        state_copy(r).wait_recv()

        @pl.when(c < nc - 1)
        def _():
            m.ssend[r] = (m.fresh[r] + kept(r) * m.sin[r].astype(F32)).astype(BF16)
            state_copy(r).start()

    def serve_grad(r):
        grad_copy(r).wait_recv()

        @pl.when(c > 0)
        def _():
            m.gsend[r] = (m.local[r] + kept(r) * m.gin[r].astype(F32)).astype(BF16)
            grad_copy(r).start()

    hops = nc - 1 - c
    soon = R == 4 and nc > 2
    if soon:
        state_late = (c > 2) | ((c == 2) & (nc > 3))
        grad_late = hops > 2
    else:
        state_late, grad_late = c > 0, hops > 0

    def state_point(place, r):
        if soon:
            for who, item in place:
                @pl.when((c == who) & r)
                def _():
                    serve_state(item)

    def grad_point(place, r):
        if soon:
            for who, item in place:
                @pl.when((hops == who) & r)
                def _():
                    serve_grad(item)

    for k in range(nd):
        half_arrived(k)
    halo_v = nn(m.nrmh[...], m.wall[:, :V]).astype(BF16)
    m.hfix[...] = nn(m.early[...], halo_v)

    @pl.loop(0, R)
    def _(r):
        acc = nn(m.nrm[row(r), :], m.wall[:, :Z])
        m.v[row(r), :] = acc[:, :V].astype(BF16)
        raw = jnp.transpose(acc[:, V:].astype(BF16).astype(F32))[0:GROUP]
        pre = raw + bias_col
        step = jnp.maximum(pre, 0.0) + jnp.log1p(jnp.exp(-jnp.abs(pre)))
        m.pre[:, row(r)] = pre
        m.step[:, row(r)] = step
        run = exact_rows(step * rate_col, m.upper[...])
        m.runr[r] = run
        m.tot[0:GROUP, :] = run
        m.tot[GROUP : 2 * GROUP, :] = step
        m.tot[2 * GROUP : 3 * GROUP, :] = jnp.exp(run) * m.carried[pl.ds(r, 1), :]
        m.tot[3 * GROUP : 4 * GROUP, :] = jnp.exp(run[:, T - 1 : T] - run) * m.closing[pl.ds(r, 1), :]
        m.cols[row(r), :] = jnp.transpose(m.tot[...])
        for a in range(0, V, WIDE):
            part = slice(a, min(a + WIDE, V))
            value = m.v[row(r), part]
            conv = value.astype(F32) * m.par[0:1, part] + m.par[4:5, part]
            first = jnp.zeros((EDGE, conv.shape[1]), F32)
            for j in range(1, z.K):
                tap = m.par[j : j + 1, part]
                conv = conv + nn(m.down[r, j - 1], value) * tap
                first = first + m.hfix[pl.ds((r * (z.K - 1) + j - 1) * HALO, EDGE), part] * tap
            conv = jnp.concatenate([conv[0:EDGE] + first, conv[EDGE:]], axis=0)
            logistic = sigmoid(conv)
            m.mix[row(r), part] = (conv * logistic).astype(BF16)
            m.slope[row(r), part] = logistic * (1.0 + conv * (1.0 - logistic))
        state_point([(1, 0)], r == 2)
        state_point([(1, 1)], r == 3)
        for p in range(pairs):
            scaled = m.mix[row(r), lanes_of(p)].astype(F32) * widened(m.cols[row(r), :], STEP, p)
            m.xs[row(r), pair(p)] = scaled.astype(BF16)
            m.xt[row(r), pair(p)] = (scaled * widened(m.cols[row(r), :], TRAIL, p)).astype(BF16)
        m.fresh[r] = tn(m.mix[row(r), BX], m.xt[row(r), :])

        @pl.when(c == 0)
        def _():
            m.ssend[r] = m.fresh[r].astype(BF16)
            state_copy(r).start()

        for s in range(2, nc):
            pl.when(r == min(s - 2, R - 1))(lambda: w_step(3, s))
        for s in range(3, nc):
            pl.when(r == min(s - 3, R - 1))(lambda: w_step(2, s))

    state_point([(2, 0)], True)

    @pl.loop(0, R)
    def _(r):
        b, cm = m.mix[row(r), BX], m.mix[row(r), CX]
        m.scores[...] = nt(cm, b) * m.past[r].astype(F32)
        for p in range(pairs):
            for a in range(0, T, LANES):
                rows, seen = slice(a, a + LANES), a + LANES
                here = pl.ds(pl.multiple_of(r * T, 16) + a, LANES)
                both = []
                for h in (2 * p, 2 * p + 1):
                    decay = jnp.exp(jnp.minimum(m.cols[here, h : h + 1] - m.runr[r, h : h + 1, :seen], 0.0))
                    weight = (decay * m.scores[rows, :seen]).astype(BF16)
                    both.append(nn(weight, m.xs[pl.ds(pl.multiple_of(r * T, 16), seen), pair(p)]))
                m.ins[here, pair(p)] = jnp.where(low_lanes[:LANES], both[0], both[1])
        state_point([(1, 2)], r == 0)
        state_point([(2, 1)], r == 2)

    state_point([(1, 3)], True)
    w_rest(2)
    w_rest(3)

    def sums_copy(r, k):
        return copy(
            m.sums.at[t, r], m.sums.at[t, r], m.x_send.at[r, k], m.x_recv.at[r, t], (d, c, at_ten(k))
        )

    def sums_arrived(r, who):
        copy(
            m.sums.at[who, r], m.sums.at[who, r], m.x_send.at[r, 0], m.x_recv.at[r, who], (d, c, t)
        ).wait_recv()

    def mine(r):
        return pl.ds(pl.multiple_of(r * T + odd * half, 16), half)

    def theirs(r):
        return pl.ds(pl.multiple_of(r * T + (1 - odd) * half, 16), half)

    def near_copy(a, r):
        return copy(m.as_.at[a, r], m.ar_.at[a, r], m.a_send.at[a, r], m.a_recv.at[a, r], (d, c, across))

    def far_copy(a, r):
        return copy(m.bs_.at[a, r], m.br_.at[a, r], m.b_send.at[a, r], m.b_recv.at[a, r], (d, c, far))

    def back_copy(a, r):
        out = (m.ov, m.iv)[a].at[mine(r)]
        return copy(out, out, m.c_send.at[a, r], m.c_recv.at[a, r], (d, c, across))

    def back_arrived(a, r):
        out = (m.ov, m.iv)[a].at[theirs(r)]
        copy(out, out, m.c_send.at[a, r], m.c_recv.at[a, r], (d, c, across)).wait_recv()

    def give(a, r, value):
        first, second = value[:half], value[half:]
        m.as_[a, r] = jnp.where(odd == 0, second, first).astype(BF16)
        near_copy(a, r).start()
        m.keep[r] = jnp.where(odd == 0, first, second)

    def chip_sum(a, r):
        near_copy(a, r).wait_recv()
        m.bs_[a, r] = (m.keep[r] + m.ar_[a, r].astype(F32)).astype(BF16)
        if ntn == 4:
            far_copy(a, r).start()

    def full_sum(a, r):
        total = m.bs_[a, r].astype(F32)
        if ntn == 4:
            far_copy(a, r).wait_recv()
            total = total + m.br_[a, r].astype(F32)
        return total

    def serve_late(r):
        if soon and nc > 3:
            pl.when((c > 2) | (r >= 2))(lambda: serve_state(r))
        else:
            serve_state(r)

    def gating(r):
        pl.when(state_late)(lambda: serve_late(r))
        cm = m.mix[row(r), CX]
        gate = nn(m.nrm[row(r), :], m.wall[:, Z:])
        m.zv[row(r), :] = gate.astype(BF16)
        m.dy[row(r), :] = nn(m.cv[row(r), :], m.wo[...])
        m.ys[row(r), :] = nn(cm, m.sin[r])
        squares = jnp.zeros((T, LANES), F32)
        inner = jnp.zeros((T, LANES), F32)
        for p in range(pairs):
            carried = m.ys[row(r), pair(p)] * widened(m.cols[row(r), :], LEAD, p)
            m.ys[row(r), pair(p)] = carried
            ssd = m.ins[row(r), pair(p)] + carried + m.par[6:7, pair(p)] * m.mix[row(r), lanes_of(p)].astype(F32)
            m.ssd[row(r), pair(p)] = ssd
            gate = m.zv[row(r), pair(p)].astype(F32)
            gated = ssd * (gate * sigmoid(gate))
            m.gated[row(r), pair(p)] = gated
            scaled = gated * m.par[5:6, pair(p)]
            m.yg[row(r), pair(p)] = scaled.astype(BF16)
            squares = squares + gated * gated
            inner = inner + scaled * m.dy[row(r), pair(p)]
        squares = jnp.sum(squares, axis=-1, keepdims=True)
        inner = jnp.sum(inner, axis=-1, keepdims=True)
        both = jnp.where(lane == 0, squares, jnp.where(lane == 1, inner, 0.0))
        m.sums[t, r] = jnp.transpose(both)[0:8, :]
        for k in range(1, ntn):
            sums_copy(r, k).start()
        give(0, r, nt(m.yg[row(r), :], m.wo[...]))

    def ungating(r):
        for k in range(1, ntn):
            sums_arrived(r, at_ten(k))
        total = m.sums[0, r]
        for who in range(1, ntn):
            total = total + m.sums[who, r]
        scale = lax.rsqrt(total[0:1] * (1.0 / (C * ntn)) + EPS)
        inner = total[1:2] * (1.0 / (C * ntn)) * scale * scale * scale
        m.tot[0:1, :] = scale
        m.tot[1:2, :] = inner
        columns = jnp.transpose(m.tot[...])
        m.rms[row(r), :] = columns
        scale = jnp.broadcast_to(columns[:, 0:1], (T, LANES))
        inner = jnp.broadcast_to(columns[:, 1:2], (T, LANES))
        for p in range(pairs):
            gated, dy, ssd = m.gated[row(r), pair(p)], m.dy[row(r), pair(p)], m.ssd[row(r), pair(p)]
            gate = m.zv[row(r), pair(p)].astype(F32)
            gain = m.par[5:6, pair(p)]
            normal = gated * scale
            m.sm[5:6, pair(p)] += jnp.sum(dy * normal, axis=0, keepdims=True)
            m.yg[row(r), pair(p)] = (normal * gain).astype(BF16)
            d_gated = scale * dy * gain - gated * inner
            logistic = sigmoid(gate)
            m.dcat[row(r), Z + p * LANES : Z + (p + 1) * LANES] = (
                d_gated * ssd * (logistic * (1.0 + gate * (1.0 - logistic)))
            ).astype(BF16)
            d_ssd = d_gated * (gate * logistic)
            m.ssd[row(r), pair(p)] = d_ssd
            m.wds[row(r), pair(p)] = (d_ssd * widened(m.cols[row(r), :], LEAD, p)).astype(BF16)
        m.local[r] = tn(m.mix[row(r), CX], m.wds[row(r), :])

        @pl.when(c == nc - 1)
        def _():
            m.gsend[r] = m.local[r].astype(BF16)
            if nc > 1:
                grad_copy(r).start()

    @pl.loop(0, R + 1)
    def _(i):
        pl.when(i < R)(lambda: gating(i))

        @pl.when(i >= 1)
        def _():
            ungating(i - 1)

        grad_point([(1, 0)], i == 3)
        grad_point([(1, 1)], i == 4)

        @pl.when(i == R - 1)
        def _():
            pl.loop(0, R - 1)(lambda r: chip_sum(0, r))

        pl.when(i == R)(lambda: chip_sum(0, R - 1))

    gall, gyr, gzs, gzr = (m.ga0, m.ga1, m.ga2), (m.gy0, m.gy1, m.gy2), (m.gz0, m.gz1, m.gz2), (m.gr0, m.gr1, m.gr2)
    tall = (rp, rp, rp + HALO)

    def rs_dp(part, j, k):
        cc = at_ctx(j)
        return copy(
            gall[part].at[rows_at(at_dp(k) * nc + cc, tall[part])],
            gyr[part].at[k - 1, rows_at(cc, tall[part])],
            m.ry_send.at[part, j, k - 1],
            m.ry_recv.at[part, j, k - 1],
            (at_dp(k), c, t),
        )

    def rs_ctx(part, j):
        cc = at_ctx(j)
        return copy(
            gzs[part].at[rows_at(cc, tall[part])],
            gzr[part].at[c],
            m.rz_send.at[part, j],
            m.rz_recv.at[part, c],
            (d, cc, t),
        )

    def rs_arrived(part, cc):
        copy(gzr[part].at[cc], gzr[part].at[cc], m.rz_send.at[part, 0], m.rz_recv.at[part, cc], (d, c, t)).wait_recv()

    def rs_start(part):
        for j in list(range(1, nc)) + [0]:
            for k in range(1, nd):
                rs_dp(part, j, k).start()

    def rs_middle(part, j):
        cc = at_ctx(j)
        total = gall[part][rows_at(d * nc + cc, tall[part]), :].astype(F32)
        for k in range(1, nd):
            rs_dp(part, j, k).wait_recv()
            total = total + gyr[part][k - 1, rows_at(cc, tall[part]), :].astype(F32)
        own = j == 0

        def keep():
            gzr[part][c] = total.astype(BF16)

        def send():
            gzs[part][rows_at(cc, tall[part]), :] = total.astype(BF16)
            rs_ctx(part, j).start()

        if isinstance(j, int):
            keep() if own else send()
        else:
            pl.when(own)(keep)
            pl.when(jnp.logical_not(own))(send)

    def rs_end(part):
        for k in range(1, nc):
            rs_arrived(part, at_ctx(k))
        total = gzr[part][0].astype(F32)
        for cc in range(1, nc):
            total = total + gzr[part][cc].astype(F32)
        return total

    def rs_sent(part):
        for j in range(nc):
            for k in range(1, nd):
                rs_dp(part, j, k).wait_send()
            if j:
                rs_ctx(part, j).wait_send()

    m.ga1[:, C:] = nn(m.cott[...], m.yg[...]).astype(BF16)
    m.ga1[:, :C] = nn(m.nrmt[...], m.dcat[:, Z:]).astype(BF16)
    rs_start(1)
    grad_point([(1, 2), (2, 0)], True)

    @pl.loop(0, R)
    def _(r):
        b, cm = m.mix[row(r), BX], m.mix[row(r), CX]
        m.scores[...] = nt(b, cm) * m.next[r].astype(F32)
        start = pl.multiple_of(r * T, 16)
        for a in range(0, T, LANES):
            rows, here, after = slice(a, a + LANES), pl.ds(start + a, LANES), pl.ds(start + a, T - a)
            losses = jnp.zeros((LANES, LANES), F32)
            for p in range(pairs):
                ds_pair = m.ssd[after, pair(p)].astype(BF16)
                xs_pair = m.xs[here, pair(p)]
                both = []
                for h in (2 * p, 2 * p + 1):
                    pick = low_lanes[:LANES] if h % 2 == 0 else ~low_lanes[:LANES]
                    decay = jnp.exp(jnp.minimum(m.runr[r, h : h + 1, a:] - m.cols[here, h : h + 1], 0.0))
                    weight = decay * m.scores[rows, a:]
                    both.append(nn(weight.astype(BF16), ds_pair))
                    d_weight = nt(jnp.where(pick, xs_pair, jnp.zeros_like(xs_pair)), ds_pair)
                    flow = d_weight * weight
                    if h == 0:
                        m.dsc[rows, a:] = d_weight * decay
                    else:
                        m.dsc[rows, a:] += d_weight * decay
                    losses = jnp.where(lane[:LANES] == h, jnp.sum(flow, axis=1, keepdims=True), losses)
                    down = jnp.sum(flow, axis=0, keepdims=True)
                    if a == 0:
                        m.drow[r, h : h + 1, :] = down
                    else:
                        m.drow[r, h : h + 1, a:] += down
                m.ins[here, pair(p)] = jnp.where(low_lanes[:LANES], both[0], both[1])
            m.drun[here, :] = exact_right(m.ssd[here, :] * m.ys[here, :], fold_run) - losses
            d_scores = (m.dsc[rows, a:] * m.next[r, rows, a:].astype(F32)).astype(BF16)
            m.gated[here, :LANES] = nn(d_scores, m.mix[after, CX])
            d_after = tn(d_scores, m.mix[here, BX])
            if a == 0:
                m.gated[after, LANES:S] = d_after
            else:
                m.gated[after, LANES:S] += d_after

        grad_point([(1, 3), (2, 1)], r == 0)
        grad_point([(2, 2)], r == 1)
        grad_point([(2, 3)], r == 2)

    def final_out(r):
        value = m.hv[mine(r), :].astype(F32) + m.rms[mine(r), 0:1] * full_sum(0, r)
        m.ov[mine(r), :] = value.astype(BF16)
        back_copy(0, r).start()

    def adjoint(r):
        pl.when(grad_late)(lambda: serve_grad(r))
        b = m.mix[row(r), BX]
        grad = m.gin[r]
        for p in range(pairs):
            trailing = widened(m.cols[row(r), :], TRAIL, p)
            reach = nn(b, m.gin[r, :, pair(p)]) * trailing
            x = m.mix[row(r), lanes_of(p)].astype(F32)
            d_xs = m.ins[row(r), pair(p)] + reach
            d_ssd = m.ssd[row(r), pair(p)]
            m.prod[:, pair(p)] = m.xs[row(r), pair(p)].astype(F32) * reach
            m.prod[:, C + p * LANES : C + (p + 1) * LANES] = d_xs * x
            m.sm[7:8, LANES + p * LANES : 2 * LANES + p * LANES] += jnp.sum(d_ssd * x, axis=0, keepdims=True)
            m.dy[row(r), pair(p)] = (
                d_xs * widened(m.cols[row(r), :], STEP, p) + m.par[6:7, pair(p)] * d_ssd
            ) * m.slope[row(r), lanes_of(p)]
        m.gated[row(r), :Q] = (
            m.gated[row(r), :LANES] + nt(m.xt[row(r), :], grad)
        ) * m.slope[row(r), BX]
        m.gated[row(r), Q:S] = (
            m.gated[row(r), LANES:S] + nt(m.wds[row(r), :], m.sin[r])
        ) * m.slope[row(r), CX]

        @pl.when(c > 0)
        def _():
            first = pl.ds(pl.multiple_of(r * T, 16), EDGE)
            m.edge[r, :, BX] = m.gated[first, :Q]
            m.edge[r, :, Q : Q + C] = m.dy[first, :]
            m.edge[r, :, CX] = m.gated[first, Q:S]
            edge_copy(r).start()

        m.drun[row(r), :] += exact_right(m.prod[:, :C], fold_through) + exact_right(m.prod[:, C:], fold_step)
        joint = jnp.sum(grad.astype(F32) * m.sin[r].astype(F32), axis=0, keepdims=True)
        joint = exact_right(jnp.broadcast_to(joint, (8, C)), fold_run)[0:1]
        last = m.cols[pl.ds(r * T + T - 1, 1), :]
        kept_lanes = jnp.concatenate([last[:, LEAD : LEAD + H], jnp.zeros((1, LANES - H), F32)], axis=1)
        m.drun[pl.ds(r * T + T - 1, 1), :] += joint * kept_lanes
        turned = jnp.transpose(m.drun[row(r), :])
        through = jnp.sum(turned[GROUP : 2 * GROUP], axis=1, keepdims=True)
        d_run = turned[0:GROUP] + m.drow[r]
        d_run = d_run + jnp.where(iota((GROUP, T), 1) == T - 1, through, 0.0)
        d_growth = exact_rows(d_run, m.lower[...])
        d_step = turned[2 * GROUP : 3 * GROUP] + rate_col * d_growth
        d_pre = d_step * sigmoid(m.pre[:, row(r)])
        m.hacc[0:GROUP, :] += d_pre
        m.hacc[GROUP : 2 * GROUP, :] += m.step[:, row(r)] * d_growth * rate_col
        d_pre = jnp.where(iota((GROUP, T), 0) < H, d_pre, 0.0)
        m.gstep[...] += nn(jnp.concatenate([d_pre, jnp.zeros_like(d_pre)], axis=0).astype(BF16), m.nrm[row(r), :])
        m.tot[0:GROUP, :] = d_pre
        m.dcat[row(r), V:Z] = jnp.transpose(m.tot[...]).astype(BF16)

    def finish(r):
        @pl.when(c < nc - 1)
        def _():
            edge_copy(r).wait_recv()

        edge = m.dce[r]
        edge = jnp.concatenate([edge, jnp.zeros_like(edge)], axis=0).astype(BF16)
        m.lfix[...] = nn(m.late[r], edge)
        cuts = [(m.gated, 0, 0, Q), (m.gated, Q, Q + C, Q)]
        cuts += [(m.dy, a, Q + a, min(WIDE, C - a)) for a in range(0, C, WIDE)]
        for held, place, first, size in cuts:
            part = slice(first, first + size)
            d_conv = held[row(r), place : place + size]
            low = d_conv.astype(BF16)
            value = m.v[row(r), part].astype(F32)
            m.sm[4:5, part] += jnp.sum(d_conv, axis=0, keepdims=True)
            m.sm[0:1, part] += jnp.sum(d_conv * value, axis=0, keepdims=True)
            d_v = d_conv * m.par[0:1, part]
            for j in range(1, z.K):
                moved = nn(m.up[r, j - 1], low)
                moved = jnp.concatenate(
                    [moved[: T - HALO], moved[T - HALO :] + m.lfix[(j - 1) * HALO : j * HALO, part]], axis=0
                )
                d_v = d_v + moved * m.par[j : j + 1, part]
                m.sm[j : j + 1, part] += jnp.sum(moved * value, axis=0, keepdims=True)
            m.dcat[row(r), part] = d_v.astype(BF16)

    def finish_norm(r):
        value = nt(m.dcat[row(r), :], m.wall[...])
        give(1, r, value)
        u = m.hv[row(r), :].astype(F32)
        mean = jnp.sum(u * u, axis=-1, keepdims=True) * (1.0 / z.d_true)
        m.sm[6:7, :D] += jnp.sum(value * (u * lax.rsqrt(mean + EPS)), axis=0, keepdims=True)

    m.tot[...] = jnp.zeros_like(m.tot)

    def first_sums(j, upward):
        up = c + j < nc
        pl.when(up if upward else jnp.logical_not(up))(lambda: rs_middle(1, j))

    @pl.loop(0, R)
    def _(r):
        pl.when(r == 0)(lambda: final_out(0))
        adjoint(r)
        for j in range(1, min(nc, 3)):
            pl.when(r == min(2 * j - 2, R - 1))(lambda: first_sums(j, True))

    @pl.loop(0, R)
    def _(r):
        finish(r)
        finish_norm(r)
        for k in range(1, R):
            pl.when(r == (k - 1 if k < R - 1 else R - 1))(lambda: final_out(k))
        for j in range(3, nc):
            pl.when(r == min(j - 3, R - 1))(lambda: first_sums(j, True))
        for j in range(1, nc):
            pl.when(r == min(j - 1, R - 1))(lambda: first_sums(j, False))
        pl.when(r == R - 1)(lambda: rs_middle(1, 0))
        pl.when(r >= 1)(lambda: chip_sum(1, r - 1))

    def small_copy(index):
        return copy(m.sa.at[d * nc + c], m.sa.at[d * nc + c], m.sa_send.at[index], m.sa_recv.at[d * nc + c], others[index])

    def small_arrived(dd, cc):
        there = m.sa.at[dd * nc + cc]
        copy(there, there, m.sa_send.at[0], m.sa_recv.at[dd * nc + cc], (d, c, t)).wait_recv()

    def common_copy(k):
        return copy(m.sb2.at[t], m.sb2.at[t], m.st_send.at[k], m.st_recv.at[t], (d, c, at_ten(k)))

    def common_arrived(who):
        copy(m.sb2.at[who], m.sb2.at[who], m.st_send.at[0], m.st_recv.at[who], (d, c, t)).wait_recv()

    m.tile[...] = jnp.zeros_like(m.tile)
    m.tile[0 : 2 * GROUP, :] = jnp.broadcast_to(
        jnp.sum(m.hacc[...], axis=1, keepdims=True), (2 * GROUP, LANES)
    )
    m.sm[7:8, 0:LANES] = jnp.transpose(m.tile[...])[0:1, :]
    m.sa[d * nc + c] = jnp.concatenate([m.sm[...], jnp.zeros_like(m.sm)], axis=0).astype(BF16)
    for index in range(len(others)):
        small_copy(index).start()

    width = S // ntn
    starts = [k * width + (C if k * width >= Q else 0) for k in range(ntn)]
    quarters = [m.dcat[:, first : first + width] for first in starts]
    value = nn(m.nrmt[...], jnp.concatenate(quarters[0::2] + quarters[1::2], axis=1))

    def share_copy():
        return copy(m.shs, m.shr, m.sh_send.at[0], m.sh_recv.at[0], (d, c, across))

    m.shk[...] = jnp.where(odd == 0, value[:, : z.Q], value[:, z.Q :])
    m.shs[...] = jnp.where(odd == 0, value[:, z.Q :], value[:, : z.Q]).astype(BF16)
    share_copy().start()

    m.ga0[...] = nn(m.nrmt[...], m.dcat[:, Q : Q + C]).astype(BF16)
    share_copy().wait_recv()
    for b in range(nd * nc):
        here = slice(b * rp, (b + 1) * rp)
        there = b * (rp + HALO)
        m.ga2[there : there + rp, :] = (m.shk[here, :] + m.shr[here, :].astype(F32)).astype(BF16)
        steps = m.gstep[:, here]
        m.ga2[there + rp : there + rp + HALO, :] = jnp.concatenate(
            [steps, jnp.zeros((HALO, LANES - rp), F32)], axis=1
        ).astype(BF16)
    rs_start(2)
    rs_start(0)
    chip_sum(1, R - 1)

    def last_copy():
        return copy(m.ls, m.lr, m.sh_send.at[1], m.sh_recv.at[1], (d, c, far))

    def store(a, r):
        return pltpu.make_async_copy((m.ov, m.iv)[a].at[row(r)], (m.out, m.ing)[a].at[row(r)], m.l_out.at[a, r])

    def input_row(r):
        u = m.hv[mine(r), :].astype(F32)
        mean = jnp.sum(u * u, axis=-1, keepdims=True) * (1.0 / z.d_true)
        scale = lax.rsqrt(mean + EPS)
        unit = u * scale
        d_unit = full_sum(1, r) * gain_in
        inner = jnp.sum(d_unit * unit, axis=-1, keepdims=True) * (1.0 / z.d_true)
        value = m.cv[mine(r), :].astype(F32) + scale * (d_unit - unit * inner)
        m.iv[mine(r), :] = value.astype(BF16)
        back_copy(1, r).start()

    for dd in range(nd):
        for cc in range(nc):
            pl.when((dd != d) | (cc != c))(lambda: small_arrived(dd, cc))
    total = m.sa[0].astype(F32)
    for who in range(1, nd * nc):
        total = total + m.sa[who].astype(F32)
    m.sb2[t] = total[0:8]
    for k in range(1, ntn):
        common_copy(k).start()
    for r in range(R):
        back_arrived(0, r)
        store(0, r).start()
    for j in list(range(1, nc)) + [0]:
        rs_middle(2, j)
    m.gw1[...] = rs_end(1)

    @pl.loop(0, R)
    def _(r):
        input_row(r)
        pl.when(r >= 1)(lambda: back_arrived(1, r - 1))
        pl.when(r >= 1)(lambda: store(1, r - 1).start())

        @pl.when(r == 0)
        def _():
            rs_middle(0, 1 % nc)

        @pl.when(r == 1)
        def _():
            for j in list(range(2, nc)) + ([0] if nc > 1 else []):
                rs_middle(0, j)

        @pl.when(r == min(2, R - 1))
        def _():
            value = rs_end(2)
            if ntn == 4:
                m.ls[...] = value
                last_copy().start()
            else:
                m.gw2[...] = value

    for k in range(1, ntn):
        common_arrived(at_ten(k))
    common = m.sb2[0]
    for who in range(1, ntn):
        common = common + m.sb2[who]
    rows8, lanes8 = iota((8, z.WL), 0), iota((8, z.WL), 1)
    shared_here = (rows8 == 6) | ((rows8 < 5) & ((lanes8 < Q) | (lanes8 >= Q + C)))
    m.small[...] = jnp.where(shared_here, common, m.sb2[t])
    m.gw0[...] = rs_end(0)
    if ntn == 4:
        last_copy().wait_recv()
        m.gw2[0:rp, :] = m.ls[0:rp, :] + m.lr[0:rp, :]
        m.gw2[rp:, :] = m.ls[rp:, :]
        last_copy().wait_send()
    back_arrived(1, R - 1)
    store(1, R - 1).start()

    for a in range(2):
        for r in range(R):
            store(a, r).wait()
            back_copy(a, r).wait_send()
            near_copy(a, r).wait_send()
            if ntn == 4:
                far_copy(a, r).wait_send()
    for p in range(PIECES):
        w_sent(p)
    for k in range(nd):
        half_copy(k).wait_send()
    for part in range(3):
        rs_sent(part)
    for r in range(R):
        for k in range(1, ntn):
            sums_copy(r, k).wait_send()

        @pl.when(c < nc - 1)
        def _():
            halo_copy(r).wait_send()
            state_copy(r).wait_send()

        @pl.when(c > 0)
        def _():
            grad_copy(r).wait_send()
            edge_copy(r).wait_send()

    share_copy().wait_send()
    for index in range(len(others)):
        small_copy(index).wait_send()
    for k in range(1, ntn):
        common_copy(k).wait_send()


def finishing(z, out, ing, gw0, gw1, gw2, small, *outs):
    (o_out, o_ing, norm, heads, shared, step, taps, bias, staps, sbias, dsb, drate, dskip, gain, outw, tile, sems) = outs
    C, S, D, H, rp, rows = z.C, z.S, z.D, z.H, z.rp, z.rows
    V = C + S
    head = C // H
    moves = [pltpu.make_async_copy(out, o_out, sems.at[0]), pltpu.make_async_copy(ing, o_ing, sems.at[1])]
    for move in moves:
        move.start()
    norm[...] = small[6, :D]
    heads[:, 0, :] = gw1[0:rows, :C]
    heads[:, 1, :] = gw0[0:rows, :]
    width = S // z.ntn
    tile[...] = jnp.zeros_like(tile)
    tile[0:rp, :] = gw2[0:rp, :]
    pair = jnp.transpose(tile[...])
    if z.ntn == 4:
        upper = lax.axis_index("tensor") >= 2
        pair = jnp.where(upper, pair[width:], pair[:width])
    shared[...] = pair[:, 0:rows]
    step[...] = gw2[rp : rp + H, 0:rows]
    Q = z.Q
    taps[...] = small[0 : z.K, Q : Q + C]
    bias[...] = small[4, Q : Q + C]
    staps[:, :Q] = small[0 : z.K, :Q]
    staps[:, Q:] = small[0 : z.K, Q + C : V]
    sbias[...] = jnp.concatenate([small[4:5, :Q], small[4:5, Q + C : V]], axis=1)[0]
    dsb[...] = small[7, :H]
    drate[...] = small[7, GROUP : GROUP + H]
    lanes = iota((1, H), 1)
    skip = jnp.zeros((1, H), F32)
    for h in range(H):
        begin = LANES + h * head
        skip = jnp.where(lanes == h, jnp.sum(small[7:8, begin : begin + head], axis=1, keepdims=True), skip)
    tile[0:1, 0:H] = skip
    dskip[...] = tile[0, 0:H]
    gain[...] = small[5, :C]
    outw[...] = gw1[0:rows, C:]
    for move in moves:
        move.wait()


def on_device(z, hidden_in, segment_ids, norm_gain, head_projection, shared_projection, step_projection,
              conv_heads, bias_heads, conv_shared, bias_shared, step_bias, log_decay, skip_gain, gate_gain,
              output_weight, out_cotangent):
    R, T, D, C, H, S = z.R, z.T, z.D, z.C, z.H, z.S
    rp, nd, nc, ntn, rows = z.rp, z.nd, z.nc, z.ntn, z.rows
    V = C + S
    blocks = nd * nc
    R8 = 8 * -(-R // 8)

    def widen(value):
        if rp == rows:
            return value
        value = value.reshape(value.shape[:-1] + (blocks, rows))
        value = jnp.pad(value, [(0, 0)] * (value.ndim - 1) + [(0, rp - rows)])
        return value.reshape(value.shape[:-2] + (D,))

    def narrow(value):
        if rp == rows:
            return value
        return value.reshape(value.shape[:-1] + (blocks, rp))[..., :rows].reshape(value.shape[:-1] + (z.d_true,))

    def taller(value, dim):
        if rp == rows:
            return value
        return jnp.pad(value, [(0, rp - rows if k == dim else 0) for k in range(value.ndim)])

    dma, vmem = pltpu.SemaphoreType.DMA, pltpu.VMEM
    N = R * T
    half = T // 2
    k0 = max(nd - 1, 1)
    ins = dict(
        hid=widen(hidden_in.reshape(N, z.d_true)), cot=widen(out_cotangent.reshape(N, z.d_true)),
        seg=segment_ids, ng=widen(norm_gain), hp=taller(head_projection, 0),
        shp=taller(shared_projection, 0), stp=taller(step_projection.T, 1), ow=taller(output_weight.T, 0),
        ch=conv_heads, bh=bias_heads, cs=conv_shared, bs=bias_shared, sb=step_bias[None],
        ld=log_decay[None], sk=skip_gain[None], gg=gate_gain,
    )
    outs = dict(
        out=jax.ShapeDtypeStruct((N, D), BF16),
        ing=jax.ShapeDtypeStruct((N, D), BF16),
        gw0=jax.ShapeDtypeStruct((rp, C), F32),
        gw1=jax.ShapeDtypeStruct((rp, 2 * C), F32),
        gw2=jax.ShapeDtypeStruct((rp + HALO, z.Q), F32),
        small=jax.ShapeDtypeStruct((8, z.WL), F32),
    )
    scratch = dict(
        hv=vmem((N, D), BF16), cv=vmem((N, D), BF16), ov=vmem((N, D), BF16), iv=vmem((N, D), BF16),
        wall=vmem((D, V + LANES + C), BF16), wo=vmem((D, C), BF16), wt=vmem((blocks, GROUP, LANES), F32),
        hcol=vmem((GROUP, LANES), F32), tile=vmem((LANES, LANES), F32), gain=vmem((8, D), F32), par=vmem((16, V), F32),
        segc=vmem((T, LANES), F32), segr=vmem((R8, T), F32), carried=vmem((R8, T), F32), closing=vmem((R8, T), F32),
        segb=vmem((R8, LANES), F32), sega=vmem((R8, LANES), F32),
        early=vmem((R * (z.K - 1) * HALO, R * HALO), BF16), late=vmem((R, (z.K - 1) * HALO, HALO), BF16),
        hfix=vmem((R * (z.K - 1) * HALO, V), F32), lfix=vmem(((z.K - 1) * HALO, V), F32),
        down=vmem((R, z.K - 1, T, T), BF16), up=vmem((R, z.K - 1, T, T), BF16), lower=vmem((T, T), BF16), upper=vmem((T, T), BF16),
        past=vmem((R, T, T), BF16), next=vmem((R, T, T), BF16),
        hh=vmem((R * HALO, D), BF16), nrmh=vmem((R * HALO, D), BF16),
        nrm=vmem((N, D), BF16), nrmt=vmem((D, N), BF16), cott=vmem((D, N), BF16),
        v=vmem((N, V), BF16), mix=vmem((N, V), BF16), slope=vmem((N, V), F32),
        pre=vmem((GROUP, N), F32), step=vmem((GROUP, N), F32), cols=vmem((N, LANES), F32), xt=vmem((N, C), BF16),
        runr=vmem((R, 8, T), F32), xs=vmem((N, C), BF16),
        fresh=vmem((R, LANES, C), F32), local=vmem((R, LANES, C), F32),
        ssend=vmem((R, LANES, C), BF16), sin=vmem((R, LANES, C), BF16),
        gsend=vmem((R, LANES, C), BF16), gin=vmem((R, LANES, C), BF16),
        scores=vmem((T, T), F32), dsc=vmem((T, T), F32), drow=vmem((R, GROUP, T), F32), tot=vmem((LANES, T), F32),
        ins=vmem((N, C), F32), ys=vmem((N, C), F32), ssd=vmem((N, C), F32), zv=vmem((N, C), BF16),
        gated=vmem((N, max(C, S)), F32), dy=vmem((N, C), F32),
        yg=vmem((N, C), BF16), wds=vmem((N, C), BF16),
        rms=vmem((N, LANES), F32), sums=vmem((ntn, R, 8, T), F32),
        as_=vmem((2, R, half, D), BF16), ar_=vmem((2, R, half, D), BF16),
        bs_=vmem((2, R, half, D), BF16), br_=vmem((2, R, half, D), BF16), keep=vmem((R, half, D), F32),
        ga0=vmem((D, C), BF16), ga1=vmem((D, 2 * C), BF16), ga2=vmem((blocks * (rp + HALO), z.Q), BF16),
        gy0=vmem((k0, nc * rp, C), BF16), gy1=vmem((k0, nc * rp, 2 * C), BF16), gy2=vmem((k0, nc * (rp + HALO), z.Q), BF16),
        gz0=vmem((nc * rp, C), BF16), gz1=vmem((nc * rp, 2 * C), BF16), gz2=vmem((nc * (rp + HALO), z.Q), BF16),
        gr0=vmem((nc, rp, C), BF16), gr1=vmem((nc, rp, 2 * C), BF16), gr2=vmem((nc, rp + HALO, z.Q), BF16),
        drun=vmem((N, LANES), F32), edge=vmem((R, EDGE, V), F32),
        dce=vmem((R, EDGE, V), F32), dcat=vmem((N, V + LANES + C), BF16),
        prod=vmem((T, 2 * C), F32), hacc=vmem((2 * GROUP, T), F32), gstep=vmem((HALO, D), F32),
        shs=vmem((D, z.Q), BF16), shr=vmem((D, z.Q), BF16), shk=vmem((D, z.Q), F32),
        ls=vmem((rp + HALO, z.Q), F32), lr=vmem((rp + HALO, z.Q), F32),
        sm=vmem((8, z.WL), F32), sa=vmem((blocks, 16, z.WL), BF16), sb2=vmem((ntn, 8, z.WL), F32),
        l_in=dma((2,)), l_out=dma((2, R)),
        wz_send=dma((PIECES, 2, nc, z.SUB)), wd_send=dma((PIECES, nc, nd, z.SUB)), w_recv=dma((PIECES, nd, nc, z.SUB)),
        wh_send=dma((nd,)), wh_recv=dma((nd,)),
        h_send=dma((R,)), h_recv=dma((R,)),
        s_send=dma((R,)), s_recv=dma((R,)), g_send=dma((R,)), g_recv=dma((R,)), e_send=dma((R,)), e_recv=dma((R,)),
        x_send=dma((R, ntn)), x_recv=dma((R, ntn)),
        a_send=dma((2, R)), a_recv=dma((2, R)), b_send=dma((2, R)), b_recv=dma((2, R)),
        c_send=dma((2, R)), c_recv=dma((2, R)),
        ry_send=dma((3, nc, k0)), ry_recv=dma((3, nc, k0)), rz_send=dma((3, nc)), rz_recv=dma((3, nc)),
        sh_send=dma((2,)), sh_recv=dma((2,)),
        st_send=dma((ntn,)), st_recv=dma((ntn,)), sa_send=dma((max(blocks - 1, 1),)), sa_recv=dma((blocks,)),
    )
    names = list(ins) + list(outs) + list(scratch)
    whole = pl.BlockSpec(memory_space=pltpu.VMEM)
    large = pl.BlockSpec(memory_space=pl.ANY)
    raw = pl.pallas_call(
        functools.partial(kernel, z, names),
        out_shape=list(outs.values()),
        in_specs=[large] * 2 + [whole] * (len(ins) - 2),
        out_specs=[large] * 2 + [whole] * (len(outs) - 2),
        scratch_shapes=list(scratch.values()),
        compiler_params=pltpu.CompilerParams(
            collective_id=0, has_side_effects=True, vmem_limit_bytes=z.limit
        ),
    )(*ins.values())

    shapes = [
        ((N, D), BF16), ((N, D), BF16), ((D,), F32), ((rows, 2, C), F32), ((S // ntn, rows), F32), ((H, rows), F32),
        ((z.K, C), F32), ((C,), F32), ((z.K, S), F32), ((S,), F32), ((H,), F32), ((H,), F32), ((H,), F32),
        ((C,), F32), ((rows, C), F32),
    ]
    outs = pl.pallas_call(
        functools.partial(finishing, z),
        out_shape=[jax.ShapeDtypeStruct(*shape) for shape in shapes],
        in_specs=[whole] * 6,
        out_specs=[large] * 2 + [whole] * (len(shapes) - 2),
        scratch_shapes=[vmem((LANES, LANES), F32), dma((2,))],
        compiler_params=pltpu.CompilerParams(vmem_limit_bytes=z.limit),
    )(*raw)
    (block_out, input_grad, norm, heads, shared, step, taps, bias, staps, sbias, dsb, drate, dskip, gain, outw) = outs
    return (
        narrow(block_out).reshape(hidden_in.shape),
        narrow(input_grad).reshape(hidden_in.shape),
        narrow(norm),
        heads, shared.T, step.T, taps, bias, staps, sbias, dsb, drate, dskip, gain, outw.T,
    )


def solution(mesh):
    nd, nc, ntn = (mesh.shape[name] for name in ("dp", "context", "tensor"))

    def body(*args):
        hidden, heads, shared = args[0], args[3], args[4]
        micro, seqs, tokens, width = hidden.shape
        rows = heads.shape[0]
        rp = -(-rows // 16) * 16
        inner = heads.shape[2]
        z = types.SimpleNamespace(
            R=micro * seqs, T=tokens, d_true=width, D=rp * nd * nc, rows=rows, rp=rp, nd=nd, nc=nc, ntn=ntn,
            C=inner, H=args[10].shape[0], S=shared.shape[1], K=args[6].shape[0],
            Q=shared.shape[1] // 2, limit=62 << 20,
            SUB=3 if rp % 48 == 0 else 1,
        )
        z.WL = max(inner + z.S, z.D, LANES + inner)
        return on_device(z, *args)

    return jax.shard_map(
        body,
        mesh=mesh,
        in_specs=(
            P(None, "dp", "context", None),
            P(None, "dp", None),
            P(),
            P(("dp", "context"), None, "tensor"),
            P(("dp", "context"), None),
            P(("dp", "context"), "tensor"),
            P(None, "tensor"),
            P("tensor"),
            P(),
            P(),
            P("tensor"),
            P("tensor"),
            P("tensor"),
            P("tensor"),
            P("tensor", ("dp", "context")),
            P(None, "dp", "context", None),
        ),
        out_specs=(
            P(None, "dp", "context", None),
            P(None, "dp", "context", None),
            P(),
            P(("dp", "context"), None, "tensor"),
            P(("dp", "context"), "tensor"),
            P(("dp", "context"), "tensor"),
            P(None, "tensor"),
            P("tensor"),
            P(),
            P(),
            P("tensor"),
            P("tensor"),
            P("tensor"),
            P("tensor"),
            P("tensor", ("dp", "context")),
        ),
        check_vma=False,
    )
```

```python
import functools
import types

import jax
import jax.numpy as jnp
from jax import lax
from jax.experimental import pallas as pl
from jax.experimental.pallas import tpu as pltpu
from jax.sharding import PartitionSpec as P

EPS = 1e-05
F32 = jnp.float32
BF16 = jnp.bfloat16
MESH = pl.DeviceIdType.MESH
LANES = 128
HALO = 16
EDGE = 8
PIECES = 4
WIDE = 256
GROUP = 8


def nn(a, b):
    return lax.dot_general(a, b, (((1,), (0,)), ((), ())), preferred_element_type=F32)


def nt(a, b):
    return lax.dot_general(a, b, (((1,), (1,)), ((), ())), preferred_element_type=F32)


def tn(a, b):
    return lax.dot_general(a, b, (((0,), (0,)), ((), ())), preferred_element_type=F32)


def pieces_of(value, count):
    pieces = []
    for _ in range(count):
        piece = value.astype(BF16)
        pieces.append(piece)
        value = value - piece.astype(F32)
    return pieces


def exact_rows(value, ones):
    pieces = [piece.astype(F32) for piece in pieces_of(value, 3)]
    stacked = jnp.concatenate(pieces + [jnp.zeros_like(value)], axis=0).astype(BF16)
    out = nn(stacked, ones)
    return out[0:8] + out[8:16] + out[16:24]


def exact_right(value, ones):
    return sum(nn(piece, ones) for piece in pieces_of(value, 2))


def sigmoid(value):
    return 0.5 * jnp.tanh(0.5 * value) + 0.5


def iota(shape, dim):
    return lax.broadcasted_iota(jnp.int32, shape, dim)


def kernel(z, names, *refs):
    m = types.SimpleNamespace(**dict(zip(names, refs)))
    R, T, D, C, H, S = z.R, z.T, z.D, z.C, z.H, z.S
    rp, nd, nc, ntn = z.rp, z.nd, z.nc, z.ntn
    pairs = H // 2
    head = C // H
    V = C + S
    Z = V + LANES
    Q = z.Q
    BX, CX = slice(0, Q), slice(Q + C, V)
    half = T // 2
    d, c, t = lax.axis_index("dp"), lax.axis_index("context"), lax.axis_index("tensor")
    odd = lax.rem(t, 2)
    across = t + 1 - 2 * odd
    far = lax.rem(t + 2, 4) if ntn == 4 else t

    def at_ctx(k):
        return lax.rem(c + k, nc)

    def at_dp(k):
        return lax.rem(d + k, nd)

    def at_ten(k):
        return lax.rem(t + k, ntn)

    def rows_at(place, size):
        return pl.ds(pl.multiple_of(place * size, 16), size)

    def block(dd, cc):
        return rows_at(dd * nc + cc, rp)

    def row(r):
        return rows_at(r, T)

    def lanes_at(place, size):
        return pl.ds(pl.multiple_of(place, LANES), size)

    def copy(src, dst, send, recv, dev):
        return pltpu.make_async_remote_copy(
            src_ref=src, dst_ref=dst, send_sem=send, recv_sem=recv, device_id=dev, device_id_type=MESH
        )

    def load(which):
        return pltpu.make_async_copy((m.hid, m.cot)[which], (m.hv, m.cv)[which], m.l_in.at[which])

    load(0).start()
    load(1).start()
    barrier = pltpu.get_barrier_semaphore()
    others = [(at_dp(k), at_ctx(j), t) for k in range(nd) for j in range(nc) if k or j]
    peers = list(others)
    peers += [(d, c, at_ten(k)) for k in range(1, ntn)]
    for peer in peers:
        pl.semaphore_signal(barrier, inc=1, device_id=peer, device_id_type=MESH)

    m.wall[block(d, c), Q : Q + C] = m.hp[:, 1, :]
    m.wall[block(d, c), lanes_at(odd * (Q + C), Q)] = jnp.where(odd == 0, m.shp[:, :Q], m.shp[:, Q:])
    m.wt[d * nc + c] = jnp.zeros((GROUP, LANES), F32)
    m.wt[d * nc + c, 0:H, 0:rp] = m.stp[...].astype(F32)
    pl.semaphore_wait(barrier, len(peers))

    def subs(p):
        return z.SUB if p == 0 else 1

    def slot(p, dd, cc, u):
        if p == 1:
            return m.wt.at[dd * nc + cc]
        if p == 3:
            return m.wo.at[block(dd, cc)]
        place, size = ((odd * Q, Q + C), None, (Z, C))[p]
        rows = rp // subs(p)
        return m.wall.at[rows_at((dd * nc + cc) * subs(p) + u, rows), lanes_at(place, size)]

    def w_ctx(p, u, s, right):
        cc, to = (c - s, c + 1) if right else (c + s, c - 1)
        here = slot(p, d, cc, u)
        return copy(here, here, m.wz_send.at[p, int(right), s, u], m.w_recv.at[p, d, cc, u], (d, to, t))

    def w_dp(p, u, cc, k):
        here = slot(p, d, cc, u)
        return copy(here, here, m.wd_send.at[p, cc, k, u], m.w_recv.at[p, d, cc, u], (at_dp(k), c, t))

    def w_arrived(p, u, dd, cc):
        there = slot(p, dd, cc, u)
        copy(there, there, m.wd_send.at[p, cc, 0, u], m.w_recv.at[p, dd, cc, u], (d, c, t)).wait_recv()

    def w_each(p, s, act):
        for u in range(subs(p)):
            if s < nc - 1:
                pl.when((c - s >= 0) & (c < nc - 1))(lambda: act(w_ctx(p, u, s, True)))
                pl.when((c + s < nc) & (c > 0))(lambda: act(w_ctx(p, u, s, False)))
            for k in range(1, nd):
                if s == 0:
                    act(w_dp(p, u, c, k))
                else:
                    pl.when(c - s >= 0)(lambda: act(w_dp(p, u, c - s, k)))
                    pl.when(c + s < nc)(lambda: act(w_dp(p, u, c + s, k)))

    def w_start(p):
        w_each(p, 0, lambda one: one.start())

    def w_step(p, s):
        for u in range(subs(p)):
            for right in (True, False):
                cc = c - s if right else c + s

                @pl.when((cc >= 0) & (cc < nc))
                def _():
                    w_arrived(p, u, d, cc)
                    if s < nc - 1:
                        pl.when(c < nc - 1 if right else c > 0)(lambda: w_ctx(p, u, s, right).start())
                    for k in range(1, nd):
                        w_dp(p, u, cc, k).start()

    def w_rest(p):
        for k in range(1, nd):
            for cc in range(nc):
                for u in range(subs(p)):
                    w_arrived(p, u, at_dp(k), cc)

    def w_sent(p):
        for s in range(nc):
            w_each(p, s, lambda one: one.wait_send())

    def half_rows(dd):
        return rows_at(dd, nc * rp)

    def half_copy(k):
        here = m.wall.at[half_rows(at_dp(k)), lanes_at(odd * (Q + C), Q)]
        return copy(here, here, m.wh_send.at[k], m.wh_recv.at[k], (d, c, across))

    def half_arrived(k):
        there = m.wall.at[half_rows(at_dp(k)), lanes_at((1 - odd) * (Q + C), Q)]
        copy(there, there, m.wh_send.at[k], m.wh_recv.at[k], (d, c, across)).wait_recv()

    def halo_copy(r):
        return copy(
            m.hv.at[pl.ds(pl.multiple_of(r * T + T - HALO, 16), HALO)],
            m.hh.at[rows_at(r, HALO)],
            m.h_send.at[r],
            m.h_recv.at[r],
            (d, c + 1, t),
        )

    w_start(0)
    w_start(1)
    load(0).wait()

    @pl.when(c < nc - 1)
    def _():
        for r in range(R):
            halo_copy(r).start()

    m.wall[block(d, c), Z:] = m.hp[:, 0, :]
    m.wo[block(d, c), :] = m.ow[...]

    m.par[0 : z.K, BX] = m.cs[:, :Q]
    m.par[0 : z.K, Q : Q + C] = m.ch[...]
    m.par[0 : z.K, CX] = m.cs[:, Q:]
    m.par[5:6, :S] = m.bs[...][None]
    m.par[4:5, BX] = m.par[5:6, :Q]
    m.par[4:5, Q : Q + C] = m.bh[...][None]
    m.par[4:5, CX] = m.par[5:6, Q:S]
    m.par[5:6, :C] = m.gg[...][None]
    for h in range(H):
        m.par[6:7, h * head : (h + 1) * head] = jnp.broadcast_to(m.sk[0:1, h : h + 1], (1, head))
    m.gain[0:1, :] = m.ng[...][None]
    m.tile[...] = jnp.zeros_like(m.tile)
    m.tile[0:1, 0:H] = m.sb[...]
    m.tile[1:2, 0:H] = -jnp.exp(m.ld[...])
    turned = jnp.transpose(m.tile[...])
    m.hcol[...] = turned[0:GROUP, :]
    bias_col, rate_col = m.hcol[:, 0:1], m.hcol[:, 1:2]
    gain_in = m.gain[0:1, :]

    def normalize(u):
        u = u.astype(F32)
        mean = jnp.sum(u * u, axis=-1, keepdims=True) * (1.0 / z.d_true)
        return (u * lax.rsqrt(mean + EPS)) * gain_in

    length = m.seg.shape[-1]
    begin = c * T
    seqs = m.seg.shape[1]

    def ids_at(place, size):
        place = pl.multiple_of(place, LANES)
        lines = [m.seg[r // seqs, r % seqs : r % seqs + 1, pl.ds(place, size)] for r in range(R)]
        return jnp.concatenate(lines + [jnp.zeros_like(lines[0])] * (-R % 8), axis=0).astype(F32)

    now = ids_at(begin, T)
    before = jnp.where(c == 0, -1.0, ids_at(jnp.maximum(begin - LANES, 0), LANES))
    behind = jnp.where(c == nc - 1, -2.0, ids_at(jnp.minimum(begin + T, length - LANES), LANES))
    m.segr[...] = now
    m.segb[...] = before
    m.sega[...] = behind
    m.carried[...] = (now == before[:, LANES - 1 : LANES]).astype(F32)
    m.closing[...] = (now == now[:, T - 1 : T]).astype(F32)
    m.tot[...] = jnp.zeros_like(m.tot)
    m.tot[0 : now.shape[0], :] = now
    m.segc[...] = jnp.transpose(m.tot[...])
    away = iota((T, T), 0) - iota((T, T), 1)
    m.lower[...] = (away >= 0).astype(BF16)
    m.upper[...] = (away <= 0).astype(BF16)
    for r in range(R):
        same = m.segc[:, r : r + 1] == m.segr[r : r + 1, :]
        m.past[r] = (same & (away >= 0)).astype(BF16)
        m.next[r] = (same & (away <= 0)).astype(BF16)
        for j in range(1, z.K):
            m.down[r, j - 1] = (same & (away == j)).astype(BF16)
            m.up[r, j - 1] = (same & (away == -j)).astype(BF16)

    @pl.when(c == 0)
    def _():
        m.hh[...] = jnp.zeros_like(m.hh)
        m.sin[...] = jnp.zeros_like(m.sin)

    @pl.when(c == nc - 1)
    def _():
        m.gin[...] = jnp.zeros_like(m.gin)
        m.dce[...] = jnp.zeros_like(m.dce)

    m.sm[...] = jnp.zeros_like(m.sm)
    m.hacc[...] = jnp.zeros_like(m.hacc)
    m.drow[...] = jnp.zeros_like(m.drow)
    m.gstep[...] = jnp.zeros_like(m.gstep)

    @pl.loop(0, R)
    def _(r):
        value = normalize(m.hv[row(r), :]).astype(BF16)
        m.nrm[row(r), :] = value
        m.nrmt[:, row(r)] = jnp.transpose(value)

    load(1).wait()

    @pl.loop(0, R)
    def _(r):
        m.cott[:, row(r)] = jnp.transpose(m.cv[row(r), :])

    reach = iota((HALO, HALO), 1) - HALO - iota((HALO, HALO), 0)
    ahead = iota((HALO, HALO), 1) + HALO - iota((HALO, HALO), 0)
    m.early[...] = jnp.zeros_like(m.early)
    for r in range(R):
        near = m.segc[0:HALO, r : r + 1] == m.segb[r : r + 1, LANES - HALO : LANES]
        late = m.segc[T - HALO : T, r : r + 1] == m.sega[r : r + 1, 0:HALO]
        for j in range(1, z.K):
            first = ((r * (z.K - 1)) + j - 1) * HALO
            m.early[first : first + HALO, r * HALO : (r + 1) * HALO] = (near & (reach == -j)).astype(BF16)
            m.late[r, (j - 1) * HALO : j * HALO, :] = (late & (ahead == j)).astype(BF16)

    w_step(0, 1)
    w_step(1, 1)
    w_start(2)

    @pl.when(c > 0)
    def _():
        for r in range(R):
            halo_copy(r).wait_recv()

    m.nrmh[...] = normalize(m.hh[...]).astype(BF16)
    for s in range(2, nc):
        w_step(0, s)
        w_step(1, s)
        if s == 2:
            w_start(3)
    half_copy(0).start()
    w_step(2, 1)
    w_rest(1)

    m.tile[...] = jnp.zeros_like(m.tile)
    for b in range(nd * nc):
        m.tile[0:GROUP, :] = m.wt[b]
        m.wall[b * rp : (b + 1) * rp, V:Z] = jnp.transpose(m.tile[...])[0:rp, :].astype(BF16)
    w_rest(0)
    for k in range(1, nd):
        half_copy(k).start()
    w_step(3, 1)
    if nc > 2:
        w_step(2, 2)

    low_lanes = iota((T, LANES), 1) < head
    lane = iota((T, LANES), 1)
    fold = (iota((C, LANES), 0) // head == iota((C, LANES), 1)).astype(F32)
    fold_run = fold.astype(BF16)
    fold_through = (
        (iota((C, LANES), 0) // head == iota((C, LANES), 1) - GROUP).astype(F32) - fold
    ).astype(BF16)
    fold_step = (iota((C, LANES), 0) // head == iota((C, LANES), 1) - 2 * GROUP).astype(BF16)
    RUN, STEP, LEAD, TRAIL = 0, GROUP, 2 * GROUP, 3 * GROUP

    def widened(values, base, p):
        a = base + 2 * p
        return jnp.where(low_lanes[: values.shape[0]], values[:, a : a + 1], values[:, a + 1 : a + 2])

    def spread(values, base):
        return jnp.concatenate([widened(values, base, p) for p in range(pairs)], axis=1)

    def state_copy(r):
        return copy(m.ssend.at[r], m.sin.at[r], m.s_send.at[r], m.s_recv.at[r], (d, c + 1, t))

    def grad_copy(r):
        return copy(m.gsend.at[r], m.gin.at[r], m.g_send.at[r], m.g_recv.at[r], (d, c - 1, t))

    def edge_copy(r):
        return copy(m.edge.at[r], m.dce.at[r], m.e_send.at[r], m.e_recv.at[r], (d, c - 1, t))

    def kept(r):
        return spread(m.cols[pl.ds(r * T + T - 1, 1), :], LEAD)

    def pair(p):
        return slice(p * LANES, (p + 1) * LANES)

    def lanes_of(p):
        return slice(Q + p * LANES, Q + (p + 1) * LANES)

    def serve_state(r):
        state_copy(r).wait_recv()

        @pl.when(c < nc - 1)
        def _():
            m.ssend[r] = (m.fresh[r] + kept(r) * m.sin[r].astype(F32)).astype(BF16)
            state_copy(r).start()

    def serve_grad(r):
        grad_copy(r).wait_recv()

        @pl.when(c > 0)
        def _():
            m.gsend[r] = (m.local[r] + kept(r) * m.gin[r].astype(F32)).astype(BF16)
            grad_copy(r).start()

    hops = nc - 1 - c
    soon = R == 4 and nc > 2
    if soon:
        state_late = (c > 2) | ((c == 2) & (nc > 3))
        grad_late = hops > 2
    else:
        state_late, grad_late = c > 0, hops > 0

    def state_point(place, r):
        if soon:
            for who, item in place:
                @pl.when((c == who) & r)
                def _():
                    serve_state(item)

    def grad_point(place, r):
        if soon:
            for who, item in place:
                @pl.when((hops == who) & r)
                def _():
                    serve_grad(item)

    for k in range(nd):
        half_arrived(k)
    halo_v = nn(m.nrmh[...], m.wall[:, :V]).astype(BF16)
    m.hfix[...] = nn(m.early[...], halo_v)

    @pl.loop(0, R)
    def _(r):
        acc = nn(m.nrm[row(r), :], m.wall[:, :Z])
        m.v[row(r), :] = acc[:, :V].astype(BF16)
        raw = jnp.transpose(acc[:, V:].astype(BF16).astype(F32))[0:GROUP]
        pre = raw + bias_col
        step = jnp.maximum(pre, 0.0) + jnp.log1p(jnp.exp(-jnp.abs(pre)))
        m.pre[:, row(r)] = pre
        m.step[:, row(r)] = step
        run = exact_rows(step * rate_col, m.upper[...])
        m.runr[r] = run
        m.tot[0:GROUP, :] = run
        m.tot[GROUP : 2 * GROUP, :] = step
        m.tot[2 * GROUP : 3 * GROUP, :] = jnp.exp(run) * m.carried[pl.ds(r, 1), :]
        m.tot[3 * GROUP : 4 * GROUP, :] = jnp.exp(run[:, T - 1 : T] - run) * m.closing[pl.ds(r, 1), :]
        m.cols[row(r), :] = jnp.transpose(m.tot[...])
        for a in range(0, V, WIDE):
            part = slice(a, min(a + WIDE, V))
            value = m.v[row(r), part]
            conv = value.astype(F32) * m.par[0:1, part] + m.par[4:5, part]
            first = jnp.zeros((EDGE, conv.shape[1]), F32)
            for j in range(1, z.K):
                tap = m.par[j : j + 1, part]
                conv = conv + nn(m.down[r, j - 1], value) * tap
                first = first + m.hfix[pl.ds((r * (z.K - 1) + j - 1) * HALO, EDGE), part] * tap
            conv = jnp.concatenate([conv[0:EDGE] + first, conv[EDGE:]], axis=0)
            logistic = sigmoid(conv)
            m.mix[row(r), part] = (conv * logistic).astype(BF16)
            m.slope[row(r), part] = logistic * (1.0 + conv * (1.0 - logistic))
        state_point([(1, 0)], r == 2)
        state_point([(1, 1)], r == 3)
        for p in range(pairs):
            scaled = m.mix[row(r), lanes_of(p)].astype(F32) * widened(m.cols[row(r), :], STEP, p)
            m.xs[row(r), pair(p)] = scaled.astype(BF16)
            m.xt[row(r), pair(p)] = (scaled * widened(m.cols[row(r), :], TRAIL, p)).astype(BF16)
        m.fresh[r] = tn(m.mix[row(r), BX], m.xt[row(r), :])

        @pl.when(c == 0)
        def _():
            m.ssend[r] = m.fresh[r].astype(BF16)
            state_copy(r).start()

        for s in range(2, nc):
            pl.when(r == min(s - 2, R - 1))(lambda: w_step(3, s))
        for s in range(3, nc):
            pl.when(r == min(s - 3, R - 1))(lambda: w_step(2, s))

    state_point([(2, 0)], True)

    @pl.loop(0, R)
    def _(r):
        b, cm = m.mix[row(r), BX], m.mix[row(r), CX]
        m.scores[...] = nt(cm, b) * m.past[r].astype(F32)
        for p in range(pairs):
            for a in range(0, T, LANES):
                rows, seen = slice(a, a + LANES), a + LANES
                here = pl.ds(pl.multiple_of(r * T, 16) + a, LANES)
                both = []
                for h in (2 * p, 2 * p + 1):
                    decay = jnp.exp(jnp.minimum(m.cols[here, h : h + 1] - m.runr[r, h : h + 1, :seen], 0.0))
                    weight = (decay * m.scores[rows, :seen]).astype(BF16)
                    both.append(nn(weight, m.xs[pl.ds(pl.multiple_of(r * T, 16), seen), pair(p)]))
                m.ins[here, pair(p)] = jnp.where(low_lanes[:LANES], both[0], both[1])
        state_point([(1, 2)], r == 0)
        state_point([(2, 1)], r == 2)

    state_point([(1, 3)], True)
    w_rest(2)
    w_rest(3)

    def sums_copy(r, k):
        return copy(
            m.sums.at[t, r], m.sums.at[t, r], m.x_send.at[r, k], m.x_recv.at[r, t], (d, c, at_ten(k))
        )

    def sums_arrived(r, who):
        copy(
            m.sums.at[who, r], m.sums.at[who, r], m.x_send.at[r, 0], m.x_recv.at[r, who], (d, c, t)
        ).wait_recv()

    def mine(r):
        return pl.ds(pl.multiple_of(r * T + odd * half, 16), half)

    def theirs(r):
        return pl.ds(pl.multiple_of(r * T + (1 - odd) * half, 16), half)

    def near_copy(a, r):
        return copy(m.as_.at[a, r], m.ar_.at[a, r], m.a_send.at[a, r], m.a_recv.at[a, r], (d, c, across))

    def far_copy(a, r):
        return copy(m.bs_.at[a, r], m.br_.at[a, r], m.b_send.at[a, r], m.b_recv.at[a, r], (d, c, far))

    def back_copy(a, r):
        out = (m.ov, m.iv)[a].at[mine(r)]
        return copy(out, out, m.c_send.at[a, r], m.c_recv.at[a, r], (d, c, across))

    def back_arrived(a, r):
        out = (m.ov, m.iv)[a].at[theirs(r)]
        copy(out, out, m.c_send.at[a, r], m.c_recv.at[a, r], (d, c, across)).wait_recv()

    def give(a, r, value):
        first, second = value[:half], value[half:]
        m.as_[a, r] = jnp.where(odd == 0, second, first).astype(BF16)
        near_copy(a, r).start()
        m.keep[r] = jnp.where(odd == 0, first, second)

    def chip_sum(a, r):
        near_copy(a, r).wait_recv()
        m.bs_[a, r] = (m.keep[r] + m.ar_[a, r].astype(F32)).astype(BF16)
        if ntn == 4:
            far_copy(a, r).start()

    def full_sum(a, r):
        total = m.bs_[a, r].astype(F32)
        if ntn == 4:
            far_copy(a, r).wait_recv()
            total = total + m.br_[a, r].astype(F32)
        return total

    def serve_late(r):
        if soon and nc > 3:
            pl.when((c > 2) | (r >= 2))(lambda: serve_state(r))
        else:
            serve_state(r)

    def gating(r):
        pl.when(state_late)(lambda: serve_late(r))
        cm = m.mix[row(r), CX]
        gate = nn(m.nrm[row(r), :], m.wall[:, Z:])
        m.zv[row(r), :] = gate.astype(BF16)
        m.dy[row(r), :] = nn(m.cv[row(r), :], m.wo[...])
        m.ys[row(r), :] = nn(cm, m.sin[r])
        squares = jnp.zeros((T, LANES), F32)
        inner = jnp.zeros((T, LANES), F32)
        for p in range(pairs):
            carried = m.ys[row(r), pair(p)] * widened(m.cols[row(r), :], LEAD, p)
            m.ys[row(r), pair(p)] = carried
            ssd = m.ins[row(r), pair(p)] + carried + m.par[6:7, pair(p)] * m.mix[row(r), lanes_of(p)].astype(F32)
            m.ssd[row(r), pair(p)] = ssd
            gate = m.zv[row(r), pair(p)].astype(F32)
            gated = ssd * (gate * sigmoid(gate))
            m.gated[row(r), pair(p)] = gated
            scaled = gated * m.par[5:6, pair(p)]
            m.yg[row(r), pair(p)] = scaled.astype(BF16)
            squares = squares + gated * gated
            inner = inner + scaled * m.dy[row(r), pair(p)]
        squares = jnp.sum(squares, axis=-1, keepdims=True)
        inner = jnp.sum(inner, axis=-1, keepdims=True)
        both = jnp.where(lane == 0, squares, jnp.where(lane == 1, inner, 0.0))
        m.sums[t, r] = jnp.transpose(both)[0:8, :]
        for k in range(1, ntn):
            sums_copy(r, k).start()
        give(0, r, nt(m.yg[row(r), :], m.wo[...]))

    def ungating(r):
        for k in range(1, ntn):
            sums_arrived(r, at_ten(k))
        total = m.sums[0, r]
        for who in range(1, ntn):
            total = total + m.sums[who, r]
        scale = lax.rsqrt(total[0:1] * (1.0 / (C * ntn)) + EPS)
        inner = total[1:2] * (1.0 / (C * ntn)) * scale * scale * scale
        m.tot[0:1, :] = scale
        m.tot[1:2, :] = inner
        columns = jnp.transpose(m.tot[...])
        m.rms[row(r), :] = columns
        scale = jnp.broadcast_to(columns[:, 0:1], (T, LANES))
        inner = jnp.broadcast_to(columns[:, 1:2], (T, LANES))
        for p in range(pairs):
            gated, dy, ssd = m.gated[row(r), pair(p)], m.dy[row(r), pair(p)], m.ssd[row(r), pair(p)]
            gate = m.zv[row(r), pair(p)].astype(F32)
            gain = m.par[5:6, pair(p)]
            normal = gated * scale
            m.sm[5:6, pair(p)] += jnp.sum(dy * normal, axis=0, keepdims=True)
            m.yg[row(r), pair(p)] = (normal * gain).astype(BF16)
            d_gated = scale * dy * gain - gated * inner
            logistic = sigmoid(gate)
            m.dcat[row(r), Z + p * LANES : Z + (p + 1) * LANES] = (
                d_gated * ssd * (logistic * (1.0 + gate * (1.0 - logistic)))
            ).astype(BF16)
            d_ssd = d_gated * (gate * logistic)
            m.ssd[row(r), pair(p)] = d_ssd
            m.wds[row(r), pair(p)] = (d_ssd * widened(m.cols[row(r), :], LEAD, p)).astype(BF16)
        m.local[r] = tn(m.mix[row(r), CX], m.wds[row(r), :])

        @pl.when(c == nc - 1)
        def _():
            m.gsend[r] = m.local[r].astype(BF16)
            if nc > 1:
                grad_copy(r).start()

    @pl.loop(0, R + 2)
    def _(i):
        pl.when(i < R)(lambda: gating(i))

        @pl.when(i >= 2)
        def _():
            ungating(i - 2)

        grad_point([(1, 0)], i == R + 1)

        @pl.when(i == R - 1)
        def _():
            pl.loop(0, R - 1)(lambda r: chip_sum(0, r))

        pl.when(i == R)(lambda: chip_sum(0, R - 1))

    gall, gyr, gzs, gzr = (m.ga0, m.ga1, m.ga2), (m.gy0, m.gy1, m.gy2), (m.gz0, m.gz1, m.gz2), (m.gr0, m.gr1, m.gr2)
    tall = (rp, rp, rp + HALO)

    def rs_dp(part, j, k):
        cc = at_ctx(j)
        return copy(
            gall[part].at[rows_at(at_dp(k) * nc + cc, tall[part])],
            gyr[part].at[k - 1, rows_at(cc, tall[part])],
            m.ry_send.at[part, j, k - 1],
            m.ry_recv.at[part, j, k - 1],
            (at_dp(k), c, t),
        )

    def rs_ctx(part, j):
        cc = at_ctx(j)
        return copy(
            gzs[part].at[rows_at(cc, tall[part])],
            gzr[part].at[c],
            m.rz_send.at[part, j],
            m.rz_recv.at[part, c],
            (d, cc, t),
        )

    def rs_arrived(part, cc):
        copy(gzr[part].at[cc], gzr[part].at[cc], m.rz_send.at[part, 0], m.rz_recv.at[part, cc], (d, c, t)).wait_recv()

    def rs_start(part):
        for j in list(range(1, nc)) + [0]:
            for k in range(1, nd):
                rs_dp(part, j, k).start()

    def rs_middle(part, j):
        cc = at_ctx(j)
        total = gall[part][rows_at(d * nc + cc, tall[part]), :].astype(F32)
        for k in range(1, nd):
            rs_dp(part, j, k).wait_recv()
            total = total + gyr[part][k - 1, rows_at(cc, tall[part]), :].astype(F32)
        own = j == 0

        def keep():
            gzr[part][c] = total.astype(BF16)

        def send():
            gzs[part][rows_at(cc, tall[part]), :] = total.astype(BF16)
            rs_ctx(part, j).start()

        if isinstance(j, int):
            keep() if own else send()
        else:
            pl.when(own)(keep)
            pl.when(jnp.logical_not(own))(send)

    def rs_end(part):
        for k in range(1, nc):
            rs_arrived(part, at_ctx(k))
        total = gzr[part][0].astype(F32)
        for cc in range(1, nc):
            total = total + gzr[part][cc].astype(F32)
        return total

    def rs_sent(part):
        for j in range(nc):
            for k in range(1, nd):
                rs_dp(part, j, k).wait_send()
            if j:
                rs_ctx(part, j).wait_send()

    m.ga1[:, C:] = nn(m.cott[...], m.yg[...]).astype(BF16)
    m.ga1[:, :C] = nn(m.nrmt[...], m.dcat[:, Z:]).astype(BF16)
    rs_start(1)
    grad_point([(1, 1), (1, 2), (2, 0)], True)

    @pl.loop(0, R)
    def _(r):
        b, cm = m.mix[row(r), BX], m.mix[row(r), CX]
        m.scores[...] = nt(b, cm) * m.next[r].astype(F32)
        start = pl.multiple_of(r * T, 16)
        for a in range(0, T, LANES):
            rows, here, after = slice(a, a + LANES), pl.ds(start + a, LANES), pl.ds(start + a, T - a)
            losses = jnp.zeros((LANES, LANES), F32)
            for p in range(pairs):
                ds_pair = m.ssd[after, pair(p)].astype(BF16)
                xs_pair = m.xs[here, pair(p)]
                both = []
                for h in (2 * p, 2 * p + 1):
                    pick = low_lanes[:LANES] if h % 2 == 0 else ~low_lanes[:LANES]
                    decay = jnp.exp(jnp.minimum(m.runr[r, h : h + 1, a:] - m.cols[here, h : h + 1], 0.0))
                    weight = decay * m.scores[rows, a:]
                    both.append(nn(weight.astype(BF16), ds_pair))
                    d_weight = nt(jnp.where(pick, xs_pair, jnp.zeros_like(xs_pair)), ds_pair)
                    flow = d_weight * weight
                    if h == 0:
                        m.dsc[rows, a:] = d_weight * decay
                    else:
                        m.dsc[rows, a:] += d_weight * decay
                    losses = jnp.where(lane[:LANES] == h, jnp.sum(flow, axis=1, keepdims=True), losses)
                    down = jnp.sum(flow, axis=0, keepdims=True)
                    if a == 0:
                        m.drow[r, h : h + 1, :] = down
                    else:
                        m.drow[r, h : h + 1, a:] += down
                m.ins[here, pair(p)] = jnp.where(low_lanes[:LANES], both[0], both[1])
            m.drun[here, :] = exact_right(m.ssd[here, :] * m.ys[here, :], fold_run) - losses
            d_scores = (m.dsc[rows, a:] * m.next[r, rows, a:].astype(F32)).astype(BF16)
            m.gated[here, :LANES] = nn(d_scores, m.mix[after, CX])
            d_after = tn(d_scores, m.mix[here, BX])
            if a == 0:
                m.gated[after, LANES:S] = d_after
            else:
                m.gated[after, LANES:S] += d_after

        grad_point([(1, 3), (2, 1)], r == 0)
        grad_point([(2, 2)], r == 1)
        grad_point([(2, 3)], r == 2)

    def final_out(r):
        value = m.hv[mine(r), :].astype(F32) + m.rms[mine(r), 0:1] * full_sum(0, r)
        m.ov[mine(r), :] = value.astype(BF16)
        back_copy(0, r).start()

    def adjoint(r):
        pl.when(grad_late)(lambda: serve_grad(r))
        b = m.mix[row(r), BX]
        grad = m.gin[r]
        for p in range(pairs):
            trailing = widened(m.cols[row(r), :], TRAIL, p)
            reach = nn(b, m.gin[r, :, pair(p)]) * trailing
            x = m.mix[row(r), lanes_of(p)].astype(F32)
            d_xs = m.ins[row(r), pair(p)] + reach
            d_ssd = m.ssd[row(r), pair(p)]
            m.prod[:, pair(p)] = m.xs[row(r), pair(p)].astype(F32) * reach
            m.prod[:, C + p * LANES : C + (p + 1) * LANES] = d_xs * x
            m.sm[7:8, LANES + p * LANES : 2 * LANES + p * LANES] += jnp.sum(d_ssd * x, axis=0, keepdims=True)
            m.dy[row(r), pair(p)] = (
                d_xs * widened(m.cols[row(r), :], STEP, p) + m.par[6:7, pair(p)] * d_ssd
            ) * m.slope[row(r), lanes_of(p)]
        m.gated[row(r), :Q] = (
            m.gated[row(r), :LANES] + nt(m.xt[row(r), :], grad)
        ) * m.slope[row(r), BX]
        m.gated[row(r), Q:S] = (
            m.gated[row(r), LANES:S] + nt(m.wds[row(r), :], m.sin[r])
        ) * m.slope[row(r), CX]

        @pl.when(c > 0)
        def _():
            first = pl.ds(pl.multiple_of(r * T, 16), EDGE)
            m.edge[r, :, BX] = m.gated[first, :Q]
            m.edge[r, :, Q : Q + C] = m.dy[first, :]
            m.edge[r, :, CX] = m.gated[first, Q:S]
            edge_copy(r).start()

        m.drun[row(r), :] += exact_right(m.prod[:, :C], fold_through) + exact_right(m.prod[:, C:], fold_step)
        joint = jnp.sum(grad.astype(F32) * m.sin[r].astype(F32), axis=0, keepdims=True)
        joint = exact_right(jnp.broadcast_to(joint, (8, C)), fold_run)[0:1]
        last = m.cols[pl.ds(r * T + T - 1, 1), :]
        kept_lanes = jnp.concatenate([last[:, LEAD : LEAD + H], jnp.zeros((1, LANES - H), F32)], axis=1)
        m.drun[pl.ds(r * T + T - 1, 1), :] += joint * kept_lanes
        turned = jnp.transpose(m.drun[row(r), :])
        through = jnp.sum(turned[GROUP : 2 * GROUP], axis=1, keepdims=True)
        d_run = turned[0:GROUP] + m.drow[r]
        d_run = d_run + jnp.where(iota((GROUP, T), 1) == T - 1, through, 0.0)
        d_growth = exact_rows(d_run, m.lower[...])
        d_step = turned[2 * GROUP : 3 * GROUP] + rate_col * d_growth
        d_pre = d_step * sigmoid(m.pre[:, row(r)])
        m.hacc[0:GROUP, :] += d_pre
        m.hacc[GROUP : 2 * GROUP, :] += m.step[:, row(r)] * d_growth * rate_col
        d_pre = jnp.where(iota((GROUP, T), 0) < H, d_pre, 0.0)
        m.gstep[...] += nn(jnp.concatenate([d_pre, jnp.zeros_like(d_pre)], axis=0).astype(BF16), m.nrm[row(r), :])
        m.tot[0:GROUP, :] = d_pre
        m.dcat[row(r), V:Z] = jnp.transpose(m.tot[...]).astype(BF16)

    def finish(r):
        @pl.when(c < nc - 1)
        def _():
            edge_copy(r).wait_recv()

        edge = m.dce[r]
        edge = jnp.concatenate([edge, jnp.zeros_like(edge)], axis=0).astype(BF16)
        m.lfix[...] = nn(m.late[r], edge)
        cuts = [(m.gated, 0, 0, Q), (m.gated, Q, Q + C, Q)]
        cuts += [(m.dy, a, Q + a, min(WIDE, C - a)) for a in range(0, C, WIDE)]
        for held, place, first, size in cuts:
            part = slice(first, first + size)
            d_conv = held[row(r), place : place + size]
            low = d_conv.astype(BF16)
            value = m.v[row(r), part].astype(F32)
            m.sm[4:5, part] += jnp.sum(d_conv, axis=0, keepdims=True)
            m.sm[0:1, part] += jnp.sum(d_conv * value, axis=0, keepdims=True)
            d_v = d_conv * m.par[0:1, part]
            for j in range(1, z.K):
                moved = nn(m.up[r, j - 1], low)
                moved = jnp.concatenate(
                    [moved[: T - HALO], moved[T - HALO :] + m.lfix[(j - 1) * HALO : j * HALO, part]], axis=0
                )
                d_v = d_v + moved * m.par[j : j + 1, part]
                m.sm[j : j + 1, part] += jnp.sum(moved * value, axis=0, keepdims=True)
            m.dcat[row(r), part] = d_v.astype(BF16)

    def finish_norm(r):
        value = nt(m.dcat[row(r), :], m.wall[...])
        give(1, r, value)
        u = m.hv[row(r), :].astype(F32)
        mean = jnp.sum(u * u, axis=-1, keepdims=True) * (1.0 / z.d_true)
        m.sm[6:7, :D] += jnp.sum(value * (u * lax.rsqrt(mean + EPS)), axis=0, keepdims=True)

    m.tot[...] = jnp.zeros_like(m.tot)

    def first_sums(j, upward):
        up = c + j < nc
        pl.when(up if upward else jnp.logical_not(up))(lambda: rs_middle(1, j))

    @pl.loop(0, R)
    def _(r):
        pl.when(r == 0)(lambda: final_out(0))
        adjoint(r)
        for j in range(1, min(nc, 3)):
            pl.when(r == min(2 * j - 2, R - 1))(lambda: first_sums(j, True))

    @pl.loop(0, R)
    def _(r):
        finish(r)
        pl.when(r == 0)(lambda: finish_norm(0))
        pl.when(r == min(1, R - 1))(lambda: chip_sum(1, 0))
        for k in range(1, R - 1):
            pl.when(r == min(2 * k - 1, R - 1))(lambda: final_out(k))
        for j in range(3, nc):
            pl.when(r == min(j - 1, R - 1))(lambda: first_sums(j, True))
        for j in range(1, nc):
            pl.when(r == min(j - 1, R - 1))(lambda: first_sums(j, False))

    def small_copy(index):
        return copy(m.sa.at[d * nc + c], m.sa.at[d * nc + c], m.sa_send.at[index], m.sa_recv.at[d * nc + c], others[index])

    def small_arrived(dd, cc):
        there = m.sa.at[dd * nc + cc]
        copy(there, there, m.sa_send.at[0], m.sa_recv.at[dd * nc + cc], (d, c, t)).wait_recv()

    def common_copy(k):
        return copy(m.sb2.at[t], m.sb2.at[t], m.st_send.at[k], m.st_recv.at[t], (d, c, at_ten(k)))

    def common_arrived(who):
        copy(m.sb2.at[who], m.sb2.at[who], m.st_send.at[0], m.st_recv.at[who], (d, c, t)).wait_recv()

    width = S // ntn
    starts = [k * width + (C if k * width >= Q else 0) for k in range(ntn)]
    quarters = [m.dcat[:, first : first + width] for first in starts]
    value = nn(m.nrmt[...], jnp.concatenate(quarters[0::2] + quarters[1::2], axis=1))

    def share_copy():
        return copy(m.shs, m.shr, m.sh_send.at[0], m.sh_recv.at[0], (d, c, across))

    m.shk[...] = jnp.where(odd == 0, value[:, : z.Q], value[:, z.Q :])
    m.shs[...] = jnp.where(odd == 0, value[:, z.Q :], value[:, : z.Q]).astype(BF16)
    share_copy().start()

    m.ga0[...] = nn(m.nrmt[...], m.dcat[:, Q : Q + C]).astype(BF16)
    share_copy().wait_recv()
    for b in range(nd * nc):
        here = slice(b * rp, (b + 1) * rp)
        there = b * (rp + HALO)
        m.ga2[there : there + rp, :] = (m.shk[here, :] + m.shr[here, :].astype(F32)).astype(BF16)
        steps = m.gstep[:, here]
        m.ga2[there + rp : there + rp + HALO, :] = jnp.concatenate(
            [steps, jnp.zeros((HALO, LANES - rp), F32)], axis=1
        ).astype(BF16)
    rs_start(2)
    rs_start(0)

    @pl.loop(1, R)
    def _(r):
        finish_norm(r)
        pl.when(r == min(2, R - 1))(lambda: final_out(R - 1))
        pl.when(r == 1)(lambda: rs_middle(1, 0))
        pl.when(r >= 2)(lambda: chip_sum(1, r - 1))

    m.tile[...] = jnp.zeros_like(m.tile)
    m.tile[0 : 2 * GROUP, :] = jnp.broadcast_to(
        jnp.sum(m.hacc[...], axis=1, keepdims=True), (2 * GROUP, LANES)
    )
    m.sm[7:8, 0:LANES] = jnp.transpose(m.tile[...])[0:1, :]
    m.sa[d * nc + c] = jnp.concatenate([m.sm[:, : z.WL // 2], m.sm[:, z.WL // 2 :]], axis=0).astype(BF16)
    for index in range(len(others)):
        small_copy(index).start()

    chip_sum(1, R - 1)

    def last_copy():
        return copy(m.ls, m.lr, m.sh_send.at[1], m.sh_recv.at[1], (d, c, far))

    def store(a, r):
        return pltpu.make_async_copy((m.ov, m.iv)[a].at[row(r)], (m.out, m.ing)[a].at[row(r)], m.l_out.at[a, r])

    def input_row(r):
        u = m.hv[mine(r), :].astype(F32)
        mean = jnp.sum(u * u, axis=-1, keepdims=True) * (1.0 / z.d_true)
        scale = lax.rsqrt(mean + EPS)
        unit = u * scale
        d_unit = full_sum(1, r) * gain_in
        inner = jnp.sum(d_unit * unit, axis=-1, keepdims=True) * (1.0 / z.d_true)
        value = m.cv[mine(r), :].astype(F32) + scale * (d_unit - unit * inner)
        m.iv[mine(r), :] = value.astype(BF16)
        back_copy(1, r).start()

    for r in range(R):
        back_arrived(0, r)
        store(0, r).start()
    for j in list(range(1, nc)) + [0]:
        rs_middle(2, j)
    m.gw1[...] = rs_end(1)

    @pl.loop(0, R)
    def _(r):
        input_row(r)
        pl.when(r >= 1)(lambda: back_arrived(1, r - 1))
        pl.when(r >= 1)(lambda: store(1, r - 1).start())

        @pl.when(r == 0)
        def _():
            rs_middle(0, 1 % nc)

        @pl.when(r == min(2, R - 1))
        def _():
            for dd in range(nd):
                for cc in range(nc):
                    pl.when((dd != d) | (cc != c))(lambda: small_arrived(dd, cc))
            total = m.sa[0].astype(F32)
            for who in range(1, nd * nc):
                total = total + m.sa[who].astype(F32)
            m.sb2[t] = jnp.concatenate([total[0:8], total[8:16]], axis=1)
            for k in range(1, ntn):
                common_copy(k).start()

        @pl.when(r == 1)
        def _():
            for j in list(range(2, nc)) + ([0] if nc > 1 else []):
                rs_middle(0, j)

        @pl.when(r == min(2, R - 1))
        def _():
            value = rs_end(2)
            if ntn == 4:
                m.ls[...] = value
                last_copy().start()
            else:
                m.gw2[...] = value

    for k in range(1, ntn):
        common_arrived(at_ten(k))
    common = m.sb2[0]
    for who in range(1, ntn):
        common = common + m.sb2[who]
    rows8, lanes8 = iota((8, z.WL), 0), iota((8, z.WL), 1)
    shared_here = (rows8 == 6) | ((rows8 < 5) & ((lanes8 < Q) | (lanes8 >= Q + C)))
    m.small[...] = jnp.where(shared_here, common, m.sb2[t])
    m.gw0[...] = rs_end(0)
    if ntn == 4:
        last_copy().wait_recv()
        m.gw2[0:rp, :] = m.ls[0:rp, :] + m.lr[0:rp, :]
        m.gw2[rp:, :] = m.ls[rp:, :]
        last_copy().wait_send()
    back_arrived(1, R - 1)
    store(1, R - 1).start()

    for a in range(2):
        for r in range(R):
            store(a, r).wait()
            back_copy(a, r).wait_send()
            near_copy(a, r).wait_send()
            if ntn == 4:
                far_copy(a, r).wait_send()
    for p in range(PIECES):
        w_sent(p)
    for k in range(nd):
        half_copy(k).wait_send()
    for part in range(3):
        rs_sent(part)
    for r in range(R):
        for k in range(1, ntn):
            sums_copy(r, k).wait_send()

        @pl.when(c < nc - 1)
        def _():
            halo_copy(r).wait_send()
            state_copy(r).wait_send()

        @pl.when(c > 0)
        def _():
            grad_copy(r).wait_send()
            edge_copy(r).wait_send()

    share_copy().wait_send()
    for index in range(len(others)):
        small_copy(index).wait_send()
    for k in range(1, ntn):
        common_copy(k).wait_send()


def finishing(z, out, ing, gw0, gw1, gw2, small, *outs):
    (o_out, o_ing, norm, heads, shared, step, taps, bias, staps, sbias, dsb, drate, dskip, gain, outw, tile, sems) = outs
    C, S, D, H, rp, rows = z.C, z.S, z.D, z.H, z.rp, z.rows
    V = C + S
    head = C // H
    moves = [pltpu.make_async_copy(out, o_out, sems.at[0]), pltpu.make_async_copy(ing, o_ing, sems.at[1])]
    for move in moves:
        move.start()
    norm[...] = small[6, :D]
    heads[:, 0, :] = gw1[0:rows, :C]
    heads[:, 1, :] = gw0[0:rows, :]
    width = S // z.ntn
    tile[...] = jnp.zeros_like(tile)
    tile[0:rp, :] = gw2[0:rp, :]
    pair = jnp.transpose(tile[...])
    if z.ntn == 4:
        upper = lax.axis_index("tensor") >= 2
        pair = jnp.where(upper, pair[width:], pair[:width])
    shared[...] = pair[:, 0:rows]
    step[...] = gw2[rp : rp + H, 0:rows]
    Q = z.Q
    taps[...] = small[0 : z.K, Q : Q + C]
    bias[...] = small[4, Q : Q + C]
    staps[:, :Q] = small[0 : z.K, :Q]
    staps[:, Q:] = small[0 : z.K, Q + C : V]
    sbias[...] = jnp.concatenate([small[4:5, :Q], small[4:5, Q + C : V]], axis=1)[0]
    dsb[...] = small[7, :H]
    drate[...] = small[7, GROUP : GROUP + H]
    lanes = iota((1, H), 1)
    skip = jnp.zeros((1, H), F32)
    for h in range(H):
        begin = LANES + h * head
        skip = jnp.where(lanes == h, jnp.sum(small[7:8, begin : begin + head], axis=1, keepdims=True), skip)
    tile[0:1, 0:H] = skip
    dskip[...] = tile[0, 0:H]
    gain[...] = small[5, :C]
    outw[...] = gw1[0:rows, C:]
    for move in moves:
        move.wait()


def on_device(z, hidden_in, segment_ids, norm_gain, head_projection, shared_projection, step_projection,
              conv_heads, bias_heads, conv_shared, bias_shared, step_bias, log_decay, skip_gain, gate_gain,
              output_weight, out_cotangent):
    R, T, D, C, H, S = z.R, z.T, z.D, z.C, z.H, z.S
    rp, nd, nc, ntn, rows = z.rp, z.nd, z.nc, z.ntn, z.rows
    V = C + S
    blocks = nd * nc
    R8 = 8 * -(-R // 8)

    def widen(value):
        if rp == rows:
            return value
        value = value.reshape(value.shape[:-1] + (blocks, rows))
        value = jnp.pad(value, [(0, 0)] * (value.ndim - 1) + [(0, rp - rows)])
        return value.reshape(value.shape[:-2] + (D,))

    def narrow(value):
        if rp == rows:
            return value
        return value.reshape(value.shape[:-1] + (blocks, rp))[..., :rows].reshape(value.shape[:-1] + (z.d_true,))

    def taller(value, dim):
        if rp == rows:
            return value
        return jnp.pad(value, [(0, rp - rows if k == dim else 0) for k in range(value.ndim)])

    dma, vmem = pltpu.SemaphoreType.DMA, pltpu.VMEM
    N = R * T
    half = T // 2
    k0 = max(nd - 1, 1)
    ins = dict(
        hid=widen(hidden_in.reshape(N, z.d_true)), cot=widen(out_cotangent.reshape(N, z.d_true)),
        seg=segment_ids, ng=widen(norm_gain), hp=taller(head_projection, 0),
        shp=taller(shared_projection, 0), stp=taller(step_projection.T, 1), ow=taller(output_weight.T, 0),
        ch=conv_heads, bh=bias_heads, cs=conv_shared, bs=bias_shared, sb=step_bias[None],
        ld=log_decay[None], sk=skip_gain[None], gg=gate_gain,
    )
    outs = dict(
        out=jax.ShapeDtypeStruct((N, D), BF16),
        ing=jax.ShapeDtypeStruct((N, D), BF16),
        gw0=jax.ShapeDtypeStruct((rp, C), F32),
        gw1=jax.ShapeDtypeStruct((rp, 2 * C), F32),
        gw2=jax.ShapeDtypeStruct((rp + HALO, z.Q), F32),
        small=jax.ShapeDtypeStruct((8, z.WL), F32),
    )
    scratch = dict(
        hv=vmem((N, D), BF16), cv=vmem((N, D), BF16), ov=vmem((N, D), BF16), iv=vmem((N, D), BF16),
        wall=vmem((D, V + LANES + C), BF16), wo=vmem((D, C), BF16), wt=vmem((blocks, GROUP, LANES), F32),
        hcol=vmem((GROUP, LANES), F32), tile=vmem((LANES, LANES), F32), gain=vmem((8, D), F32), par=vmem((16, V), F32),
        segc=vmem((T, LANES), F32), segr=vmem((R8, T), F32), carried=vmem((R8, T), F32), closing=vmem((R8, T), F32),
        segb=vmem((R8, LANES), F32), sega=vmem((R8, LANES), F32),
        early=vmem((R * (z.K - 1) * HALO, R * HALO), BF16), late=vmem((R, (z.K - 1) * HALO, HALO), BF16),
        hfix=vmem((R * (z.K - 1) * HALO, V), F32), lfix=vmem(((z.K - 1) * HALO, V), F32),
        down=vmem((R, z.K - 1, T, T), BF16), up=vmem((R, z.K - 1, T, T), BF16), lower=vmem((T, T), BF16), upper=vmem((T, T), BF16),
        past=vmem((R, T, T), BF16), next=vmem((R, T, T), BF16),
        hh=vmem((R * HALO, D), BF16), nrmh=vmem((R * HALO, D), BF16),
        nrm=vmem((N, D), BF16), nrmt=vmem((D, N), BF16), cott=vmem((D, N), BF16),
        v=vmem((N, V), BF16), mix=vmem((N, V), BF16), slope=vmem((N, V), F32),
        pre=vmem((GROUP, N), F32), step=vmem((GROUP, N), F32), cols=vmem((N, LANES), F32), xt=vmem((N, C), BF16),
        runr=vmem((R, 8, T), F32), xs=vmem((N, C), BF16),
        fresh=vmem((R, LANES, C), F32), local=vmem((R, LANES, C), F32),
        ssend=vmem((R, LANES, C), BF16), sin=vmem((R, LANES, C), BF16),
        gsend=vmem((R, LANES, C), BF16), gin=vmem((R, LANES, C), BF16),
        scores=vmem((T, T), F32), dsc=vmem((T, T), F32), drow=vmem((R, GROUP, T), F32), tot=vmem((LANES, T), F32),
        ins=vmem((N, C), F32), ys=vmem((N, C), F32), ssd=vmem((N, C), F32), zv=vmem((N, C), BF16),
        gated=vmem((N, max(C, S)), F32), dy=vmem((N, C), F32),
        yg=vmem((N, C), BF16), wds=vmem((N, C), BF16),
        rms=vmem((N, LANES), F32), sums=vmem((ntn, R, 8, T), F32),
        as_=vmem((2, R, half, D), BF16), ar_=vmem((2, R, half, D), BF16),
        bs_=vmem((2, R, half, D), BF16), br_=vmem((2, R, half, D), BF16), keep=vmem((R, half, D), F32),
        ga0=vmem((D, C), BF16), ga1=vmem((D, 2 * C), BF16), ga2=vmem((blocks * (rp + HALO), z.Q), BF16),
        gy0=vmem((k0, nc * rp, C), BF16), gy1=vmem((k0, nc * rp, 2 * C), BF16), gy2=vmem((k0, nc * (rp + HALO), z.Q), BF16),
        gz0=vmem((nc * rp, C), BF16), gz1=vmem((nc * rp, 2 * C), BF16), gz2=vmem((nc * (rp + HALO), z.Q), BF16),
        gr0=vmem((nc, rp, C), BF16), gr1=vmem((nc, rp, 2 * C), BF16), gr2=vmem((nc, rp + HALO, z.Q), BF16),
        drun=vmem((N, LANES), F32), edge=vmem((R, EDGE, V), F32),
        dce=vmem((R, EDGE, V), F32), dcat=vmem((N, V + LANES + C), BF16),
        prod=vmem((T, 2 * C), F32), hacc=vmem((2 * GROUP, T), F32), gstep=vmem((HALO, D), F32),
        shs=vmem((D, z.Q), BF16), shr=vmem((D, z.Q), BF16), shk=vmem((D, z.Q), F32),
        ls=vmem((rp + HALO, z.Q), F32), lr=vmem((rp + HALO, z.Q), F32),
        sm=vmem((8, z.WL), F32), sa=vmem((blocks, 16, z.WL // 2), BF16), sb2=vmem((ntn, 8, z.WL), F32),
        l_in=dma((2,)), l_out=dma((2, R)),
        wz_send=dma((PIECES, 2, nc, z.SUB)), wd_send=dma((PIECES, nc, nd, z.SUB)), w_recv=dma((PIECES, nd, nc, z.SUB)),
        wh_send=dma((nd,)), wh_recv=dma((nd,)),
        h_send=dma((R,)), h_recv=dma((R,)),
        s_send=dma((R,)), s_recv=dma((R,)), g_send=dma((R,)), g_recv=dma((R,)), e_send=dma((R,)), e_recv=dma((R,)),
        x_send=dma((R, ntn)), x_recv=dma((R, ntn)),
        a_send=dma((2, R)), a_recv=dma((2, R)), b_send=dma((2, R)), b_recv=dma((2, R)),
        c_send=dma((2, R)), c_recv=dma((2, R)),
        ry_send=dma((3, nc, k0)), ry_recv=dma((3, nc, k0)), rz_send=dma((3, nc)), rz_recv=dma((3, nc)),
        sh_send=dma((2,)), sh_recv=dma((2,)),
        st_send=dma((ntn,)), st_recv=dma((ntn,)), sa_send=dma((max(blocks - 1, 1),)), sa_recv=dma((blocks,)),
    )
    names = list(ins) + list(outs) + list(scratch)
    whole = pl.BlockSpec(memory_space=pltpu.VMEM)
    large = pl.BlockSpec(memory_space=pl.ANY)
    raw = pl.pallas_call(
        functools.partial(kernel, z, names),
        out_shape=list(outs.values()),
        in_specs=[large] * 2 + [whole] * (len(ins) - 2),
        out_specs=[large] * 2 + [whole] * (len(outs) - 2),
        scratch_shapes=list(scratch.values()),
        compiler_params=pltpu.CompilerParams(
            collective_id=0, has_side_effects=True, vmem_limit_bytes=z.limit
        ),
    )(*ins.values())

    shapes = [
        ((N, D), BF16), ((N, D), BF16), ((D,), F32), ((rows, 2, C), F32), ((S // ntn, rows), F32), ((H, rows), F32),
        ((z.K, C), F32), ((C,), F32), ((z.K, S), F32), ((S,), F32), ((H,), F32), ((H,), F32), ((H,), F32),
        ((C,), F32), ((rows, C), F32),
    ]
    outs = pl.pallas_call(
        functools.partial(finishing, z),
        out_shape=[jax.ShapeDtypeStruct(*shape) for shape in shapes],
        in_specs=[whole] * 6,
        out_specs=[large] * 2 + [whole] * (len(shapes) - 2),
        scratch_shapes=[vmem((LANES, LANES), F32), dma((2,))],
        compiler_params=pltpu.CompilerParams(vmem_limit_bytes=z.limit),
    )(*raw)
    (block_out, input_grad, norm, heads, shared, step, taps, bias, staps, sbias, dsb, drate, dskip, gain, outw) = outs
    return (
        narrow(block_out).reshape(hidden_in.shape),
        narrow(input_grad).reshape(hidden_in.shape),
        narrow(norm),
        heads, shared.T, step.T, taps, bias, staps, sbias, dsb, drate, dskip, gain, outw.T,
    )


def solution(mesh):
    nd, nc, ntn = (mesh.shape[name] for name in ("dp", "context", "tensor"))

    def body(*args):
        hidden, heads, shared = args[0], args[3], args[4]
        micro, seqs, tokens, width = hidden.shape
        rows = heads.shape[0]
        rp = -(-rows // 16) * 16
        inner = heads.shape[2]
        z = types.SimpleNamespace(
            R=micro * seqs, T=tokens, d_true=width, D=rp * nd * nc, rows=rows, rp=rp, nd=nd, nc=nc, ntn=ntn,
            C=inner, H=args[10].shape[0], S=shared.shape[1], K=args[6].shape[0],
            Q=shared.shape[1] // 2, limit=62 << 20,
            SUB=3 if rp % 48 == 0 else 1,
        )
        z.WL = max(inner + z.S, z.D, LANES + inner)
        return on_device(z, *args)

    return jax.shard_map(
        body,
        mesh=mesh,
        in_specs=(
            P(None, "dp", "context", None),
            P(None, "dp", None),
            P(),
            P(("dp", "context"), None, "tensor"),
            P(("dp", "context"), None),
            P(("dp", "context"), "tensor"),
            P(None, "tensor"),
            P("tensor"),
            P(),
            P(),
            P("tensor"),
            P("tensor"),
            P("tensor"),
            P("tensor"),
            P("tensor", ("dp", "context")),
            P(None, "dp", "context", None),
        ),
        out_specs=(
            P(None, "dp", "context", None),
            P(None, "dp", "context", None),
            P(),
            P(("dp", "context"), None, "tensor"),
            P(("dp", "context"), "tensor"),
            P(("dp", "context"), "tensor"),
            P(None, "tensor"),
            P("tensor"),
            P(),
            P(),
            P("tensor"),
            P("tensor"),
            P("tensor"),
            P("tensor"),
            P("tensor", ("dp", "context")),
        ),
        check_vma=False,
    )
```

```python
import functools
import types

import jax
import jax.numpy as jnp
from jax import lax
from jax.experimental import pallas as pl
from jax.experimental.pallas import tpu as pltpu
from jax.sharding import PartitionSpec as P

EPS = 1e-05
F32 = jnp.float32
BF16 = jnp.bfloat16
MESH = pl.DeviceIdType.MESH
LANES = 128
HALO = 16
EDGE = 8
PIECES = 4
WIDE = 256
GROUP = 8


def nn(a, b):
    return lax.dot_general(a, b, (((1,), (0,)), ((), ())), preferred_element_type=F32)


def nt(a, b):
    return lax.dot_general(a, b, (((1,), (1,)), ((), ())), preferred_element_type=F32)


def tn(a, b):
    return lax.dot_general(a, b, (((0,), (0,)), ((), ())), preferred_element_type=F32)


def pieces_of(value, count):
    pieces = []
    for _ in range(count):
        piece = value.astype(BF16)
        pieces.append(piece)
        value = value - piece.astype(F32)
    return pieces


def exact_rows(value, ones):
    pieces = [piece.astype(F32) for piece in pieces_of(value, 3)]
    stacked = jnp.concatenate(pieces + [jnp.zeros_like(value)], axis=0).astype(BF16)
    out = nn(stacked, ones)
    return out[0:8] + out[8:16] + out[16:24]


def exact_right(value, ones):
    return sum(nn(piece, ones) for piece in pieces_of(value, 2))


def sigmoid(value):
    return 0.5 * jnp.tanh(0.5 * value) + 0.5


def iota(shape, dim):
    return lax.broadcasted_iota(jnp.int32, shape, dim)


def kernel(z, names, *refs):
    m = types.SimpleNamespace(**dict(zip(names, refs)))
    R, T, D, C, H, S = z.R, z.T, z.D, z.C, z.H, z.S
    rp, nd, nc, ntn = z.rp, z.nd, z.nc, z.ntn
    pairs = H // 2
    head = C // H
    V = C + S
    Z = V + LANES
    Q = z.Q
    BX, CX = slice(0, Q), slice(Q + C, V)
    half = T // 2
    d, c, t = lax.axis_index("dp"), lax.axis_index("context"), lax.axis_index("tensor")
    odd = lax.rem(t, 2)
    across = t + 1 - 2 * odd
    far = lax.rem(t + 2, 4) if ntn == 4 else t

    def at_ctx(k):
        return lax.rem(c + k, nc)

    def at_dp(k):
        return lax.rem(d + k, nd)

    def at_ten(k):
        return lax.rem(t + k, ntn)

    def rows_at(place, size):
        return pl.ds(pl.multiple_of(place * size, 16), size)

    def block(dd, cc):
        return rows_at(dd * nc + cc, rp)

    def row(r):
        return rows_at(r, T)

    def lanes_at(place, size):
        return pl.ds(pl.multiple_of(place, LANES), size)

    def copy(src, dst, send, recv, dev):
        return pltpu.make_async_remote_copy(
            src_ref=src, dst_ref=dst, send_sem=send, recv_sem=recv, device_id=dev, device_id_type=MESH
        )

    def load(which):
        return pltpu.make_async_copy((m.hid, m.cot)[which], (m.hv, m.cv)[which], m.l_in.at[which])

    load(0).start()
    load(1).start()
    barrier = pltpu.get_barrier_semaphore()
    others = [(at_dp(k), at_ctx(j), t) for k in range(nd) for j in range(nc) if k or j]
    peers = [(at_dp(k), c, t) for k in range(1, nd)]
    peers += [(d, c, at_ten(k)) for k in range(1, ntn)]
    for peer in peers:
        pl.semaphore_signal(barrier, inc=1, device_id=peer, device_id_type=MESH)
    for here, step in ((c > 0, -1), (c < nc - 1, 1)):

        @pl.when(here)
        def _():
            pl.semaphore_signal(barrier, inc=1, device_id=(d, c + step, t), device_id_type=MESH)


    m.wall[block(d, c), Q : Q + C] = m.hp[:, 1, :]
    m.wall[block(d, c), lanes_at(odd * (Q + C), Q)] = jnp.where(odd == 0, m.shp[:, :Q], m.shp[:, Q:])
    m.wt[d * nc + c] = jnp.zeros((GROUP, LANES), F32)
    m.wt[d * nc + c, 0:H, 0:rp] = m.stp[...].astype(F32)
    pl.semaphore_wait(barrier, len(peers) + (c > 0).astype(jnp.int32) + (c < nc - 1).astype(jnp.int32))

    def subs(p):
        return z.SUB if p == 0 else 1

    def slot(p, dd, cc, u):
        if p == 1:
            return m.wt.at[dd * nc + cc]
        if p == 3:
            return m.wo.at[block(dd, cc)]
        place, size = ((odd * Q, Q + C), None, (Z, C))[p]
        rows = rp // subs(p)
        return m.wall.at[rows_at((dd * nc + cc) * subs(p) + u, rows), lanes_at(place, size)]

    def w_ctx(p, u, s, right):
        cc, to = (c - s, c + 1) if right else (c + s, c - 1)
        here = slot(p, d, cc, u)
        return copy(here, here, m.wz_send.at[p, int(right), s, u], m.w_recv.at[p, d, cc, u], (d, to, t))

    def w_dp(p, u, cc, k):
        here = slot(p, d, cc, u)
        return copy(here, here, m.wd_send.at[p, cc, k, u], m.w_recv.at[p, d, cc, u], (at_dp(k), c, t))

    def w_arrived(p, u, dd, cc):
        there = slot(p, dd, cc, u)
        copy(there, there, m.wd_send.at[p, cc, 0, u], m.w_recv.at[p, dd, cc, u], (d, c, t)).wait_recv()

    def w_each(p, s, act):
        for u in range(subs(p)):
            if s < nc - 1:
                pl.when((c - s >= 0) & (c < nc - 1))(lambda: act(w_ctx(p, u, s, True)))
                pl.when((c + s < nc) & (c > 0))(lambda: act(w_ctx(p, u, s, False)))
            for k in range(1, nd):
                if s == 0:
                    act(w_dp(p, u, c, k))
                else:
                    pl.when(c - s >= 0)(lambda: act(w_dp(p, u, c - s, k)))
                    pl.when(c + s < nc)(lambda: act(w_dp(p, u, c + s, k)))

    def w_start(p):
        w_each(p, 0, lambda one: one.start())

    def w_step(p, s):
        for u in range(subs(p)):
            for right in (True, False):
                cc = c - s if right else c + s

                @pl.when((cc >= 0) & (cc < nc))
                def _():
                    w_arrived(p, u, d, cc)
                    if s < nc - 1:
                        pl.when(c < nc - 1 if right else c > 0)(lambda: w_ctx(p, u, s, right).start())
                    for k in range(1, nd):
                        w_dp(p, u, cc, k).start()

    def w_rest(p):
        for k in range(1, nd):
            for cc in range(nc):
                for u in range(subs(p)):
                    w_arrived(p, u, at_dp(k), cc)

    def w_sent(p):
        for s in range(nc):
            w_each(p, s, lambda one: one.wait_send())

    def half_rows(dd):
        return rows_at(dd, nc * rp)

    def half_copy(k):
        here = m.wall.at[half_rows(at_dp(k)), lanes_at(odd * (Q + C), Q)]
        return copy(here, here, m.wh_send.at[k], m.wh_recv.at[k], (d, c, across))

    def half_arrived(k):
        there = m.wall.at[half_rows(at_dp(k)), lanes_at((1 - odd) * (Q + C), Q)]
        copy(there, there, m.wh_send.at[k], m.wh_recv.at[k], (d, c, across)).wait_recv()

    def halo_copy(r):
        return copy(
            m.hv.at[pl.ds(pl.multiple_of(r * T + T - HALO, 16), HALO)],
            m.hh.at[rows_at(r, HALO)],
            m.h_send.at[r],
            m.h_recv.at[r],
            (d, c + 1, t),
        )

    w_start(0)
    w_start(1)
    load(0).wait()

    @pl.when(c < nc - 1)
    def _():
        for r in range(R):
            halo_copy(r).start()

    m.wall[block(d, c), Z:] = m.hp[:, 0, :]
    m.wo[block(d, c), :] = m.ow[...]

    m.par[0 : z.K, BX] = m.cs[:, :Q]
    m.par[0 : z.K, Q : Q + C] = m.ch[...]
    m.par[0 : z.K, CX] = m.cs[:, Q:]
    m.par[5:6, :S] = m.bs[...][None]
    m.par[4:5, BX] = m.par[5:6, :Q]
    m.par[4:5, Q : Q + C] = m.bh[...][None]
    m.par[4:5, CX] = m.par[5:6, Q:S]
    m.par[5:6, :C] = m.gg[...][None]
    for h in range(H):
        m.par[6:7, h * head : (h + 1) * head] = jnp.broadcast_to(m.sk[0:1, h : h + 1], (1, head))
    m.gain[0:1, :] = m.ng[...][None]
    m.tile[...] = jnp.zeros_like(m.tile)
    m.tile[0:1, 0:H] = m.sb[...]
    m.tile[1:2, 0:H] = -jnp.exp(m.ld[...])
    turned = jnp.transpose(m.tile[...])
    m.hcol[...] = turned[0:GROUP, :]
    bias_col, rate_col = m.hcol[:, 0:1], m.hcol[:, 1:2]
    gain_in = m.gain[0:1, :]

    def normalize(u):
        u = u.astype(F32)
        mean = jnp.sum(u * u, axis=-1, keepdims=True) * (1.0 / z.d_true)
        return (u * lax.rsqrt(mean + EPS)) * gain_in

    length = m.seg.shape[-1]
    begin = c * T
    seqs = m.seg.shape[1]

    def ids_at(place, size):
        place = pl.multiple_of(place, LANES)
        lines = [m.seg[r // seqs, r % seqs : r % seqs + 1, pl.ds(place, size)] for r in range(R)]
        return jnp.concatenate(lines + [jnp.zeros_like(lines[0])] * (-R % 8), axis=0).astype(F32)

    now = ids_at(begin, T)
    before = jnp.where(c == 0, -1.0, ids_at(jnp.maximum(begin - LANES, 0), LANES))
    behind = jnp.where(c == nc - 1, -2.0, ids_at(jnp.minimum(begin + T, length - LANES), LANES))
    m.segr[...] = now
    m.segb[...] = before
    m.sega[...] = behind
    m.carried[...] = (now == before[:, LANES - 1 : LANES]).astype(F32)
    m.closing[...] = (now == now[:, T - 1 : T]).astype(F32)
    m.tot[...] = jnp.zeros_like(m.tot)
    m.tot[0 : now.shape[0], :] = now
    m.segc[...] = jnp.transpose(m.tot[...])
    away = iota((T, T), 0) - iota((T, T), 1)
    m.lower[...] = (away >= 0).astype(BF16)
    m.upper[...] = (away <= 0).astype(BF16)
    for r in range(R):
        same = m.segc[:, r : r + 1] == m.segr[r : r + 1, :]
        m.past[r] = (same & (away >= 0)).astype(BF16)
        m.next[r] = (same & (away <= 0)).astype(BF16)
        for j in range(1, z.K):
            m.down[r, j - 1] = (same & (away == j)).astype(BF16)
            m.up[r, j - 1] = (same & (away == -j)).astype(BF16)

    @pl.when(c == 0)
    def _():
        m.hh[...] = jnp.zeros_like(m.hh)
        m.sin[...] = jnp.zeros_like(m.sin)

    @pl.when(c == nc - 1)
    def _():
        m.gin[...] = jnp.zeros_like(m.gin)
        m.dce[...] = jnp.zeros_like(m.dce)

    m.sm[...] = jnp.zeros_like(m.sm)
    m.hacc[...] = jnp.zeros_like(m.hacc)
    m.drow[...] = jnp.zeros_like(m.drow)
    m.gstep[...] = jnp.zeros_like(m.gstep)

    @pl.loop(0, R)
    def _(r):
        value = normalize(m.hv[row(r), :]).astype(BF16)
        m.nrm[row(r), :] = value
        m.nrmt[:, row(r)] = jnp.transpose(value)

    load(1).wait()

    @pl.loop(0, R)
    def _(r):
        m.cott[:, row(r)] = jnp.transpose(m.cv[row(r), :])

    reach = iota((HALO, HALO), 1) - HALO - iota((HALO, HALO), 0)
    ahead = iota((HALO, HALO), 1) + HALO - iota((HALO, HALO), 0)
    m.early[...] = jnp.zeros_like(m.early)
    for r in range(R):
        near = m.segc[0:HALO, r : r + 1] == m.segb[r : r + 1, LANES - HALO : LANES]
        late = m.segc[T - HALO : T, r : r + 1] == m.sega[r : r + 1, 0:HALO]
        for j in range(1, z.K):
            first = ((r * (z.K - 1)) + j - 1) * HALO
            m.early[first : first + HALO, r * HALO : (r + 1) * HALO] = (near & (reach == -j)).astype(BF16)
            m.late[r, (j - 1) * HALO : j * HALO, :] = (late & (ahead == j)).astype(BF16)

    w_step(0, 1)
    w_step(1, 1)
    w_start(2)

    @pl.when(c > 0)
    def _():
        for r in range(R):
            halo_copy(r).wait_recv()

    m.nrmh[...] = normalize(m.hh[...]).astype(BF16)
    for s in range(2, nc):
        w_step(0, s)
        w_step(1, s)
        if s == 2:
            w_start(3)
    half_copy(0).start()
    w_step(2, 1)
    w_rest(1)

    m.tile[...] = jnp.zeros_like(m.tile)
    for b in range(nd * nc):
        m.tile[0:GROUP, :] = m.wt[b]
        m.wall[b * rp : (b + 1) * rp, V:Z] = jnp.transpose(m.tile[...])[0:rp, :].astype(BF16)
    w_rest(0)
    for k in range(1, nd):
        half_copy(k).start()
    w_step(3, 1)
    if nc > 2:
        w_step(2, 2)

    low_lanes = iota((T, LANES), 1) < head
    lane = iota((T, LANES), 1)
    fold = (iota((C, LANES), 0) // head == iota((C, LANES), 1)).astype(F32)
    fold_run = fold.astype(BF16)
    fold_through = (
        (iota((C, LANES), 0) // head == iota((C, LANES), 1) - GROUP).astype(F32) - fold
    ).astype(BF16)
    fold_step = (iota((C, LANES), 0) // head == iota((C, LANES), 1) - 2 * GROUP).astype(BF16)
    RUN, STEP, LEAD, TRAIL = 0, GROUP, 2 * GROUP, 3 * GROUP

    def widened(values, base, p):
        a = base + 2 * p
        return jnp.where(low_lanes[: values.shape[0]], values[:, a : a + 1], values[:, a + 1 : a + 2])

    def spread(values, base):
        return jnp.concatenate([widened(values, base, p) for p in range(pairs)], axis=1)

    def state_copy(r):
        return copy(m.ssend.at[r], m.sin.at[r], m.s_send.at[r], m.s_recv.at[r], (d, c + 1, t))

    def grad_copy(r):
        return copy(m.gsend.at[r], m.gin.at[r], m.g_send.at[r], m.g_recv.at[r], (d, c - 1, t))

    def edge_copy(r):
        return copy(m.edge.at[r], m.dce.at[r], m.e_send.at[r], m.e_recv.at[r], (d, c - 1, t))

    def kept(r):
        return spread(m.cols[pl.ds(r * T + T - 1, 1), :], LEAD)

    def pair(p):
        return slice(p * LANES, (p + 1) * LANES)

    def lanes_of(p):
        return slice(Q + p * LANES, Q + (p + 1) * LANES)

    def serve_state(r):
        state_copy(r).wait_recv()

        @pl.when(c < nc - 1)
        def _():
            m.ssend[r] = (m.fresh[r] + kept(r) * m.sin[r].astype(F32)).astype(BF16)
            state_copy(r).start()

    def serve_grad(r):
        grad_copy(r).wait_recv()

        @pl.when(c > 0)
        def _():
            m.gsend[r] = (m.local[r] + kept(r) * m.gin[r].astype(F32)).astype(BF16)
            grad_copy(r).start()

    hops = nc - 1 - c
    soon = R == 4 and nc > 2
    if soon:
        state_late = (c > 2) | ((c == 2) & (nc > 3))
        grad_late = hops > 2
    else:
        state_late, grad_late = c > 0, hops > 0

    def state_point(place, r):
        if soon:
            for who, item in place:
                @pl.when((c == who) & r)
                def _():
                    serve_state(item)

    def grad_point(place, r):
        if soon:
            for who, item in place:
                @pl.when((hops == who) & r)
                def _():
                    serve_grad(item)

    for k in range(nd):
        half_arrived(k)
    halo_v = nn(m.nrmh[...], m.wall[:, :V]).astype(BF16)
    m.hfix[...] = nn(m.early[...], halo_v)

    @pl.loop(0, R)
    def _(r):
        acc = nn(m.nrm[row(r), :], m.wall[:, :Z])
        m.v[row(r), :] = acc[:, :V].astype(BF16)
        raw = jnp.transpose(acc[:, V:].astype(BF16).astype(F32))[0:GROUP]
        pre = raw + bias_col
        step = jnp.maximum(pre, 0.0) + jnp.log1p(jnp.exp(-jnp.abs(pre)))
        m.pre[:, row(r)] = pre
        m.step[:, row(r)] = step
        run = exact_rows(step * rate_col, m.upper[...])
        m.runr[r] = run
        m.tot[0:GROUP, :] = run
        m.tot[GROUP : 2 * GROUP, :] = step
        m.tot[2 * GROUP : 3 * GROUP, :] = jnp.exp(run) * m.carried[pl.ds(r, 1), :]
        m.tot[3 * GROUP : 4 * GROUP, :] = jnp.exp(run[:, T - 1 : T] - run) * m.closing[pl.ds(r, 1), :]
        m.cols[row(r), :] = jnp.transpose(m.tot[...])
        for a in range(0, V, WIDE):
            part = slice(a, min(a + WIDE, V))
            value = m.v[row(r), part]
            conv = value.astype(F32) * m.par[0:1, part] + m.par[4:5, part]
            first = jnp.zeros((EDGE, conv.shape[1]), F32)
            for j in range(1, z.K):
                tap = m.par[j : j + 1, part]
                conv = conv + nn(m.down[r, j - 1], value) * tap
                first = first + m.hfix[pl.ds((r * (z.K - 1) + j - 1) * HALO, EDGE), part] * tap
            conv = jnp.concatenate([conv[0:EDGE] + first, conv[EDGE:]], axis=0)
            logistic = sigmoid(conv)
            m.mix[row(r), part] = (conv * logistic).astype(BF16)
            m.slope[row(r), part] = logistic * (1.0 + conv * (1.0 - logistic))
        state_point([(1, 0)], r == 2)
        state_point([(1, 1)], r == 3)
        for p in range(pairs):
            scaled = m.mix[row(r), lanes_of(p)].astype(F32) * widened(m.cols[row(r), :], STEP, p)
            m.xs[row(r), pair(p)] = scaled.astype(BF16)
            m.xt[row(r), pair(p)] = (scaled * widened(m.cols[row(r), :], TRAIL, p)).astype(BF16)
        m.fresh[r] = tn(m.mix[row(r), BX], m.xt[row(r), :])

        @pl.when(c == 0)
        def _():
            m.ssend[r] = m.fresh[r].astype(BF16)
            state_copy(r).start()

        for s in range(2, nc):
            pl.when(r == min(s - 2, R - 1))(lambda: w_step(3, s))
        for s in range(3, nc):
            pl.when(r == min(s - 3, R - 1))(lambda: w_step(2, s))

    state_point([(2, 0)], True)

    @pl.loop(0, R)
    def _(r):
        b, cm = m.mix[row(r), BX], m.mix[row(r), CX]
        m.scores[...] = nt(cm, b) * m.past[r].astype(F32)
        for p in range(pairs):
            for a in range(0, T, LANES):
                rows, seen = slice(a, a + LANES), a + LANES
                here = pl.ds(pl.multiple_of(r * T, 16) + a, LANES)
                both = []
                for h in (2 * p, 2 * p + 1):
                    decay = jnp.exp(jnp.minimum(m.cols[here, h : h + 1] - m.runr[r, h : h + 1, :seen], 0.0))
                    weight = (decay * m.scores[rows, :seen]).astype(BF16)
                    both.append(nn(weight, m.xs[pl.ds(pl.multiple_of(r * T, 16), seen), pair(p)]))
                m.ins[here, pair(p)] = jnp.where(low_lanes[:LANES], both[0], both[1])
        state_point([(1, 2)], r == 0)
        state_point([(2, 1)], r == 2)

    state_point([(1, 3)], True)
    w_rest(2)
    w_rest(3)

    def sums_copy(r, k):
        return copy(
            m.sums.at[t, r], m.sums.at[t, r], m.x_send.at[r, k], m.x_recv.at[r, t], (d, c, at_ten(k))
        )

    def sums_arrived(r, who):
        copy(
            m.sums.at[who, r], m.sums.at[who, r], m.x_send.at[r, 0], m.x_recv.at[r, who], (d, c, t)
        ).wait_recv()

    def mine(r):
        return pl.ds(pl.multiple_of(r * T + odd * half, 16), half)

    def theirs(r):
        return pl.ds(pl.multiple_of(r * T + (1 - odd) * half, 16), half)

    def near_copy(a, r):
        return copy(m.as_.at[a, r], m.ar_.at[a, r], m.a_send.at[a, r], m.a_recv.at[a, r], (d, c, across))

    def far_copy(a, r):
        return copy(m.bs_.at[a, r], m.br_.at[a, r], m.b_send.at[a, r], m.b_recv.at[a, r], (d, c, far))

    def back_copy(a, r):
        out = (m.out, m.ing)[a].at[mine(r)]
        return copy(out, out, m.c_send.at[a, r], m.c_recv.at[a, r], (d, c, across))

    def back_arrived(a, r):
        out = (m.out, m.ing)[a].at[theirs(r)]
        copy(out, out, m.c_send.at[a, r], m.c_recv.at[a, r], (d, c, across)).wait_recv()

    def give(a, r, value):
        first, second = value[:half], value[half:]
        m.as_[a, r] = jnp.where(odd == 0, second, first).astype(BF16)
        near_copy(a, r).start()
        m.keep[r] = jnp.where(odd == 0, first, second)

    def chip_sum(a, r):
        near_copy(a, r).wait_recv()
        m.bs_[a, r] = (m.keep[r] + m.ar_[a, r].astype(F32)).astype(BF16)
        if ntn == 4:
            far_copy(a, r).start()

    def full_sum(a, r):
        total = m.bs_[a, r].astype(F32)
        if ntn == 4:
            far_copy(a, r).wait_recv()
            total = total + m.br_[a, r].astype(F32)
        return total

    def serve_late(r):
        if soon and nc > 3:
            pl.when((c > 2) | (r >= 2))(lambda: serve_state(r))
        else:
            serve_state(r)

    def gating(r):
        pl.when(state_late)(lambda: serve_late(r))
        cm = m.mix[row(r), CX]
        gate = nn(m.nrm[row(r), :], m.wall[:, Z:])
        m.zv[row(r), :] = gate.astype(BF16)
        m.dy[row(r), :] = nn(m.cv[row(r), :], m.wo[...])
        m.ys[row(r), :] = nn(cm, m.sin[r])
        squares = jnp.zeros((T, LANES), F32)
        inner = jnp.zeros((T, LANES), F32)
        for p in range(pairs):
            carried = m.ys[row(r), pair(p)] * widened(m.cols[row(r), :], LEAD, p)
            m.ys[row(r), pair(p)] = carried
            ssd = m.ins[row(r), pair(p)] + carried + m.par[6:7, pair(p)] * m.mix[row(r), lanes_of(p)].astype(F32)
            m.ssd[row(r), pair(p)] = ssd
            gate = m.zv[row(r), pair(p)].astype(F32)
            gated = ssd * (gate * sigmoid(gate))
            m.gated[row(r), pair(p)] = gated
            scaled = gated * m.par[5:6, pair(p)]
            m.yg[row(r), pair(p)] = scaled.astype(BF16)
            squares = squares + gated * gated
            inner = inner + scaled * m.dy[row(r), pair(p)]
        squares = jnp.sum(squares, axis=-1, keepdims=True)
        inner = jnp.sum(inner, axis=-1, keepdims=True)
        both = jnp.where(lane == 0, squares, jnp.where(lane == 1, inner, 0.0))
        m.sums[t, r] = jnp.transpose(both)[0:8, :]
        for k in range(1, ntn):
            sums_copy(r, k).start()
        give(0, r, nt(m.yg[row(r), :], m.wo[...]))

    def ungating(r):
        for k in range(1, ntn):
            sums_arrived(r, at_ten(k))
        total = m.sums[0, r]
        for who in range(1, ntn):
            total = total + m.sums[who, r]
        scale = lax.rsqrt(total[0:1] * (1.0 / (C * ntn)) + EPS)
        inner = total[1:2] * (1.0 / (C * ntn)) * scale * scale * scale
        m.tot[0:1, :] = scale
        m.tot[1:2, :] = inner
        columns = jnp.transpose(m.tot[...])
        m.rms[row(r), :] = columns
        scale = jnp.broadcast_to(columns[:, 0:1], (T, LANES))
        inner = jnp.broadcast_to(columns[:, 1:2], (T, LANES))
        for p in range(pairs):
            gated, dy, ssd = m.gated[row(r), pair(p)], m.dy[row(r), pair(p)], m.ssd[row(r), pair(p)]
            gate = m.zv[row(r), pair(p)].astype(F32)
            gain = m.par[5:6, pair(p)]
            normal = gated * scale
            m.sm[5:6, pair(p)] += jnp.sum(dy * normal, axis=0, keepdims=True)
            m.yg[row(r), pair(p)] = (normal * gain).astype(BF16)
            d_gated = scale * dy * gain - gated * inner
            logistic = sigmoid(gate)
            m.dcat[row(r), Z + p * LANES : Z + (p + 1) * LANES] = (
                d_gated * ssd * (logistic * (1.0 + gate * (1.0 - logistic)))
            ).astype(BF16)
            d_ssd = d_gated * (gate * logistic)
            m.ssd[row(r), pair(p)] = d_ssd
            m.wds[row(r), pair(p)] = (d_ssd * widened(m.cols[row(r), :], LEAD, p)).astype(BF16)
        m.local[r] = tn(m.mix[row(r), CX], m.wds[row(r), :])

        @pl.when(c == nc - 1)
        def _():
            m.gsend[r] = m.local[r].astype(BF16)
            if nc > 1:
                grad_copy(r).start()

    @pl.loop(0, R + 2)
    def _(i):
        pl.when(i < R)(lambda: gating(i))

        @pl.when(i >= 2)
        def _():
            ungating(i - 2)

        grad_point([(1, 0)], i == R + 1)

        @pl.when(i == R - 1)
        def _():
            pl.loop(0, R - 1)(lambda r: chip_sum(0, r))

        pl.when(i == R)(lambda: chip_sum(0, R - 1))

    gall, gyr, gzs, gzr = (m.ga0, m.ga1, m.ga2), (m.gy0, m.gy1, m.gy2), (m.gz0, m.gz1, m.gz2), (m.gr0, m.gr1, m.gr2)
    tall = (rp, rp, rp + HALO)

    def rs_dp(part, j, k):
        cc = at_ctx(j)
        return copy(
            gall[part].at[rows_at(at_dp(k) * nc + cc, tall[part])],
            gyr[part].at[k - 1, rows_at(cc, tall[part])],
            m.ry_send.at[part, j, k - 1],
            m.ry_recv.at[part, j, k - 1],
            (at_dp(k), c, t),
        )

    def rs_ctx(part, j):
        cc = at_ctx(j)
        return copy(
            gzs[part].at[rows_at(cc, tall[part])],
            gzr[part].at[c],
            m.rz_send.at[part, j],
            m.rz_recv.at[part, c],
            (d, cc, t),
        )

    def rs_arrived(part, cc):
        copy(gzr[part].at[cc], gzr[part].at[cc], m.rz_send.at[part, 0], m.rz_recv.at[part, cc], (d, c, t)).wait_recv()

    def rs_start(part):
        for j in list(range(1, nc)) + [0]:
            for k in range(1, nd):
                rs_dp(part, j, k).start()

    def rs_middle(part, j):
        cc = at_ctx(j)
        total = gall[part][rows_at(d * nc + cc, tall[part]), :].astype(F32)
        for k in range(1, nd):
            rs_dp(part, j, k).wait_recv()
            total = total + gyr[part][k - 1, rows_at(cc, tall[part]), :].astype(F32)
        own = j == 0

        def keep():
            gzr[part][c] = total.astype(BF16)

        def send():
            gzs[part][rows_at(cc, tall[part]), :] = total.astype(BF16)
            rs_ctx(part, j).start()

        if isinstance(j, int):
            keep() if own else send()
        else:
            pl.when(own)(keep)
            pl.when(jnp.logical_not(own))(send)

    def rs_end(part):
        for k in range(1, nc):
            rs_arrived(part, at_ctx(k))
        total = gzr[part][0].astype(F32)
        for cc in range(1, nc):
            total = total + gzr[part][cc].astype(F32)
        return total

    def rs_sent(part):
        for j in range(nc):
            for k in range(1, nd):
                rs_dp(part, j, k).wait_send()
            if j:
                rs_ctx(part, j).wait_send()

    m.ga1[:, C:] = nn(m.cott[...], m.yg[...]).astype(BF16)
    m.ga1[:, :C] = nn(m.nrmt[...], m.dcat[:, Z:]).astype(BF16)
    rs_start(1)
    grad_point([(1, 1), (1, 2), (2, 0)], True)

    @pl.loop(0, R)
    def _(r):
        b, cm = m.mix[row(r), BX], m.mix[row(r), CX]
        m.scores[...] = nt(b, cm) * m.next[r].astype(F32)
        start = pl.multiple_of(r * T, 16)
        for a in range(0, T, LANES):
            rows, here, after = slice(a, a + LANES), pl.ds(start + a, LANES), pl.ds(start + a, T - a)
            losses = jnp.zeros((LANES, LANES), F32)
            for p in range(pairs):
                ds_pair = m.ssd[after, pair(p)].astype(BF16)
                xs_pair = m.xs[here, pair(p)]
                both = []
                for h in (2 * p, 2 * p + 1):
                    pick = low_lanes[:LANES] if h % 2 == 0 else ~low_lanes[:LANES]
                    decay = jnp.exp(jnp.minimum(m.runr[r, h : h + 1, a:] - m.cols[here, h : h + 1], 0.0))
                    weight = decay * m.scores[rows, a:]
                    both.append(nn(weight.astype(BF16), ds_pair))
                    d_weight = nt(jnp.where(pick, xs_pair, jnp.zeros_like(xs_pair)), ds_pair)
                    flow = d_weight * weight
                    if h == 0:
                        m.dsc[rows, a:] = d_weight * decay
                    else:
                        m.dsc[rows, a:] += d_weight * decay
                    losses = jnp.where(lane[:LANES] == h, jnp.sum(flow, axis=1, keepdims=True), losses)
                    down = jnp.sum(flow, axis=0, keepdims=True)
                    if a == 0:
                        m.drow[r, h : h + 1, :] = down
                    else:
                        m.drow[r, h : h + 1, a:] += down
                m.ins[here, pair(p)] = jnp.where(low_lanes[:LANES], both[0], both[1])
            m.drun[here, :] = exact_right(m.ssd[here, :] * m.ys[here, :], fold_run) - losses
            d_scores = (m.dsc[rows, a:] * m.next[r, rows, a:].astype(F32)).astype(BF16)
            m.gated[here, :LANES] = nn(d_scores, m.mix[after, CX])
            d_after = tn(d_scores, m.mix[here, BX])
            if a == 0:
                m.gated[after, LANES:S] = d_after
            else:
                m.gated[after, LANES:S] += d_after

        grad_point([(1, 3), (2, 1)], r == 0)
        grad_point([(2, 2)], r == 1)
        grad_point([(2, 3)], r == 2)

    def final_out(r):
        value = m.hv[mine(r), :].astype(F32) + m.rms[mine(r), 0:1] * full_sum(0, r)
        m.out[mine(r), :] = value.astype(BF16)
        back_copy(0, r).start()

    def adjoint(r):
        pl.when(grad_late)(lambda: serve_grad(r))
        b = m.mix[row(r), BX]
        grad = m.gin[r]
        for p in range(pairs):
            trailing = widened(m.cols[row(r), :], TRAIL, p)
            reach = nn(b, m.gin[r, :, pair(p)]) * trailing
            x = m.mix[row(r), lanes_of(p)].astype(F32)
            d_xs = m.ins[row(r), pair(p)] + reach
            d_ssd = m.ssd[row(r), pair(p)]
            m.prod[:, pair(p)] = m.xs[row(r), pair(p)].astype(F32) * reach
            m.prod[:, C + p * LANES : C + (p + 1) * LANES] = d_xs * x
            m.sm[7:8, LANES + p * LANES : 2 * LANES + p * LANES] += jnp.sum(d_ssd * x, axis=0, keepdims=True)
            m.dy[row(r), pair(p)] = (
                d_xs * widened(m.cols[row(r), :], STEP, p) + m.par[6:7, pair(p)] * d_ssd
            ) * m.slope[row(r), lanes_of(p)]
        m.gated[row(r), :Q] = (
            m.gated[row(r), :LANES] + nt(m.xt[row(r), :], grad)
        ) * m.slope[row(r), BX]
        m.gated[row(r), Q:S] = (
            m.gated[row(r), LANES:S] + nt(m.wds[row(r), :], m.sin[r])
        ) * m.slope[row(r), CX]

        @pl.when(c > 0)
        def _():
            first = pl.ds(pl.multiple_of(r * T, 16), EDGE)
            m.edge[r, :, BX] = m.gated[first, :Q]
            m.edge[r, :, Q : Q + C] = m.dy[first, :]
            m.edge[r, :, CX] = m.gated[first, Q:S]
            edge_copy(r).start()

        m.drun[row(r), :] += exact_right(m.prod[:, :C], fold_through) + exact_right(m.prod[:, C:], fold_step)
        joint = jnp.sum(grad.astype(F32) * m.sin[r].astype(F32), axis=0, keepdims=True)
        joint = exact_right(jnp.broadcast_to(joint, (8, C)), fold_run)[0:1]
        last = m.cols[pl.ds(r * T + T - 1, 1), :]
        kept_lanes = jnp.concatenate([last[:, LEAD : LEAD + H], jnp.zeros((1, LANES - H), F32)], axis=1)
        m.drun[pl.ds(r * T + T - 1, 1), :] += joint * kept_lanes
        turned = jnp.transpose(m.drun[row(r), :])
        through = jnp.sum(turned[GROUP : 2 * GROUP], axis=1, keepdims=True)
        d_run = turned[0:GROUP] + m.drow[r]
        d_run = d_run + jnp.where(iota((GROUP, T), 1) == T - 1, through, 0.0)
        d_growth = exact_rows(d_run, m.lower[...])
        d_step = turned[2 * GROUP : 3 * GROUP] + rate_col * d_growth
        d_pre = d_step * sigmoid(m.pre[:, row(r)])
        m.hacc[0:GROUP, :] += d_pre
        m.hacc[GROUP : 2 * GROUP, :] += m.step[:, row(r)] * d_growth * rate_col
        d_pre = jnp.where(iota((GROUP, T), 0) < H, d_pre, 0.0)
        m.gstep[...] += nn(jnp.concatenate([d_pre, jnp.zeros_like(d_pre)], axis=0).astype(BF16), m.nrm[row(r), :])
        m.tot[0:GROUP, :] = d_pre
        m.dcat[row(r), V:Z] = jnp.transpose(m.tot[...]).astype(BF16)

    def finish(r):
        @pl.when(c < nc - 1)
        def _():
            edge_copy(r).wait_recv()

        edge = m.dce[r]
        edge = jnp.concatenate([edge, jnp.zeros_like(edge)], axis=0).astype(BF16)
        m.lfix[...] = nn(m.late[r], edge)
        cuts = [(m.gated, 0, 0, Q), (m.gated, Q, Q + C, Q)]
        cuts += [(m.dy, a, Q + a, min(WIDE, C - a)) for a in range(0, C, WIDE)]
        for held, place, first, size in cuts:
            part = slice(first, first + size)
            d_conv = held[row(r), place : place + size]
            low = d_conv.astype(BF16)
            value = m.v[row(r), part].astype(F32)
            m.sm[4:5, part] += jnp.sum(d_conv, axis=0, keepdims=True)
            m.sm[0:1, part] += jnp.sum(d_conv * value, axis=0, keepdims=True)
            d_v = d_conv * m.par[0:1, part]
            for j in range(1, z.K):
                moved = nn(m.up[r, j - 1], low)
                moved = jnp.concatenate(
                    [moved[: T - HALO], moved[T - HALO :] + m.lfix[(j - 1) * HALO : j * HALO, part]], axis=0
                )
                d_v = d_v + moved * m.par[j : j + 1, part]
                m.sm[j : j + 1, part] += jnp.sum(moved * value, axis=0, keepdims=True)
            m.dcat[row(r), part] = d_v.astype(BF16)

    def finish_norm(r):
        value = nt(m.dcat[row(r), :], m.wall[...])
        give(1, r, value)
        u = m.hv[row(r), :].astype(F32)
        mean = jnp.sum(u * u, axis=-1, keepdims=True) * (1.0 / z.d_true)
        m.sm[6:7, :D] += jnp.sum(value * (u * lax.rsqrt(mean + EPS)), axis=0, keepdims=True)

    m.tot[...] = jnp.zeros_like(m.tot)

    def first_sums(j, upward):
        up = c + j < nc
        pl.when(up if upward else jnp.logical_not(up))(lambda: rs_middle(1, j))

    @pl.loop(0, R)
    def _(r):
        pl.when(r == 0)(lambda: final_out(0))
        adjoint(r)
        for j in range(1, min(nc, 3)):
            pl.when(r == min(2 * j - 2, R - 1))(lambda: first_sums(j, True))

    @pl.loop(0, R)
    def _(r):
        finish(r)
        pl.when(r == 0)(lambda: finish_norm(0))
        pl.when(r == min(1, R - 1))(lambda: chip_sum(1, 0))
        for k in range(1, R - 1):
            pl.when(r == min(2 * k - 1, R - 1))(lambda: final_out(k))
        for j in range(3, nc):
            pl.when(r == min(j - 1, R - 1))(lambda: first_sums(j, True))
        for j in range(1, nc):
            pl.when(r == min(j - 1, R - 1))(lambda: first_sums(j, False))

    def small_copy(index):
        return copy(m.sa.at[d * nc + c], m.sa.at[d * nc + c], m.sa_send.at[index], m.sa_recv.at[d * nc + c], others[index])

    def small_arrived(dd, cc):
        there = m.sa.at[dd * nc + cc]
        copy(there, there, m.sa_send.at[0], m.sa_recv.at[dd * nc + cc], (d, c, t)).wait_recv()

    def common_copy(k):
        return copy(m.sb2.at[t], m.sb2.at[t], m.st_send.at[k], m.st_recv.at[t], (d, c, at_ten(k)))

    def common_arrived(who):
        copy(m.sb2.at[who], m.sb2.at[who], m.st_send.at[0], m.st_recv.at[who], (d, c, t)).wait_recv()

    width = S // ntn
    starts = [k * width + (C if k * width >= Q else 0) for k in range(ntn)]
    quarters = [m.dcat[:, first : first + width] for first in starts]
    value = nn(m.nrmt[...], jnp.concatenate(quarters[0::2] + quarters[1::2], axis=1))

    def share_copy():
        return copy(m.shs, m.shr, m.sh_send.at[0], m.sh_recv.at[0], (d, c, across))

    m.shk[...] = jnp.where(odd == 0, value[:, : z.Q], value[:, z.Q :])
    m.shs[...] = jnp.where(odd == 0, value[:, z.Q :], value[:, : z.Q]).astype(BF16)
    share_copy().start()

    m.ga0[...] = nn(m.nrmt[...], m.dcat[:, Q : Q + C]).astype(BF16)
    share_copy().wait_recv()
    for b in range(nd * nc):
        here = slice(b * rp, (b + 1) * rp)
        there = b * (rp + HALO)
        m.ga2[there : there + rp, :] = (m.shk[here, :] + m.shr[here, :].astype(F32)).astype(BF16)
        steps = m.gstep[:, here]
        m.ga2[there + rp : there + rp + HALO, :] = jnp.concatenate(
            [steps, jnp.zeros((HALO, LANES - rp), F32)], axis=1
        ).astype(BF16)
    rs_start(2)
    rs_start(0)

    @pl.loop(1, R)
    def _(r):
        finish_norm(r)
        pl.when(r == min(2, R - 1))(lambda: final_out(R - 1))
        pl.when(r == 1)(lambda: rs_middle(1, 0))
        pl.when(r >= 2)(lambda: chip_sum(1, r - 1))

    m.tile[...] = jnp.zeros_like(m.tile)
    m.tile[0 : 2 * GROUP, :] = jnp.broadcast_to(
        jnp.sum(m.hacc[...], axis=1, keepdims=True), (2 * GROUP, LANES)
    )
    m.sm[7:8, 0:LANES] = jnp.transpose(m.tile[...])[0:1, :]
    m.sa[d * nc + c] = jnp.concatenate([m.sm[:, : z.WL // 2], m.sm[:, z.WL // 2 :]], axis=0).astype(BF16)
    for index in range(len(others)):
        small_copy(index).start()

    chip_sum(1, R - 1)

    def last_copy():
        return copy(m.ls, m.lr, m.sh_send.at[1], m.sh_recv.at[1], (d, c, far))

    def input_row(r):
        u = m.hv[mine(r), :].astype(F32)
        mean = jnp.sum(u * u, axis=-1, keepdims=True) * (1.0 / z.d_true)
        scale = lax.rsqrt(mean + EPS)
        unit = u * scale
        d_unit = full_sum(1, r) * gain_in
        inner = jnp.sum(d_unit * unit, axis=-1, keepdims=True) * (1.0 / z.d_true)
        value = m.cv[mine(r), :].astype(F32) + scale * (d_unit - unit * inner)
        m.ing[mine(r), :] = value.astype(BF16)
        back_copy(1, r).start()

    for r in range(R):
        back_arrived(0, r)
    for j in list(range(1, nc)) + [0]:
        rs_middle(2, j)
    m.gw1[...] = rs_end(1)

    @pl.loop(0, R)
    def _(r):
        input_row(r)
        pl.when(r >= 1)(lambda: back_arrived(1, r - 1))

        @pl.when(r == 0)
        def _():
            rs_middle(0, 1 % nc)

        @pl.when(r == min(2, R - 1))
        def _():
            for dd in range(nd):
                for cc in range(nc):
                    pl.when((dd != d) | (cc != c))(lambda: small_arrived(dd, cc))
            total = m.sa[0].astype(F32)
            for who in range(1, nd * nc):
                total = total + m.sa[who].astype(F32)
            m.sb2[t] = jnp.concatenate([total[0:8], total[8:16]], axis=1)
            for k in range(1, ntn):
                common_copy(k).start()

        @pl.when(r == 1)
        def _():
            for j in list(range(2, nc)) + ([0] if nc > 1 else []):
                rs_middle(0, j)

        @pl.when(r == min(2, R - 1))
        def _():
            value = rs_end(2)
            if ntn == 4:
                m.ls[...] = value
                last_copy().start()
            else:
                m.gw2[...] = value

    for k in range(1, ntn):
        common_arrived(at_ten(k))
    common = m.sb2[0]
    for who in range(1, ntn):
        common = common + m.sb2[who]
    rows8, lanes8 = iota((8, z.WL), 0), iota((8, z.WL), 1)
    shared_here = (rows8 == 6) | ((rows8 < 5) & ((lanes8 < Q) | (lanes8 >= Q + C)))
    m.small[...] = jnp.where(shared_here, common, m.sb2[t])
    m.gw0[...] = rs_end(0)
    if ntn == 4:
        last_copy().wait_recv()
        m.gw2[0:rp, :] = m.ls[0:rp, :] + m.lr[0:rp, :]
        m.gw2[rp:, :] = m.ls[rp:, :]
        last_copy().wait_send()
    back_arrived(1, R - 1)

    for a in range(2):
        for r in range(R):
            back_copy(a, r).wait_send()
            near_copy(a, r).wait_send()
            if ntn == 4:
                far_copy(a, r).wait_send()
    for p in range(PIECES):
        w_sent(p)
    for k in range(nd):
        half_copy(k).wait_send()
    for part in range(3):
        rs_sent(part)
    for r in range(R):
        for k in range(1, ntn):
            sums_copy(r, k).wait_send()

        @pl.when(c < nc - 1)
        def _():
            halo_copy(r).wait_send()
            state_copy(r).wait_send()

        @pl.when(c > 0)
        def _():
            grad_copy(r).wait_send()
            edge_copy(r).wait_send()

    share_copy().wait_send()
    for index in range(len(others)):
        small_copy(index).wait_send()
    for k in range(1, ntn):
        common_copy(k).wait_send()


def finishing(z, out, ing, gw0, gw1, gw2, small, *outs):
    (o_out, o_ing, norm, heads, shared, step, taps, bias, staps, sbias, dsb, drate, dskip, gain, outw, tile, sems) = outs
    C, S, D, H, rp, rows = z.C, z.S, z.D, z.H, z.rp, z.rows
    V = C + S
    head = C // H
    moves = [pltpu.make_async_copy(out, o_out, sems.at[0]), pltpu.make_async_copy(ing, o_ing, sems.at[1])]
    for move in moves:
        move.start()
    norm[...] = small[6, :D]
    heads[:, 0, :] = gw1[0:rows, :C]
    heads[:, 1, :] = gw0[0:rows, :]
    width = S // z.ntn
    tile[...] = jnp.zeros_like(tile)
    tile[0:rp, :] = gw2[0:rp, :]
    pair = jnp.transpose(tile[...])
    if z.ntn == 4:
        upper = lax.axis_index("tensor") >= 2
        pair = jnp.where(upper, pair[width:], pair[:width])
    shared[...] = pair[:, 0:rows]
    step[...] = gw2[rp : rp + H, 0:rows]
    Q = z.Q
    taps[...] = small[0 : z.K, Q : Q + C]
    bias[...] = small[4, Q : Q + C]
    staps[:, :Q] = small[0 : z.K, :Q]
    staps[:, Q:] = small[0 : z.K, Q + C : V]
    sbias[...] = jnp.concatenate([small[4:5, :Q], small[4:5, Q + C : V]], axis=1)[0]
    dsb[...] = small[7, :H]
    drate[...] = small[7, GROUP : GROUP + H]
    lanes = iota((1, H), 1)
    skip = jnp.zeros((1, H), F32)
    for h in range(H):
        begin = LANES + h * head
        skip = jnp.where(lanes == h, jnp.sum(small[7:8, begin : begin + head], axis=1, keepdims=True), skip)
    tile[0:1, 0:H] = skip
    dskip[...] = tile[0, 0:H]
    gain[...] = small[5, :C]
    outw[...] = gw1[0:rows, C:]
    for move in moves:
        move.wait()


def on_device(z, hidden_in, segment_ids, norm_gain, head_projection, shared_projection, step_projection,
              conv_heads, bias_heads, conv_shared, bias_shared, step_bias, log_decay, skip_gain, gate_gain,
              output_weight, out_cotangent):
    R, T, D, C, H, S = z.R, z.T, z.D, z.C, z.H, z.S
    rp, nd, nc, ntn, rows = z.rp, z.nd, z.nc, z.ntn, z.rows
    V = C + S
    blocks = nd * nc
    R8 = 8 * -(-R // 8)

    def widen(value):
        if rp == rows:
            return value
        value = value.reshape(value.shape[:-1] + (blocks, rows))
        value = jnp.pad(value, [(0, 0)] * (value.ndim - 1) + [(0, rp - rows)])
        return value.reshape(value.shape[:-2] + (D,))

    def narrow(value):
        if rp == rows:
            return value
        return value.reshape(value.shape[:-1] + (blocks, rp))[..., :rows].reshape(value.shape[:-1] + (z.d_true,))

    def taller(value, dim):
        if rp == rows:
            return value
        return jnp.pad(value, [(0, rp - rows if k == dim else 0) for k in range(value.ndim)])

    dma, vmem = pltpu.SemaphoreType.DMA, pltpu.VMEM
    N = R * T
    half = T // 2
    k0 = max(nd - 1, 1)
    ins = dict(
        hid=widen(hidden_in.reshape(N, z.d_true)), cot=widen(out_cotangent.reshape(N, z.d_true)),
        seg=segment_ids, ng=widen(norm_gain), hp=taller(head_projection, 0),
        shp=taller(shared_projection, 0), stp=taller(step_projection.T, 1), ow=taller(output_weight.T, 0),
        ch=conv_heads, bh=bias_heads, cs=conv_shared, bs=bias_shared, sb=step_bias[None],
        ld=log_decay[None], sk=skip_gain[None], gg=gate_gain,
    )
    outs = dict(
        out=pltpu.VMEM((N, D), BF16),
        ing=pltpu.VMEM((N, D), BF16),
        gw0=pltpu.VMEM((rp, C), F32),
        gw1=pltpu.VMEM((rp, 2 * C), F32),
        gw2=pltpu.VMEM((rp + HALO, z.Q), F32),
        small=pltpu.VMEM((8, z.WL), F32),
    )
    scratch = dict(
        hv=vmem((N, D), BF16), cv=vmem((N, D), BF16),
        wall=vmem((D, V + LANES + C), BF16), wo=vmem((D, C), BF16), wt=vmem((blocks, GROUP, LANES), F32),
        hcol=vmem((GROUP, LANES), F32), tile=vmem((LANES, LANES), F32), gain=vmem((8, D), F32), par=vmem((16, V), F32),
        segc=vmem((T, LANES), F32), segr=vmem((R8, T), F32), carried=vmem((R8, T), F32), closing=vmem((R8, T), F32),
        segb=vmem((R8, LANES), F32), sega=vmem((R8, LANES), F32),
        early=vmem((R * (z.K - 1) * HALO, R * HALO), BF16), late=vmem((R, (z.K - 1) * HALO, HALO), BF16),
        hfix=vmem((R * (z.K - 1) * HALO, V), F32), lfix=vmem(((z.K - 1) * HALO, V), F32),
        down=vmem((R, z.K - 1, T, T), BF16), up=vmem((R, z.K - 1, T, T), BF16), lower=vmem((T, T), BF16), upper=vmem((T, T), BF16),
        past=vmem((R, T, T), BF16), next=vmem((R, T, T), BF16),
        hh=vmem((R * HALO, D), BF16), nrmh=vmem((R * HALO, D), BF16),
        nrm=vmem((N, D), BF16), nrmt=vmem((D, N), BF16), cott=vmem((D, N), BF16),
        v=vmem((N, V), BF16), mix=vmem((N, V), BF16), slope=vmem((N, V), F32),
        pre=vmem((GROUP, N), F32), step=vmem((GROUP, N), F32), cols=vmem((N, LANES), F32), xt=vmem((N, C), BF16),
        runr=vmem((R, 8, T), F32), xs=vmem((N, C), BF16),
        fresh=vmem((R, LANES, C), F32), local=vmem((R, LANES, C), F32),
        ssend=vmem((R, LANES, C), BF16), sin=vmem((R, LANES, C), BF16),
        gsend=vmem((R, LANES, C), BF16), gin=vmem((R, LANES, C), BF16),
        scores=vmem((T, T), F32), dsc=vmem((T, T), F32), drow=vmem((R, GROUP, T), F32), tot=vmem((LANES, T), F32),
        ins=vmem((N, C), F32), ys=vmem((N, C), F32), ssd=vmem((N, C), F32), zv=vmem((N, C), BF16),
        gated=vmem((N, max(C, S)), F32), dy=vmem((N, C), F32),
        yg=vmem((N, C), BF16), wds=vmem((N, C), BF16),
        rms=vmem((N, LANES), F32), sums=vmem((ntn, R, 8, T), F32),
        as_=vmem((2, R, half, D), BF16), ar_=vmem((2, R, half, D), BF16),
        bs_=vmem((2, R, half, D), BF16), br_=vmem((2, R, half, D), BF16), keep=vmem((R, half, D), F32),
        ga0=vmem((D, C), BF16), ga1=vmem((D, 2 * C), BF16), ga2=vmem((blocks * (rp + HALO), z.Q), BF16),
        gy0=vmem((k0, nc * rp, C), BF16), gy1=vmem((k0, nc * rp, 2 * C), BF16), gy2=vmem((k0, nc * (rp + HALO), z.Q), BF16),
        gz0=vmem((nc * rp, C), BF16), gz1=vmem((nc * rp, 2 * C), BF16), gz2=vmem((nc * (rp + HALO), z.Q), BF16),
        gr0=vmem((nc, rp, C), BF16), gr1=vmem((nc, rp, 2 * C), BF16), gr2=vmem((nc, rp + HALO, z.Q), BF16),
        drun=vmem((N, LANES), F32), edge=vmem((R, EDGE, V), F32),
        dce=vmem((R, EDGE, V), F32), dcat=vmem((N, V + LANES + C), BF16),
        prod=vmem((T, 2 * C), F32), hacc=vmem((2 * GROUP, T), F32), gstep=vmem((HALO, D), F32),
        shs=vmem((D, z.Q), BF16), shr=vmem((D, z.Q), BF16), shk=vmem((D, z.Q), F32),
        ls=vmem((rp + HALO, z.Q), F32), lr=vmem((rp + HALO, z.Q), F32),
        sm=vmem((8, z.WL), F32), sa=vmem((blocks, 16, z.WL // 2), BF16), sb2=vmem((ntn, 8, z.WL), F32),
        l_in=dma((2,)),
        wz_send=dma((PIECES, 2, nc, z.SUB)), wd_send=dma((PIECES, nc, nd, z.SUB)), w_recv=dma((PIECES, nd, nc, z.SUB)),
        wh_send=dma((nd,)), wh_recv=dma((nd,)),
        h_send=dma((R,)), h_recv=dma((R,)),
        s_send=dma((R,)), s_recv=dma((R,)), g_send=dma((R,)), g_recv=dma((R,)), e_send=dma((R,)), e_recv=dma((R,)),
        x_send=dma((R, ntn)), x_recv=dma((R, ntn)),
        a_send=dma((2, R)), a_recv=dma((2, R)), b_send=dma((2, R)), b_recv=dma((2, R)),
        c_send=dma((2, R)), c_recv=dma((2, R)),
        ry_send=dma((3, nc, k0)), ry_recv=dma((3, nc, k0)), rz_send=dma((3, nc)), rz_recv=dma((3, nc)),
        sh_send=dma((2,)), sh_recv=dma((2,)),
        st_send=dma((ntn,)), st_recv=dma((ntn,)), sa_send=dma((max(blocks - 1, 1),)), sa_recv=dma((blocks,)),
    )
    names = list(ins) + list(outs) + list(scratch)
    whole = pl.BlockSpec(memory_space=pltpu.VMEM)
    large = pl.BlockSpec(memory_space=pl.ANY)
    raw = pl.pallas_call(
        functools.partial(kernel, z, names),
        out_shape=list(outs.values()),
        in_specs=[large] * 2 + [whole] * (len(ins) - 2),
        out_specs=[whole] * len(outs),
        scratch_shapes=list(scratch.values()),
        compiler_params=pltpu.CompilerParams(
            collective_id=0, has_side_effects=True, vmem_limit_bytes=z.limit
        ),
    )(*ins.values())

    shapes = [
        ((N, D), BF16), ((N, D), BF16), ((D,), F32), ((rows, 2, C), F32), ((S // ntn, rows), F32), ((H, rows), F32),
        ((z.K, C), F32), ((C,), F32), ((z.K, S), F32), ((S,), F32), ((H,), F32), ((H,), F32), ((H,), F32),
        ((C,), F32), ((rows, C), F32),
    ]
    outs = pl.pallas_call(
        functools.partial(finishing, z),
        out_shape=[jax.ShapeDtypeStruct(*shape) for shape in shapes],
        in_specs=[whole] * 6,
        out_specs=[large] * 2 + [whole] * (len(shapes) - 2),
        scratch_shapes=[vmem((LANES, LANES), F32), dma((2,))],
        compiler_params=pltpu.CompilerParams(vmem_limit_bytes=z.limit),
    )(*[pltpu.with_memory_space_constraint(value, pltpu.VMEM) for value in raw])
    (block_out, input_grad, norm, heads, shared, step, taps, bias, staps, sbias, dsb, drate, dskip, gain, outw) = outs
    return (
        narrow(block_out).reshape(hidden_in.shape),
        narrow(input_grad).reshape(hidden_in.shape),
        narrow(norm),
        heads, shared.T, step.T, taps, bias, staps, sbias, dsb, drate, dskip, gain, outw.T,
    )


def solution(mesh):
    nd, nc, ntn = (mesh.shape[name] for name in ("dp", "context", "tensor"))

    def body(*args):
        hidden, heads, shared = args[0], args[3], args[4]
        micro, seqs, tokens, width = hidden.shape
        rows = heads.shape[0]
        rp = -(-rows // 16) * 16
        inner = heads.shape[2]
        z = types.SimpleNamespace(
            R=micro * seqs, T=tokens, d_true=width, D=rp * nd * nc, rows=rows, rp=rp, nd=nd, nc=nc, ntn=ntn,
            C=inner, H=args[10].shape[0], S=shared.shape[1], K=args[6].shape[0],
            Q=shared.shape[1] // 2, limit=59 << 20,
            SUB=3 if rp % 48 == 0 else 1,
        )
        z.WL = max(inner + z.S, z.D, LANES + inner)
        return on_device(z, *args)

    return jax.shard_map(
        body,
        mesh=mesh,
        in_specs=(
            P(None, "dp", "context", None),
            P(None, "dp", None),
            P(),
            P(("dp", "context"), None, "tensor"),
            P(("dp", "context"), None),
            P(("dp", "context"), "tensor"),
            P(None, "tensor"),
            P("tensor"),
            P(),
            P(),
            P("tensor"),
            P("tensor"),
            P("tensor"),
            P("tensor"),
            P("tensor", ("dp", "context")),
            P(None, "dp", "context", None),
        ),
        out_specs=(
            P(None, "dp", "context", None),
            P(None, "dp", "context", None),
            P(),
            P(("dp", "context"), None, "tensor"),
            P(("dp", "context"), "tensor"),
            P(("dp", "context"), "tensor"),
            P(None, "tensor"),
            P("tensor"),
            P(),
            P(),
            P("tensor"),
            P("tensor"),
            P("tensor"),
            P("tensor"),
            P("tensor", ("dp", "context")),
        ),
        check_vma=False,
    )
```

```python
import functools
import types

import jax
import jax.numpy as jnp
from jax import lax
from jax.experimental import pallas as pl
from jax.experimental.pallas import tpu as pltpu
from jax.sharding import PartitionSpec as P

EPS = 1e-05
F32 = jnp.float32
BF16 = jnp.bfloat16
MESH = pl.DeviceIdType.MESH
LANES = 128
HALO = 16
EDGE = 8
PIECES = 4
WIDE = 256
GROUP = 8


def nn(a, b):
    return lax.dot_general(a, b, (((1,), (0,)), ((), ())), preferred_element_type=F32)


def nt(a, b):
    return lax.dot_general(a, b, (((1,), (1,)), ((), ())), preferred_element_type=F32)


def tn(a, b):
    return lax.dot_general(a, b, (((0,), (0,)), ((), ())), preferred_element_type=F32)


def pieces_of(value, count):
    pieces = []
    for _ in range(count):
        piece = value.astype(BF16)
        pieces.append(piece)
        value = value - piece.astype(F32)
    return pieces


def exact_rows(value, ones):
    pieces = [piece.astype(F32) for piece in pieces_of(value, 3)]
    stacked = jnp.concatenate(pieces + [jnp.zeros_like(value)], axis=0).astype(BF16)
    out = nn(stacked, ones)
    return out[0:8] + out[8:16] + out[16:24]


def exact_right(value, ones):
    return sum(nn(piece, ones) for piece in pieces_of(value, 2))


def sigmoid(value):
    return 0.5 * jnp.tanh(0.5 * value) + 0.5


def iota(shape, dim):
    return lax.broadcasted_iota(jnp.int32, shape, dim)


def kernel(z, names, *refs):
    m = types.SimpleNamespace(**dict(zip(names, refs)))
    R, T, D, C, H, S = z.R, z.T, z.D, z.C, z.H, z.S
    rp, nd, nc, ntn = z.rp, z.nd, z.nc, z.ntn
    pairs = H // 2
    head = C // H
    V = C + S
    Z = V + LANES
    Q = z.Q
    BX, CX = slice(0, Q), slice(Q + C, V)
    half = T // 2
    d, c, t = lax.axis_index("dp"), lax.axis_index("context"), lax.axis_index("tensor")
    odd = lax.rem(t, 2)
    across = t + 1 - 2 * odd
    far = lax.rem(t + 2, 4) if ntn == 4 else t

    def at_ctx(k):
        return lax.rem(c + k, nc)

    def at_dp(k):
        return lax.rem(d + k, nd)

    def at_ten(k):
        return lax.rem(t + k, ntn)

    def rows_at(place, size):
        return pl.ds(pl.multiple_of(place * size, 16), size)

    def block(dd, cc):
        return rows_at(dd * nc + cc, rp)

    def row(r):
        return rows_at(r, T)

    def lanes_at(place, size):
        return pl.ds(pl.multiple_of(place, LANES), size)

    def copy(src, dst, send, recv, dev):
        return pltpu.make_async_remote_copy(
            src_ref=src, dst_ref=dst, send_sem=send, recv_sem=recv, device_id=dev, device_id_type=MESH
        )

    def load(which):
        return pltpu.make_async_copy((m.hid, m.cot)[which], (m.hv, m.cv)[which], m.l_in.at[which])

    barrier = pltpu.get_barrier_semaphore()
    others = [(at_dp(k), at_ctx(j), t) for k in range(nd) for j in range(nc) if k or j]
    peers = [(at_dp(k), c, t) for k in range(1, nd)]
    peers += [(d, c, at_ten(k)) for k in range(1, ntn)]
    for peer in peers:
        pl.semaphore_signal(barrier, inc=1, device_id=peer, device_id_type=MESH)
    for here, step in ((c > 0, -1), (c < nc - 1, 1)):

        @pl.when(here)
        def _():
            pl.semaphore_signal(barrier, inc=1, device_id=(d, c + step, t), device_id_type=MESH)


    small_loads = []
    for index, name in enumerate(z.small):
        small_loads.append(pltpu.make_async_copy(getattr(m, name), getattr(m, name + "_v"), m.a_in.at[index]))
        small_loads[-1].start()
        setattr(m, name, getattr(m, name + "_v"))
    load(0).start()
    load(1).start()
    for one in small_loads:
        one.wait()
    m.wall[block(d, c), Q : Q + C] = m.hp[:, 1, :]
    m.wall[block(d, c), lanes_at(odd * (Q + C), Q)] = jnp.where(odd == 0, m.shp[:, :Q], m.shp[:, Q:])
    m.wt[d * nc + c] = jnp.zeros((GROUP, LANES), F32)
    m.wt[d * nc + c, 0:H, 0:rp] = m.stp[...].astype(F32)
    pl.semaphore_wait(barrier, len(peers) + (c > 0).astype(jnp.int32) + (c < nc - 1).astype(jnp.int32))

    def subs(p):
        return z.SUB if p == 0 else 1

    def slot(p, dd, cc, u):
        if p == 1:
            return m.wt.at[dd * nc + cc]
        if p == 3:
            return m.wo.at[block(dd, cc)]
        place, size = ((odd * Q, Q + C), None, (Z, C))[p]
        rows = rp // subs(p)
        return m.wall.at[rows_at((dd * nc + cc) * subs(p) + u, rows), lanes_at(place, size)]

    def w_ctx(p, u, s, right):
        cc, to = (c - s, c + 1) if right else (c + s, c - 1)
        here = slot(p, d, cc, u)
        return copy(here, here, m.wz_send.at[p, int(right), s, u], m.w_recv.at[p, d, cc, u], (d, to, t))

    def w_dp(p, u, cc, k):
        here = slot(p, d, cc, u)
        return copy(here, here, m.wd_send.at[p, cc, k, u], m.w_recv.at[p, d, cc, u], (at_dp(k), c, t))

    def w_arrived(p, u, dd, cc):
        there = slot(p, dd, cc, u)
        copy(there, there, m.wd_send.at[p, cc, 0, u], m.w_recv.at[p, dd, cc, u], (d, c, t)).wait_recv()

    def w_each(p, s, act):
        for u in range(subs(p)):
            if s < nc - 1:
                pl.when((c - s >= 0) & (c < nc - 1))(lambda: act(w_ctx(p, u, s, True)))
                pl.when((c + s < nc) & (c > 0))(lambda: act(w_ctx(p, u, s, False)))
            for k in range(1, nd):
                if s == 0:
                    act(w_dp(p, u, c, k))
                else:
                    pl.when(c - s >= 0)(lambda: act(w_dp(p, u, c - s, k)))
                    pl.when(c + s < nc)(lambda: act(w_dp(p, u, c + s, k)))

    def w_start(p):
        w_each(p, 0, lambda one: one.start())

    def w_step(p, s):
        for u in range(subs(p)):
            for right in (True, False):
                cc = c - s if right else c + s

                @pl.when((cc >= 0) & (cc < nc))
                def _():
                    w_arrived(p, u, d, cc)
                    if s < nc - 1:
                        pl.when(c < nc - 1 if right else c > 0)(lambda: w_ctx(p, u, s, right).start())
                    for k in range(1, nd):
                        w_dp(p, u, cc, k).start()

    def w_rest(p):
        for k in range(1, nd):
            for cc in range(nc):
                for u in range(subs(p)):
                    w_arrived(p, u, at_dp(k), cc)

    def w_sent(p):
        for s in range(nc):
            w_each(p, s, lambda one: one.wait_send())

    def half_rows(dd):
        return rows_at(dd, nc * rp)

    def half_copy(k):
        here = m.wall.at[half_rows(at_dp(k)), lanes_at(odd * (Q + C), Q)]
        return copy(here, here, m.wh_send.at[k], m.wh_recv.at[k], (d, c, across))

    def half_arrived(k):
        there = m.wall.at[half_rows(at_dp(k)), lanes_at((1 - odd) * (Q + C), Q)]
        copy(there, there, m.wh_send.at[k], m.wh_recv.at[k], (d, c, across)).wait_recv()

    def halo_copy(r):
        return copy(
            m.hv.at[pl.ds(pl.multiple_of(r * T + T - HALO, 16), HALO)],
            m.hh.at[rows_at(r, HALO)],
            m.h_send.at[r],
            m.h_recv.at[r],
            (d, c + 1, t),
        )

    w_start(0)
    w_start(1)
    load(0).wait()

    @pl.when(c < nc - 1)
    def _():
        for r in range(R):
            halo_copy(r).start()

    m.wall[block(d, c), Z:] = m.hp[:, 0, :]
    m.wo[block(d, c), :] = m.ow[...]

    m.par[0 : z.K, BX] = m.cs[:, :Q]
    m.par[0 : z.K, Q : Q + C] = m.ch[...]
    m.par[0 : z.K, CX] = m.cs[:, Q:]
    m.par[5:6, :S] = m.bs[...][None]
    m.par[4:5, BX] = m.par[5:6, :Q]
    m.par[4:5, Q : Q + C] = m.bh[...][None]
    m.par[4:5, CX] = m.par[5:6, Q:S]
    m.par[5:6, :C] = m.gg[...][None]
    for h in range(H):
        m.par[6:7, h * head : (h + 1) * head] = jnp.broadcast_to(m.sk[0:1, h : h + 1], (1, head))
    m.gain[0:1, :] = m.ng[...][None]
    m.tile[...] = jnp.zeros_like(m.tile)
    m.tile[0:1, 0:H] = m.sb[...]
    m.tile[1:2, 0:H] = -jnp.exp(m.ld[...])
    turned = jnp.transpose(m.tile[...])
    m.hcol[...] = turned[0:GROUP, :]
    bias_col, rate_col = m.hcol[:, 0:1], m.hcol[:, 1:2]
    gain_in = m.gain[0:1, :]

    def normalize(u):
        u = u.astype(F32)
        mean = jnp.sum(u * u, axis=-1, keepdims=True) * (1.0 / z.d_true)
        return (u * lax.rsqrt(mean + EPS)) * gain_in

    length = m.seg.shape[-1]
    begin = c * T
    seqs = m.seg.shape[1]

    def ids_at(place, size):
        place = pl.multiple_of(place, LANES)
        lines = [m.seg[r // seqs, r % seqs : r % seqs + 1, pl.ds(place, size)] for r in range(R)]
        return jnp.concatenate(lines + [jnp.zeros_like(lines[0])] * (-R % 8), axis=0).astype(F32)

    now = ids_at(begin, T)
    before = jnp.where(c == 0, -1.0, ids_at(jnp.maximum(begin - LANES, 0), LANES))
    behind = jnp.where(c == nc - 1, -2.0, ids_at(jnp.minimum(begin + T, length - LANES), LANES))
    m.segr[...] = now
    m.segb[...] = before
    m.sega[...] = behind
    m.carried[...] = (now == before[:, LANES - 1 : LANES]).astype(F32)
    m.closing[...] = (now == now[:, T - 1 : T]).astype(F32)
    m.tot[...] = jnp.zeros_like(m.tot)
    m.tot[0 : now.shape[0], :] = now
    m.segc[...] = jnp.transpose(m.tot[...])
    away = iota((T, T), 0) - iota((T, T), 1)
    m.lower[...] = (away >= 0).astype(BF16)
    m.upper[...] = (away <= 0).astype(BF16)
    for r in range(R):
        same = m.segc[:, r : r + 1] == m.segr[r : r + 1, :]
        m.past[r] = (same & (away >= 0)).astype(BF16)
        m.next[r] = (same & (away <= 0)).astype(BF16)
        for j in range(1, z.K):
            m.down[r, j - 1] = (same & (away == j)).astype(BF16)
            m.up[r, j - 1] = (same & (away == -j)).astype(BF16)

    @pl.when(c == 0)
    def _():
        m.hh[...] = jnp.zeros_like(m.hh)
        m.sin[...] = jnp.zeros_like(m.sin)

    @pl.when(c == nc - 1)
    def _():
        m.gin[...] = jnp.zeros_like(m.gin)
        m.dce[...] = jnp.zeros_like(m.dce)

    m.sm[...] = jnp.zeros_like(m.sm)
    m.hacc[...] = jnp.zeros_like(m.hacc)
    m.drow[...] = jnp.zeros_like(m.drow)
    m.gstep[...] = jnp.zeros_like(m.gstep)

    @pl.loop(0, R)
    def _(r):
        value = normalize(m.hv[row(r), :]).astype(BF16)
        m.nrm[row(r), :] = value
        m.nrmt[:, row(r)] = jnp.transpose(value)

    load(1).wait()

    @pl.loop(0, R)
    def _(r):
        m.cott[:, row(r)] = jnp.transpose(m.cv[row(r), :])

    reach = iota((HALO, HALO), 1) - HALO - iota((HALO, HALO), 0)
    ahead = iota((HALO, HALO), 1) + HALO - iota((HALO, HALO), 0)
    m.early[...] = jnp.zeros_like(m.early)
    for r in range(R):
        near = m.segc[0:HALO, r : r + 1] == m.segb[r : r + 1, LANES - HALO : LANES]
        late = m.segc[T - HALO : T, r : r + 1] == m.sega[r : r + 1, 0:HALO]
        for j in range(1, z.K):
            first = ((r * (z.K - 1)) + j - 1) * HALO
            m.early[first : first + HALO, r * HALO : (r + 1) * HALO] = (near & (reach == -j)).astype(BF16)
            m.late[r, (j - 1) * HALO : j * HALO, :] = (late & (ahead == j)).astype(BF16)

    w_step(0, 1)
    w_step(1, 1)
    w_start(2)

    @pl.when(c > 0)
    def _():
        for r in range(R):
            halo_copy(r).wait_recv()

    m.nrmh[...] = normalize(m.hh[...]).astype(BF16)
    for s in range(2, nc):
        w_step(0, s)
        w_step(1, s)
        if s == 2:
            w_start(3)
    half_copy(0).start()
    w_step(2, 1)
    w_rest(1)

    m.tile[...] = jnp.zeros_like(m.tile)
    for b in range(nd * nc):
        m.tile[0:GROUP, :] = m.wt[b]
        m.wall[b * rp : (b + 1) * rp, V:Z] = jnp.transpose(m.tile[...])[0:rp, :].astype(BF16)
    w_rest(0)
    for k in range(1, nd):
        half_copy(k).start()
    w_step(3, 1)
    if nc > 2:
        w_step(2, 2)

    low_lanes = iota((T, LANES), 1) < head
    lane = iota((T, LANES), 1)
    fold = (iota((C, LANES), 0) // head == iota((C, LANES), 1)).astype(F32)
    fold_run = fold.astype(BF16)
    fold_through = (
        (iota((C, LANES), 0) // head == iota((C, LANES), 1) - GROUP).astype(F32) - fold
    ).astype(BF16)
    fold_step = (iota((C, LANES), 0) // head == iota((C, LANES), 1) - 2 * GROUP).astype(BF16)
    RUN, STEP, LEAD, TRAIL = 0, GROUP, 2 * GROUP, 3 * GROUP

    def widened(values, base, p):
        a = base + 2 * p
        return jnp.where(low_lanes[: values.shape[0]], values[:, a : a + 1], values[:, a + 1 : a + 2])

    def spread(values, base):
        return jnp.concatenate([widened(values, base, p) for p in range(pairs)], axis=1)

    def state_copy(r):
        return copy(m.ssend.at[r], m.sin.at[r], m.s_send.at[r], m.s_recv.at[r], (d, c + 1, t))

    def grad_copy(r):
        return copy(m.gsend.at[r], m.gin.at[r], m.g_send.at[r], m.g_recv.at[r], (d, c - 1, t))

    def edge_copy(r):
        return copy(m.edge.at[r], m.dce.at[r], m.e_send.at[r], m.e_recv.at[r], (d, c - 1, t))

    def kept(r):
        return spread(m.cols[pl.ds(r * T + T - 1, 1), :], LEAD)

    def pair(p):
        return slice(p * LANES, (p + 1) * LANES)

    def lanes_of(p):
        return slice(Q + p * LANES, Q + (p + 1) * LANES)

    def serve_state(r):
        state_copy(r).wait_recv()

        @pl.when(c < nc - 1)
        def _():
            m.ssend[r] = (m.fresh[r] + kept(r) * m.sin[r].astype(F32)).astype(BF16)
            state_copy(r).start()

    def serve_grad(r):
        grad_copy(r).wait_recv()

        @pl.when(c > 0)
        def _():
            m.gsend[r] = (m.local[r] + kept(r) * m.gin[r].astype(F32)).astype(BF16)
            grad_copy(r).start()

    hops = nc - 1 - c
    soon = R == 4 and nc > 2
    if soon:
        state_late = (c > 2) | ((c == 2) & (nc > 3))
        grad_late = hops > 2
    else:
        state_late, grad_late = c > 0, hops > 0

    def state_point(place, r):
        if soon:
            for who, item in place:
                @pl.when((c == who) & r)
                def _():
                    serve_state(item)

    def grad_point(place, r):
        if soon:
            for who, item in place:
                @pl.when((hops == who) & r)
                def _():
                    serve_grad(item)

    for k in range(nd):
        half_arrived(k)
    halo_v = nn(m.nrmh[...], m.wall[:, :V]).astype(BF16)
    m.hfix[...] = nn(m.early[...], halo_v)

    @pl.loop(0, R)
    def _(r):
        acc = nn(m.nrm[row(r), :], m.wall[:, :Z])
        m.v[row(r), :] = acc[:, :V].astype(BF16)
        raw = jnp.transpose(acc[:, V:].astype(BF16).astype(F32))[0:GROUP]
        pre = raw + bias_col
        step = jnp.maximum(pre, 0.0) + jnp.log1p(jnp.exp(-jnp.abs(pre)))
        m.pre[:, row(r)] = pre
        m.step[:, row(r)] = step
        run = exact_rows(step * rate_col, m.upper[...])
        m.runr[r] = run
        m.tot[0:GROUP, :] = run
        m.tot[GROUP : 2 * GROUP, :] = step
        m.tot[2 * GROUP : 3 * GROUP, :] = jnp.exp(run) * m.carried[pl.ds(r, 1), :]
        m.tot[3 * GROUP : 4 * GROUP, :] = jnp.exp(run[:, T - 1 : T] - run) * m.closing[pl.ds(r, 1), :]
        m.cols[row(r), :] = jnp.transpose(m.tot[...])
        for a in range(0, V, WIDE):
            part = slice(a, min(a + WIDE, V))
            value = m.v[row(r), part]
            conv = value.astype(F32) * m.par[0:1, part] + m.par[4:5, part]
            first = jnp.zeros((EDGE, conv.shape[1]), F32)
            for j in range(1, z.K):
                tap = m.par[j : j + 1, part]
                conv = conv + nn(m.down[r, j - 1], value) * tap
                first = first + m.hfix[pl.ds((r * (z.K - 1) + j - 1) * HALO, EDGE), part] * tap
            conv = jnp.concatenate([conv[0:EDGE] + first, conv[EDGE:]], axis=0)
            logistic = sigmoid(conv)
            m.mix[row(r), part] = (conv * logistic).astype(BF16)
            m.slope[row(r), part] = logistic * (1.0 + conv * (1.0 - logistic))
        state_point([(1, 0)], r == 2)
        state_point([(1, 1)], r == 3)
        for p in range(pairs):
            scaled = m.mix[row(r), lanes_of(p)].astype(F32) * widened(m.cols[row(r), :], STEP, p)
            m.xs[row(r), pair(p)] = scaled.astype(BF16)
            m.xt[row(r), pair(p)] = (scaled * widened(m.cols[row(r), :], TRAIL, p)).astype(BF16)
        m.fresh[r] = tn(m.mix[row(r), BX], m.xt[row(r), :])

        @pl.when(c == 0)
        def _():
            m.ssend[r] = m.fresh[r].astype(BF16)
            state_copy(r).start()

        for s in range(2, nc):
            pl.when(r == min(s - 2, R - 1))(lambda: w_step(3, s))
        for s in range(3, nc):
            pl.when(r == min(s - 3, R - 1))(lambda: w_step(2, s))

    state_point([(2, 0)], True)

    @pl.loop(0, R)
    def _(r):
        b, cm = m.mix[row(r), BX], m.mix[row(r), CX]
        m.scores[...] = nt(cm, b) * m.past[r].astype(F32)
        for p in range(pairs):
            for a in range(0, T, LANES):
                rows, seen = slice(a, a + LANES), a + LANES
                here = pl.ds(pl.multiple_of(r * T, 16) + a, LANES)
                both = []
                for h in (2 * p, 2 * p + 1):
                    decay = jnp.exp(jnp.minimum(m.cols[here, h : h + 1] - m.runr[r, h : h + 1, :seen], 0.0))
                    weight = (decay * m.scores[rows, :seen]).astype(BF16)
                    both.append(nn(weight, m.xs[pl.ds(pl.multiple_of(r * T, 16), seen), pair(p)]))
                m.ins[here, pair(p)] = jnp.where(low_lanes[:LANES], both[0], both[1])
        state_point([(1, 2)], r == 0)
        state_point([(2, 1)], r == 2)

    state_point([(1, 3)], True)
    w_rest(2)
    w_rest(3)

    def sums_copy(r, k):
        return copy(
            m.sums.at[t, r], m.sums.at[t, r], m.x_send.at[r, k], m.x_recv.at[r, t], (d, c, at_ten(k))
        )

    def sums_arrived(r, who):
        copy(
            m.sums.at[who, r], m.sums.at[who, r], m.x_send.at[r, 0], m.x_recv.at[r, who], (d, c, t)
        ).wait_recv()

    def mine(r):
        return pl.ds(pl.multiple_of(r * T + odd * half, 16), half)

    def theirs(r):
        return pl.ds(pl.multiple_of(r * T + (1 - odd) * half, 16), half)

    def near_copy(a, r):
        return copy(m.as_.at[a, r], m.ar_.at[a, r], m.a_send.at[a, r], m.a_recv.at[a, r], (d, c, across))

    def far_copy(a, r):
        return copy(m.bs_.at[a, r], m.br_.at[a, r], m.b_send.at[a, r], m.b_recv.at[a, r], (d, c, far))

    def back_copy(a, r):
        out = (m.out, m.ing)[a].at[mine(r)]
        return copy(out, out, m.c_send.at[a, r], m.c_recv.at[a, r], (d, c, across))

    def back_arrived(a, r):
        out = (m.out, m.ing)[a].at[theirs(r)]
        copy(out, out, m.c_send.at[a, r], m.c_recv.at[a, r], (d, c, across)).wait_recv()

    def give(a, r, value):
        first, second = value[:half], value[half:]
        m.as_[a, r] = jnp.where(odd == 0, second, first).astype(BF16)
        near_copy(a, r).start()
        m.keep[r] = jnp.where(odd == 0, first, second)

    def chip_sum(a, r):
        near_copy(a, r).wait_recv()
        m.bs_[a, r] = (m.keep[r] + m.ar_[a, r].astype(F32)).astype(BF16)
        if ntn == 4:
            far_copy(a, r).start()

    def full_sum(a, r):
        total = m.bs_[a, r].astype(F32)
        if ntn == 4:
            far_copy(a, r).wait_recv()
            total = total + m.br_[a, r].astype(F32)
        return total

    def serve_late(r):
        if soon and nc > 3:
            pl.when((c > 2) | (r >= 2))(lambda: serve_state(r))
        else:
            serve_state(r)

    def gating(r):
        pl.when(state_late)(lambda: serve_late(r))
        cm = m.mix[row(r), CX]
        gate = nn(m.nrm[row(r), :], m.wall[:, Z:])
        m.zv[row(r), :] = gate.astype(BF16)
        m.dy[row(r), :] = nn(m.cv[row(r), :], m.wo[...])
        m.ys[row(r), :] = nn(cm, m.sin[r])
        squares = jnp.zeros((T, LANES), F32)
        inner = jnp.zeros((T, LANES), F32)
        for p in range(pairs):
            carried = m.ys[row(r), pair(p)] * widened(m.cols[row(r), :], LEAD, p)
            m.ys[row(r), pair(p)] = carried
            ssd = m.ins[row(r), pair(p)] + carried + m.par[6:7, pair(p)] * m.mix[row(r), lanes_of(p)].astype(F32)
            m.ssd[row(r), pair(p)] = ssd
            gate = m.zv[row(r), pair(p)].astype(F32)
            gated = ssd * (gate * sigmoid(gate))
            m.gated[row(r), pair(p)] = gated
            scaled = gated * m.par[5:6, pair(p)]
            m.yg[row(r), pair(p)] = scaled.astype(BF16)
            squares = squares + gated * gated
            inner = inner + scaled * m.dy[row(r), pair(p)]
        squares = jnp.sum(squares, axis=-1, keepdims=True)
        inner = jnp.sum(inner, axis=-1, keepdims=True)
        both = jnp.where(lane == 0, squares, jnp.where(lane == 1, inner, 0.0))
        m.sums[t, r] = jnp.transpose(both)[0:8, :]
        for k in range(1, ntn):
            sums_copy(r, k).start()
        give(0, r, nt(m.yg[row(r), :], m.wo[...]))

    def ungating(r):
        for k in range(1, ntn):
            sums_arrived(r, at_ten(k))
        total = m.sums[0, r]
        for who in range(1, ntn):
            total = total + m.sums[who, r]
        scale = lax.rsqrt(total[0:1] * (1.0 / (C * ntn)) + EPS)
        inner = total[1:2] * (1.0 / (C * ntn)) * scale * scale * scale
        m.tot[0:1, :] = scale
        m.tot[1:2, :] = inner
        columns = jnp.transpose(m.tot[...])
        m.rms[row(r), :] = columns
        scale = jnp.broadcast_to(columns[:, 0:1], (T, LANES))
        inner = jnp.broadcast_to(columns[:, 1:2], (T, LANES))
        for p in range(pairs):
            gated, dy, ssd = m.gated[row(r), pair(p)], m.dy[row(r), pair(p)], m.ssd[row(r), pair(p)]
            gate = m.zv[row(r), pair(p)].astype(F32)
            gain = m.par[5:6, pair(p)]
            normal = gated * scale
            m.sm[5:6, pair(p)] += jnp.sum(dy * normal, axis=0, keepdims=True)
            m.yg[row(r), pair(p)] = (normal * gain).astype(BF16)
            d_gated = scale * dy * gain - gated * inner
            logistic = sigmoid(gate)
            m.dcat[row(r), Z + p * LANES : Z + (p + 1) * LANES] = (
                d_gated * ssd * (logistic * (1.0 + gate * (1.0 - logistic)))
            ).astype(BF16)
            d_ssd = d_gated * (gate * logistic)
            m.ssd[row(r), pair(p)] = d_ssd
            m.wds[row(r), pair(p)] = (d_ssd * widened(m.cols[row(r), :], LEAD, p)).astype(BF16)
        m.local[r] = tn(m.mix[row(r), CX], m.wds[row(r), :])

        @pl.when(c == nc - 1)
        def _():
            m.gsend[r] = m.local[r].astype(BF16)
            if nc > 1:
                grad_copy(r).start()

    @pl.loop(0, R + 2)
    def _(i):
        pl.when(i < R)(lambda: gating(i))

        @pl.when(i >= 2)
        def _():
            ungating(i - 2)

        grad_point([(1, 0)], i == R + 1)

        @pl.when(i == R - 1)
        def _():
            pl.loop(0, R - 1)(lambda r: chip_sum(0, r))

        pl.when(i == R)(lambda: chip_sum(0, R - 1))

    gall, gyr, gzs, gzr = (m.ga0, m.ga1, m.ga2), (m.gy0, m.gy1, m.gy2), (m.gz0, m.gz1, m.gz2), (m.gr0, m.gr1, m.gr2)
    tall = (rp, rp, rp + HALO)

    def rs_dp(part, j, k):
        cc = at_ctx(j)
        return copy(
            gall[part].at[rows_at(at_dp(k) * nc + cc, tall[part])],
            gyr[part].at[k - 1, rows_at(cc, tall[part])],
            m.ry_send.at[part, j, k - 1],
            m.ry_recv.at[part, j, k - 1],
            (at_dp(k), c, t),
        )

    def rs_ctx(part, j):
        cc = at_ctx(j)
        return copy(
            gzs[part].at[rows_at(cc, tall[part])],
            gzr[part].at[c],
            m.rz_send.at[part, j],
            m.rz_recv.at[part, c],
            (d, cc, t),
        )

    def rs_arrived(part, cc):
        copy(gzr[part].at[cc], gzr[part].at[cc], m.rz_send.at[part, 0], m.rz_recv.at[part, cc], (d, c, t)).wait_recv()

    def rs_start(part):
        for j in list(range(1, nc)) + [0]:
            for k in range(1, nd):
                rs_dp(part, j, k).start()

    def rs_middle(part, j):
        cc = at_ctx(j)
        total = gall[part][rows_at(d * nc + cc, tall[part]), :].astype(F32)
        for k in range(1, nd):
            rs_dp(part, j, k).wait_recv()
            total = total + gyr[part][k - 1, rows_at(cc, tall[part]), :].astype(F32)
        own = j == 0

        def keep():
            gzr[part][c] = total.astype(BF16)

        def send():
            gzs[part][rows_at(cc, tall[part]), :] = total.astype(BF16)
            rs_ctx(part, j).start()

        if isinstance(j, int):
            keep() if own else send()
        else:
            pl.when(own)(keep)
            pl.when(jnp.logical_not(own))(send)

    def rs_end(part):
        for k in range(1, nc):
            rs_arrived(part, at_ctx(k))
        total = gzr[part][0].astype(F32)
        for cc in range(1, nc):
            total = total + gzr[part][cc].astype(F32)
        return total

    def rs_sent(part):
        for j in range(nc):
            for k in range(1, nd):
                rs_dp(part, j, k).wait_send()
            if j:
                rs_ctx(part, j).wait_send()

    m.ga1[:, C:] = nn(m.cott[...], m.yg[...]).astype(BF16)
    m.ga1[:, :C] = nn(m.nrmt[...], m.dcat[:, Z:]).astype(BF16)
    rs_start(1)
    grad_point([(1, 1), (1, 2), (2, 0)], True)

    @pl.loop(0, R)
    def _(r):
        b, cm = m.mix[row(r), BX], m.mix[row(r), CX]
        m.scores[...] = nt(b, cm) * m.next[r].astype(F32)
        start = pl.multiple_of(r * T, 16)
        for a in range(0, T, LANES):
            rows, here, after = slice(a, a + LANES), pl.ds(start + a, LANES), pl.ds(start + a, T - a)
            losses = jnp.zeros((LANES, LANES), F32)
            for p in range(pairs):
                ds_pair = m.ssd[after, pair(p)].astype(BF16)
                xs_pair = m.xs[here, pair(p)]
                both = []
                for h in (2 * p, 2 * p + 1):
                    pick = low_lanes[:LANES] if h % 2 == 0 else ~low_lanes[:LANES]
                    decay = jnp.exp(jnp.minimum(m.runr[r, h : h + 1, a:] - m.cols[here, h : h + 1], 0.0))
                    weight = decay * m.scores[rows, a:]
                    both.append(nn(weight.astype(BF16), ds_pair))
                    d_weight = nt(jnp.where(pick, xs_pair, jnp.zeros_like(xs_pair)), ds_pair)
                    flow = d_weight * weight
                    if h == 0:
                        m.dsc[rows, a:] = d_weight * decay
                    else:
                        m.dsc[rows, a:] += d_weight * decay
                    losses = jnp.where(lane[:LANES] == h, jnp.sum(flow, axis=1, keepdims=True), losses)
                    down = jnp.sum(flow, axis=0, keepdims=True)
                    if a == 0:
                        m.drow[r, h : h + 1, :] = down
                    else:
                        m.drow[r, h : h + 1, a:] += down
                m.ins[here, pair(p)] = jnp.where(low_lanes[:LANES], both[0], both[1])
            m.drun[here, :] = exact_right(m.ssd[here, :] * m.ys[here, :], fold_run) - losses
            d_scores = (m.dsc[rows, a:] * m.next[r, rows, a:].astype(F32)).astype(BF16)
            m.gated[here, :LANES] = nn(d_scores, m.mix[after, CX])
            d_after = tn(d_scores, m.mix[here, BX])
            if a == 0:
                m.gated[after, LANES:S] = d_after
            else:
                m.gated[after, LANES:S] += d_after

        grad_point([(1, 3), (2, 1)], r == 0)
        grad_point([(2, 2)], r == 1)
        grad_point([(2, 3)], r == 2)

    def final_out(r):
        value = m.hv[mine(r), :].astype(F32) + m.rms[mine(r), 0:1] * full_sum(0, r)
        m.out[mine(r), :] = value.astype(BF16)
        back_copy(0, r).start()

    def adjoint(r):
        pl.when(grad_late)(lambda: serve_grad(r))
        b = m.mix[row(r), BX]
        grad = m.gin[r]
        for p in range(pairs):
            trailing = widened(m.cols[row(r), :], TRAIL, p)
            reach = nn(b, m.gin[r, :, pair(p)]) * trailing
            x = m.mix[row(r), lanes_of(p)].astype(F32)
            d_xs = m.ins[row(r), pair(p)] + reach
            d_ssd = m.ssd[row(r), pair(p)]
            m.prod[:, pair(p)] = m.xs[row(r), pair(p)].astype(F32) * reach
            m.prod[:, C + p * LANES : C + (p + 1) * LANES] = d_xs * x
            m.sm[7:8, LANES + p * LANES : 2 * LANES + p * LANES] += jnp.sum(d_ssd * x, axis=0, keepdims=True)
            m.dy[row(r), pair(p)] = (
                d_xs * widened(m.cols[row(r), :], STEP, p) + m.par[6:7, pair(p)] * d_ssd
            ) * m.slope[row(r), lanes_of(p)]
        m.gated[row(r), :Q] = (
            m.gated[row(r), :LANES] + nt(m.xt[row(r), :], grad)
        ) * m.slope[row(r), BX]
        m.gated[row(r), Q:S] = (
            m.gated[row(r), LANES:S] + nt(m.wds[row(r), :], m.sin[r])
        ) * m.slope[row(r), CX]

        @pl.when(c > 0)
        def _():
            first = pl.ds(pl.multiple_of(r * T, 16), EDGE)
            m.edge[r, :, BX] = m.gated[first, :Q]
            m.edge[r, :, Q : Q + C] = m.dy[first, :]
            m.edge[r, :, CX] = m.gated[first, Q:S]
            edge_copy(r).start()

        m.drun[row(r), :] += exact_right(m.prod[:, :C], fold_through) + exact_right(m.prod[:, C:], fold_step)
        joint = jnp.sum(grad.astype(F32) * m.sin[r].astype(F32), axis=0, keepdims=True)
        joint = exact_right(jnp.broadcast_to(joint, (8, C)), fold_run)[0:1]
        last = m.cols[pl.ds(r * T + T - 1, 1), :]
        kept_lanes = jnp.concatenate([last[:, LEAD : LEAD + H], jnp.zeros((1, LANES - H), F32)], axis=1)
        m.drun[pl.ds(r * T + T - 1, 1), :] += joint * kept_lanes
        turned = jnp.transpose(m.drun[row(r), :])
        through = jnp.sum(turned[GROUP : 2 * GROUP], axis=1, keepdims=True)
        d_run = turned[0:GROUP] + m.drow[r]
        d_run = d_run + jnp.where(iota((GROUP, T), 1) == T - 1, through, 0.0)
        d_growth = exact_rows(d_run, m.lower[...])
        d_step = turned[2 * GROUP : 3 * GROUP] + rate_col * d_growth
        d_pre = d_step * sigmoid(m.pre[:, row(r)])
        m.hacc[0:GROUP, :] += d_pre
        m.hacc[GROUP : 2 * GROUP, :] += m.step[:, row(r)] * d_growth * rate_col
        d_pre = jnp.where(iota((GROUP, T), 0) < H, d_pre, 0.0)
        m.gstep[...] += nn(jnp.concatenate([d_pre, jnp.zeros_like(d_pre)], axis=0).astype(BF16), m.nrm[row(r), :])
        m.tot[0:GROUP, :] = d_pre
        m.dcat[row(r), V:Z] = jnp.transpose(m.tot[...]).astype(BF16)

    def finish(r):
        @pl.when(c < nc - 1)
        def _():
            edge_copy(r).wait_recv()

        edge = m.dce[r]
        edge = jnp.concatenate([edge, jnp.zeros_like(edge)], axis=0).astype(BF16)
        m.lfix[...] = nn(m.late[r], edge)
        cuts = [(m.gated, 0, 0, Q), (m.gated, Q, Q + C, Q)]
        cuts += [(m.dy, a, Q + a, min(WIDE, C - a)) for a in range(0, C, WIDE)]
        for held, place, first, size in cuts:
            part = slice(first, first + size)
            d_conv = held[row(r), place : place + size]
            low = d_conv.astype(BF16)
            value = m.v[row(r), part].astype(F32)
            m.sm[4:5, part] += jnp.sum(d_conv, axis=0, keepdims=True)
            m.sm[0:1, part] += jnp.sum(d_conv * value, axis=0, keepdims=True)
            d_v = d_conv * m.par[0:1, part]
            for j in range(1, z.K):
                moved = nn(m.up[r, j - 1], low)
                moved = jnp.concatenate(
                    [moved[: T - HALO], moved[T - HALO :] + m.lfix[(j - 1) * HALO : j * HALO, part]], axis=0
                )
                d_v = d_v + moved * m.par[j : j + 1, part]
                m.sm[j : j + 1, part] += jnp.sum(moved * value, axis=0, keepdims=True)
            m.dcat[row(r), part] = d_v.astype(BF16)

    def finish_norm(r):
        value = nt(m.dcat[row(r), :], m.wall[...])
        give(1, r, value)
        u = m.hv[row(r), :].astype(F32)
        mean = jnp.sum(u * u, axis=-1, keepdims=True) * (1.0 / z.d_true)
        m.sm[6:7, :D] += jnp.sum(value * (u * lax.rsqrt(mean + EPS)), axis=0, keepdims=True)

    m.tot[...] = jnp.zeros_like(m.tot)

    def first_sums(j, upward):
        up = c + j < nc
        pl.when(up if upward else jnp.logical_not(up))(lambda: rs_middle(1, j))

    @pl.loop(0, R)
    def _(r):
        pl.when(r == 0)(lambda: final_out(0))
        adjoint(r)
        for j in range(1, min(nc, 3)):
            pl.when(r == min(2 * j - 2, R - 1))(lambda: first_sums(j, True))

    @pl.loop(0, R)
    def _(r):
        finish(r)
        pl.when(r < 3)(lambda: finish_norm(r))
        pl.when((r >= 1) & (r - 1 < 3))(lambda: chip_sum(1, r - 1))
        for k in range(1, R - 1):
            pl.when(r == min(2 * k - 1, R - 1))(lambda: final_out(k))
        for j in range(3, nc):
            pl.when(r == min(j - 1, R - 1))(lambda: first_sums(j, True))
        for j in range(1, nc):
            pl.when(r == min(j - 1, R - 1))(lambda: first_sums(j, False))

    def small_copy(index):
        return copy(m.sa.at[d * nc + c], m.sa.at[d * nc + c], m.sa_send.at[index], m.sa_recv.at[d * nc + c], others[index])

    def small_arrived(dd, cc):
        there = m.sa.at[dd * nc + cc]
        copy(there, there, m.sa_send.at[0], m.sa_recv.at[dd * nc + cc], (d, c, t)).wait_recv()

    def common_copy(k):
        return copy(m.sb2.at[t], m.sb2.at[t], m.st_send.at[k], m.st_recv.at[t], (d, c, at_ten(k)))

    def common_arrived(who):
        copy(m.sb2.at[who], m.sb2.at[who], m.st_send.at[0], m.st_recv.at[who], (d, c, t)).wait_recv()

    width = S // ntn
    starts = [k * width + (C if k * width >= Q else 0) for k in range(ntn)]
    quarters = [m.dcat[:, first : first + width] for first in starts]
    value = nn(m.nrmt[...], jnp.concatenate(quarters[0::2] + quarters[1::2], axis=1))

    def share_copy():
        return copy(m.shs, m.shr, m.sh_send.at[0], m.sh_recv.at[0], (d, c, across))

    m.shk[...] = jnp.where(odd == 0, value[:, : z.Q], value[:, z.Q :])
    m.shs[...] = jnp.where(odd == 0, value[:, z.Q :], value[:, : z.Q]).astype(BF16)
    share_copy().start()

    m.ga0[...] = nn(m.nrmt[...], m.dcat[:, Q : Q + C]).astype(BF16)
    share_copy().wait_recv()
    for b in range(nd * nc):
        here = slice(b * rp, (b + 1) * rp)
        there = b * (rp + HALO)
        m.ga2[there : there + rp, :] = (m.shk[here, :] + m.shr[here, :].astype(F32)).astype(BF16)
        steps = m.gstep[:, here]
        m.ga2[there + rp : there + rp + HALO, :] = jnp.concatenate(
            [steps, jnp.zeros((HALO, LANES - rp), F32)], axis=1
        ).astype(BF16)
    rs_start(2)
    rs_start(0)

    @pl.loop(3, R)
    def _(r):
        finish_norm(r)
        pl.when(r == max(2, 3))(lambda: final_out(R - 1))
        pl.when(r == 3)(lambda: rs_middle(1, 0))
        pl.when(r >= 4)(lambda: chip_sum(1, r - 1))

    m.tile[...] = jnp.zeros_like(m.tile)
    m.tile[0 : 2 * GROUP, :] = jnp.broadcast_to(
        jnp.sum(m.hacc[...], axis=1, keepdims=True), (2 * GROUP, LANES)
    )
    m.sm[7:8, 0:LANES] = jnp.transpose(m.tile[...])[0:1, :]
    m.sa[d * nc + c] = jnp.concatenate([m.sm[:, : z.WL // 2], m.sm[:, z.WL // 2 :]], axis=0).astype(BF16)
    for index in range(len(others)):
        small_copy(index).start()

    chip_sum(1, R - 1)

    def last_copy():
        return copy(m.ls, m.lr, m.sh_send.at[1], m.sh_recv.at[1], (d, c, far))

    def input_row(r):
        u = m.hv[mine(r), :].astype(F32)
        mean = jnp.sum(u * u, axis=-1, keepdims=True) * (1.0 / z.d_true)
        scale = lax.rsqrt(mean + EPS)
        unit = u * scale
        d_unit = full_sum(1, r) * gain_in
        inner = jnp.sum(d_unit * unit, axis=-1, keepdims=True) * (1.0 / z.d_true)
        value = m.cv[mine(r), :].astype(F32) + scale * (d_unit - unit * inner)
        m.ing[mine(r), :] = value.astype(BF16)
        back_copy(1, r).start()

    for r in range(R):
        back_arrived(0, r)
    for j in list(range(1, nc)) + [0]:
        rs_middle(2, j)
    m.gw1[...] = rs_end(1)

    @pl.loop(0, R)
    def _(r):
        input_row(r)
        pl.when(r >= 1)(lambda: back_arrived(1, r - 1))

        @pl.when(r == 0)
        def _():
            rs_middle(0, 1 % nc)

        @pl.when(r == min(2, R - 1))
        def _():
            for dd in range(nd):
                for cc in range(nc):
                    pl.when((dd != d) | (cc != c))(lambda: small_arrived(dd, cc))
            total = m.sa[0].astype(F32)
            for who in range(1, nd * nc):
                total = total + m.sa[who].astype(F32)
            m.sb2[t] = jnp.concatenate([total[0:8], total[8:16]], axis=1)
            for k in range(1, ntn):
                common_copy(k).start()

        @pl.when(r == 1)
        def _():
            for j in list(range(2, nc)) + ([0] if nc > 1 else []):
                rs_middle(0, j)

        @pl.when(r == min(2, R - 1))
        def _():
            value = rs_end(2)
            if ntn == 4:
                m.ls[...] = value
                last_copy().start()
            else:
                m.gw2[...] = value

    for k in range(1, ntn):
        common_arrived(at_ten(k))
    common = m.sb2[0]
    for who in range(1, ntn):
        common = common + m.sb2[who]
    rows8, lanes8 = iota((8, z.WL), 0), iota((8, z.WL), 1)
    shared_here = (rows8 == 6) | ((rows8 < 5) & ((lanes8 < Q) | (lanes8 >= Q + C)))
    m.small[...] = jnp.where(shared_here, common, m.sb2[t])
    m.gw0[...] = rs_end(0)
    if ntn == 4:
        last_copy().wait_recv()
        m.gw2[0:rp, :] = m.ls[0:rp, :] + m.lr[0:rp, :]
        m.gw2[rp:, :] = m.ls[rp:, :]
        last_copy().wait_send()
    back_arrived(1, R - 1)

    for a in range(2):
        for r in range(R):
            back_copy(a, r).wait_send()
            near_copy(a, r).wait_send()
            if ntn == 4:
                far_copy(a, r).wait_send()
    for p in range(PIECES):
        w_sent(p)
    for k in range(nd):
        half_copy(k).wait_send()
    for part in range(3):
        rs_sent(part)
    for r in range(R):
        for k in range(1, ntn):
            sums_copy(r, k).wait_send()

        @pl.when(c < nc - 1)
        def _():
            halo_copy(r).wait_send()
            state_copy(r).wait_send()

        @pl.when(c > 0)
        def _():
            grad_copy(r).wait_send()
            edge_copy(r).wait_send()

    share_copy().wait_send()
    for index in range(len(others)):
        small_copy(index).wait_send()
    for k in range(1, ntn):
        common_copy(k).wait_send()


def finishing(z, out, ing, gw0, gw1, gw2, small, *outs):
    (o_out, o_ing, norm, heads, shared, step, taps, bias, staps, sbias, dsb, drate, dskip, gain, outw, tile, sems) = outs
    C, S, D, H, rp, rows = z.C, z.S, z.D, z.H, z.rp, z.rows
    V = C + S
    head = C // H
    moves = [pltpu.make_async_copy(out, o_out, sems.at[0]), pltpu.make_async_copy(ing, o_ing, sems.at[1])]
    for move in moves:
        move.start()
    norm[...] = small[6, :D]
    heads[:, 0, :] = gw1[0:rows, :C]
    heads[:, 1, :] = gw0[0:rows, :]
    width = S // z.ntn
    tile[...] = jnp.zeros_like(tile)
    tile[0:rp, :] = gw2[0:rp, :]
    pair = jnp.transpose(tile[...])
    if z.ntn == 4:
        upper = lax.axis_index("tensor") >= 2
        pair = jnp.where(upper, pair[width:], pair[:width])
    shared[...] = pair[:, 0:rows]
    step[...] = gw2[rp : rp + H, 0:rows]
    Q = z.Q
    taps[...] = small[0 : z.K, Q : Q + C]
    bias[...] = small[4, Q : Q + C]
    staps[:, :Q] = small[0 : z.K, :Q]
    staps[:, Q:] = small[0 : z.K, Q + C : V]
    sbias[...] = jnp.concatenate([small[4:5, :Q], small[4:5, Q + C : V]], axis=1)[0]
    dsb[...] = small[7, :H]
    drate[...] = small[7, GROUP : GROUP + H]
    lanes = iota((1, H), 1)
    skip = jnp.zeros((1, H), F32)
    for h in range(H):
        begin = LANES + h * head
        skip = jnp.where(lanes == h, jnp.sum(small[7:8, begin : begin + head], axis=1, keepdims=True), skip)
    tile[0:1, 0:H] = skip
    dskip[...] = tile[0, 0:H]
    gain[...] = small[5, :C]
    outw[...] = gw1[0:rows, C:]
    for move in moves:
        move.wait()


def on_device(z, hidden_in, segment_ids, norm_gain, head_projection, shared_projection, step_projection,
              conv_heads, bias_heads, conv_shared, bias_shared, step_bias, log_decay, skip_gain, gate_gain,
              output_weight, out_cotangent):
    R, T, D, C, H, S = z.R, z.T, z.D, z.C, z.H, z.S
    rp, nd, nc, ntn, rows = z.rp, z.nd, z.nc, z.ntn, z.rows
    V = C + S
    blocks = nd * nc
    R8 = 8 * -(-R // 8)

    def widen(value):
        if rp == rows:
            return value
        value = value.reshape(value.shape[:-1] + (blocks, rows))
        value = jnp.pad(value, [(0, 0)] * (value.ndim - 1) + [(0, rp - rows)])
        return value.reshape(value.shape[:-2] + (D,))

    def narrow(value):
        if rp == rows:
            return value
        return value.reshape(value.shape[:-1] + (blocks, rp))[..., :rows].reshape(value.shape[:-1] + (z.d_true,))

    def taller(value, dim):
        if rp == rows:
            return value
        return jnp.pad(value, [(0, rp - rows if k == dim else 0) for k in range(value.ndim)])

    dma, vmem = pltpu.SemaphoreType.DMA, pltpu.VMEM
    N = R * T
    half = T // 2
    k0 = max(nd - 1, 1)
    ins = dict(
        hid=widen(hidden_in.reshape(N, z.d_true)), cot=widen(out_cotangent.reshape(N, z.d_true)),
        seg=segment_ids, ng=widen(norm_gain), hp=taller(head_projection, 0),
        shp=taller(shared_projection, 0), stp=taller(step_projection.T, 1), ow=taller(output_weight.T, 0),
        ch=conv_heads, bh=bias_heads, cs=conv_shared, bs=bias_shared, sb=step_bias[None],
        ld=log_decay[None], sk=skip_gain[None], gg=gate_gain,
    )
    outs = dict(
        out=pltpu.VMEM((N, D), BF16),
        ing=pltpu.VMEM((N, D), BF16),
        gw0=pltpu.VMEM((rp, C), F32),
        gw1=pltpu.VMEM((rp, 2 * C), F32),
        gw2=pltpu.VMEM((rp + HALO, z.Q), F32),
        small=pltpu.VMEM((8, z.WL), F32),
    )
    scratch = dict(
        hv=vmem((N, D), BF16), cv=vmem((N, D), BF16),
        wall=vmem((D, V + LANES + C), BF16), wo=vmem((D, C), BF16), wt=vmem((blocks, GROUP, LANES), F32),
        hcol=vmem((GROUP, LANES), F32), tile=vmem((LANES, LANES), F32), gain=vmem((8, D), F32), par=vmem((16, V), F32),
        segc=vmem((T, LANES), F32), segr=vmem((R8, T), F32), carried=vmem((R8, T), F32), closing=vmem((R8, T), F32),
        segb=vmem((R8, LANES), F32), sega=vmem((R8, LANES), F32),
        early=vmem((R * (z.K - 1) * HALO, R * HALO), BF16), late=vmem((R, (z.K - 1) * HALO, HALO), BF16),
        hfix=vmem((R * (z.K - 1) * HALO, V), F32), lfix=vmem(((z.K - 1) * HALO, V), F32),
        down=vmem((R, z.K - 1, T, T), BF16), up=vmem((R, z.K - 1, T, T), BF16), lower=vmem((T, T), BF16), upper=vmem((T, T), BF16),
        past=vmem((R, T, T), BF16), next=vmem((R, T, T), BF16),
        hh=vmem((R * HALO, D), BF16), nrmh=vmem((R * HALO, D), BF16),
        nrm=vmem((N, D), BF16), nrmt=vmem((D, N), BF16), cott=vmem((D, N), BF16),
        v=vmem((N, V), BF16), mix=vmem((N, V), BF16), slope=vmem((N, V), F32),
        pre=vmem((GROUP, N), F32), step=vmem((GROUP, N), F32), cols=vmem((N, LANES), F32), xt=vmem((N, C), BF16),
        runr=vmem((R, 8, T), F32), xs=vmem((N, C), BF16),
        fresh=vmem((R, LANES, C), F32), local=vmem((R, LANES, C), F32),
        ssend=vmem((R, LANES, C), BF16), sin=vmem((R, LANES, C), BF16),
        gsend=vmem((R, LANES, C), BF16), gin=vmem((R, LANES, C), BF16),
        scores=vmem((T, T), F32), dsc=vmem((T, T), F32), drow=vmem((R, GROUP, T), F32), tot=vmem((LANES, T), F32),
        ins=vmem((N, C), F32), ys=vmem((N, C), F32), ssd=vmem((N, C), F32), zv=vmem((N, C), BF16),
        gated=vmem((N, max(C, S)), F32), dy=vmem((N, C), F32),
        yg=vmem((N, C), BF16), wds=vmem((N, C), BF16),
        rms=vmem((N, LANES), F32), sums=vmem((ntn, R, 8, T), F32),
        as_=vmem((2, R, half, D), BF16), ar_=vmem((2, R, half, D), BF16),
        bs_=vmem((2, R, half, D), BF16), br_=vmem((2, R, half, D), BF16), keep=vmem((R, half, D), F32),
        ga0=vmem((D, C), BF16), ga1=vmem((D, 2 * C), BF16), ga2=vmem((blocks * (rp + HALO), z.Q), BF16),
        gy0=vmem((k0, nc * rp, C), BF16), gy1=vmem((k0, nc * rp, 2 * C), BF16), gy2=vmem((k0, nc * (rp + HALO), z.Q), BF16),
        gz0=vmem((nc * rp, C), BF16), gz1=vmem((nc * rp, 2 * C), BF16), gz2=vmem((nc * (rp + HALO), z.Q), BF16),
        gr0=vmem((nc, rp, C), BF16), gr1=vmem((nc, rp, 2 * C), BF16), gr2=vmem((nc, rp + HALO, z.Q), BF16),
        drun=vmem((N, LANES), F32), edge=vmem((R, EDGE, V), F32),
        dce=vmem((R, EDGE, V), F32), dcat=vmem((N, V + LANES + C), BF16),
        prod=vmem((T, 2 * C), F32), hacc=vmem((2 * GROUP, T), F32), gstep=vmem((HALO, D), F32),
        shs=vmem((D, z.Q), BF16), shr=vmem((D, z.Q), BF16), shk=vmem((D, z.Q), F32),
        ls=vmem((rp + HALO, z.Q), F32), lr=vmem((rp + HALO, z.Q), F32),
        sm=vmem((8, z.WL), F32), sa=vmem((blocks, 16, z.WL // 2), BF16), sb2=vmem((ntn, 8, z.WL), F32),
        l_in=dma((2,)),
        wz_send=dma((PIECES, 2, nc, z.SUB)), wd_send=dma((PIECES, nc, nd, z.SUB)), w_recv=dma((PIECES, nd, nc, z.SUB)),
        wh_send=dma((nd,)), wh_recv=dma((nd,)),
        h_send=dma((R,)), h_recv=dma((R,)),
        s_send=dma((R,)), s_recv=dma((R,)), g_send=dma((R,)), g_recv=dma((R,)), e_send=dma((R,)), e_recv=dma((R,)),
        x_send=dma((R, ntn)), x_recv=dma((R, ntn)),
        a_send=dma((2, R)), a_recv=dma((2, R)), b_send=dma((2, R)), b_recv=dma((2, R)),
        c_send=dma((2, R)), c_recv=dma((2, R)),
        ry_send=dma((3, nc, k0)), ry_recv=dma((3, nc, k0)), rz_send=dma((3, nc)), rz_recv=dma((3, nc)),
        sh_send=dma((2,)), sh_recv=dma((2,)),
        st_send=dma((ntn,)), st_recv=dma((ntn,)), sa_send=dma((max(blocks - 1, 1),)), sa_recv=dma((blocks,)),
    )
    z.small = list(ins)[2:]
    for name in z.small:
        scratch[name + "_v"] = vmem(ins[name].shape, ins[name].dtype)
    scratch["a_in"] = dma((len(z.small),))
    names = list(ins) + list(outs) + list(scratch)
    whole = pl.BlockSpec(memory_space=pltpu.VMEM)
    large = pl.BlockSpec(memory_space=pl.ANY)
    raw = pl.pallas_call(
        functools.partial(kernel, z, names),
        out_shape=list(outs.values()),
        in_specs=[large] * len(ins),
        out_specs=[whole] * len(outs),
        scratch_shapes=list(scratch.values()),
        compiler_params=pltpu.CompilerParams(
            collective_id=0, has_side_effects=True, vmem_limit_bytes=z.limit
        ),
    )(*ins.values())

    shapes = [
        ((N, D), BF16), ((N, D), BF16), ((D,), F32), ((rows, 2, C), F32), ((S // ntn, rows), F32), ((H, rows), F32),
        ((z.K, C), F32), ((C,), F32), ((z.K, S), F32), ((S,), F32), ((H,), F32), ((H,), F32), ((H,), F32),
        ((C,), F32), ((rows, C), F32),
    ]
    outs = pl.pallas_call(
        functools.partial(finishing, z),
        out_shape=[jax.ShapeDtypeStruct(*shape) for shape in shapes],
        in_specs=[whole] * 6,
        out_specs=[large] * 2 + [whole] * (len(shapes) - 2),
        scratch_shapes=[vmem((LANES, LANES), F32), dma((2,))],
        compiler_params=pltpu.CompilerParams(vmem_limit_bytes=z.limit),
    )(*[pltpu.with_memory_space_constraint(value, pltpu.VMEM) for value in raw])
    (block_out, input_grad, norm, heads, shared, step, taps, bias, staps, sbias, dsb, drate, dskip, gain, outw) = outs
    return (
        narrow(block_out).reshape(hidden_in.shape),
        narrow(input_grad).reshape(hidden_in.shape),
        narrow(norm),
        heads, shared.T, step.T, taps, bias, staps, sbias, dsb, drate, dskip, gain, outw.T,
    )


def solution(mesh):
    nd, nc, ntn = (mesh.shape[name] for name in ("dp", "context", "tensor"))

    def body(*args):
        hidden, heads, shared = args[0], args[3], args[4]
        micro, seqs, tokens, width = hidden.shape
        rows = heads.shape[0]
        rp = -(-rows // 16) * 16
        inner = heads.shape[2]
        z = types.SimpleNamespace(
            R=micro * seqs, T=tokens, d_true=width, D=rp * nd * nc, rows=rows, rp=rp, nd=nd, nc=nc, ntn=ntn,
            C=inner, H=args[10].shape[0], S=shared.shape[1], K=args[6].shape[0],
            Q=shared.shape[1] // 2, limit=59 << 20,
            SUB=3 if rp % 48 == 0 else 1,
        )
        z.WL = max(inner + z.S, z.D, LANES + inner)
        return on_device(z, *args)

    return jax.shard_map(
        body,
        mesh=mesh,
        in_specs=(
            P(None, "dp", "context", None),
            P(None, "dp", None),
            P(),
            P(("dp", "context"), None, "tensor"),
            P(("dp", "context"), None),
            P(("dp", "context"), "tensor"),
            P(None, "tensor"),
            P("tensor"),
            P(),
            P(),
            P("tensor"),
            P("tensor"),
            P("tensor"),
            P("tensor"),
            P("tensor", ("dp", "context")),
            P(None, "dp", "context", None),
        ),
        out_specs=(
            P(None, "dp", "context", None),
            P(None, "dp", "context", None),
            P(),
            P(("dp", "context"), None, "tensor"),
            P(("dp", "context"), "tensor"),
            P(("dp", "context"), "tensor"),
            P(None, "tensor"),
            P("tensor"),
            P(),
            P(),
            P("tensor"),
            P("tensor"),
            P("tensor"),
            P("tensor"),
            P("tensor", ("dp", "context")),
        ),
        check_vma=False,
    )
```
